32 devices in a mesh: dp: 2 (over x), ctx: 4 (over y, core), mp: 4 (over z).
Axes of the slice: x: 2, y: 2, z: 4, core: 2. Of those that a mesh axis runs over, the one named last changes fastest.
Arguments:
- hidden_in: bfloat16 [2, 1024, 2560], P('dp', 'ctx'), may hold values from -6 to 6
- cotangent: bfloat16 [2, 1024, 2560], P('dp', 'ctx'), may hold values from -6 to 6
- lengths: int32 [2], P('dp'), may hold values from 1024 to 1024, as said below
- norm_attn: bfloat16 [2560], P(('dp', 'ctx')), may hold values from 0.099609375 to 1.8984375
- w_query: bfloat16 [2560, 2560], P(('dp', 'ctx'), 'mp'), may hold values from -0.15625 to 0.15625
- w_key: bfloat16 [2560, 640], P(('dp', 'ctx'), 'mp'), may hold values from -0.125 to 0.125
- w_value: bfloat16 [2560, 640], P(('dp', 'ctx'), 'mp'), may hold values from -0.125 to 0.125
- w_output: bfloat16 [2560, 2560], P('mp', ('dp', 'ctx')), may hold values from -0.5 to 0.5
- norm_mlp: bfloat16 [2560], P(('dp', 'ctx')), may hold values from 0.099609375 to 1.8984375
- w_gate: bfloat16 [2560, 7168], P(('dp', 'ctx'), 'mp'), may hold values from -0.125 to 0.125
- w_up: bfloat16 [2560, 7168], P(('dp', 'ctx'), 'mp'), may hold values from -0.125 to 0.125
- w_down: bfloat16 [7168, 2560], P('mp', ('dp', 'ctx')), may hold values from -0.0625 to 0.0625
Outputs:
- layer_out: bfloat16 [2, 1024, 2560], P('dp', 'ctx')
- input_grad: bfloat16 [2, 1024, 2560], P('dp', 'ctx')
- grad_norm_attn: float32 [2560], P(('dp', 'ctx'))
- grad_query: float32 [2560, 2560], P(('dp', 'ctx'), 'mp')
- grad_key: float32 [2560, 640], P(('dp', 'ctx'), 'mp')
- grad_value: float32 [2560, 640], P(('dp', 'ctx'), 'mp')
- grad_output: float32 [2560, 2560], P('mp', ('dp', 'ctx'))
- grad_norm_mlp: float32 [2560], P(('dp', 'ctx'))
- grad_gate: float32 [2560, 7168], P(('dp', 'ctx'), 'mp')
- grad_up: float32 [2560, 7168], P(('dp', 'ctx'), 'mp')
- grad_down: float32 [7168, 2560], P('mp', ('dp', 'ctx'))
The draws below stay inside these ranges and needn't reach their ends.
Inputs may be any that keep to these rules, and one draw needn't show every extreme that they name: `lengths`: among the 1 sequence of each index of dp (sequences s with the same s) one is longer than 768; at least one sequence in all has length 1024.
All inputs are finite; a program needn't handle non-finite values.
Results may differ from the reference program's by a relative error of at most 0.017.
Values may be sent and summed in bfloat16 or wider, within the bound.
A program may use at most 256 MiB of HBM per device.

```python
import math
import jax
import jax.numpy as jnp
from jax import lax

D = 2560
HEADS = 32
KV_HEADS = 8
HEAD = 80
FF = 7168
SEQ_DP = 1
SLOT_DEV = 256
MIN_LEN = 1024
SEQS = 2
SLOTS = 1024


def draw_lengths(key, part):
    key = jax.random.fold_in(key, 29)
    key_near, key_base, key_top, key_pick = jax.random.split(key, 4)
    group_count = SEQS // SEQ_DP
    drawn_len = jax.random.randint(key_base, (group_count, SEQ_DP), MIN_LEN, SLOTS + 1)
    near_low = max(MIN_LEN, SLOTS - SLOT_DEV + 1)
    near_len = jax.random.randint(key_near, (group_count, 1), near_low, SLOTS + 1)
    chosen = jax.random.randint(key_pick, (group_count, 1), 0, SEQ_DP)
    top_group = jax.random.randint(key_top, (), 0, group_count)
    group_len = jnp.where(jnp.arange(group_count)[:, None] == top_group, SLOTS, near_len)
    picked = jnp.arange(SEQ_DP)[None, :] == chosen
    return jnp.where(picked, group_len, drawn_len).reshape(SEQS).astype(jnp.int32)


def block_levels(rng, extent, cuts, smallest, top_value):
    factor_of = 1.0
    for position, parts in cuts:
        draws = jax.random.uniform(jax.random.fold_in(jax.random.fold_in(rng, 6), position), (parts,), jnp.float32, smallest / len(cuts), top_value / len(cuts))
        factor_of = factor_of * jnp.repeat(jnp.exp(draws), extent[position] // parts).reshape((-1,) + (1,) * (len(extent) - 1 - position))
    return factor_of


def centred(own_key, shape, scale, bound, shards=(), kind=jnp.bfloat16):
    entries = scale * jax.random.normal(own_key, shape, jnp.float32)
    if shards:
        entries = entries * block_levels(own_key, shape, shards, -0.22, 0.18)
    return jnp.clip(entries, -bound, bound).astype(kind)


def setup_inputs(seed: int = 0) -> dict:
    streams_of = jax.random.split(jax.random.key(seed), 13)
    hidden_in = centred(streams_of[0], (SEQS, SLOTS, D), 1.0, 6.0, ((0, 2), (1, 4)))
    cotangent = centred(streams_of[1], (SEQS, SLOTS, D), 1.0, 6.0, ((0, 2), (1, 4)))
    lengths = draw_lengths(jax.random.fold_in(streams_of[12], 71), 0)
    norm_attn = jnp.clip(1.0 + 0.18 * jax.random.normal(streams_of[3], (D,), jnp.float32), 0.099609375, 1.8984375).astype(jnp.bfloat16)
    w_query = centred(streams_of[4], (D, HEADS * HEAD), (D // 2) ** -0.5, 0.15625, ((0, 8), (1, 4)))
    w_key = centred(streams_of[5], (D, KV_HEADS * HEAD), D ** -0.5, 0.125, ((0, 8), (1, 4)))
    w_value = centred(streams_of[6], (D, KV_HEADS * HEAD), D ** -0.5, 0.125, ((0, 8), (1, 4)))
    w_output = centred(streams_of[7], (HEADS * HEAD, D), (HEADS * HEAD // 16) ** -0.5, 0.5, ((0, 4), (1, 8)))
    norm_mlp = jnp.clip(1.0 + 0.18 * jax.random.normal(streams_of[8], (D,), jnp.float32), 0.099609375, 1.8984375).astype(jnp.bfloat16)
    w_gate = centred(streams_of[9], (D, FF), D ** -0.5, 0.125, ((0, 8), (1, 4)))
    w_up = centred(streams_of[10], (D, FF), D ** -0.5, 0.125, ((0, 8), (1, 4)))
    w_down = centred(streams_of[11], (FF, D), FF ** -0.5, 0.0625, ((0, 4), (1, 8)))
    return dict(hidden_in=hidden_in, cotangent=cotangent, lengths=lengths, norm_attn=norm_attn, w_query=w_query, w_key=w_key, w_value=w_value, w_output=w_output, norm_mlp=norm_mlp, w_gate=w_gate, w_up=w_up, w_down=w_down)


EPS = 1e-05
THETA = 1000000.0
NEG = -1e+30
BEST = lax.Precision.HIGHEST

@jax.custom_vjp
def low(v):
    return lax.optimization_barrier(v.astype(jnp.bfloat16)).astype(jnp.float32)

@jax.custom_vjp
def low_back(v):
    return v

def low_keep(v):
    return (low(v), None)

def low_pass(kept, grad):
    return (grad,)

def back_keep(v):
    return (v, None)

def back_low(kept, grad):
    return (low(grad),)
low.defvjp(low_keep, low_pass)
low_back.defvjp(back_keep, back_low)

def rope_tables(places, head_size):
    half = head_size // 2
    freq = THETA ** (-(jnp.arange(half, dtype=jnp.float32) * 2.0 / head_size))
    angle = places[:, None] * freq[None, :]
    return (jnp.cos(angle), jnp.sin(angle))

def rotate(tensor, cosine, sine_table):
    half = tensor.shape[-1] // 2
    first_half = tensor[..., :half]
    second_half = tensor[..., half:]
    cos_b = cosine[:, None, :]
    sin_b = sine_table[:, None, :]
    return jnp.concatenate([first_half * cos_b - second_half * sin_b, second_half * cos_b + first_half * sin_b], axis=-1)

def normed(tensor, gain_row):
    return tensor * lax.rsqrt(lax.optimization_barrier(jnp.mean(tensor * tensor, axis=-1, keepdims=True)) + EPS) * gain_row

def matmul(left_side, right_side):
    return jnp.dot(left_side, right_side, precision=BEST)

def layer(inputs, length, gain_attn, query_w, key_w, value_w, output_w, gain_mlp, gate_w, up_w, down_w):
    slot_count = inputs.shape[0]
    group_size = HEADS // KV_HEADS
    places = jnp.arange(slot_count, dtype=jnp.int32)
    cosine, sine_table = rope_tables(places.astype(inputs.dtype), HEAD)
    normed_one = low(normed(inputs, gain_attn))
    query_proj = low_back(matmul(normed_one, query_w)).reshape(slot_count, HEADS, HEAD)
    key_proj = low_back(matmul(normed_one, key_w)).reshape(slot_count, KV_HEADS, HEAD)
    value_low = low(low_back(matmul(normed_one, value_w))).reshape(slot_count, KV_HEADS, HEAD)
    query_low = low(rotate(query_proj, cosine, sine_table)).reshape(slot_count, KV_HEADS, group_size, HEAD)
    key_low = low(rotate(key_proj, cosine, sine_table))
    block_rows = math.gcd(slot_count, 512)

    def attend_block(block_start):
        query_blk = lax.dynamic_slice_in_dim(query_low, block_start, block_rows, 0)
        query_places = block_start + jnp.arange(block_rows, dtype=jnp.int32)
        raw_scores = jnp.einsum('bkgh,tkh->kgbt', query_blk, key_low, precision=BEST) * HEAD ** (-0.5)
        allowed = (places[None, :] <= query_places[:, None]) & (places[None, :] < length)
        scores = low_back(jnp.where(allowed[None, None], raw_scores, NEG))
        row_max = lax.optimization_barrier(jnp.max(scores, axis=-1, keepdims=True))
        exponent = jnp.exp(scores - row_max)
        attention = low(exponent / lax.optimization_barrier(jnp.sum(exponent, axis=-1, keepdims=True)))
        mixed_heads = jnp.einsum('kgbt,tkh->bkgh', attention, value_low, precision=BEST)
        return mixed_heads.reshape(block_rows, HEADS * HEAD)
    starts = jnp.arange(slot_count // block_rows, dtype=jnp.int32) * block_rows
    mixed_all = lax.map(jax.checkpoint(attend_block), starts).reshape(slot_count, HEADS * HEAD)
    attn_low = low(low_back(mixed_all))
    branch = low_back(matmul(attn_low, output_w))
    middle = inputs + branch
    normed_two = low(normed(middle, gain_mlp))
    gate_proj = low_back(matmul(normed_two, gate_w))
    up_proj = low_back(matmul(normed_two, up_w))
    hidden = low(jax.nn.silu(gate_proj) * up_proj)
    mlp_out = low_back(matmul(hidden, down_w))
    valid_mask = (places < length).astype(inputs.dtype)[:, None]
    return valid_mask * (middle + mlp_out)

def reference(hidden_in, cotangent, lengths, norm_attn, w_query, w_key, w_value, w_output, norm_mlp, w_gate, w_up, w_down):
    weights_f = tuple((weight_one.astype(jnp.float32) for weight_one in (norm_attn, w_query, w_key, w_value, w_output, norm_mlp, w_gate, w_up, w_down)))

    def per_sequence(totals, members):
        inputs, grad_seq, length = members

        def applied(values_in, *weight_args):
            return layer(values_in, length, *weight_args)
        result, pullback = jax.vjp(applied, inputs, *weights_f)
        gradients = pullback(grad_seq)
        summed = tuple((total_one + grad_one for total_one, grad_one in zip(totals, gradients[1:])))
        return (summed, (result, gradients[0]))
    zeros_init = tuple((jnp.zeros(weight_one.shape, jnp.float32) for weight_one in weights_f))
    totals, (outputs, grad_inputs) = lax.scan(per_sequence, zeros_init, (hidden_in.astype(jnp.float32), cotangent.astype(jnp.float32), lengths))
    return (outputs.astype(jnp.bfloat16), grad_inputs.astype(jnp.bfloat16), totals[0], totals[1], totals[2], totals[3], totals[4], totals[5], totals[6], totals[7], totals[8])
```

```python
import jax
import jax.numpy as jnp
from jax import lax
from jax.sharding import PartitionSpec as P

HEAD = 80


EPS = 1e-05
THETA = 1000000.0
NEG = -1e30


def rope_tables(places, head_size):
    half = head_size // 2
    freq = THETA ** (-(jnp.arange(half, dtype=jnp.float32) * 2.0 / head_size))
    angle = places[:, None] * freq[None, :]
    return (jnp.cos(angle), jnp.sin(angle))


def rotate(tensor, cosine, sine_table):
    half = tensor.shape[-1] // 2
    first_half = tensor[..., :half]
    second_half = tensor[..., half:]
    cos_b = cosine[:, None, :]
    sin_b = sine_table[:, None, :]
    return jnp.concatenate(
        [first_half * cos_b - second_half * sin_b, second_half * cos_b + first_half * sin_b],
        axis=-1,
    )


def rotate_back(tensor, cosine, sine_table):
    half = tensor.shape[-1] // 2
    first_half = tensor[..., :half]
    second_half = tensor[..., half:]
    cos_b = cosine[:, None, :]
    sin_b = sine_table[:, None, :]
    return jnp.concatenate(
        [first_half * cos_b + second_half * sin_b, second_half * cos_b - first_half * sin_b],
        axis=-1,
    )


def normed(tensor, gain_row):
    return tensor * lax.rsqrt(jnp.mean(tensor * tensor, axis=-1, keepdims=True) + EPS) * gain_row


def norm_back(tensor, gain_row, grad_normed):
    scale_row = lax.rsqrt(jnp.mean(tensor * tensor, axis=-1, keepdims=True) + EPS)
    grad_scaled = grad_normed * gain_row
    grad_tensor = scale_row * grad_scaled - tensor * scale_row**3 * jnp.mean(
        grad_scaled * tensor, axis=-1, keepdims=True
    )
    grad_gain = jnp.sum(grad_normed * tensor * scale_row, axis=0)
    return (grad_tensor, grad_gain)


def masked_scores(query_seq, key_seq, length, places, kv_heads, group_size):
    query_grp = query_seq.reshape(query_seq.shape[0], kv_heads, group_size, HEAD)
    key_grp = key_seq.reshape(key_seq.shape[0], kv_heads, HEAD)
    raw_scores = jnp.einsum(
        "bkgh,tkh->kgbt", query_grp, key_grp, preferred_element_type=jnp.float32
    ) * HEAD ** (-0.5)
    key_places = jnp.arange(key_grp.shape[0], dtype=jnp.int32)
    allowed = (key_places[None, :] <= places[:, None]) & (key_places[None, :] < length)
    return jnp.where(allowed[None, None], raw_scores, NEG)


def any_mesh(
    hidden_in,
    cotangent,
    lengths,
    norm_attn,
    w_query,
    w_key,
    w_value,
    w_output,
    norm_mlp,
    w_gate,
    w_up,
    w_down,
):
    seq_count, slot_count, width_all = hidden_in.shape
    tok_rows = seq_count * slot_count
    attn_set = (
        lax.all_gather(w_query, ("dp", "ctx"), axis=0, tiled=True),
        lax.all_gather(w_key, ("dp", "ctx"), axis=0, tiled=True),
        lax.all_gather(w_value, ("dp", "ctx"), axis=0, tiled=True),
        lax.all_gather(w_output, ("dp", "ctx"), axis=1, tiled=True),
        lax.all_gather(norm_attn, ("dp", "ctx"), axis=0, tiled=True),
    )
    query_w, key_w, value_w, output_w, gain_attn = attn_set
    q_heads = query_w.shape[1] // HEAD
    kv_heads = key_w.shape[1] // HEAD
    group_size = q_heads // kv_heads
    first_slot = lax.axis_index("ctx") * slot_count
    places = first_slot + jnp.arange(slot_count, dtype=jnp.int32)
    valid_mask = (places[None, :] < lengths[:, None]).astype(jnp.float32).reshape(tok_rows, 1)
    cosine, sine_table = rope_tables(places.astype(jnp.float32), HEAD)
    inputs = hidden_in.reshape(tok_rows, width_all).astype(jnp.float32)
    gain_one = gain_attn.astype(jnp.float32)
    normed_one = normed(inputs, gain_one).astype(jnp.bfloat16)
    query_proj = jnp.dot(normed_one, query_w, preferred_element_type=jnp.float32).reshape(
        seq_count, slot_count, q_heads, HEAD
    )
    key_proj = jnp.dot(normed_one, key_w, preferred_element_type=jnp.float32).reshape(
        seq_count, slot_count, kv_heads, HEAD
    )
    value_low = (
        jnp.dot(normed_one, value_w, preferred_element_type=jnp.float32)
        .astype(jnp.bfloat16)
        .reshape(seq_count, slot_count, kv_heads * HEAD)
    )
    query_low = rotate(query_proj, cosine, sine_table).astype(jnp.bfloat16)
    key_low = (
        rotate(key_proj, cosine, sine_table)
        .astype(jnp.bfloat16)
        .reshape(seq_count, slot_count, kv_heads * HEAD)
    )
    key_all, value_all = (
        lax.all_gather(key_low, "ctx", axis=1, tiled=True),
        lax.all_gather(value_low, "ctx", axis=1, tiled=True),
    )

    def attend(members):
        query_seq, key_seq, value_seq, length = members
        scores = masked_scores(query_seq, key_seq, length, places, kv_heads, group_size)
        row_max = jnp.max(scores, axis=-1, keepdims=True)
        exponent = jnp.exp(scores - row_max)
        total = jnp.sum(exponent, axis=-1, keepdims=True)
        attention = (exponent / total).astype(jnp.bfloat16)
        value_grp = value_seq.reshape(value_seq.shape[0], kv_heads, HEAD)
        mixed_heads = jnp.einsum(
            "kgbt,tkh->bkgh", attention, value_grp, preferred_element_type=jnp.float32
        )
        return (mixed_heads.reshape(slot_count, q_heads * HEAD), (row_max + jnp.log(total))[..., 0])

    mixed_all, log_total = lax.map(attend, (query_low, key_all, value_all, lengths))
    attn_low = mixed_all.reshape(tok_rows, q_heads * HEAD).astype(jnp.bfloat16)
    branch = lax.psum(jnp.dot(attn_low, output_w, preferred_element_type=jnp.float32), "mp")
    middle = inputs + branch
    mlp_set = (
        lax.all_gather(w_gate, ("dp", "ctx"), axis=0, tiled=True),
        lax.all_gather(w_up, ("dp", "ctx"), axis=0, tiled=True),
        lax.all_gather(w_down, ("dp", "ctx"), axis=1, tiled=True),
        lax.all_gather(norm_mlp, ("dp", "ctx"), axis=0, tiled=True),
    )
    gate_w, up_w, down_w, gain_mlp = mlp_set
    gain_two = gain_mlp.astype(jnp.float32)
    normed_two = normed(middle, gain_two).astype(jnp.bfloat16)
    gate_proj = jnp.dot(normed_two, gate_w, preferred_element_type=jnp.float32)
    up_proj = jnp.dot(normed_two, up_w, preferred_element_type=jnp.float32)
    hidden = (jax.nn.silu(gate_proj) * up_proj).astype(jnp.bfloat16)
    mlp_out = lax.psum(
        jnp.dot(hidden, down_w, preferred_element_type=jnp.float32).astype(jnp.bfloat16), "mp"
    ).astype(jnp.float32)
    layer_out = (
        (valid_mask * (middle + mlp_out))
        .astype(jnp.bfloat16)
        .reshape(seq_count, slot_count, width_all)
    )
    grad_out = valid_mask * cotangent.reshape(tok_rows, width_all).astype(jnp.float32)
    grad_mlp = grad_out.astype(jnp.bfloat16)
    gate_back, up_back, down_back, gain_mlp_back = (
        lax.all_gather(w_gate, ("dp", "ctx"), axis=0, tiled=True),
        lax.all_gather(w_up, ("dp", "ctx"), axis=0, tiled=True),
        lax.all_gather(w_down, ("dp", "ctx"), axis=1, tiled=True),
        lax.all_gather(norm_mlp, ("dp", "ctx"), axis=0, tiled=True),
    )
    grad_hidden = jnp.einsum("tm,fm->tf", grad_mlp, down_back, preferred_element_type=jnp.float32)
    grad_down = jnp.einsum("tf,tm->fm", hidden, grad_mlp, preferred_element_type=jnp.float32)
    sigmoid_gate = jax.nn.sigmoid(gate_proj)
    grad_gate_low = (
        grad_hidden * up_proj * sigmoid_gate * (1.0 + gate_proj * (1.0 - sigmoid_gate))
    ).astype(jnp.bfloat16)
    grad_up_low = (grad_hidden * gate_proj * sigmoid_gate).astype(jnp.bfloat16)
    grad_gate = jnp.einsum(
        "td,tf->df", normed_two, grad_gate_low, preferred_element_type=jnp.float32
    )
    grad_up = jnp.einsum("td,tf->df", normed_two, grad_up_low, preferred_element_type=jnp.float32)
    partial_two = jnp.einsum(
        "tf,df->td", grad_gate_low, gate_back, preferred_element_type=jnp.float32
    ) + jnp.einsum("tf,df->td", grad_up_low, up_back, preferred_element_type=jnp.float32)
    grad_normed_two = lax.psum(partial_two, "mp")
    grad_middle_norm, grad_gain_two = norm_back(
        middle, gain_mlp_back.astype(jnp.float32), grad_normed_two
    )
    mlp_grads = (
        lax.psum_scatter(grad_gate, ("dp", "ctx"), scatter_dimension=0, tiled=True),
        lax.psum_scatter(grad_up, ("dp", "ctx"), scatter_dimension=0, tiled=True),
        lax.psum_scatter(grad_down, ("dp", "ctx"), scatter_dimension=1, tiled=True),
        lax.psum_scatter(grad_gain_two, ("dp", "ctx"), scatter_dimension=0, tiled=True),
    )
    grad_middle = grad_out + grad_middle_norm
    grad_branch = grad_middle.astype(jnp.bfloat16)
    query_back, key_back, value_back, output_back, gain_attn_back = (
        lax.all_gather(w_query, ("dp", "ctx"), axis=0, tiled=True),
        lax.all_gather(w_key, ("dp", "ctx"), axis=0, tiled=True),
        lax.all_gather(w_value, ("dp", "ctx"), axis=0, tiled=True),
        lax.all_gather(w_output, ("dp", "ctx"), axis=1, tiled=True),
        lax.all_gather(norm_attn, ("dp", "ctx"), axis=0, tiled=True),
    )
    grad_output = jnp.einsum("tq,td->qd", attn_low, grad_branch, preferred_element_type=jnp.float32)
    grad_attn_low = (
        jnp.einsum("td,qd->tq", grad_branch, output_back, preferred_element_type=jnp.float32)
        .astype(jnp.bfloat16)
        .reshape(seq_count, slot_count, q_heads, HEAD)
    )

    def attend_back(members):
        query_seq, key_seq, value_seq, length, log_seq, grad_seq = members
        scores = masked_scores(query_seq, key_seq, length, places, kv_heads, group_size)
        attention = jnp.exp(scores - log_seq[..., None])
        query_grp = query_seq.reshape(slot_count, kv_heads, group_size, HEAD)
        key_grp = key_seq.reshape(key_seq.shape[0], kv_heads, HEAD)
        value_grp = value_seq.reshape(value_seq.shape[0], kv_heads, HEAD)
        grad_grp = grad_seq.reshape(slot_count, kv_heads, group_size, HEAD)
        grad_attention = jnp.einsum(
            "bkgh,tkh->kgbt", grad_grp, value_grp, preferred_element_type=jnp.float32
        )
        inner = jnp.sum(attention * grad_attention, axis=-1, keepdims=True)
        grad_scores = (attention * (grad_attention - inner)).astype(jnp.bfloat16)
        scale_qk = HEAD ** (-0.5)
        grad_query_seq = (
            jnp.einsum("kgbt,tkh->bkgh", grad_scores, key_grp, preferred_element_type=jnp.float32)
            * scale_qk
        )
        grad_key_seq = (
            jnp.einsum("kgbt,bkgh->tkh", grad_scores, query_grp, preferred_element_type=jnp.float32)
            * scale_qk
        )
        grad_value_seq = jnp.einsum(
            "kgbt,bkgh->tkh",
            attention.astype(jnp.bfloat16),
            grad_grp,
            preferred_element_type=jnp.float32,
        )
        key_rows = key_grp.shape[0]
        return (
            grad_query_seq.reshape(slot_count, q_heads, HEAD),
            grad_key_seq.reshape(key_rows, kv_heads * HEAD),
            grad_value_seq.reshape(key_rows, kv_heads * HEAD),
        )

    grad_query_rot, grad_key_all, grad_value_all = lax.map(
        attend_back, (query_low, key_all, value_all, lengths, log_total, grad_attn_low)
    )
    grad_key_rot, grad_value_rot = (
        lax.psum_scatter(grad_key_all, "ctx", scatter_dimension=1, tiled=True),
        lax.psum_scatter(grad_value_all, "ctx", scatter_dimension=1, tiled=True),
    )
    grad_query_low = (
        rotate_back(grad_query_rot, cosine, sine_table)
        .astype(jnp.bfloat16)
        .reshape(tok_rows, q_heads * HEAD)
    )
    grad_key_low = (
        rotate_back(grad_key_rot.reshape(seq_count, slot_count, kv_heads, HEAD), cosine, sine_table)
        .astype(jnp.bfloat16)
        .reshape(tok_rows, kv_heads * HEAD)
    )
    grad_value_low = grad_value_rot.astype(jnp.bfloat16).reshape(tok_rows, kv_heads * HEAD)
    grad_query = jnp.einsum(
        "td,tq->dq", normed_one, grad_query_low, preferred_element_type=jnp.float32
    )
    grad_key = jnp.einsum("td,tq->dq", normed_one, grad_key_low, preferred_element_type=jnp.float32)
    grad_value = jnp.einsum(
        "td,tq->dq", normed_one, grad_value_low, preferred_element_type=jnp.float32
    )
    partial_one = jnp.einsum(
        "tq,dq->td", grad_query_low, query_back, preferred_element_type=jnp.float32
    )
    partial_one = partial_one + jnp.einsum(
        "tq,dq->td", grad_key_low, key_back, preferred_element_type=jnp.float32
    )
    partial_one = partial_one + jnp.einsum(
        "tq,dq->td", grad_value_low, value_back, preferred_element_type=jnp.float32
    )
    grad_normed_one = lax.psum(partial_one, "mp")
    grad_inputs_norm, grad_gain_one = norm_back(
        inputs, gain_attn_back.astype(jnp.float32), grad_normed_one
    )
    input_grad = (
        (grad_middle + grad_inputs_norm)
        .astype(jnp.bfloat16)
        .reshape(seq_count, slot_count, width_all)
    )
    attn_grads = (
        lax.psum_scatter(grad_query, ("dp", "ctx"), scatter_dimension=0, tiled=True),
        lax.psum_scatter(grad_key, ("dp", "ctx"), scatter_dimension=0, tiled=True),
        lax.psum_scatter(grad_value, ("dp", "ctx"), scatter_dimension=0, tiled=True),
        lax.psum_scatter(grad_output, ("dp", "ctx"), scatter_dimension=1, tiled=True),
        lax.psum_scatter(grad_gain_one, ("dp", "ctx"), scatter_dimension=0, tiled=True),
    )
    return (
        layer_out,
        input_grad,
        attn_grads[4],
        attn_grads[0],
        attn_grads[1],
        attn_grads[2],
        attn_grads[3],
        mlp_grads[3],
        mlp_grads[0],
        mlp_grads[1],
        mlp_grads[2],
    )


CORE_SWAP = [(0, 1), (1, 0), (2, 3), (3, 2)]
Y_SWAP = [(0, 2), (1, 3), (2, 0), (3, 1)]
X_SWAP = [(0, 1), (1, 0)]


def over_core(tensor):
    return lax.ppermute(tensor, "ctx", CORE_SWAP)


class Link:
    def __init__(self, axis, pairs):
        self.axis, self.pairs, self.sent = axis, pairs, []

    def send(self, tensor):
        if len(self.sent) >= 2:
            tensor, _ = lax.optimization_barrier((tensor, self.sent[-2]))
        got = lax.ppermute(tensor, self.axis, self.pairs)
        self.sent.append(got)
        return got


def on_plane(
    hidden_in,
    cotangent,
    lengths,
    norm_attn,
    w_query,
    w_key,
    w_value,
    w_output,
    norm_mlp,
    w_gate,
    w_up,
    w_down,
):
    low = jnp.bfloat16
    f32 = jnp.float32
    _, rows, width = hidden_in.shape
    part = w_query.shape[0]
    chip_part = 2 * part
    x_at, ctx_at, z_at = lax.axis_index("dp"), lax.axis_index("ctx"), lax.axis_index("mp")
    y_at, core = ctx_at // 2, ctx_at % 2
    first = core == 0
    place = 2 * x_at + y_at
    z_count = lax.axis_size("mp")
    owned = rows // z_count
    x_link, y_link = Link("dp", X_SWAP), Link("ctx", Y_SWAP)

    def relative(tensor):
        return jnp.concatenate(
            [
                lax.dynamic_slice_in_dim(tensor, (place ^ turn) * chip_part, chip_part, axis=-1)
                for turn in range(4)
            ],
            axis=-1,
        )

    def both(mine, other, axis):
        return jnp.where(
            first,
            jnp.concatenate([mine, other], axis=axis),
            jnp.concatenate([other, mine], axis=axis),
        )

    def half(tensor, which, axis):
        size = tensor.shape[axis] // 2
        return lax.dynamic_slice_in_dim(tensor, which * size, size, axis=axis)

    def cut(tensor, turn):
        return tensor[..., turn * chip_part : (turn + 1) * chip_part]

    def chip_block(pieces, split_axis, join_axis):
        keep = jnp.concatenate([half(piece, core, split_axis) for piece in pieces], axis=1)
        give = jnp.concatenate([half(piece, 1 - core, split_axis) for piece in pieces], axis=1)
        return both(keep, over_core(give), join_axis)

    def gather(block):
        middle = block.shape[0] // 2
        from_x = x_link.send(block)
        from_y = y_link.send(block)
        upper = y_link.send(from_x[:middle])
        lower = x_link.send(from_y[middle:])
        return [block, from_y, from_x, jnp.concatenate([upper, lower], axis=0)]

    def scatter(parts):
        own, for_y, for_x, for_far = parts
        middle = own.shape[0] // 2
        upper = x_link.send(for_far[:middle].astype(low))
        lower = y_link.send(for_far[middle:].astype(low))
        x_one = x_link.send(for_x[:middle].astype(low))
        y_two = y_link.send(for_y[middle:].astype(low))
        y_one = y_link.send((for_y[:middle] + upper.astype(f32)).astype(low))
        x_two = x_link.send((for_x[middle:] + lower.astype(f32)).astype(low))
        return jnp.concatenate(
            [
                own[:middle] + x_one.astype(f32) + y_one.astype(f32),
                own[middle:] + x_two.astype(f32) + y_two.astype(f32),
            ],
            axis=0,
        )

    def token_sum(total):
        mine = half(total, core, 0)
        mine = mine + over_core(half(total, 1 - core, 0).astype(low)).astype(f32)
        came_up = came_down = None

        def block(at):
            return lax.dynamic_slice_in_dim(mine, at * owned, owned, axis=0)

        last = z_count - 1
        for step in range(last):
            up = block(jnp.clip(last - step + z_at, 0, last))
            down = block(jnp.clip(z_at - last + step, 0, last))
            if step:
                up, down = up + came_up.astype(f32), down + came_down.astype(f32)
            came_up = lax.ppermute(up.astype(low), "mp", [(z, z + 1) for z in range(step + 1)])
            came_down = lax.ppermute(
                down.astype(low), "mp", [(last - z, last - z - 1) for z in range(step + 1)]
            )
        return block(z_at) + came_up.astype(f32) + came_down.astype(f32)

    def token_gather(piece):
        last = z_count - 1
        out = jnp.zeros((rows, piece.shape[1]), piece.dtype)
        out = lax.dynamic_update_slice_in_dim(out, piece, z_at * owned, axis=0)
        up = down = piece
        for step in range(last):
            up = lax.ppermute(up, "mp", [(z, z + 1) for z in range(step, last)])
            down = lax.ppermute(down, "mp", [(z + 1, z) for z in range(0, last - step)])
            at_up, at_down = z_at - 1 - step, z_at + 1 + step
            safe_up = jnp.maximum(at_up, 0) * owned
            old = lax.dynamic_slice_in_dim(out, safe_up, owned, axis=0)
            out = lax.dynamic_update_slice_in_dim(
                out, jnp.where(at_up >= 0, up, old), safe_up, axis=0
            )
            safe_down = jnp.minimum(at_down, last) * owned
            old = lax.dynamic_slice_in_dim(out, safe_down, owned, axis=0)
            out = lax.dynamic_update_slice_in_dim(
                out, jnp.where(at_down <= last, down, old), safe_down, axis=0
            )
        return out

    def matmul(left, right, dims):
        return lax.dot_general(left, right, (dims, ((), ())), preferred_element_type=f32)

    nn, nt, tn = ((1,), (0,)), ((1,), (1,)), ((0,), (0,))

    gains = both(*(lambda g: (g, over_core(g)))(jnp.stack([norm_attn, norm_mlp])), 1)
    gains_x = lax.ppermute(gains, "dp", X_SWAP)
    gains_y = lax.ppermute(gains, "ctx", Y_SWAP)
    gains_far = lax.ppermute(gains_x, "ctx", Y_SWAP)
    gains_all = jnp.concatenate([gains, gains_y, gains_x, gains_far], axis=1).astype(f32)
    gain_one, gain_two = gains_all[0], gains_all[1]

    qkv_w = gather(chip_block((w_query, w_key, w_value), 1, 0))
    out_w = gather(chip_block((w_output,), 0, 1))
    gu_w = gather(chip_block((w_gate, w_up), 1, 0))
    down_w = gather(chip_block((w_down,), 0, 1))

    length = lengths[0]
    inputs = relative(hidden_in[0]).astype(f32)
    h1_mine = normed(inputs, gain_one).astype(low)
    h1 = both(h1_mine, over_core(h1_mine), 0)
    slots = (y_at * 2) * rows + jnp.arange(2 * rows, dtype=jnp.int32)
    my_slots = ctx_at * rows + jnp.arange(rows, dtype=jnp.int32)
    valid = (my_slots < length).astype(f32)[:, None]
    dout = valid * relative(cotangent[0]).astype(f32)
    dm_mine = dout.astype(low)
    dm = both(dm_mine, over_core(dm_mine), 0)
    cosine, sine = rope_tables(slots.astype(f32), HEAD)

    qkv = sum(matmul(cut(h1, turn), qkv_w[turn], nn) for turn in (0, 2, 1, 3))
    heads = w_query.shape[1] // HEAD // 2
    kv_heads = w_key.shape[1] // HEAD // 2
    group = heads // kv_heads
    q_cols, k_cols = heads * HEAD, kv_heads * HEAD
    chip_rows = 2 * rows
    q_low = rotate(qkv[:, :q_cols].reshape(chip_rows, heads, HEAD), cosine, sine).astype(low)
    k_low = rotate(
        qkv[:, q_cols : q_cols + k_cols].reshape(chip_rows, kv_heads, HEAD), cosine, sine
    ).astype(low)
    v_low = qkv[:, q_cols + k_cols :].astype(low)
    kv_mine = jnp.concatenate([k_low.reshape(chip_rows, k_cols), v_low], axis=1)
    kv_other = lax.ppermute(kv_mine, "ctx", Y_SWAP)
    kv_all = jnp.where(
        y_at == 0,
        jnp.concatenate([kv_mine, kv_other], axis=0),
        jnp.concatenate([kv_other, kv_mine], axis=0),
    )
    keys = kv_all[:, :k_cols].reshape(2 * chip_rows, kv_heads, HEAD)
    values = kv_all[:, k_cols:].reshape(2 * chip_rows, kv_heads, HEAD)
    q_grp = q_low.reshape(chip_rows, kv_heads, group, HEAD)
    scale = HEAD ** (-0.5)
    raw = jnp.einsum("bkgh,tkh->kgbt", q_grp, keys, preferred_element_type=f32) * scale
    key_slots = jnp.arange(2 * chip_rows, dtype=jnp.int32)
    allowed = (key_slots[None, :] <= slots[:, None]) & (key_slots[None, :] < length)
    scores = jnp.where(allowed[None, None], raw, NEG)
    exponent = jnp.exp(scores - jnp.max(scores, axis=-1, keepdims=True))
    probs = exponent / jnp.sum(exponent, axis=-1, keepdims=True)
    probs_low = probs.astype(low)
    mixed = jnp.einsum("kgbt,tkh->bkgh", probs_low, values, preferred_element_type=f32)
    attn_low = mixed.reshape(chip_rows, q_cols).astype(low)
    branch = token_sum(
        jnp.concatenate([matmul(attn_low, out_w[turn], nn) for turn in range(4)], axis=1)
    )
    inputs_own = lax.dynamic_slice_in_dim(inputs, z_at * owned, owned, axis=0)
    middle = inputs_own + branch
    h2_half = token_gather(normed(middle, gain_two).astype(low))
    h2 = both(h2_half, over_core(h2_half), 0)

    ff = gu_w[0].shape[1] // 2
    gu = sum(matmul(cut(h2, turn), gu_w[turn], nn) for turn in (0, 2, 1, 3))
    gate, up = gu[:, :ff], gu[:, ff:]
    sigma = jax.nn.sigmoid(gate)
    hidden = (gate * sigma * up).astype(low)
    d_hidden = sum(matmul(cut(dm, turn), down_w[turn], nt) for turn in (0, 2, 1, 3))
    d_gate = (d_hidden * up * sigma * (1.0 + gate * (1.0 - sigma))).astype(low)
    d_up = (d_hidden * gate * sigma).astype(low)
    d_gu = jnp.concatenate([d_gate, d_up], axis=1)
    dh2 = token_sum(jnp.concatenate([matmul(d_gu, gu_w[turn], nt) for turn in range(4)], axis=1))
    grad_gu = scatter([matmul(cut(h2, turn), d_gu, tn) for turn in range(4)])
    grad_down = scatter([matmul(hidden, cut(dm, turn), tn) for turn in range(4)])
    mlp = token_sum(jnp.concatenate([matmul(hidden, down_w[turn], nn) for turn in range(4)], axis=1))

    d_norm, gain_two_part = norm_back(middle, gain_two, dh2)
    dout_own = lax.dynamic_slice_in_dim(dout, z_at * owned, owned, axis=0)
    valid_own = lax.dynamic_slice_in_dim(valid, z_at * owned, owned, axis=0)
    d_middle = dout_own + d_norm
    da_half = token_gather(d_middle.astype(low))
    da = both(da_half, over_core(da_half), 0)
    out_half = token_gather((valid_own * (middle + mlp)).astype(low))

    do = sum(matmul(cut(da, turn), out_w[turn], nt) for turn in range(4)).astype(low)
    grad_out = scatter([matmul(attn_low, cut(da, turn), tn) for turn in range(4)])
    do_grp = do.reshape(chip_rows, kv_heads, group, HEAD)
    d_probs = jnp.einsum("bkgh,tkh->kgbt", do_grp, values, preferred_element_type=f32)
    inner = jnp.sum(probs * d_probs, axis=-1, keepdims=True)
    d_scores = (probs * (d_probs - inner)).astype(low)
    dq = jnp.einsum("kgbt,tkh->bkgh", d_scores, keys, preferred_element_type=f32) * scale
    dk = jnp.einsum("kgbt,bkgh->tkh", d_scores, q_grp, preferred_element_type=f32) * scale
    dv = jnp.einsum("kgbt,bkgh->tkh", probs_low, do_grp, preferred_element_type=f32)
    dkv = jnp.concatenate(
        [dk.reshape(2 * chip_rows, k_cols), dv.reshape(2 * chip_rows, k_cols)], axis=1
    )
    dkv_mine = half(dkv, y_at, 0) + lax.ppermute(half(dkv, 1 - y_at, 0), "ctx", Y_SWAP)
    dq_low = rotate_back(dq.reshape(chip_rows, heads, HEAD), cosine, sine).astype(low)
    dk_low = rotate_back(
        dkv_mine[:, :k_cols].reshape(chip_rows, kv_heads, HEAD), cosine, sine
    ).astype(low)
    d_qkv = jnp.concatenate(
        [
            dq_low.reshape(chip_rows, q_cols),
            dk_low.reshape(chip_rows, k_cols),
            dkv_mine[:, k_cols:].astype(low),
        ],
        axis=1,
    )
    dh1 = token_sum(jnp.concatenate([matmul(d_qkv, qkv_w[turn], nt) for turn in range(4)], axis=1))
    grad_qkv = scatter([matmul(cut(h1, turn), d_qkv, tn) for turn in range(4)])
    d_norm_one, gain_one_part = norm_back(inputs_own, gain_one, dh1)
    grad_half = token_gather((d_middle + d_norm_one).astype(low))

    gain_sum = lax.psum(
        relative(jnp.stack([gain_one_part, gain_two_part])), ("dp", "ctx", "mp")
    )
    gain_mine = lax.dynamic_slice_in_dim(gain_sum, (2 * place + core) * part, part, axis=1)

    def to_rows(total):
        give = half(total, 1 - core, 0)
        return half(total, core, 0), over_core(give)

    def to_cols(total):
        give = half(total, 1 - core, 1)
        return both(half(total, core, 1), over_core(give), 0)

    gu_mine, gu_other = to_rows(grad_gu)
    qkv_mine, qkv_other = to_rows(grad_qkv)

    def joined(start, size, mine, other):
        return both(mine[:, start : start + size], other[:, start : start + size], 1)

    return (
        relative(out_half)[None],
        relative(grad_half)[None],
        gain_mine[0],
        joined(0, q_cols, qkv_mine, qkv_other),
        joined(q_cols, k_cols, qkv_mine, qkv_other),
        joined(q_cols + k_cols, k_cols, qkv_mine, qkv_other),
        to_cols(grad_out),
        gain_mine[1],
        joined(0, ff, gu_mine, gu_other),
        joined(ff, ff, gu_mine, gu_other),
        to_cols(grad_down),
    )


def solution(mesh):
    plane = dict(mesh.shape) == {"dp": 2, "ctx": 4, "mp": 4}
    return jax.shard_map(
        on_plane if plane else any_mesh,
        mesh=mesh,
        in_specs=(
            P("dp", "ctx", None),
            P("dp", "ctx", None),
            P("dp"),
            P(("dp", "ctx")),
            P(("dp", "ctx"), "mp"),
            P(("dp", "ctx"), "mp"),
            P(("dp", "ctx"), "mp"),
            P("mp", ("dp", "ctx")),
            P(("dp", "ctx")),
            P(("dp", "ctx"), "mp"),
            P(("dp", "ctx"), "mp"),
            P("mp", ("dp", "ctx")),
        ),
        out_specs=(
            P("dp", "ctx", None),
            P("dp", "ctx", None),
            P(("dp", "ctx")),
            P(("dp", "ctx"), "mp"),
            P(("dp", "ctx"), "mp"),
            P(("dp", "ctx"), "mp"),
            P("mp", ("dp", "ctx")),
            P(("dp", "ctx")),
            P(("dp", "ctx"), "mp"),
            P(("dp", "ctx"), "mp"),
            P("mp", ("dp", "ctx")),
        ),
        check_vma=False,
    )
```

```python
import functools

import jax
import jax.numpy as jnp
from jax import lax
from jax.experimental import pallas as pl
from jax.experimental.pallas import tpu as pltpu
from jax.sharding import PartitionSpec as P

HEAD = 80


EPS = 1e-05
THETA = 1000000.0
NEG = -1e30


def rope_tables(places, head_size):
    half = head_size // 2
    freq = THETA ** (-(jnp.arange(half, dtype=jnp.float32) * 2.0 / head_size))
    angle = places[:, None] * freq[None, :]
    return (jnp.cos(angle), jnp.sin(angle))


def rotate(tensor, cosine, sine_table):
    half = tensor.shape[-1] // 2
    first_half = tensor[..., :half]
    second_half = tensor[..., half:]
    cos_b = cosine[:, None, :]
    sin_b = sine_table[:, None, :]
    return jnp.concatenate(
        [first_half * cos_b - second_half * sin_b, second_half * cos_b + first_half * sin_b],
        axis=-1,
    )


def rotate_back(tensor, cosine, sine_table):
    half = tensor.shape[-1] // 2
    first_half = tensor[..., :half]
    second_half = tensor[..., half:]
    cos_b = cosine[:, None, :]
    sin_b = sine_table[:, None, :]
    return jnp.concatenate(
        [first_half * cos_b + second_half * sin_b, second_half * cos_b - first_half * sin_b],
        axis=-1,
    )


def normed(tensor, gain_row):
    return tensor * lax.rsqrt(jnp.mean(tensor * tensor, axis=-1, keepdims=True) + EPS) * gain_row


def norm_back(tensor, gain_row, grad_normed):
    scale_row = lax.rsqrt(jnp.mean(tensor * tensor, axis=-1, keepdims=True) + EPS)
    grad_scaled = grad_normed * gain_row
    grad_tensor = scale_row * grad_scaled - tensor * scale_row**3 * jnp.mean(
        grad_scaled * tensor, axis=-1, keepdims=True
    )
    grad_gain = jnp.sum(grad_normed * tensor * scale_row, axis=0)
    return (grad_tensor, grad_gain)


def masked_scores(query_seq, key_seq, length, places, kv_heads, group_size):
    query_grp = query_seq.reshape(query_seq.shape[0], kv_heads, group_size, HEAD)
    key_grp = key_seq.reshape(key_seq.shape[0], kv_heads, HEAD)
    raw_scores = jnp.einsum(
        "bkgh,tkh->kgbt", query_grp, key_grp, preferred_element_type=jnp.float32
    ) * HEAD ** (-0.5)
    key_places = jnp.arange(key_grp.shape[0], dtype=jnp.int32)
    allowed = (key_places[None, :] <= places[:, None]) & (key_places[None, :] < length)
    return jnp.where(allowed[None, None], raw_scores, NEG)


def any_mesh(
    hidden_in,
    cotangent,
    lengths,
    norm_attn,
    w_query,
    w_key,
    w_value,
    w_output,
    norm_mlp,
    w_gate,
    w_up,
    w_down,
):
    seq_count, slot_count, width_all = hidden_in.shape
    tok_rows = seq_count * slot_count
    attn_set = (
        lax.all_gather(w_query, ("dp", "ctx"), axis=0, tiled=True),
        lax.all_gather(w_key, ("dp", "ctx"), axis=0, tiled=True),
        lax.all_gather(w_value, ("dp", "ctx"), axis=0, tiled=True),
        lax.all_gather(w_output, ("dp", "ctx"), axis=1, tiled=True),
        lax.all_gather(norm_attn, ("dp", "ctx"), axis=0, tiled=True),
    )
    query_w, key_w, value_w, output_w, gain_attn = attn_set
    q_heads = query_w.shape[1] // HEAD
    kv_heads = key_w.shape[1] // HEAD
    group_size = q_heads // kv_heads
    first_slot = lax.axis_index("ctx") * slot_count
    places = first_slot + jnp.arange(slot_count, dtype=jnp.int32)
    valid_mask = (places[None, :] < lengths[:, None]).astype(jnp.float32).reshape(tok_rows, 1)
    cosine, sine_table = rope_tables(places.astype(jnp.float32), HEAD)
    inputs = hidden_in.reshape(tok_rows, width_all).astype(jnp.float32)
    gain_one = gain_attn.astype(jnp.float32)
    normed_one = normed(inputs, gain_one).astype(jnp.bfloat16)
    query_proj = jnp.dot(normed_one, query_w, preferred_element_type=jnp.float32).reshape(
        seq_count, slot_count, q_heads, HEAD
    )
    key_proj = jnp.dot(normed_one, key_w, preferred_element_type=jnp.float32).reshape(
        seq_count, slot_count, kv_heads, HEAD
    )
    value_low = (
        jnp.dot(normed_one, value_w, preferred_element_type=jnp.float32)
        .astype(jnp.bfloat16)
        .reshape(seq_count, slot_count, kv_heads * HEAD)
    )
    query_low = rotate(query_proj, cosine, sine_table).astype(jnp.bfloat16)
    key_low = (
        rotate(key_proj, cosine, sine_table)
        .astype(jnp.bfloat16)
        .reshape(seq_count, slot_count, kv_heads * HEAD)
    )
    key_all, value_all = (
        lax.all_gather(key_low, "ctx", axis=1, tiled=True),
        lax.all_gather(value_low, "ctx", axis=1, tiled=True),
    )

    def attend(members):
        query_seq, key_seq, value_seq, length = members
        scores = masked_scores(query_seq, key_seq, length, places, kv_heads, group_size)
        row_max = jnp.max(scores, axis=-1, keepdims=True)
        exponent = jnp.exp(scores - row_max)
        total = jnp.sum(exponent, axis=-1, keepdims=True)
        attention = (exponent / total).astype(jnp.bfloat16)
        value_grp = value_seq.reshape(value_seq.shape[0], kv_heads, HEAD)
        mixed_heads = jnp.einsum(
            "kgbt,tkh->bkgh", attention, value_grp, preferred_element_type=jnp.float32
        )
        return (mixed_heads.reshape(slot_count, q_heads * HEAD), (row_max + jnp.log(total))[..., 0])

    mixed_all, log_total = lax.map(attend, (query_low, key_all, value_all, lengths))
    attn_low = mixed_all.reshape(tok_rows, q_heads * HEAD).astype(jnp.bfloat16)
    branch = lax.psum(jnp.dot(attn_low, output_w, preferred_element_type=jnp.float32), "mp")
    middle = inputs + branch
    mlp_set = (
        lax.all_gather(w_gate, ("dp", "ctx"), axis=0, tiled=True),
        lax.all_gather(w_up, ("dp", "ctx"), axis=0, tiled=True),
        lax.all_gather(w_down, ("dp", "ctx"), axis=1, tiled=True),
        lax.all_gather(norm_mlp, ("dp", "ctx"), axis=0, tiled=True),
    )
    gate_w, up_w, down_w, gain_mlp = mlp_set
    gain_two = gain_mlp.astype(jnp.float32)
    normed_two = normed(middle, gain_two).astype(jnp.bfloat16)
    gate_proj = jnp.dot(normed_two, gate_w, preferred_element_type=jnp.float32)
    up_proj = jnp.dot(normed_two, up_w, preferred_element_type=jnp.float32)
    hidden = (jax.nn.silu(gate_proj) * up_proj).astype(jnp.bfloat16)
    mlp_out = lax.psum(
        jnp.dot(hidden, down_w, preferred_element_type=jnp.float32).astype(jnp.bfloat16), "mp"
    ).astype(jnp.float32)
    layer_out = (
        (valid_mask * (middle + mlp_out))
        .astype(jnp.bfloat16)
        .reshape(seq_count, slot_count, width_all)
    )
    grad_out = valid_mask * cotangent.reshape(tok_rows, width_all).astype(jnp.float32)
    grad_mlp = grad_out.astype(jnp.bfloat16)
    gate_back, up_back, down_back, gain_mlp_back = (
        lax.all_gather(w_gate, ("dp", "ctx"), axis=0, tiled=True),
        lax.all_gather(w_up, ("dp", "ctx"), axis=0, tiled=True),
        lax.all_gather(w_down, ("dp", "ctx"), axis=1, tiled=True),
        lax.all_gather(norm_mlp, ("dp", "ctx"), axis=0, tiled=True),
    )
    grad_hidden = jnp.einsum("tm,fm->tf", grad_mlp, down_back, preferred_element_type=jnp.float32)
    grad_down = jnp.einsum("tf,tm->fm", hidden, grad_mlp, preferred_element_type=jnp.float32)
    sigmoid_gate = jax.nn.sigmoid(gate_proj)
    grad_gate_low = (
        grad_hidden * up_proj * sigmoid_gate * (1.0 + gate_proj * (1.0 - sigmoid_gate))
    ).astype(jnp.bfloat16)
    grad_up_low = (grad_hidden * gate_proj * sigmoid_gate).astype(jnp.bfloat16)
    grad_gate = jnp.einsum(
        "td,tf->df", normed_two, grad_gate_low, preferred_element_type=jnp.float32
    )
    grad_up = jnp.einsum("td,tf->df", normed_two, grad_up_low, preferred_element_type=jnp.float32)
    partial_two = jnp.einsum(
        "tf,df->td", grad_gate_low, gate_back, preferred_element_type=jnp.float32
    ) + jnp.einsum("tf,df->td", grad_up_low, up_back, preferred_element_type=jnp.float32)
    grad_normed_two = lax.psum(partial_two, "mp")
    grad_middle_norm, grad_gain_two = norm_back(
        middle, gain_mlp_back.astype(jnp.float32), grad_normed_two
    )
    mlp_grads = (
        lax.psum_scatter(grad_gate, ("dp", "ctx"), scatter_dimension=0, tiled=True),
        lax.psum_scatter(grad_up, ("dp", "ctx"), scatter_dimension=0, tiled=True),
        lax.psum_scatter(grad_down, ("dp", "ctx"), scatter_dimension=1, tiled=True),
        lax.psum_scatter(grad_gain_two, ("dp", "ctx"), scatter_dimension=0, tiled=True),
    )
    grad_middle = grad_out + grad_middle_norm
    grad_branch = grad_middle.astype(jnp.bfloat16)
    query_back, key_back, value_back, output_back, gain_attn_back = (
        lax.all_gather(w_query, ("dp", "ctx"), axis=0, tiled=True),
        lax.all_gather(w_key, ("dp", "ctx"), axis=0, tiled=True),
        lax.all_gather(w_value, ("dp", "ctx"), axis=0, tiled=True),
        lax.all_gather(w_output, ("dp", "ctx"), axis=1, tiled=True),
        lax.all_gather(norm_attn, ("dp", "ctx"), axis=0, tiled=True),
    )
    grad_output = jnp.einsum("tq,td->qd", attn_low, grad_branch, preferred_element_type=jnp.float32)
    grad_attn_low = (
        jnp.einsum("td,qd->tq", grad_branch, output_back, preferred_element_type=jnp.float32)
        .astype(jnp.bfloat16)
        .reshape(seq_count, slot_count, q_heads, HEAD)
    )

    def attend_back(members):
        query_seq, key_seq, value_seq, length, log_seq, grad_seq = members
        scores = masked_scores(query_seq, key_seq, length, places, kv_heads, group_size)
        attention = jnp.exp(scores - log_seq[..., None])
        query_grp = query_seq.reshape(slot_count, kv_heads, group_size, HEAD)
        key_grp = key_seq.reshape(key_seq.shape[0], kv_heads, HEAD)
        value_grp = value_seq.reshape(value_seq.shape[0], kv_heads, HEAD)
        grad_grp = grad_seq.reshape(slot_count, kv_heads, group_size, HEAD)
        grad_attention = jnp.einsum(
            "bkgh,tkh->kgbt", grad_grp, value_grp, preferred_element_type=jnp.float32
        )
        inner = jnp.sum(attention * grad_attention, axis=-1, keepdims=True)
        grad_scores = (attention * (grad_attention - inner)).astype(jnp.bfloat16)
        scale_qk = HEAD ** (-0.5)
        grad_query_seq = (
            jnp.einsum("kgbt,tkh->bkgh", grad_scores, key_grp, preferred_element_type=jnp.float32)
            * scale_qk
        )
        grad_key_seq = (
            jnp.einsum("kgbt,bkgh->tkh", grad_scores, query_grp, preferred_element_type=jnp.float32)
            * scale_qk
        )
        grad_value_seq = jnp.einsum(
            "kgbt,bkgh->tkh",
            attention.astype(jnp.bfloat16),
            grad_grp,
            preferred_element_type=jnp.float32,
        )
        key_rows = key_grp.shape[0]
        return (
            grad_query_seq.reshape(slot_count, q_heads, HEAD),
            grad_key_seq.reshape(key_rows, kv_heads * HEAD),
            grad_value_seq.reshape(key_rows, kv_heads * HEAD),
        )

    grad_query_rot, grad_key_all, grad_value_all = lax.map(
        attend_back, (query_low, key_all, value_all, lengths, log_total, grad_attn_low)
    )
    grad_key_rot, grad_value_rot = (
        lax.psum_scatter(grad_key_all, "ctx", scatter_dimension=1, tiled=True),
        lax.psum_scatter(grad_value_all, "ctx", scatter_dimension=1, tiled=True),
    )
    grad_query_low = (
        rotate_back(grad_query_rot, cosine, sine_table)
        .astype(jnp.bfloat16)
        .reshape(tok_rows, q_heads * HEAD)
    )
    grad_key_low = (
        rotate_back(grad_key_rot.reshape(seq_count, slot_count, kv_heads, HEAD), cosine, sine_table)
        .astype(jnp.bfloat16)
        .reshape(tok_rows, kv_heads * HEAD)
    )
    grad_value_low = grad_value_rot.astype(jnp.bfloat16).reshape(tok_rows, kv_heads * HEAD)
    grad_query = jnp.einsum(
        "td,tq->dq", normed_one, grad_query_low, preferred_element_type=jnp.float32
    )
    grad_key = jnp.einsum("td,tq->dq", normed_one, grad_key_low, preferred_element_type=jnp.float32)
    grad_value = jnp.einsum(
        "td,tq->dq", normed_one, grad_value_low, preferred_element_type=jnp.float32
    )
    partial_one = jnp.einsum(
        "tq,dq->td", grad_query_low, query_back, preferred_element_type=jnp.float32
    )
    partial_one = partial_one + jnp.einsum(
        "tq,dq->td", grad_key_low, key_back, preferred_element_type=jnp.float32
    )
    partial_one = partial_one + jnp.einsum(
        "tq,dq->td", grad_value_low, value_back, preferred_element_type=jnp.float32
    )
    grad_normed_one = lax.psum(partial_one, "mp")
    grad_inputs_norm, grad_gain_one = norm_back(
        inputs, gain_attn_back.astype(jnp.float32), grad_normed_one
    )
    input_grad = (
        (grad_middle + grad_inputs_norm)
        .astype(jnp.bfloat16)
        .reshape(seq_count, slot_count, width_all)
    )
    attn_grads = (
        lax.psum_scatter(grad_query, ("dp", "ctx"), scatter_dimension=0, tiled=True),
        lax.psum_scatter(grad_key, ("dp", "ctx"), scatter_dimension=0, tiled=True),
        lax.psum_scatter(grad_value, ("dp", "ctx"), scatter_dimension=0, tiled=True),
        lax.psum_scatter(grad_output, ("dp", "ctx"), scatter_dimension=1, tiled=True),
        lax.psum_scatter(grad_gain_one, ("dp", "ctx"), scatter_dimension=0, tiled=True),
    )
    return (
        layer_out,
        input_grad,
        attn_grads[4],
        attn_grads[0],
        attn_grads[1],
        attn_grads[2],
        attn_grads[3],
        mlp_grads[3],
        mlp_grads[0],
        mlp_grads[1],
        mlp_grads[2],
    )


SPLIT = 4


class Column:
    def __init__(self, owned, width):
        self.x, self.ctx, self.z = (lax.axis_index(name) for name in ("dp", "ctx", "mp"))
        self.core = lax.rem(self.ctx, 2)
        self.last = lax.axis_size("mp") - 1
        self.owned, self.rows, self.width = owned, owned * (self.last + 1), width
        self.step = width // SPLIT
        self.sibling = (self.x, self.ctx + 1 - 2 * self.core, self.z)
        self.above, self.below = (self.x, self.ctx, self.z + 1), (self.x, self.ctx, self.z - 1)

    def enter(self):
        barrier = pltpu.get_barrier_semaphore()

        def greet(device):
            pl.semaphore_signal(
                barrier, inc=1, device_id=device, device_id_type=pl.DeviceIdType.MESH
            )

        greet(self.sibling)

        @pl.when(self.z < self.last)
        def _():
            greet(self.above)

        @pl.when(self.z > 0)
        def _():
            greet(self.below)

        ends = jnp.where(self.z == 0, 1, 0) + jnp.where(self.z == self.last, 1, 0)
        pl.semaphore_wait(barrier, 3 - ends)

    def place(self, core, block):
        return pl.ds(pl.multiple_of(core * self.rows + block * self.owned, 16), self.owned)

    def block(self, at):
        return pl.ds(pl.multiple_of(at * self.owned, 16), self.owned)

    def columns(self, piece):
        return pl.ds(piece * self.step, self.step)


def remote(src, dst, send, recv, device):
    return pltpu.make_async_remote_copy(
        src_ref=src,
        dst_ref=dst,
        send_sem=send,
        recv_sem=recv,
        device_id=device,
        device_id_type=pl.DeviceIdType.MESH,
    )


class SumChain:
    def __init__(self, col, part, held, up_out, up_in, down_out, down_in, core_sem, up_sem, down_sem):
        self.col, self.part, self.held = col, part, held
        self.ways = (
            (col.above, up_out, up_in, up_sem, 1),
            (col.below, down_out, down_in, down_sem, -1),
        )
        self.core_sem = core_sem

    def across(self, block):
        col = self.col
        return remote(
            self.part.at[col.place(1 - col.core, block)],
            self.held.at[col.block(block)],
            self.core_sem.at[0, block],
            self.core_sem.at[1, block],
            col.sibling,
        )

    def open(self):
        for block in range(self.col.last + 1):
            self.across(block).start()

    def own(self, at, cols):
        col = self.col
        mine = self.part[col.place(col.core, at), cols].astype(jnp.float32)
        return mine + self.held[col.block(at), cols].astype(jnp.float32)

    def hop(self, way, step, piece):
        device, out, into, sem, _ = way
        cols = self.col.columns(piece)
        return remote(
            out.at[step, :, cols],
            into.at[step, :, cols],
            sem.at[0, step, piece],
            sem.at[1, step, piece],
            device,
        )

    def far(self, way):
        return self.col.z if way[4] == 1 else self.col.last - self.col.z

    def step(self, step):
        col = self.col
        for way in self.ways:
            sign = way[4]

            @pl.when(self.far(way) <= step)
            def _(way=way, sign=sign):
                at = col.z + sign * (col.last - step)
                self.across(at).wait_recv()
                for piece in range(SPLIT):
                    cols = col.columns(piece)
                    out = way[1]
                    total = self.own(at, cols)
                    if step:

                        @pl.when(self.far(way) > 0)
                        def _(total=total, cols=cols, piece=piece):
                            self.hop(way, step - 1, piece).wait_recv()
                            got = way[2][step - 1, :, cols].astype(jnp.float32)
                            out[step, :, cols] = (total + got).astype(out.dtype)

                        @pl.when(self.far(way) == 0)
                        def _(total=total, cols=cols):
                            out[step, :, cols] = total.astype(out.dtype)

                    else:
                        out[step, :, cols] = total.astype(out.dtype)
                    self.hop(way, step, piece).start()

    def close(self, result):
        col = self.col
        final = col.last - 1
        self.across(col.z).wait_recv()
        result[...] = self.own(col.z, slice(None))
        for way in self.ways:

            @pl.when(self.far(way) > 0)
            def _(way=way):
                for piece in range(SPLIT):
                    self.hop(way, final, piece).wait_recv()
                result[...] += way[2][final].astype(jnp.float32)

    def drain(self):
        for block in range(self.col.last + 1):
            self.across(block).wait_send()
        for step in range(self.col.last):
            for way in self.ways:

                @pl.when(self.far(way) <= step)
                def _(way=way, step=step):
                    for piece in range(SPLIT):
                        self.hop(way, step, piece).wait_send()


class ShareChain:
    def __init__(self, col, whole, up_sem, down_sem, core_sem=None):
        self.col, self.whole, self.core_sem = col, whole, core_sem
        self.ways = ((col.above, up_sem, 1), (col.below, down_sem, -1))

    def rows(self, at):
        return self.col.block(at) if self.core_sem is None else self.col.place(self.col.core, at)

    def far(self, way):
        return self.col.z if way[2] == 1 else self.col.last - self.col.z

    def hop(self, way, step, piece, origin):
        device, sem, _ = way
        ref = self.whole.at[self.rows(origin), self.col.columns(piece)]
        return remote(ref, ref, sem.at[0, step, piece], sem.at[1, step, piece], device)

    def across(self, origin):
        ref = self.whole.at[self.rows(origin)]
        return remote(
            ref, ref, self.core_sem.at[0, origin], self.core_sem.at[1, origin], self.col.sibling
        )

    def across_in(self, origin):
        ref = self.whole.at[self.col.place(1 - self.col.core, origin)]
        return remote(
            ref, ref, self.core_sem.at[0, origin], self.core_sem.at[1, origin], self.col.sibling
        )

    def step(self, step):
        col = self.col
        for way in self.ways:
            origin = col.z - way[2] * step

            @pl.when(self.far(way) >= step)
            def _(way=way, origin=origin):
                for piece in range(SPLIT):
                    if step:
                        self.hop(way, step - 1, piece, origin).wait_recv()
                    if step < col.last:

                        @pl.when(self.far(way) < col.last)
                        def _(piece=piece):
                            self.hop(way, step, piece, origin).start()

                if step and self.core_sem is not None:
                    self.across(origin).start()

        if step == 0 and self.core_sem is not None:
            self.across(col.z).start()

    def drain(self):
        col = self.col
        for step in range(col.last):
            for way in self.ways:

                @pl.when((self.far(way) >= step) & (self.far(way) < col.last))
                def _(way=way, step=step):
                    for piece in range(SPLIT):
                        self.hop(way, step, piece, col.z - way[2] * step).wait_send()

        if self.core_sem is not None:
            for origin in range(col.last + 1):
                self.across_in(origin).wait_recv()
                self.across(origin).wait_send()


def sum_scratch(owned, z_count, width):
    hops = z_count - 1
    low = jnp.bfloat16
    return [
        pltpu.VMEM((owned * z_count, width), low),
        pltpu.VMEM((hops, owned, width), low),
        pltpu.VMEM((hops, owned, width), low),
        pltpu.VMEM((hops, owned, width), low),
        pltpu.VMEM((hops, owned, width), low),
        pltpu.SemaphoreType.DMA((2, z_count)),
        pltpu.SemaphoreType.DMA((2, hops, SPLIT)),
        pltpu.SemaphoreType.DMA((2, hops, SPLIT)),
    ]


def share_scratch(z_count, cores):
    hops = z_count - 1
    sems = [pltpu.SemaphoreType.DMA((2, hops, SPLIT))] * 2
    return sems + ([pltpu.SemaphoreType.DMA((2, z_count))] if cores else [])


def branch_kernel(part, inputs, gain, whole, middle, *scratch):
    col = Column(inputs.shape[0], inputs.shape[1])
    total = SumChain(col, part, *scratch[:8])
    share = ShareChain(col, whole, *scratch[8:])
    col.enter()
    total.open()
    for step in range(col.last):
        total.step(step)
    total.close(middle)
    middle[...] += inputs[...]
    whole[col.place(col.core, col.z)] = normed(middle[...], gain[...]).astype(whole.dtype)
    for step in range(col.last + 1):
        share.step(step)
    total.drain()
    share.drain()


def middle_kernel(
    part, mlp_part, middle, gain, dout, valid, whole, d_middle, layer, d_gain, mlp, *scratch
):
    col = Column(middle.shape[0], middle.shape[1])
    total = SumChain(col, part, *scratch[:8])
    second = SumChain(col, mlp_part, *scratch[8:16])
    share = ShareChain(col, whole, *scratch[16:])
    col.enter()
    total.open()
    second.open()
    for step in range(col.last):
        total.step(step)
    total.close(d_middle)
    d_norm, d_gain_row = norm_back(middle[...], gain[...], d_middle[...])
    d_gain[...] = d_gain_row[None]
    d_middle[...] = dout[...] + d_norm
    whole[col.place(col.core, col.z)] = d_middle[...].astype(whole.dtype)
    for step in range(col.last + 1):
        share.step(step)
        if step < col.last:
            second.step(step)
    second.close(mlp)
    layer[...] = (valid[...] * (middle[...] + mlp[...])).astype(layer.dtype)
    total.drain()
    second.drain()
    share.drain()


def input_kernel(
    part, layer, d_middle, inputs, gain, layer_all, grad_all, d_gain, d_normed, *scratch
):
    col = Column(inputs.shape[0], inputs.shape[1])
    total = SumChain(col, part, *scratch[:8])
    first = ShareChain(col, layer_all, *scratch[8:10])
    share = ShareChain(col, grad_all, *scratch[10:])
    layer_all[col.block(col.z)] = layer[...]
    col.enter()
    total.open()
    for step in range(col.last + 1):
        if step < col.last:
            total.step(step)
        first.step(step)
    total.close(d_normed)
    d_norm, d_gain_row = norm_back(inputs[...], gain[...], d_normed[...])
    d_gain[...] = d_gain_row[None]
    grad_all[col.block(col.z)] = (d_middle[...] + d_norm).astype(grad_all.dtype)
    for step in range(col.last + 1):
        share.step(step)
    total.drain()
    first.drain()
    share.drain()


def column_call(body, outs, scratch, collective_id, name):
    return pl.pallas_call(
        body,
        out_shape=[jax.ShapeDtypeStruct(shape, dtype) for shape, dtype in outs],
        scratch_shapes=scratch,
        name=name,
        cost_estimate=pl.CostEstimate(flops=0, bytes_accessed=150_000_000, transcendentals=0),
        compiler_params=pltpu.CompilerParams(
            collective_id=collective_id, has_side_effects=True, vmem_limit_bytes=32 * 2**20
        ),
    )


CORE_SWAP = [(0, 1), (1, 0), (2, 3), (3, 2)]
Y_SWAP = [(0, 2), (1, 3), (2, 0), (3, 1)]
X_SWAP = [(0, 1), (1, 0)]


def over_core(tensor):
    return lax.ppermute(tensor, "ctx", CORE_SWAP)


class Link:
    def __init__(self, axis, pairs):
        self.axis, self.pairs, self.sent = axis, pairs, []

    def send(self, tensor):
        if len(self.sent) >= 2:
            tensor, _ = lax.optimization_barrier((tensor, self.sent[-2]))
        got = lax.ppermute(tensor, self.axis, self.pairs)
        self.sent.append(got)
        return got


def on_plane(
    hidden_in,
    cotangent,
    lengths,
    norm_attn,
    w_query,
    w_key,
    w_value,
    w_output,
    norm_mlp,
    w_gate,
    w_up,
    w_down,
):
    low = jnp.bfloat16
    f32 = jnp.float32
    _, rows, width = hidden_in.shape
    part = w_query.shape[0]
    chip_part = 2 * part
    x_at, ctx_at, z_at = lax.axis_index("dp"), lax.axis_index("ctx"), lax.axis_index("mp")
    y_at, core = ctx_at // 2, ctx_at % 2
    first = core == 0
    place = 2 * x_at + y_at
    z_count = lax.axis_size("mp")
    owned = rows // z_count
    x_link, y_link = Link("dp", X_SWAP), Link("ctx", Y_SWAP)

    def relative(tensor):
        return jnp.concatenate(
            [
                lax.dynamic_slice_in_dim(tensor, (place ^ turn) * chip_part, chip_part, axis=-1)
                for turn in range(4)
            ],
            axis=-1,
        )

    def both(mine, other, axis):
        return jnp.where(
            first,
            jnp.concatenate([mine, other], axis=axis),
            jnp.concatenate([other, mine], axis=axis),
        )

    def half(tensor, which, axis):
        size = tensor.shape[axis] // 2
        return lax.dynamic_slice_in_dim(tensor, which * size, size, axis=axis)

    def cut(tensor, turn):
        return tensor[..., turn * chip_part : (turn + 1) * chip_part]

    def chip_block(pieces, split_axis, join_axis):
        keep = jnp.concatenate([half(piece, core, split_axis) for piece in pieces], axis=1)
        give = jnp.concatenate([half(piece, 1 - core, split_axis) for piece in pieces], axis=1)
        return both(keep, over_core(give), join_axis)

    def gather(block):
        middle = block.shape[0] // 2
        from_x = x_link.send(block)
        from_y = y_link.send(block)
        upper = y_link.send(from_x[:middle])
        lower = x_link.send(from_y[middle:])
        return [block, from_y, from_x, jnp.concatenate([upper, lower], axis=0)]

    def scatter(parts):
        own, for_y, for_x, for_far = parts
        middle = own.shape[0] // 2
        upper = x_link.send(for_far[:middle].astype(low))
        lower = y_link.send(for_far[middle:].astype(low))
        x_one = x_link.send(for_x[:middle].astype(low))
        y_two = y_link.send(for_y[middle:].astype(low))
        y_one = y_link.send((for_y[:middle] + upper.astype(f32)).astype(low))
        x_two = x_link.send((for_x[middle:] + lower.astype(f32)).astype(low))
        return jnp.concatenate(
            [
                own[:middle] + x_one.astype(f32) + y_one.astype(f32),
                own[middle:] + x_two.astype(f32) + y_two.astype(f32),
            ],
            axis=0,
        )

    def matmul(left, right, dims):
        return lax.dot_general(left, right, (dims, ((), ())), preferred_element_type=f32)

    def parts(left, blocks, dims):
        return jnp.concatenate([matmul(left, block, dims).astype(low) for block in blocks], axis=1)

    nn, nt, tn = ((1,), (0,)), ((1,), (1,)), ((0,), (0,))

    gains = both(*(lambda g: (g, over_core(g)))(jnp.stack([norm_attn, norm_mlp])), 1)
    gains_x = lax.ppermute(gains, "dp", X_SWAP)
    gains_y = lax.ppermute(gains, "ctx", Y_SWAP)
    gains_far = lax.ppermute(gains_x, "ctx", Y_SWAP)
    gains_all = jnp.concatenate([gains, gains_y, gains_x, gains_far], axis=1).astype(f32)
    gain_one, gain_two = gains_all[0], gains_all[1]

    qkv_w = gather(chip_block((w_query, w_key, w_value), 1, 0))
    out_w = gather(chip_block((w_output,), 0, 1))
    gu_w = gather(chip_block((w_gate, w_up), 1, 0))
    down_w = gather(chip_block((w_down,), 0, 1))

    length = lengths[0]
    inputs = relative(hidden_in[0]).astype(f32)
    h1_mine = normed(inputs, gain_one).astype(low)
    h1 = both(h1_mine, over_core(h1_mine), 0)
    slots = (y_at * 2) * rows + jnp.arange(2 * rows, dtype=jnp.int32)
    my_slots = ctx_at * rows + jnp.arange(rows, dtype=jnp.int32)
    valid = (my_slots < length).astype(f32)[:, None]
    dout = valid * relative(cotangent[0]).astype(f32)
    dm_mine = dout.astype(low)
    dm = both(dm_mine, over_core(dm_mine), 0)
    cosine, sine = rope_tables(slots.astype(f32), HEAD)

    qkv = sum(matmul(cut(h1, turn), qkv_w[turn], nn) for turn in (0, 2, 1, 3))
    heads = w_query.shape[1] // HEAD // 2
    kv_heads = w_key.shape[1] // HEAD // 2
    group = heads // kv_heads
    q_cols, k_cols = heads * HEAD, kv_heads * HEAD
    chip_rows = 2 * rows
    q_low = rotate(qkv[:, :q_cols].reshape(chip_rows, heads, HEAD), cosine, sine).astype(low)
    k_low = rotate(
        qkv[:, q_cols : q_cols + k_cols].reshape(chip_rows, kv_heads, HEAD), cosine, sine
    ).astype(low)
    v_low = qkv[:, q_cols + k_cols :].astype(low)
    kv_mine = jnp.concatenate([k_low.reshape(chip_rows, k_cols), v_low], axis=1)
    kv_other = lax.ppermute(kv_mine, "ctx", Y_SWAP)
    kv_all = jnp.where(
        y_at == 0,
        jnp.concatenate([kv_mine, kv_other], axis=0),
        jnp.concatenate([kv_other, kv_mine], axis=0),
    )
    keys = kv_all[:, :k_cols].reshape(2 * chip_rows, kv_heads, HEAD)
    values = kv_all[:, k_cols:].reshape(2 * chip_rows, kv_heads, HEAD)
    q_grp = q_low.reshape(chip_rows, kv_heads, group, HEAD)
    scale = HEAD ** (-0.5)
    raw = jnp.einsum("bkgh,tkh->kgbt", q_grp, keys, preferred_element_type=f32) * scale
    key_slots = jnp.arange(2 * chip_rows, dtype=jnp.int32)
    allowed = (key_slots[None, :] <= slots[:, None]) & (key_slots[None, :] < length)
    scores = jnp.where(allowed[None, None], raw, NEG)
    exponent = jnp.exp(scores - jnp.max(scores, axis=-1, keepdims=True))
    probs = exponent / jnp.sum(exponent, axis=-1, keepdims=True)
    probs_low = probs.astype(low)
    mixed = jnp.einsum("kgbt,tkh->bkgh", probs_low, values, preferred_element_type=f32)
    attn_low = mixed.reshape(chip_rows, q_cols).astype(low)
    branch = parts(attn_low, out_w, nn)
    inputs_own = lax.dynamic_slice_in_dim(inputs, z_at * owned, owned, axis=0)
    whole, half_rows, own = (2 * rows, width), (rows, width), (owned, width)
    h2, middle = column_call(
        branch_kernel,
        [(whole, low), (own, f32)],
        sum_scratch(owned, z_count, width) + share_scratch(z_count, True),
        1,
        "branch_sum",
    )(branch, inputs_own, gain_two[None])

    ff = gu_w[0].shape[1] // 2
    gu = sum(matmul(cut(h2, turn), gu_w[turn], nn) for turn in (0, 2, 1, 3))
    gate, up = gu[:, :ff], gu[:, ff:]
    sigma = jax.nn.sigmoid(gate)
    hidden = (gate * sigma * up).astype(low)
    d_hidden = sum(matmul(cut(dm, turn), down_w[turn], nt) for turn in (0, 2, 1, 3))
    d_gate = (d_hidden * up * sigma * (1.0 + gate * (1.0 - sigma))).astype(low)
    d_up = (d_hidden * gate * sigma).astype(low)
    d_gu = jnp.concatenate([d_gate, d_up], axis=1)
    dh2 = parts(d_gu, gu_w, nt)
    grad_gu = scatter([matmul(cut(h2, turn), d_gu, tn) for turn in range(4)])
    grad_down = scatter([matmul(hidden, cut(dm, turn), tn) for turn in range(4)])
    mlp = parts(hidden, down_w, nn)
    dout_own = lax.dynamic_slice_in_dim(dout, z_at * owned, owned, axis=0)
    valid_own = lax.dynamic_slice_in_dim(valid, z_at * owned, owned, axis=0)
    da, d_middle, layer_own, gain_two_part = column_call(
        middle_kernel,
        [(whole, low), (own, f32), (own, low), ((1, width), f32)],
        [pltpu.VMEM(own, f32)]
        + sum_scratch(owned, z_count, width) * 2
        + share_scratch(z_count, True),
        2,
        "middle_sum",
    )(dh2, mlp, middle, gain_two[None], dout_own, valid_own)

    do = sum(matmul(cut(da, turn), out_w[turn], nt) for turn in range(4)).astype(low)
    grad_out = scatter([matmul(attn_low, cut(da, turn), tn) for turn in range(4)])
    do_grp = do.reshape(chip_rows, kv_heads, group, HEAD)
    d_probs = jnp.einsum("bkgh,tkh->kgbt", do_grp, values, preferred_element_type=f32)
    inner = jnp.sum(probs * d_probs, axis=-1, keepdims=True)
    d_scores = (probs * (d_probs - inner)).astype(low)
    dq = jnp.einsum("kgbt,tkh->bkgh", d_scores, keys, preferred_element_type=f32) * scale
    dk = jnp.einsum("kgbt,bkgh->tkh", d_scores, q_grp, preferred_element_type=f32) * scale
    dv = jnp.einsum("kgbt,bkgh->tkh", probs_low, do_grp, preferred_element_type=f32)
    dkv = jnp.concatenate(
        [dk.reshape(2 * chip_rows, k_cols), dv.reshape(2 * chip_rows, k_cols)], axis=1
    )
    dkv_mine = half(dkv, y_at, 0) + lax.ppermute(half(dkv, 1 - y_at, 0), "ctx", Y_SWAP)
    dq_low = rotate_back(dq.reshape(chip_rows, heads, HEAD), cosine, sine).astype(low)
    dk_low = rotate_back(
        dkv_mine[:, :k_cols].reshape(chip_rows, kv_heads, HEAD), cosine, sine
    ).astype(low)
    d_qkv = jnp.concatenate(
        [
            dq_low.reshape(chip_rows, q_cols),
            dk_low.reshape(chip_rows, k_cols),
            dkv_mine[:, k_cols:].astype(low),
        ],
        axis=1,
    )
    dh1 = parts(d_qkv, qkv_w, nt)
    grad_qkv = scatter([matmul(cut(h1, turn), d_qkv, tn) for turn in range(4)])
    out_half, grad_half, gain_one_part = column_call(
        input_kernel,
        [(half_rows, low), (half_rows, low), ((1, width), f32)],
        [pltpu.VMEM(own, f32)]
        + sum_scratch(owned, z_count, width)
        + share_scratch(z_count, False) * 2,
        3,
        "input_sum",
    )(dh1, layer_own, d_middle, inputs_own, gain_one[None])

    gain_part = jnp.concatenate([gain_one_part, gain_two_part], axis=0)
    gain_sum = (
        cut(gain_part, 0)
        + lax.ppermute(cut(gain_part, 1), "ctx", Y_SWAP)
        + lax.ppermute(cut(gain_part, 2), "dp", X_SWAP)
        + lax.ppermute(lax.ppermute(cut(gain_part, 3), "ctx", Y_SWAP), "dp", X_SWAP)
    )
    gain_mine = half(gain_sum, core, 1) + over_core(half(gain_sum, 1 - core, 1))
    for flip in (1, 2):
        gain_mine = gain_mine + lax.ppermute(
            gain_mine, "mp", [(z, z ^ flip) for z in range(z_count)]
        )

    def to_rows(total):
        give = half(total, 1 - core, 0)
        return half(total, core, 0), over_core(give)

    def to_cols(total):
        give = half(total, 1 - core, 1)
        return both(half(total, core, 1), over_core(give), 0)

    gu_mine, gu_other = to_rows(grad_gu)
    qkv_mine, qkv_other = to_rows(grad_qkv)

    def joined(start, size, mine, other):
        return both(mine[:, start : start + size], other[:, start : start + size], 1)

    return (
        relative(out_half)[None],
        relative(grad_half)[None],
        gain_mine[0],
        joined(0, q_cols, qkv_mine, qkv_other),
        joined(q_cols, k_cols, qkv_mine, qkv_other),
        joined(q_cols + k_cols, k_cols, qkv_mine, qkv_other),
        to_cols(grad_out),
        gain_mine[1],
        joined(0, ff, gu_mine, gu_other),
        joined(ff, ff, gu_mine, gu_other),
        to_cols(grad_down),
    )


def solution(mesh):
    plane = dict(mesh.shape) == {"dp": 2, "ctx": 4, "mp": 4}
    return jax.shard_map(
        on_plane if plane else any_mesh,
        mesh=mesh,
        in_specs=(
            P("dp", "ctx", None),
            P("dp", "ctx", None),
            P("dp"),
            P(("dp", "ctx")),
            P(("dp", "ctx"), "mp"),
            P(("dp", "ctx"), "mp"),
            P(("dp", "ctx"), "mp"),
            P("mp", ("dp", "ctx")),
            P(("dp", "ctx")),
            P(("dp", "ctx"), "mp"),
            P(("dp", "ctx"), "mp"),
            P("mp", ("dp", "ctx")),
        ),
        out_specs=(
            P("dp", "ctx", None),
            P("dp", "ctx", None),
            P(("dp", "ctx")),
            P(("dp", "ctx"), "mp"),
            P(("dp", "ctx"), "mp"),
            P(("dp", "ctx"), "mp"),
            P("mp", ("dp", "ctx")),
            P(("dp", "ctx")),
            P(("dp", "ctx"), "mp"),
            P(("dp", "ctx"), "mp"),
            P("mp", ("dp", "ctx")),
        ),
        check_vma=False,
    )
```

```python
import functools

import jax
import jax.numpy as jnp
from jax import lax
from jax.experimental import pallas as pl
from jax.experimental.pallas import tpu as pltpu
from jax.sharding import PartitionSpec as P

HEAD = 80


EPS = 1e-05
THETA = 1000000.0
NEG = -1e30


def rope_tables(places, head_size):
    half = head_size // 2
    freq = THETA ** (-(jnp.arange(half, dtype=jnp.float32) * 2.0 / head_size))
    angle = places[:, None] * freq[None, :]
    return (jnp.cos(angle), jnp.sin(angle))


def rotate(tensor, cosine, sine_table):
    half = tensor.shape[-1] // 2
    first_half = tensor[..., :half]
    second_half = tensor[..., half:]
    cos_b = cosine[:, None, :]
    sin_b = sine_table[:, None, :]
    return jnp.concatenate(
        [first_half * cos_b - second_half * sin_b, second_half * cos_b + first_half * sin_b],
        axis=-1,
    )


def rotate_back(tensor, cosine, sine_table):
    half = tensor.shape[-1] // 2
    first_half = tensor[..., :half]
    second_half = tensor[..., half:]
    cos_b = cosine[:, None, :]
    sin_b = sine_table[:, None, :]
    return jnp.concatenate(
        [first_half * cos_b + second_half * sin_b, second_half * cos_b - first_half * sin_b],
        axis=-1,
    )


def normed(tensor, gain_row):
    return tensor * lax.rsqrt(jnp.mean(tensor * tensor, axis=-1, keepdims=True) + EPS) * gain_row


def norm_back(tensor, gain_row, grad_normed):
    scale_row = lax.rsqrt(jnp.mean(tensor * tensor, axis=-1, keepdims=True) + EPS)
    grad_scaled = grad_normed * gain_row
    grad_tensor = scale_row * grad_scaled - tensor * scale_row**3 * jnp.mean(
        grad_scaled * tensor, axis=-1, keepdims=True
    )
    grad_gain = jnp.sum(grad_normed * tensor * scale_row, axis=0)
    return (grad_tensor, grad_gain)


def masked_scores(query_seq, key_seq, length, places, kv_heads, group_size):
    query_grp = query_seq.reshape(query_seq.shape[0], kv_heads, group_size, HEAD)
    key_grp = key_seq.reshape(key_seq.shape[0], kv_heads, HEAD)
    raw_scores = jnp.einsum(
        "bkgh,tkh->kgbt", query_grp, key_grp, preferred_element_type=jnp.float32
    ) * HEAD ** (-0.5)
    key_places = jnp.arange(key_grp.shape[0], dtype=jnp.int32)
    allowed = (key_places[None, :] <= places[:, None]) & (key_places[None, :] < length)
    return jnp.where(allowed[None, None], raw_scores, NEG)


def any_mesh(
    hidden_in,
    cotangent,
    lengths,
    norm_attn,
    w_query,
    w_key,
    w_value,
    w_output,
    norm_mlp,
    w_gate,
    w_up,
    w_down,
):
    seq_count, slot_count, width_all = hidden_in.shape
    tok_rows = seq_count * slot_count
    attn_set = (
        lax.all_gather(w_query, ("dp", "ctx"), axis=0, tiled=True),
        lax.all_gather(w_key, ("dp", "ctx"), axis=0, tiled=True),
        lax.all_gather(w_value, ("dp", "ctx"), axis=0, tiled=True),
        lax.all_gather(w_output, ("dp", "ctx"), axis=1, tiled=True),
        lax.all_gather(norm_attn, ("dp", "ctx"), axis=0, tiled=True),
    )
    query_w, key_w, value_w, output_w, gain_attn = attn_set
    q_heads = query_w.shape[1] // HEAD
    kv_heads = key_w.shape[1] // HEAD
    group_size = q_heads // kv_heads
    first_slot = lax.axis_index("ctx") * slot_count
    places = first_slot + jnp.arange(slot_count, dtype=jnp.int32)
    valid_mask = (places[None, :] < lengths[:, None]).astype(jnp.float32).reshape(tok_rows, 1)
    cosine, sine_table = rope_tables(places.astype(jnp.float32), HEAD)
    inputs = hidden_in.reshape(tok_rows, width_all).astype(jnp.float32)
    gain_one = gain_attn.astype(jnp.float32)
    normed_one = normed(inputs, gain_one).astype(jnp.bfloat16)
    query_proj = jnp.dot(normed_one, query_w, preferred_element_type=jnp.float32).reshape(
        seq_count, slot_count, q_heads, HEAD
    )
    key_proj = jnp.dot(normed_one, key_w, preferred_element_type=jnp.float32).reshape(
        seq_count, slot_count, kv_heads, HEAD
    )
    value_low = (
        jnp.dot(normed_one, value_w, preferred_element_type=jnp.float32)
        .astype(jnp.bfloat16)
        .reshape(seq_count, slot_count, kv_heads * HEAD)
    )
    query_low = rotate(query_proj, cosine, sine_table).astype(jnp.bfloat16)
    key_low = (
        rotate(key_proj, cosine, sine_table)
        .astype(jnp.bfloat16)
        .reshape(seq_count, slot_count, kv_heads * HEAD)
    )
    key_all, value_all = (
        lax.all_gather(key_low, "ctx", axis=1, tiled=True),
        lax.all_gather(value_low, "ctx", axis=1, tiled=True),
    )

    def attend(members):
        query_seq, key_seq, value_seq, length = members
        scores = masked_scores(query_seq, key_seq, length, places, kv_heads, group_size)
        row_max = jnp.max(scores, axis=-1, keepdims=True)
        exponent = jnp.exp(scores - row_max)
        total = jnp.sum(exponent, axis=-1, keepdims=True)
        attention = (exponent / total).astype(jnp.bfloat16)
        value_grp = value_seq.reshape(value_seq.shape[0], kv_heads, HEAD)
        mixed_heads = jnp.einsum(
            "kgbt,tkh->bkgh", attention, value_grp, preferred_element_type=jnp.float32
        )
        return (mixed_heads.reshape(slot_count, q_heads * HEAD), (row_max + jnp.log(total))[..., 0])

    mixed_all, log_total = lax.map(attend, (query_low, key_all, value_all, lengths))
    attn_low = mixed_all.reshape(tok_rows, q_heads * HEAD).astype(jnp.bfloat16)
    branch = lax.psum(jnp.dot(attn_low, output_w, preferred_element_type=jnp.float32), "mp")
    middle = inputs + branch
    mlp_set = (
        lax.all_gather(w_gate, ("dp", "ctx"), axis=0, tiled=True),
        lax.all_gather(w_up, ("dp", "ctx"), axis=0, tiled=True),
        lax.all_gather(w_down, ("dp", "ctx"), axis=1, tiled=True),
        lax.all_gather(norm_mlp, ("dp", "ctx"), axis=0, tiled=True),
    )
    gate_w, up_w, down_w, gain_mlp = mlp_set
    gain_two = gain_mlp.astype(jnp.float32)
    normed_two = normed(middle, gain_two).astype(jnp.bfloat16)
    gate_proj = jnp.dot(normed_two, gate_w, preferred_element_type=jnp.float32)
    up_proj = jnp.dot(normed_two, up_w, preferred_element_type=jnp.float32)
    hidden = (jax.nn.silu(gate_proj) * up_proj).astype(jnp.bfloat16)
    mlp_out = lax.psum(
        jnp.dot(hidden, down_w, preferred_element_type=jnp.float32).astype(jnp.bfloat16), "mp"
    ).astype(jnp.float32)
    layer_out = (
        (valid_mask * (middle + mlp_out))
        .astype(jnp.bfloat16)
        .reshape(seq_count, slot_count, width_all)
    )
    grad_out = valid_mask * cotangent.reshape(tok_rows, width_all).astype(jnp.float32)
    grad_mlp = grad_out.astype(jnp.bfloat16)
    gate_back, up_back, down_back, gain_mlp_back = (
        lax.all_gather(w_gate, ("dp", "ctx"), axis=0, tiled=True),
        lax.all_gather(w_up, ("dp", "ctx"), axis=0, tiled=True),
        lax.all_gather(w_down, ("dp", "ctx"), axis=1, tiled=True),
        lax.all_gather(norm_mlp, ("dp", "ctx"), axis=0, tiled=True),
    )
    grad_hidden = jnp.einsum("tm,fm->tf", grad_mlp, down_back, preferred_element_type=jnp.float32)
    grad_down = jnp.einsum("tf,tm->fm", hidden, grad_mlp, preferred_element_type=jnp.float32)
    sigmoid_gate = jax.nn.sigmoid(gate_proj)
    grad_gate_low = (
        grad_hidden * up_proj * sigmoid_gate * (1.0 + gate_proj * (1.0 - sigmoid_gate))
    ).astype(jnp.bfloat16)
    grad_up_low = (grad_hidden * gate_proj * sigmoid_gate).astype(jnp.bfloat16)
    grad_gate = jnp.einsum(
        "td,tf->df", normed_two, grad_gate_low, preferred_element_type=jnp.float32
    )
    grad_up = jnp.einsum("td,tf->df", normed_two, grad_up_low, preferred_element_type=jnp.float32)
    partial_two = jnp.einsum(
        "tf,df->td", grad_gate_low, gate_back, preferred_element_type=jnp.float32
    ) + jnp.einsum("tf,df->td", grad_up_low, up_back, preferred_element_type=jnp.float32)
    grad_normed_two = lax.psum(partial_two, "mp")
    grad_middle_norm, grad_gain_two = norm_back(
        middle, gain_mlp_back.astype(jnp.float32), grad_normed_two
    )
    mlp_grads = (
        lax.psum_scatter(grad_gate, ("dp", "ctx"), scatter_dimension=0, tiled=True),
        lax.psum_scatter(grad_up, ("dp", "ctx"), scatter_dimension=0, tiled=True),
        lax.psum_scatter(grad_down, ("dp", "ctx"), scatter_dimension=1, tiled=True),
        lax.psum_scatter(grad_gain_two, ("dp", "ctx"), scatter_dimension=0, tiled=True),
    )
    grad_middle = grad_out + grad_middle_norm
    grad_branch = grad_middle.astype(jnp.bfloat16)
    query_back, key_back, value_back, output_back, gain_attn_back = (
        lax.all_gather(w_query, ("dp", "ctx"), axis=0, tiled=True),
        lax.all_gather(w_key, ("dp", "ctx"), axis=0, tiled=True),
        lax.all_gather(w_value, ("dp", "ctx"), axis=0, tiled=True),
        lax.all_gather(w_output, ("dp", "ctx"), axis=1, tiled=True),
        lax.all_gather(norm_attn, ("dp", "ctx"), axis=0, tiled=True),
    )
    grad_output = jnp.einsum("tq,td->qd", attn_low, grad_branch, preferred_element_type=jnp.float32)
    grad_attn_low = (
        jnp.einsum("td,qd->tq", grad_branch, output_back, preferred_element_type=jnp.float32)
        .astype(jnp.bfloat16)
        .reshape(seq_count, slot_count, q_heads, HEAD)
    )

    def attend_back(members):
        query_seq, key_seq, value_seq, length, log_seq, grad_seq = members
        scores = masked_scores(query_seq, key_seq, length, places, kv_heads, group_size)
        attention = jnp.exp(scores - log_seq[..., None])
        query_grp = query_seq.reshape(slot_count, kv_heads, group_size, HEAD)
        key_grp = key_seq.reshape(key_seq.shape[0], kv_heads, HEAD)
        value_grp = value_seq.reshape(value_seq.shape[0], kv_heads, HEAD)
        grad_grp = grad_seq.reshape(slot_count, kv_heads, group_size, HEAD)
        grad_attention = jnp.einsum(
            "bkgh,tkh->kgbt", grad_grp, value_grp, preferred_element_type=jnp.float32
        )
        inner = jnp.sum(attention * grad_attention, axis=-1, keepdims=True)
        grad_scores = (attention * (grad_attention - inner)).astype(jnp.bfloat16)
        scale_qk = HEAD ** (-0.5)
        grad_query_seq = (
            jnp.einsum("kgbt,tkh->bkgh", grad_scores, key_grp, preferred_element_type=jnp.float32)
            * scale_qk
        )
        grad_key_seq = (
            jnp.einsum("kgbt,bkgh->tkh", grad_scores, query_grp, preferred_element_type=jnp.float32)
            * scale_qk
        )
        grad_value_seq = jnp.einsum(
            "kgbt,bkgh->tkh",
            attention.astype(jnp.bfloat16),
            grad_grp,
            preferred_element_type=jnp.float32,
        )
        key_rows = key_grp.shape[0]
        return (
            grad_query_seq.reshape(slot_count, q_heads, HEAD),
            grad_key_seq.reshape(key_rows, kv_heads * HEAD),
            grad_value_seq.reshape(key_rows, kv_heads * HEAD),
        )

    grad_query_rot, grad_key_all, grad_value_all = lax.map(
        attend_back, (query_low, key_all, value_all, lengths, log_total, grad_attn_low)
    )
    grad_key_rot, grad_value_rot = (
        lax.psum_scatter(grad_key_all, "ctx", scatter_dimension=1, tiled=True),
        lax.psum_scatter(grad_value_all, "ctx", scatter_dimension=1, tiled=True),
    )
    grad_query_low = (
        rotate_back(grad_query_rot, cosine, sine_table)
        .astype(jnp.bfloat16)
        .reshape(tok_rows, q_heads * HEAD)
    )
    grad_key_low = (
        rotate_back(grad_key_rot.reshape(seq_count, slot_count, kv_heads, HEAD), cosine, sine_table)
        .astype(jnp.bfloat16)
        .reshape(tok_rows, kv_heads * HEAD)
    )
    grad_value_low = grad_value_rot.astype(jnp.bfloat16).reshape(tok_rows, kv_heads * HEAD)
    grad_query = jnp.einsum(
        "td,tq->dq", normed_one, grad_query_low, preferred_element_type=jnp.float32
    )
    grad_key = jnp.einsum("td,tq->dq", normed_one, grad_key_low, preferred_element_type=jnp.float32)
    grad_value = jnp.einsum(
        "td,tq->dq", normed_one, grad_value_low, preferred_element_type=jnp.float32
    )
    partial_one = jnp.einsum(
        "tq,dq->td", grad_query_low, query_back, preferred_element_type=jnp.float32
    )
    partial_one = partial_one + jnp.einsum(
        "tq,dq->td", grad_key_low, key_back, preferred_element_type=jnp.float32
    )
    partial_one = partial_one + jnp.einsum(
        "tq,dq->td", grad_value_low, value_back, preferred_element_type=jnp.float32
    )
    grad_normed_one = lax.psum(partial_one, "mp")
    grad_inputs_norm, grad_gain_one = norm_back(
        inputs, gain_attn_back.astype(jnp.float32), grad_normed_one
    )
    input_grad = (
        (grad_middle + grad_inputs_norm)
        .astype(jnp.bfloat16)
        .reshape(seq_count, slot_count, width_all)
    )
    attn_grads = (
        lax.psum_scatter(grad_query, ("dp", "ctx"), scatter_dimension=0, tiled=True),
        lax.psum_scatter(grad_key, ("dp", "ctx"), scatter_dimension=0, tiled=True),
        lax.psum_scatter(grad_value, ("dp", "ctx"), scatter_dimension=0, tiled=True),
        lax.psum_scatter(grad_output, ("dp", "ctx"), scatter_dimension=1, tiled=True),
        lax.psum_scatter(grad_gain_one, ("dp", "ctx"), scatter_dimension=0, tiled=True),
    )
    return (
        layer_out,
        input_grad,
        attn_grads[4],
        attn_grads[0],
        attn_grads[1],
        attn_grads[2],
        attn_grads[3],
        mlp_grads[3],
        mlp_grads[0],
        mlp_grads[1],
        mlp_grads[2],
    )


SPLIT = 4


class Column:
    def __init__(self, owned, width):
        self.x, self.ctx, self.z = (lax.axis_index(name) for name in ("dp", "ctx", "mp"))
        self.core = lax.rem(self.ctx, 2)
        self.last = lax.axis_size("mp") - 1
        self.owned, self.rows, self.width = owned, owned * (self.last + 1), width
        self.step = width // SPLIT
        self.sibling = (self.x, self.ctx + 1 - 2 * self.core, self.z)
        self.above, self.below = (self.x, self.ctx, self.z + 1), (self.x, self.ctx, self.z - 1)
        self.neighbours = (self.sibling,)

    def enter(self):
        barrier = pltpu.get_barrier_semaphore()

        def greet(device):
            pl.semaphore_signal(
                barrier, inc=1, device_id=device, device_id_type=pl.DeviceIdType.MESH
            )

        for device in self.neighbours:
            greet(device)

        @pl.when(self.z < self.last)
        def _():
            greet(self.above)

        @pl.when(self.z > 0)
        def _():
            greet(self.below)

        ends = jnp.where(self.z == 0, 1, 0) + jnp.where(self.z == self.last, 1, 0)
        pl.semaphore_wait(barrier, len(self.neighbours) + 2 - ends)

    def place(self, core, block):
        return pl.ds(pl.multiple_of(core * self.rows + block * self.owned, 16), self.owned)

    def block(self, at):
        return pl.ds(pl.multiple_of(at * self.owned, 16), self.owned)

    def columns(self, piece):
        return pl.ds(piece * self.step, self.step)


def remote(src, dst, send, recv, device):
    return pltpu.make_async_remote_copy(
        src_ref=src,
        dst_ref=dst,
        send_sem=send,
        recv_sem=recv,
        device_id=device,
        device_id_type=pl.DeviceIdType.MESH,
    )


class SumChain:
    def __init__(self, col, part, held, up_out, up_in, down_out, down_in, core_sem, up_sem, down_sem):
        self.col, self.part, self.held = col, part, held
        self.ways = (
            (col.above, up_out, up_in, up_sem, 1),
            (col.below, down_out, down_in, down_sem, -1),
        )
        self.core_sem = core_sem

    def across(self, block):
        col = self.col
        return remote(
            self.part.at[col.place(1 - col.core, block)],
            self.held.at[col.block(block)],
            self.core_sem.at[0, block],
            self.core_sem.at[1, block],
            col.sibling,
        )

    def open(self):
        for block in range(self.col.last + 1):
            self.across(block).start()

    def own(self, at, cols):
        col = self.col
        mine = self.part[col.place(col.core, at), cols].astype(jnp.float32)
        return mine + self.held[col.block(at), cols].astype(jnp.float32)

    def hop(self, way, step, piece):
        device, out, into, sem, _ = way
        cols = self.col.columns(piece)
        return remote(
            out.at[step, :, cols],
            into.at[step, :, cols],
            sem.at[0, step, piece],
            sem.at[1, step, piece],
            device,
        )

    def far(self, way):
        return self.col.z if way[4] == 1 else self.col.last - self.col.z

    def step(self, step):
        col = self.col
        for way in self.ways:
            sign = way[4]

            @pl.when(self.far(way) <= step)
            def _(way=way, sign=sign):
                at = col.z + sign * (col.last - step)
                self.across(at).wait_recv()
                for piece in range(SPLIT):
                    cols = col.columns(piece)
                    out = way[1]
                    total = self.own(at, cols)
                    if step:

                        @pl.when(self.far(way) > 0)
                        def _(total=total, cols=cols, piece=piece):
                            self.hop(way, step - 1, piece).wait_recv()
                            got = way[2][step - 1, :, cols].astype(jnp.float32)
                            out[step, :, cols] = (total + got).astype(out.dtype)

                        @pl.when(self.far(way) == 0)
                        def _(total=total, cols=cols):
                            out[step, :, cols] = total.astype(out.dtype)

                    else:
                        out[step, :, cols] = total.astype(out.dtype)
                    self.hop(way, step, piece).start()

    def close(self, result):
        col = self.col
        final = col.last - 1
        self.across(col.z).wait_recv()
        result[...] = self.own(col.z, slice(None))
        for way in self.ways:

            @pl.when(self.far(way) > 0)
            def _(way=way):
                for piece in range(SPLIT):
                    self.hop(way, final, piece).wait_recv()
                result[...] += way[2][final].astype(jnp.float32)

    def drain(self):
        for block in range(self.col.last + 1):
            self.across(block).wait_send()
        for step in range(self.col.last):
            for way in self.ways:

                @pl.when(self.far(way) <= step)
                def _(way=way, step=step):
                    for piece in range(SPLIT):
                        self.hop(way, step, piece).wait_send()


class ShareChain:
    def __init__(self, col, whole, up_sem, down_sem, core_sem=None):
        self.col, self.whole, self.core_sem = col, whole, core_sem
        self.ways = ((col.above, up_sem, 1), (col.below, down_sem, -1))

    def rows(self, at):
        return self.col.block(at) if self.core_sem is None else self.col.place(self.col.core, at)

    def far(self, way):
        return self.col.z if way[2] == 1 else self.col.last - self.col.z

    def hop(self, way, step, piece, origin):
        device, sem, _ = way
        ref = self.whole.at[self.rows(origin), self.col.columns(piece)]
        return remote(ref, ref, sem.at[0, step, piece], sem.at[1, step, piece], device)

    def across(self, origin):
        ref = self.whole.at[self.rows(origin)]
        return remote(
            ref, ref, self.core_sem.at[0, origin], self.core_sem.at[1, origin], self.col.sibling
        )

    def across_in(self, origin):
        ref = self.whole.at[self.col.place(1 - self.col.core, origin)]
        return remote(
            ref, ref, self.core_sem.at[0, origin], self.core_sem.at[1, origin], self.col.sibling
        )

    def step(self, step):
        col = self.col
        for way in self.ways:
            origin = col.z - way[2] * step

            @pl.when(self.far(way) >= step)
            def _(way=way, origin=origin):
                for piece in range(SPLIT):
                    if step:
                        self.hop(way, step - 1, piece, origin).wait_recv()
                    if step < col.last:

                        @pl.when(self.far(way) < col.last)
                        def _(piece=piece):
                            self.hop(way, step, piece, origin).start()

                if step and self.core_sem is not None:
                    self.across(origin).start()

        if step == 0 and self.core_sem is not None:
            self.across(col.z).start()

    def drain(self):
        col = self.col
        for step in range(col.last):
            for way in self.ways:

                @pl.when((self.far(way) >= step) & (self.far(way) < col.last))
                def _(way=way, step=step):
                    for piece in range(SPLIT):
                        self.hop(way, step, piece, col.z - way[2] * step).wait_send()

        if self.core_sem is not None:
            for origin in range(col.last + 1):
                self.across_in(origin).wait_recv()
                self.across(origin).wait_send()


def sum_scratch(owned, z_count, width):
    hops = z_count - 1
    low = jnp.bfloat16
    return [
        pltpu.VMEM((owned * z_count, width), low),
        pltpu.VMEM((hops, owned, width), low),
        pltpu.VMEM((hops, owned, width), low),
        pltpu.VMEM((hops, owned, width), low),
        pltpu.VMEM((hops, owned, width), low),
        pltpu.SemaphoreType.DMA((2, z_count)),
        pltpu.SemaphoreType.DMA((2, hops, SPLIT)),
        pltpu.SemaphoreType.DMA((2, hops, SPLIT)),
    ]


def share_scratch(z_count, cores):
    hops = z_count - 1
    sems = [pltpu.SemaphoreType.DMA((2, hops, SPLIT))] * 2
    return sems + ([pltpu.SemaphoreType.DMA((2, z_count))] if cores else [])


GROUP = 384


class Plane(Column):
    def __init__(self, owned, width):
        super().__init__(owned, width)
        self.over_x = (1 - self.x, self.ctx, self.z)
        self.over_y = (self.x, lax.rem(self.ctx + 2, 4), self.z)
        self.part = width // 4
        self.middle = width // 8

        self.neighbours = (self.sibling, self.over_x, self.over_y)


def start_kernel(
    hidden,
    gains,
    keep,
    give,
    gate,
    up,
    down,
    output,
    qkv,
    h1,
    w,
    gains_all,
    out_own,
    wide,
    down_t,
    out_t,
    core_sem,
    gain_sem,
    x_sem,
    y_sem,
    far_sem,
    local_sem,
    wide_sem,
    out_sem,
    h1_sem,
):
    x_at, ctx_at, z_at = (lax.axis_index(name) for name in ("dp", "ctx", "mp"))
    core = lax.rem(ctx_at, 2)
    y_at = (ctx_at - core) // 2
    rows, part = hidden.shape[0], keep.shape[0]
    chip_part = 2 * part
    ff = gate.shape[1] // 2
    groups = ff // 128

    def device(turn, flip):
        x_to = 1 - x_at if turn >= 2 else x_at
        y_to = 1 - y_at if turn % 2 else y_at
        core_to = 1 - core if flip else core
        return (x_to, 2 * y_to + core_to, z_at)

    def half_rows(which):
        return pl.ds(pl.multiple_of(which * part, 16), part)

    sibling, over_x, over_y = device(0, 1), device(2, 0), device(1, 0)
    barrier = pltpu.get_barrier_semaphore()
    others = [(turn, flip) for turn in range(4) for flip in range(2) if turn or flip]
    for turn, flip in others:
        pl.semaphore_signal(
            barrier, inc=1, device_id=device(turn, flip), device_id_type=pl.DeviceIdType.MESH
        )
    w[0, half_rows(core)] = keep[...]
    gains_all[core] = gains[...]
    pl.semaphore_wait(barrier, len(others))

    mine = half_rows(core)
    swap = remote(give, w.at[0, mine], core_sem.at[0], core_sem.at[1], sibling)
    swap.start()

    def gain_copy(turn, flip):
        slot = 2 * turn + core
        index = 2 * turn + flip
        return remote(
            gains, gains_all.at[slot], gain_sem.at[0, index], gain_sem.at[1, index], device(turn, flip)
        )

    for turn, flip in others:
        gain_copy(turn, flip).start()

    def cross(which, to_x):
        sem = x_sem if to_x else y_sem
        rows_of = half_rows(which)
        return remote(
            w.at[0, rows_of],
            w.at[2 if to_x else 1, rows_of],
            sem.at[0, which],
            sem.at[1, which],
            over_x if to_x else over_y,
        )

    cross(core, True).start()
    cross(core, False).start()

    def wide_copies(group, kind, source):
        from_here = pl.ds(pl.multiple_of(core * ff + group * 128, 128), 128)
        from_there = pl.ds(pl.multiple_of((1 - core) * ff + group * 128, 128), 128)
        to = pl.ds(pl.multiple_of(group * GROUP + kind * 128, 128), 128)
        here = pltpu.make_async_copy(
            source.at[:, from_here], wide.at[mine, to], local_sem.at[kind, group]
        )
        there = remote(
            source.at[:, from_there],
            wide.at[mine, to],
            wide_sem.at[0, kind, group],
            wide_sem.at[1, kind, group],
            sibling,
        )
        return here, there

    def each_wide(kind, source, act):
        def body(group, carry):
            for copy in wide_copies(group, kind, source):
                act(copy)
            return carry

        lax.fori_loop(0, groups, body, 0)

    each_wide(0, gate, lambda copy: copy.start())
    each_wide(1, up, lambda copy: copy.start())
    swap.wait_recv()
    cross(1 - core, True).start()
    cross(1 - core, False).start()

    down_t[...] = down[...].T
    each_wide(2, down_t, lambda copy: copy.start())
    q_rows = output.shape[0] // 2
    out_own[mine, q_rows:] = jnp.zeros((part, out_own.shape[1] - q_rows), out_own.dtype)
    out_t[:, q_rows:] = jnp.zeros((part, out_own.shape[1] - q_rows), out_own.dtype)
    out_own[mine, :q_rows] = output[pl.ds(pl.multiple_of(core * q_rows, 16), q_rows), :].T
    out_t[:, :q_rows] = output[pl.ds(pl.multiple_of((1 - core) * q_rows, 16), q_rows), :].T
    out_copy = remote(out_t, out_own.at[mine], out_sem.at[0], out_sem.at[1], sibling)
    out_copy.start()

    for turn, flip in others:
        gain_copy(turn, flip).wait_recv()
    place = 2 * x_at + y_at
    squares = hidden[...].astype(jnp.float32)
    scale = lax.rsqrt(jnp.mean(squares * squares, axis=-1, keepdims=True) + EPS)
    my_rows = pl.ds(pl.multiple_of(core * rows, 16), rows)
    for turn in range(4):
        at = (x_at if turn < 2 else 1 - x_at) * 2 + (1 - y_at if turn % 2 else y_at)
        block = hidden[:, pl.ds(pl.multiple_of(at * chip_part, 128), chip_part)]
        gain = gains_all[2 * turn] + gains_all[2 * turn + 1]
        h1[my_rows, turn * chip_part : (turn + 1) * chip_part] = (
            block.astype(jnp.float32) * scale * gain[:1]
        ).astype(h1.dtype)
    h1_copy = remote(h1.at[my_rows], h1.at[my_rows], h1_sem.at[0], h1_sem.at[1], sibling)
    h1_copy.start()

    def relay(to_x):
        which = 1 if to_x else 0
        rows_of = half_rows(which)
        return remote(
            w.at[1 if to_x else 2, rows_of],
            w.at[3, rows_of],
            far_sem.at[0, which],
            far_sem.at[1, which],
            over_x if to_x else over_y,
        )

    def block_dot(turn):
        left = h1[:, turn * chip_part : (turn + 1) * chip_part]
        return jnp.dot(left, w[turn], preferred_element_type=jnp.float32)

    cross(0, True).wait_recv()
    relay(False).start()
    cross(1, False).wait_recv()
    relay(True).start()
    h1_copy.wait_recv()
    qkv[...] = block_dot(0)
    cross(1, True).wait_recv()
    qkv[...] += block_dot(2)
    cross(0, False).wait_recv()
    qkv[...] += block_dot(1)
    relay(False).wait_recv()
    relay(True).wait_recv()
    qkv[...] += block_dot(3)

    for kind, source in enumerate((gate, up, down_t)):
        each_wide(kind, source, lambda copy: copy.wait())
    swap.wait_send()
    out_copy.wait()
    h1_copy.wait_send()
    for turn, flip in others:
        gain_copy(turn, flip).wait_send()
    for which in range(2):
        for to_x in (True, False):
            cross(which, to_x).wait_send()
    relay(True).wait_send()
    relay(False).wait_send()


class Gather:
    def __init__(self, plane, own, w, x_sem, y_sem, far_sem, local_sem):
        self.plane, self.own, self.w = plane, own, w
        self.x_sem, self.y_sem, self.far_sem, self.local_sem = x_sem, y_sem, far_sem, local_sem
        self.groups = own.shape[1] // GROUP

    def columns(self, group):
        return pl.ds(pl.multiple_of(group * GROUP, 128), GROUP)

    def cross(self, group, to_x):
        plane, cols = self.plane, self.columns(group)
        sem = self.x_sem if to_x else self.y_sem
        return remote(
            self.own.at[:, cols],
            self.w.at[2 if to_x else 1, :, cols],
            sem.at[0, group],
            sem.at[1, group],
            plane.over_x if to_x else plane.over_y,
        )

    def relay(self, group, to_x):
        plane, cols = self.plane, self.columns(group)
        rows = pl.ds(plane.middle, plane.middle) if to_x else pl.ds(0, plane.middle)
        kind = 1 if to_x else 0
        return remote(
            self.w.at[1 if to_x else 2, rows, cols],
            self.w.at[3, rows, cols],
            self.far_sem.at[0, kind, group],
            self.far_sem.at[1, kind, group],
            plane.over_x if to_x else plane.over_y,
        )

    def load(self):
        return pltpu.make_async_copy(self.own, self.w.at[0], self.local_sem.at[0])

    def send(self, group):
        self.cross(group, True).start()
        self.cross(group, False).start()

    def pump(self, group):
        self.cross(group, True).wait_recv()
        self.relay(group, False).start()
        self.cross(group, False).wait_recv()
        self.relay(group, True).start()

        @pl.when(group + 2 < self.groups)
        def _():
            self.send(group + 2)

    def arrive(self, group):
        self.relay(group, False).wait_recv()
        self.relay(group, True).wait_recv()

    def drain(self):
        def body(group, carry):
            for to_x in (True, False):
                self.cross(group, to_x).wait_send()
                self.relay(group, to_x).wait_send()
            return carry

        lax.fori_loop(0, self.groups, body, 0)


class Scatter:
    def __init__(self, plane, stage, upper, lower, x_one, y_two, sem):
        self.plane, self.stage, self.sem = plane, stage, sem
        first, second = pl.ds(0, plane.middle), pl.ds(plane.middle, plane.middle)
        self.kinds = (
            (2, first, upper, plane.over_x),
            (2, second, lower, plane.over_y),
            (1, first, x_one, plane.over_x),
            (0, second, y_two, plane.over_y),
        )

    def copies(self, group):
        cols = pl.ds(pl.multiple_of(group * GROUP, 128), GROUP)
        for kind, (block, rows, into, device) in enumerate(self.kinds):
            yield remote(
                self.stage.at[block, rows, cols],
                into.at[:, cols],
                self.sem.at[0, kind, group],
                self.sem.at[1, kind, group],
                device,
            )

    def send(self, group):
        for copy in self.copies(group):
            copy.start()

    def drain(self, groups):
        def body(group, carry):
            for copy in self.copies(group):
                copy.wait()
            return carry

        lax.fori_loop(0, groups, body, 0)


NT = (((1,), (1,)), ((), ()))


def mlp_kernel(
    branch,
    inputs,
    gain,
    dout,
    valid,
    dm,
    own,
    da,
    d_middle,
    layer,
    d_gain,
    own_grad,
    stage,
    upper,
    lower,
    x_one,
    y_two,
    w,
    h2,
    h2_t,
    dm_t,
    part,
    mlp_part,
    dh2,
    middle,
    mlp,
    zd,
    tile,
    tile_own,
    x_sem,
    y_sem,
    far_sem,
    local_sem,
    scatter_sem,
    *scratch,
):
    f32 = jnp.float32
    plane = Plane(inputs.shape[0], inputs.shape[1])
    size = plane.part
    gather = Gather(plane, own, w, x_sem, y_sem, far_sem, local_sem)
    groups = gather.groups
    scatter = Scatter(plane, stage, upper, lower, x_one, y_two, scatter_sem)
    total = SumChain(plane, part, *scratch[:8])
    share = ShareChain(plane, h2, *scratch[8:11])
    total_back = SumChain(plane, part, *scratch[11:19])
    second = SumChain(plane, mlp_part, *scratch[:5], *scratch[19:22])
    share_back = ShareChain(plane, da, *scratch[22:25])

    def cut(turn):
        return slice(turn * size, (turn + 1) * size)

    load_part = pltpu.make_async_copy(branch, part, local_sem.at[1])
    load_part.start()
    gather.load().start()
    load_part.wait()
    plane.enter()
    total.open()
    gather.send(0)
    gather.send(1)
    for step in range(plane.last):
        total.step(step)
        if step == 0:
            for turn in range(4):
                dm_t[cut(turn)] = dm[:, cut(turn)].T
    total.close(middle)
    middle[...] += inputs[...]
    h2[plane.place(plane.core, plane.z)] = normed(middle[...], gain[...]).astype(h2.dtype)
    gather.pump(0)
    for step in range(plane.last + 1):
        share.step(step)
        if step == 1:
            gather.pump(1)
        if step == plane.last:
            gather.pump(2)
    total.drain()
    share.drain()
    for turn in range(4):
        h2_t[cut(turn)] = h2[:, cut(turn)].T
    dh2[...] = jnp.zeros_like(dh2)
    gather.load().wait()

    def group_body(group, carry):
        start = pl.multiple_of(group * GROUP, 128)
        gu_cols, down_cols = pl.ds(start, 256), pl.ds(start + 256, 128)
        cols = pl.ds(start, GROUP)
        gather.arrive(group)
        gu = jnp.zeros((dm.shape[0], 256), f32)
        d_hidden = jnp.zeros((dm.shape[0], 128), f32)
        for turn in range(4):
            gu += jnp.dot(h2[:, cut(turn)], w[turn, :, gu_cols], preferred_element_type=f32)
            d_hidden += jnp.dot(dm[:, cut(turn)], w[turn, :, down_cols], preferred_element_type=f32)
        gate, up = gu[:, :128], gu[:, 128:]
        sigma = jax.nn.sigmoid(gate)
        silu = gate * sigma
        zd[:, pl.ds(start, 128)] = (
            d_hidden * up * sigma * (1.0 + gate * (1.0 - sigma))
        ).astype(zd.dtype)
        zd[:, pl.ds(start + 128, 128)] = (d_hidden * silu).astype(zd.dtype)
        zd[:, down_cols] = (silu * up).astype(zd.dtype)
        d_gu, hidden = zd[:, gu_cols], zd[:, down_cols]
        for turn in range(4):
            dh2[:, cut(turn)] += lax.dot_general(
                d_gu, w[turn, :, gu_cols], NT, preferred_element_type=f32
            )
            grad_gu = jnp.dot(h2_t[cut(turn)], d_gu, preferred_element_type=f32)
            grad_down = jnp.dot(dm_t[cut(turn)], hidden, preferred_element_type=f32)
            if turn:
                tile[turn - 1, :, :256] = grad_gu.astype(tile.dtype)
                tile[turn - 1, :, 256:] = grad_down.astype(tile.dtype)
            else:
                tile_own[:, :256] = grad_gu
                tile_own[:, 256:] = grad_down
        keep = pltpu.make_async_copy(tile, stage.at[:, :, cols], local_sem.at[2])
        keep_own = pltpu.make_async_copy(tile_own, own_grad.at[:, cols], local_sem.at[3])
        keep.start()
        keep_own.start()

        @pl.when(group + 3 < groups)
        def _():
            gather.pump(group + 3)

        keep.wait()
        keep_own.wait()

        @pl.when(group == 3)
        def _():
            for before in range(3):
                scatter.send(before)

        @pl.when(group >= 3)
        def _():
            scatter.send(group)

        return carry

    lax.fori_loop(0, groups, group_body, 0)
    for turn in range(4):
        part[:, cut(turn)] = dh2[:, cut(turn)].astype(part.dtype)
    total_back.open()
    for step in range(plane.last):
        total_back.step(step)
        for turn in range(4):
            if turn % plane.last == step:
                out = jnp.zeros((dm.shape[0], size), f32)
                for group in range(groups):
                    cols = slice(group * GROUP + 256, group * GROUP + 384)
                    out += lax.dot_general(
                        zd[:, cols], w[turn, :, cols], NT, preferred_element_type=f32
                    )
                mlp_part[:, cut(turn)] = out.astype(mlp_part.dtype)
    second.open()
    total_back.close(d_middle)
    d_norm, d_gain_row = norm_back(middle[...], gain[...], d_middle[...])
    d_gain[...] = d_gain_row[None]
    d_middle[...] = dout[...] + d_norm
    da[plane.place(plane.core, plane.z)] = d_middle[...].astype(da.dtype)
    for step in range(plane.last + 1):
        share_back.step(step)
        if step < plane.last:
            second.step(step)
    second.close(mlp)
    layer[...] = (valid[...] * (middle[...] + mlp[...])).astype(layer.dtype)
    total_back.drain()
    second.drain()
    share_back.drain()
    gather.drain()
    scatter.drain(groups)


def input_kernel(
    part, layer, d_middle, inputs, gain, layer_all, grad_all, d_gain, d_normed, *scratch
):
    col = Column(inputs.shape[0], inputs.shape[1])
    total = SumChain(col, part, *scratch[:8])
    first = ShareChain(col, layer_all, *scratch[8:10])
    share = ShareChain(col, grad_all, *scratch[10:])
    layer_all[col.block(col.z)] = layer[...]
    col.enter()
    total.open()
    for step in range(col.last + 1):
        if step < col.last:
            total.step(step)
        first.step(step)
    total.close(d_normed)
    d_norm, d_gain_row = norm_back(inputs[...], gain[...], d_normed[...])
    d_gain[...] = d_gain_row[None]
    grad_all[col.block(col.z)] = (d_middle[...] + d_norm).astype(grad_all.dtype)
    for step in range(col.last + 1):
        share.step(step)
    total.drain()
    first.drain()
    share.drain()


def column_call(body, outs, scratch, collective_id, name):
    return pl.pallas_call(
        body,
        out_shape=[jax.ShapeDtypeStruct(shape, dtype) for shape, dtype in outs],
        scratch_shapes=scratch,
        name=name,
        cost_estimate=pl.CostEstimate(flops=0, bytes_accessed=150_000_000, transcendentals=0),
        compiler_params=pltpu.CompilerParams(
            collective_id=collective_id, has_side_effects=True, vmem_limit_bytes=32 * 2**20
        ),
    )


CORE_SWAP = [(0, 1), (1, 0), (2, 3), (3, 2)]
Y_SWAP = [(0, 2), (1, 3), (2, 0), (3, 1)]
X_SWAP = [(0, 1), (1, 0)]


def over_core(tensor):
    return lax.ppermute(tensor, "ctx", CORE_SWAP)


class Link:
    def __init__(self, axis, pairs):
        self.axis, self.pairs, self.sent = axis, pairs, []

    def send(self, tensor):
        if len(self.sent) >= 2:
            tensor, _ = lax.optimization_barrier((tensor, self.sent[-2]))
        got = lax.ppermute(tensor, self.axis, self.pairs)
        self.sent.append(got)
        return got


def on_plane(
    hidden_in,
    cotangent,
    lengths,
    norm_attn,
    w_query,
    w_key,
    w_value,
    w_output,
    norm_mlp,
    w_gate,
    w_up,
    w_down,
):
    low = jnp.bfloat16
    f32 = jnp.float32
    _, rows, width = hidden_in.shape
    part = w_query.shape[0]
    chip_part, chip_rows = 2 * part, 2 * rows
    x_at, ctx_at, z_at = lax.axis_index("dp"), lax.axis_index("ctx"), lax.axis_index("mp")
    y_at, core = ctx_at // 2, ctx_at % 2
    first = core == 0
    place = 2 * x_at + y_at
    z_count = lax.axis_size("mp")
    owned = rows // z_count
    x_link, y_link = Link("dp", X_SWAP), Link("ctx", Y_SWAP)

    def relative(tensor):
        return jnp.concatenate(
            [
                lax.dynamic_slice_in_dim(tensor, (place ^ turn) * chip_part, chip_part, axis=-1)
                for turn in range(4)
            ],
            axis=-1,
        )

    def both(mine, other, axis):
        return jnp.where(
            first,
            jnp.concatenate([mine, other], axis=axis),
            jnp.concatenate([other, mine], axis=axis),
        )

    def half(tensor, which, axis):
        size = tensor.shape[axis] // 2
        return lax.dynamic_slice_in_dim(tensor, which * size, size, axis=axis)

    def cut(tensor, turn):
        return tensor[..., turn * chip_part : (turn + 1) * chip_part]

    def after(tensor, other):
        return lax.optimization_barrier((tensor, other))[0]

    def gather(block):
        middle = block.shape[0] // 2
        from_x = x_link.send(block)
        from_y = y_link.send(block)
        upper = y_link.send(from_x[:middle])
        lower = x_link.send(from_y[middle:])
        return [block, from_y, from_x, jnp.concatenate([upper, lower], axis=0)]

    def scatter_first(parts):
        _, for_y, for_x, for_far = parts
        middle = for_far.shape[0] // 2
        upper = x_link.send(for_far[:middle].astype(low))
        lower = y_link.send(for_far[middle:].astype(low))
        x_one = x_link.send(for_x[:middle].astype(low))
        y_two = y_link.send(for_y[middle:].astype(low))
        return upper, lower, x_one, y_two

    def scatter_second(parts, came):
        _, for_y, for_x, _ = parts
        middle = for_y.shape[0] // 2
        upper, lower, _, _ = came
        y_one = y_link.send((for_y[:middle].astype(f32) + upper.astype(f32)).astype(low))
        x_two = x_link.send((for_x[middle:].astype(f32) + lower.astype(f32)).astype(low))
        return y_one, x_two

    def scatter_end(parts, came, last):
        own = parts[0]
        middle = own.shape[0] // 2
        _, _, x_one, y_two = came
        y_one, x_two = last
        return jnp.concatenate(
            [
                own[:middle] + x_one.astype(f32) + y_one.astype(f32),
                own[middle:] + x_two.astype(f32) + y_two.astype(f32),
            ],
            axis=0,
        )

    def matmul(left, right, dims):
        return lax.dot_general(left, right, (dims, ((), ())), preferred_element_type=f32)

    def parts(left, blocks, dims):
        return jnp.concatenate([matmul(left, block, dims).astype(low) for block in blocks], axis=1)

    nn, nt, tn = ((1,), (0,)), ((1,), (1,)), ((0,), (0,))

    heads = w_query.shape[1] // HEAD // 2
    kv_heads = w_key.shape[1] // HEAD // 2
    group = heads // kv_heads
    q_cols, k_cols = heads * HEAD, kv_heads * HEAD
    qkv_cols = q_cols + 2 * k_cols
    ff = w_gate.shape[1] // 2

    def lanes(count):
        return -(-count // 128) * 128

    def qkv_half(which):
        pieces = [half(weight, which, 1) for weight in (w_query, w_key, w_value)]
        pad = jnp.zeros((part, lanes(qkv_cols) - qkv_cols), low)
        return jnp.concatenate(pieces + [pad], axis=1)

    gains = jnp.zeros((8, chip_part), f32)
    gain_rows = jnp.stack([norm_attn, norm_mlp]).astype(f32)
    gains = lax.dynamic_update_slice(gains, gain_rows, (0, core * part))

    any_space = pl.BlockSpec(memory_space=pl.ANY)
    vmem = pl.BlockSpec(memory_space=pltpu.VMEM)
    wide_cols = 3 * ff
    groups = wide_cols // GROUP
    dma = pltpu.SemaphoreType.DMA
    qkv, h1, qkv_w, gains_all, out_own, wide = pl.pallas_call(
        start_kernel,
        out_shape=[
            jax.ShapeDtypeStruct((chip_rows, lanes(qkv_cols)), f32),
            jax.ShapeDtypeStruct((chip_rows, width), low),
            jax.ShapeDtypeStruct((4, chip_part, lanes(qkv_cols)), low),
            jax.ShapeDtypeStruct((8, 8, chip_part), f32),
            jax.ShapeDtypeStruct((chip_part, lanes(q_cols)), low),
            jax.ShapeDtypeStruct((chip_part, wide_cols), low),
        ],
        in_specs=[vmem, vmem, vmem, vmem, any_space, any_space, vmem, vmem],
        out_specs=[vmem, vmem, vmem, vmem, vmem, any_space],
        scratch_shapes=[
            pltpu.VMEM((part, 2 * ff), low),
            pltpu.VMEM((part, lanes(q_cols)), low),
            dma((2,)),
            dma((2, 8)),
            dma((2, 2)),
            dma((2, 2)),
            dma((2, 2)),
            dma((3, groups)),
            dma((2, 3, groups)),
            dma((2,)),
            dma((2,)),
        ],
        name="start",
        cost_estimate=pl.CostEstimate(flops=0, bytes_accessed=100_000_000, transcendentals=0),
        compiler_params=pltpu.CompilerParams(
            collective_id=1, has_side_effects=True, vmem_limit_bytes=32 * 2**20
        ),
    )(hidden_in[0], gains, qkv_half(core), qkv_half(1 - core), w_gate, w_up, w_down, w_output)
    gains_rel = (gains_all[0::2] + gains_all[1::2])[:, :2]
    gain_one, gain_two = (gains_rel[:, row].reshape(1, width) for row in range(2))
    out_w = gather(out_own)

    length = lengths[0]
    hidden_own = lax.dynamic_slice_in_dim(hidden_in[0], z_at * owned, owned, axis=0)
    inputs_own = relative(hidden_own).astype(f32)
    slots = (y_at * 2) * rows + jnp.arange(chip_rows, dtype=jnp.int32)
    my_slots = ctx_at * rows + jnp.arange(rows, dtype=jnp.int32)
    valid = (my_slots < length).astype(f32)[:, None]
    dout = valid * relative(cotangent[0]).astype(f32)
    dm_mine = dout.astype(low)
    dm = both(dm_mine, over_core(dm_mine), 0)
    dout_own = lax.dynamic_slice_in_dim(dout, z_at * owned, owned, axis=0)
    valid_own = lax.dynamic_slice_in_dim(valid, z_at * owned, owned, axis=0)
    cosine, sine = rope_tables(slots.astype(f32), HEAD)

    q_low = rotate(qkv[:, :q_cols].reshape(chip_rows, heads, HEAD), cosine, sine).astype(low)
    k_low = rotate(
        qkv[:, q_cols : q_cols + k_cols].reshape(chip_rows, kv_heads, HEAD), cosine, sine
    ).astype(low)
    v_low = qkv[:, q_cols + k_cols : qkv_cols].astype(low)
    kv_mine = jnp.concatenate([k_low.reshape(chip_rows, k_cols), v_low], axis=1)
    kv_other = lax.ppermute(kv_mine, "ctx", Y_SWAP)
    kv_all = jnp.where(
        y_at == 0,
        jnp.concatenate([kv_mine, kv_other], axis=0),
        jnp.concatenate([kv_other, kv_mine], axis=0),
    )
    keys = kv_all[:, :k_cols].reshape(2 * chip_rows, kv_heads, HEAD)
    values = kv_all[:, k_cols:].reshape(2 * chip_rows, kv_heads, HEAD)
    q_grp = q_low.reshape(chip_rows, kv_heads, group, HEAD)
    scale = HEAD ** (-0.5)
    raw = jnp.einsum("bkgh,tkh->kgbt", q_grp, keys, preferred_element_type=f32) * scale
    key_slots = jnp.arange(2 * chip_rows, dtype=jnp.int32)
    allowed = (key_slots[None, :] <= slots[:, None]) & (key_slots[None, :] < length)
    scores = jnp.where(allowed[None, None], raw, NEG)
    exponent = jnp.exp(scores - jnp.max(scores, axis=-1, keepdims=True))
    probs = exponent / jnp.sum(exponent, axis=-1, keepdims=True)
    probs_low = probs.astype(low)
    mixed = jnp.einsum("kgbt,tkh->bkgh", probs_low, values, preferred_element_type=f32)
    attn_low = mixed.reshape(chip_rows, q_cols).astype(low)
    out_w = [block[:, :q_cols] for block in out_w]
    branch = parts(attn_low, out_w, nt)

    whole, half_rows, own = (chip_rows, width), (rows, width), (owned, width)
    middle_rows = chip_part // 2
    hops = z_count - 1
    vm = pltpu.VMEM
    outs = [
        (whole, low, vmem),
        (own, f32, vmem),
        (own, low, vmem),
        ((1, width), f32, vmem),
        ((chip_part, wide_cols), f32, any_space),
        ((3, chip_part, wide_cols), low, any_space),
    ] + [((middle_rows, wide_cols), low, any_space)] * 4
    da, d_middle, layer_own, gain_two_part, own_grad, stage, upper, lower, x_one, y_two = (
        pl.pallas_call(
            mlp_kernel,
            out_shape=[jax.ShapeDtypeStruct(shape, dtype) for shape, dtype, _ in outs],
            in_specs=[any_space, vmem, vmem, vmem, vmem, vmem, any_space],
            out_specs=[spec for _, _, spec in outs],
            scratch_shapes=[
                vm((4, chip_part, wide_cols), low),
                vm(whole, low),
                vm((width, chip_rows), low),
                vm((width, chip_rows), low),
                vm(whole, low),
                vm(whole, low),
                vm(whole, f32),
                vm(own, f32),
                vm(own, f32),
                vm((chip_rows, wide_cols), low),
                vm((3, chip_part, GROUP), low),
                vm((chip_part, GROUP), f32),
                dma((2, groups)),
                dma((2, groups)),
                dma((2, 2, groups)),
                dma((4,)),
                dma((2, 4, groups)),
            ]
            + sum_scratch(owned, z_count, width)
            + share_scratch(z_count, True)
            + sum_scratch(owned, z_count, width)
            + sum_scratch(owned, z_count, width)[5:]
            + share_scratch(z_count, True),
            name="mlp",
            cost_estimate=pl.CostEstimate(
                flops=0, bytes_accessed=600_000_000, transcendentals=0
            ),
            compiler_params=pltpu.CompilerParams(
                collective_id=2, has_side_effects=True, vmem_limit_bytes=63 * 2**20
            ),
        )(branch, inputs_own, gain_two, dout_own, valid_own, dm, wide)
    )

    wide_parts = (own_grad, stage[0], stage[1], stage[2])
    wide_came = (upper, lower, x_one, y_two)
    wide_last = scatter_second(wide_parts, wide_came)
    do = sum(matmul(cut(da, turn), out_w[turn], nn) for turn in range(4)).astype(low)
    out_parts = [matmul(cut(da, turn), attn_low, tn) for turn in range(4)]
    do_grp = do.reshape(chip_rows, kv_heads, group, HEAD)
    d_probs = jnp.einsum("bkgh,tkh->kgbt", do_grp, values, preferred_element_type=f32)
    inner = jnp.sum(probs * d_probs, axis=-1, keepdims=True)
    d_scores = (probs * (d_probs - inner)).astype(low)
    dq = jnp.einsum("kgbt,tkh->bkgh", d_scores, keys, preferred_element_type=f32) * scale
    dk = jnp.einsum("kgbt,bkgh->tkh", d_scores, q_grp, preferred_element_type=f32) * scale
    dv = jnp.einsum("kgbt,bkgh->tkh", probs_low, do_grp, preferred_element_type=f32)
    dkv = jnp.concatenate(
        [dk.reshape(2 * chip_rows, k_cols), dv.reshape(2 * chip_rows, k_cols)], axis=1
    )
    dkv_mine = half(dkv, y_at, 0) + lax.ppermute(half(dkv, 1 - y_at, 0), "ctx", Y_SWAP)
    dq_low = rotate_back(dq.reshape(chip_rows, heads, HEAD), cosine, sine).astype(low)
    dk_low = rotate_back(
        dkv_mine[:, :k_cols].reshape(chip_rows, kv_heads, HEAD), cosine, sine
    ).astype(low)
    d_qkv = jnp.concatenate(
        [
            dq_low.reshape(chip_rows, q_cols),
            dk_low.reshape(chip_rows, k_cols),
            dkv_mine[:, k_cols:].astype(low),
        ],
        axis=1,
    )
    qkv_blocks = [qkv_w[turn, :, :qkv_cols] for turn in range(4)]
    dh1 = parts(d_qkv, qkv_blocks, nt)
    qkv_parts = [matmul(cut(h1, turn), d_qkv, tn) for turn in range(4)]
    out_came = scatter_first(out_parts)
    qkv_came = scatter_first(qkv_parts)
    out_half, grad_half, gain_one_part = column_call(
        input_kernel,
        [(half_rows, low), (half_rows, low), ((1, width), f32)],
        [pltpu.VMEM(own, f32)]
        + sum_scratch(owned, z_count, width)
        + share_scratch(z_count, False) * 2,
        3,
        "input_sum",
    )(dh1, layer_own, d_middle, inputs_own, gain_one)
    out_half, grad_half, gain_one_part = after(
        (out_half, grad_half, gain_one_part), (wide_last, out_came, qkv_came)
    )
    qkv_last = scatter_second(qkv_parts, qkv_came)
    out_last = scatter_second(out_parts, out_came)
    grad_wide = scatter_end(wide_parts, wide_came, wide_last)
    grad_qkv = scatter_end(qkv_parts, qkv_came, qkv_last)
    grad_out = scatter_end(out_parts, out_came, out_last)
    gain_part = jnp.concatenate([gain_one_part, gain_two_part], axis=0)
    gain_sum = (
        cut(gain_part, 0)
        + lax.ppermute(cut(gain_part, 1), "ctx", Y_SWAP)
        + lax.ppermute(cut(gain_part, 2), "dp", X_SWAP)
        + lax.ppermute(lax.ppermute(cut(gain_part, 3), "ctx", Y_SWAP), "dp", X_SWAP)
    )
    gain_mine = half(gain_sum, core, 1) + over_core(half(gain_sum, 1 - core, 1))
    for flip in (1, 2):
        gain_mine = gain_mine + lax.ppermute(
            gain_mine, "mp", [(z, z ^ flip) for z in range(z_count)]
        )

    def to_rows(total):
        give = half(total, 1 - core, 0)
        return half(total, core, 0), over_core(give)

    wide_mine, wide_other = to_rows(grad_wide)
    qkv_mine, qkv_other = to_rows(grad_qkv)
    out_mine, out_other = to_rows(grad_out)

    def joined(start, size, mine, other):
        return both(mine[:, start : start + size], other[:, start : start + size], 1)

    def kind(total, which):
        return total.reshape(part, groups, 3, 128)[:, :, which].reshape(part, ff)

    return (
        relative(out_half)[None],
        relative(grad_half)[None],
        gain_mine[0],
        joined(0, q_cols, qkv_mine, qkv_other),
        joined(q_cols, k_cols, qkv_mine, qkv_other),
        joined(q_cols + k_cols, k_cols, qkv_mine, qkv_other),
        both(out_mine.T, out_other.T, 0),
        gain_mine[1],
        both(kind(wide_mine, 0), kind(wide_other, 0), 1),
        both(kind(wide_mine, 1), kind(wide_other, 1), 1),
        both(kind(wide_mine, 2).T, kind(wide_other, 2).T, 0),
    )


def solution(mesh):
    plane = dict(mesh.shape) == {"dp": 2, "ctx": 4, "mp": 4}
    return jax.shard_map(
        on_plane if plane else any_mesh,
        mesh=mesh,
        in_specs=(
            P("dp", "ctx", None),
            P("dp", "ctx", None),
            P("dp"),
            P(("dp", "ctx")),
            P(("dp", "ctx"), "mp"),
            P(("dp", "ctx"), "mp"),
            P(("dp", "ctx"), "mp"),
            P("mp", ("dp", "ctx")),
            P(("dp", "ctx")),
            P(("dp", "ctx"), "mp"),
            P(("dp", "ctx"), "mp"),
            P("mp", ("dp", "ctx")),
        ),
        out_specs=(
            P("dp", "ctx", None),
            P("dp", "ctx", None),
            P(("dp", "ctx")),
            P(("dp", "ctx"), "mp"),
            P(("dp", "ctx"), "mp"),
            P(("dp", "ctx"), "mp"),
            P("mp", ("dp", "ctx")),
            P(("dp", "ctx")),
            P(("dp", "ctx"), "mp"),
            P(("dp", "ctx"), "mp"),
            P("mp", ("dp", "ctx")),
        ),
        check_vma=False,
    )
```

```python
import functools

import jax
import jax.numpy as jnp
from jax import lax
from jax.experimental import pallas as pl
from jax.experimental.pallas import tpu as pltpu
from jax.sharding import PartitionSpec as P

HEAD = 80


EPS = 1e-05
THETA = 1000000.0
NEG = -1e30


def rope_tables(places, head_size):
    half = head_size // 2
    freq = THETA ** (-(jnp.arange(half, dtype=jnp.float32) * 2.0 / head_size))
    angle = places[:, None] * freq[None, :]
    return (jnp.cos(angle), jnp.sin(angle))


def rotate(tensor, cosine, sine_table):
    half = tensor.shape[-1] // 2
    first_half = tensor[..., :half]
    second_half = tensor[..., half:]
    cos_b = cosine[:, None, :]
    sin_b = sine_table[:, None, :]
    return jnp.concatenate(
        [first_half * cos_b - second_half * sin_b, second_half * cos_b + first_half * sin_b],
        axis=-1,
    )


def rotate_back(tensor, cosine, sine_table):
    half = tensor.shape[-1] // 2
    first_half = tensor[..., :half]
    second_half = tensor[..., half:]
    cos_b = cosine[:, None, :]
    sin_b = sine_table[:, None, :]
    return jnp.concatenate(
        [first_half * cos_b + second_half * sin_b, second_half * cos_b - first_half * sin_b],
        axis=-1,
    )


def normed(tensor, gain_row):
    return tensor * lax.rsqrt(jnp.mean(tensor * tensor, axis=-1, keepdims=True) + EPS) * gain_row


def norm_back(tensor, gain_row, grad_normed):
    scale_row = lax.rsqrt(jnp.mean(tensor * tensor, axis=-1, keepdims=True) + EPS)
    grad_scaled = grad_normed * gain_row
    grad_tensor = scale_row * grad_scaled - tensor * scale_row**3 * jnp.mean(
        grad_scaled * tensor, axis=-1, keepdims=True
    )
    grad_gain = jnp.sum(grad_normed * tensor * scale_row, axis=0)
    return (grad_tensor, grad_gain)


def masked_scores(query_seq, key_seq, length, places, kv_heads, group_size):
    query_grp = query_seq.reshape(query_seq.shape[0], kv_heads, group_size, HEAD)
    key_grp = key_seq.reshape(key_seq.shape[0], kv_heads, HEAD)
    raw_scores = jnp.einsum(
        "bkgh,tkh->kgbt", query_grp, key_grp, preferred_element_type=jnp.float32
    ) * HEAD ** (-0.5)
    key_places = jnp.arange(key_grp.shape[0], dtype=jnp.int32)
    allowed = (key_places[None, :] <= places[:, None]) & (key_places[None, :] < length)
    return jnp.where(allowed[None, None], raw_scores, NEG)


def any_mesh(
    hidden_in,
    cotangent,
    lengths,
    norm_attn,
    w_query,
    w_key,
    w_value,
    w_output,
    norm_mlp,
    w_gate,
    w_up,
    w_down,
):
    seq_count, slot_count, width_all = hidden_in.shape
    tok_rows = seq_count * slot_count
    attn_set = (
        lax.all_gather(w_query, ("dp", "ctx"), axis=0, tiled=True),
        lax.all_gather(w_key, ("dp", "ctx"), axis=0, tiled=True),
        lax.all_gather(w_value, ("dp", "ctx"), axis=0, tiled=True),
        lax.all_gather(w_output, ("dp", "ctx"), axis=1, tiled=True),
        lax.all_gather(norm_attn, ("dp", "ctx"), axis=0, tiled=True),
    )
    query_w, key_w, value_w, output_w, gain_attn = attn_set
    q_heads = query_w.shape[1] // HEAD
    kv_heads = key_w.shape[1] // HEAD
    group_size = q_heads // kv_heads
    first_slot = lax.axis_index("ctx") * slot_count
    places = first_slot + jnp.arange(slot_count, dtype=jnp.int32)
    valid_mask = (places[None, :] < lengths[:, None]).astype(jnp.float32).reshape(tok_rows, 1)
    cosine, sine_table = rope_tables(places.astype(jnp.float32), HEAD)
    inputs = hidden_in.reshape(tok_rows, width_all).astype(jnp.float32)
    gain_one = gain_attn.astype(jnp.float32)
    normed_one = normed(inputs, gain_one).astype(jnp.bfloat16)
    query_proj = jnp.dot(normed_one, query_w, preferred_element_type=jnp.float32).reshape(
        seq_count, slot_count, q_heads, HEAD
    )
    key_proj = jnp.dot(normed_one, key_w, preferred_element_type=jnp.float32).reshape(
        seq_count, slot_count, kv_heads, HEAD
    )
    value_low = (
        jnp.dot(normed_one, value_w, preferred_element_type=jnp.float32)
        .astype(jnp.bfloat16)
        .reshape(seq_count, slot_count, kv_heads * HEAD)
    )
    query_low = rotate(query_proj, cosine, sine_table).astype(jnp.bfloat16)
    key_low = (
        rotate(key_proj, cosine, sine_table)
        .astype(jnp.bfloat16)
        .reshape(seq_count, slot_count, kv_heads * HEAD)
    )
    key_all, value_all = (
        lax.all_gather(key_low, "ctx", axis=1, tiled=True),
        lax.all_gather(value_low, "ctx", axis=1, tiled=True),
    )

    def attend(members):
        query_seq, key_seq, value_seq, length = members
        scores = masked_scores(query_seq, key_seq, length, places, kv_heads, group_size)
        row_max = jnp.max(scores, axis=-1, keepdims=True)
        exponent = jnp.exp(scores - row_max)
        total = jnp.sum(exponent, axis=-1, keepdims=True)
        attention = (exponent / total).astype(jnp.bfloat16)
        value_grp = value_seq.reshape(value_seq.shape[0], kv_heads, HEAD)
        mixed_heads = jnp.einsum(
            "kgbt,tkh->bkgh", attention, value_grp, preferred_element_type=jnp.float32
        )
        return (mixed_heads.reshape(slot_count, q_heads * HEAD), (row_max + jnp.log(total))[..., 0])

    mixed_all, log_total = lax.map(attend, (query_low, key_all, value_all, lengths))
    attn_low = mixed_all.reshape(tok_rows, q_heads * HEAD).astype(jnp.bfloat16)
    branch = lax.psum(jnp.dot(attn_low, output_w, preferred_element_type=jnp.float32), "mp")
    middle = inputs + branch
    mlp_set = (
        lax.all_gather(w_gate, ("dp", "ctx"), axis=0, tiled=True),
        lax.all_gather(w_up, ("dp", "ctx"), axis=0, tiled=True),
        lax.all_gather(w_down, ("dp", "ctx"), axis=1, tiled=True),
        lax.all_gather(norm_mlp, ("dp", "ctx"), axis=0, tiled=True),
    )
    gate_w, up_w, down_w, gain_mlp = mlp_set
    gain_two = gain_mlp.astype(jnp.float32)
    normed_two = normed(middle, gain_two).astype(jnp.bfloat16)
    gate_proj = jnp.dot(normed_two, gate_w, preferred_element_type=jnp.float32)
    up_proj = jnp.dot(normed_two, up_w, preferred_element_type=jnp.float32)
    hidden = (jax.nn.silu(gate_proj) * up_proj).astype(jnp.bfloat16)
    mlp_out = lax.psum(
        jnp.dot(hidden, down_w, preferred_element_type=jnp.float32).astype(jnp.bfloat16), "mp"
    ).astype(jnp.float32)
    layer_out = (
        (valid_mask * (middle + mlp_out))
        .astype(jnp.bfloat16)
        .reshape(seq_count, slot_count, width_all)
    )
    grad_out = valid_mask * cotangent.reshape(tok_rows, width_all).astype(jnp.float32)
    grad_mlp = grad_out.astype(jnp.bfloat16)
    gate_back, up_back, down_back, gain_mlp_back = (
        lax.all_gather(w_gate, ("dp", "ctx"), axis=0, tiled=True),
        lax.all_gather(w_up, ("dp", "ctx"), axis=0, tiled=True),
        lax.all_gather(w_down, ("dp", "ctx"), axis=1, tiled=True),
        lax.all_gather(norm_mlp, ("dp", "ctx"), axis=0, tiled=True),
    )
    grad_hidden = jnp.einsum("tm,fm->tf", grad_mlp, down_back, preferred_element_type=jnp.float32)
    grad_down = jnp.einsum("tf,tm->fm", hidden, grad_mlp, preferred_element_type=jnp.float32)
    sigmoid_gate = jax.nn.sigmoid(gate_proj)
    grad_gate_low = (
        grad_hidden * up_proj * sigmoid_gate * (1.0 + gate_proj * (1.0 - sigmoid_gate))
    ).astype(jnp.bfloat16)
    grad_up_low = (grad_hidden * gate_proj * sigmoid_gate).astype(jnp.bfloat16)
    grad_gate = jnp.einsum(
        "td,tf->df", normed_two, grad_gate_low, preferred_element_type=jnp.float32
    )
    grad_up = jnp.einsum("td,tf->df", normed_two, grad_up_low, preferred_element_type=jnp.float32)
    partial_two = jnp.einsum(
        "tf,df->td", grad_gate_low, gate_back, preferred_element_type=jnp.float32
    ) + jnp.einsum("tf,df->td", grad_up_low, up_back, preferred_element_type=jnp.float32)
    grad_normed_two = lax.psum(partial_two, "mp")
    grad_middle_norm, grad_gain_two = norm_back(
        middle, gain_mlp_back.astype(jnp.float32), grad_normed_two
    )
    mlp_grads = (
        lax.psum_scatter(grad_gate, ("dp", "ctx"), scatter_dimension=0, tiled=True),
        lax.psum_scatter(grad_up, ("dp", "ctx"), scatter_dimension=0, tiled=True),
        lax.psum_scatter(grad_down, ("dp", "ctx"), scatter_dimension=1, tiled=True),
        lax.psum_scatter(grad_gain_two, ("dp", "ctx"), scatter_dimension=0, tiled=True),
    )
    grad_middle = grad_out + grad_middle_norm
    grad_branch = grad_middle.astype(jnp.bfloat16)
    query_back, key_back, value_back, output_back, gain_attn_back = (
        lax.all_gather(w_query, ("dp", "ctx"), axis=0, tiled=True),
        lax.all_gather(w_key, ("dp", "ctx"), axis=0, tiled=True),
        lax.all_gather(w_value, ("dp", "ctx"), axis=0, tiled=True),
        lax.all_gather(w_output, ("dp", "ctx"), axis=1, tiled=True),
        lax.all_gather(norm_attn, ("dp", "ctx"), axis=0, tiled=True),
    )
    grad_output = jnp.einsum("tq,td->qd", attn_low, grad_branch, preferred_element_type=jnp.float32)
    grad_attn_low = (
        jnp.einsum("td,qd->tq", grad_branch, output_back, preferred_element_type=jnp.float32)
        .astype(jnp.bfloat16)
        .reshape(seq_count, slot_count, q_heads, HEAD)
    )

    def attend_back(members):
        query_seq, key_seq, value_seq, length, log_seq, grad_seq = members
        scores = masked_scores(query_seq, key_seq, length, places, kv_heads, group_size)
        attention = jnp.exp(scores - log_seq[..., None])
        query_grp = query_seq.reshape(slot_count, kv_heads, group_size, HEAD)
        key_grp = key_seq.reshape(key_seq.shape[0], kv_heads, HEAD)
        value_grp = value_seq.reshape(value_seq.shape[0], kv_heads, HEAD)
        grad_grp = grad_seq.reshape(slot_count, kv_heads, group_size, HEAD)
        grad_attention = jnp.einsum(
            "bkgh,tkh->kgbt", grad_grp, value_grp, preferred_element_type=jnp.float32
        )
        inner = jnp.sum(attention * grad_attention, axis=-1, keepdims=True)
        grad_scores = (attention * (grad_attention - inner)).astype(jnp.bfloat16)
        scale_qk = HEAD ** (-0.5)
        grad_query_seq = (
            jnp.einsum("kgbt,tkh->bkgh", grad_scores, key_grp, preferred_element_type=jnp.float32)
            * scale_qk
        )
        grad_key_seq = (
            jnp.einsum("kgbt,bkgh->tkh", grad_scores, query_grp, preferred_element_type=jnp.float32)
            * scale_qk
        )
        grad_value_seq = jnp.einsum(
            "kgbt,bkgh->tkh",
            attention.astype(jnp.bfloat16),
            grad_grp,
            preferred_element_type=jnp.float32,
        )
        key_rows = key_grp.shape[0]
        return (
            grad_query_seq.reshape(slot_count, q_heads, HEAD),
            grad_key_seq.reshape(key_rows, kv_heads * HEAD),
            grad_value_seq.reshape(key_rows, kv_heads * HEAD),
        )

    grad_query_rot, grad_key_all, grad_value_all = lax.map(
        attend_back, (query_low, key_all, value_all, lengths, log_total, grad_attn_low)
    )
    grad_key_rot, grad_value_rot = (
        lax.psum_scatter(grad_key_all, "ctx", scatter_dimension=1, tiled=True),
        lax.psum_scatter(grad_value_all, "ctx", scatter_dimension=1, tiled=True),
    )
    grad_query_low = (
        rotate_back(grad_query_rot, cosine, sine_table)
        .astype(jnp.bfloat16)
        .reshape(tok_rows, q_heads * HEAD)
    )
    grad_key_low = (
        rotate_back(grad_key_rot.reshape(seq_count, slot_count, kv_heads, HEAD), cosine, sine_table)
        .astype(jnp.bfloat16)
        .reshape(tok_rows, kv_heads * HEAD)
    )
    grad_value_low = grad_value_rot.astype(jnp.bfloat16).reshape(tok_rows, kv_heads * HEAD)
    grad_query = jnp.einsum(
        "td,tq->dq", normed_one, grad_query_low, preferred_element_type=jnp.float32
    )
    grad_key = jnp.einsum("td,tq->dq", normed_one, grad_key_low, preferred_element_type=jnp.float32)
    grad_value = jnp.einsum(
        "td,tq->dq", normed_one, grad_value_low, preferred_element_type=jnp.float32
    )
    partial_one = jnp.einsum(
        "tq,dq->td", grad_query_low, query_back, preferred_element_type=jnp.float32
    )
    partial_one = partial_one + jnp.einsum(
        "tq,dq->td", grad_key_low, key_back, preferred_element_type=jnp.float32
    )
    partial_one = partial_one + jnp.einsum(
        "tq,dq->td", grad_value_low, value_back, preferred_element_type=jnp.float32
    )
    grad_normed_one = lax.psum(partial_one, "mp")
    grad_inputs_norm, grad_gain_one = norm_back(
        inputs, gain_attn_back.astype(jnp.float32), grad_normed_one
    )
    input_grad = (
        (grad_middle + grad_inputs_norm)
        .astype(jnp.bfloat16)
        .reshape(seq_count, slot_count, width_all)
    )
    attn_grads = (
        lax.psum_scatter(grad_query, ("dp", "ctx"), scatter_dimension=0, tiled=True),
        lax.psum_scatter(grad_key, ("dp", "ctx"), scatter_dimension=0, tiled=True),
        lax.psum_scatter(grad_value, ("dp", "ctx"), scatter_dimension=0, tiled=True),
        lax.psum_scatter(grad_output, ("dp", "ctx"), scatter_dimension=1, tiled=True),
        lax.psum_scatter(grad_gain_one, ("dp", "ctx"), scatter_dimension=0, tiled=True),
    )
    return (
        layer_out,
        input_grad,
        attn_grads[4],
        attn_grads[0],
        attn_grads[1],
        attn_grads[2],
        attn_grads[3],
        mlp_grads[3],
        mlp_grads[0],
        mlp_grads[1],
        mlp_grads[2],
    )


SPLIT = 4


class Column:
    def __init__(self, owned, width):
        self.x, self.ctx, self.z = (lax.axis_index(name) for name in ("dp", "ctx", "mp"))
        self.core = lax.rem(self.ctx, 2)
        self.last = lax.axis_size("mp") - 1
        self.owned, self.rows, self.width = owned, owned * (self.last + 1), width
        self.step = width // SPLIT
        self.sibling = (self.x, self.ctx + 1 - 2 * self.core, self.z)
        self.above, self.below = (self.x, self.ctx, self.z + 1), (self.x, self.ctx, self.z - 1)
        self.neighbours = (self.sibling,)

    def enter(self):
        barrier = pltpu.get_barrier_semaphore()

        def greet(device):
            pl.semaphore_signal(
                barrier, inc=1, device_id=device, device_id_type=pl.DeviceIdType.MESH
            )

        for device in self.neighbours:
            greet(device)

        @pl.when(self.z < self.last)
        def _():
            greet(self.above)

        @pl.when(self.z > 0)
        def _():
            greet(self.below)

        ends = jnp.where(self.z == 0, 1, 0) + jnp.where(self.z == self.last, 1, 0)
        pl.semaphore_wait(barrier, len(self.neighbours) + 2 - ends)

    def place(self, core, block):
        return pl.ds(pl.multiple_of(core * self.rows + block * self.owned, 16), self.owned)

    def block(self, at):
        return pl.ds(pl.multiple_of(at * self.owned, 16), self.owned)

    def columns(self, piece):
        return pl.ds(piece * self.step, self.step)


def remote(src, dst, send, recv, device):
    return pltpu.make_async_remote_copy(
        src_ref=src,
        dst_ref=dst,
        send_sem=send,
        recv_sem=recv,
        device_id=device,
        device_id_type=pl.DeviceIdType.MESH,
    )


class SumChain:
    def __init__(self, col, part, held, up_out, up_in, down_out, down_in, core_sem, up_sem, down_sem):
        self.col, self.part, self.held = col, part, held
        self.ways = (
            (col.above, up_out, up_in, up_sem, 1),
            (col.below, down_out, down_in, down_sem, -1),
        )
        self.core_sem = core_sem

    def across(self, block):
        col = self.col
        return remote(
            self.part.at[col.place(1 - col.core, block)],
            self.held.at[col.block(block)],
            self.core_sem.at[0, block],
            self.core_sem.at[1, block],
            col.sibling,
        )

    def open(self):
        for block in range(self.col.last + 1):
            self.across(block).start()

    def own(self, at, cols):
        col = self.col
        mine = self.part[col.place(col.core, at), cols].astype(jnp.float32)
        return mine + self.held[col.block(at), cols].astype(jnp.float32)

    def hop(self, way, step, piece):
        device, out, into, sem, _ = way
        cols = self.col.columns(piece)
        return remote(
            out.at[step, :, cols],
            into.at[step, :, cols],
            sem.at[0, step, piece],
            sem.at[1, step, piece],
            device,
        )

    def far(self, way):
        return self.col.z if way[4] == 1 else self.col.last - self.col.z

    def step(self, step):
        col = self.col
        for way in self.ways:
            sign = way[4]

            @pl.when(self.far(way) <= step)
            def _(way=way, sign=sign):
                at = col.z + sign * (col.last - step)
                self.across(at).wait_recv()
                for piece in range(SPLIT):
                    cols = col.columns(piece)
                    out = way[1]
                    total = self.own(at, cols)
                    if step:

                        @pl.when(self.far(way) > 0)
                        def _(total=total, cols=cols, piece=piece):
                            self.hop(way, step - 1, piece).wait_recv()
                            got = way[2][step - 1, :, cols].astype(jnp.float32)
                            out[step, :, cols] = (total + got).astype(out.dtype)

                        @pl.when(self.far(way) == 0)
                        def _(total=total, cols=cols):
                            out[step, :, cols] = total.astype(out.dtype)

                    else:
                        out[step, :, cols] = total.astype(out.dtype)
                    self.hop(way, step, piece).start()

    def close(self, result):
        col = self.col
        final = col.last - 1
        self.across(col.z).wait_recv()
        result[...] = self.own(col.z, slice(None))
        for way in self.ways:

            @pl.when(self.far(way) > 0)
            def _(way=way):
                for piece in range(SPLIT):
                    self.hop(way, final, piece).wait_recv()
                result[...] += way[2][final].astype(jnp.float32)

    def drain(self):
        for block in range(self.col.last + 1):
            self.across(block).wait_send()
        for step in range(self.col.last):
            for way in self.ways:

                @pl.when(self.far(way) <= step)
                def _(way=way, step=step):
                    for piece in range(SPLIT):
                        self.hop(way, step, piece).wait_send()


class ShareChain:
    def __init__(self, col, whole, up_sem, down_sem, core_sem=None):
        self.col, self.whole, self.core_sem = col, whole, core_sem
        self.ways = ((col.above, up_sem, 1), (col.below, down_sem, -1))

    def rows(self, at):
        return self.col.block(at) if self.core_sem is None else self.col.place(self.col.core, at)

    def far(self, way):
        return self.col.z if way[2] == 1 else self.col.last - self.col.z

    def hop(self, way, step, piece, origin):
        device, sem, _ = way
        ref = self.whole.at[self.rows(origin), self.col.columns(piece)]
        return remote(ref, ref, sem.at[0, step, piece], sem.at[1, step, piece], device)

    def across(self, origin):
        ref = self.whole.at[self.rows(origin)]
        return remote(
            ref, ref, self.core_sem.at[0, origin], self.core_sem.at[1, origin], self.col.sibling
        )

    def across_in(self, origin):
        ref = self.whole.at[self.col.place(1 - self.col.core, origin)]
        return remote(
            ref, ref, self.core_sem.at[0, origin], self.core_sem.at[1, origin], self.col.sibling
        )

    def step(self, step):
        col = self.col
        for way in self.ways:
            origin = col.z - way[2] * step

            @pl.when(self.far(way) >= step)
            def _(way=way, origin=origin):
                for piece in range(SPLIT):
                    if step:
                        self.hop(way, step - 1, piece, origin).wait_recv()
                    if step < col.last:

                        @pl.when(self.far(way) < col.last)
                        def _(piece=piece):
                            self.hop(way, step, piece, origin).start()

                if step and self.core_sem is not None:
                    self.across(origin).start()

        if step == 0 and self.core_sem is not None:
            self.across(col.z).start()

    def drain(self):
        col = self.col
        for step in range(col.last):
            for way in self.ways:

                @pl.when((self.far(way) >= step) & (self.far(way) < col.last))
                def _(way=way, step=step):
                    for piece in range(SPLIT):
                        self.hop(way, step, piece, col.z - way[2] * step).wait_send()

        if self.core_sem is not None:
            for origin in range(col.last + 1):
                self.across_in(origin).wait_recv()
                self.across(origin).wait_send()


def sum_scratch(owned, z_count, width):
    hops = z_count - 1
    low = jnp.bfloat16
    return [
        pltpu.VMEM((owned * z_count, width), low),
        pltpu.VMEM((hops, owned, width), low),
        pltpu.VMEM((hops, owned, width), low),
        pltpu.VMEM((hops, owned, width), low),
        pltpu.VMEM((hops, owned, width), low),
        pltpu.SemaphoreType.DMA((2, z_count)),
        pltpu.SemaphoreType.DMA((2, hops, SPLIT)),
        pltpu.SemaphoreType.DMA((2, hops, SPLIT)),
    ]


def share_scratch(z_count, cores):
    hops = z_count - 1
    sems = [pltpu.SemaphoreType.DMA((2, hops, SPLIT))] * 2
    return sems + ([pltpu.SemaphoreType.DMA((2, z_count))] if cores else [])


GROUP = 384


class Plane(Column):
    def __init__(self, owned, width):
        super().__init__(owned, width)
        self.over_x = (1 - self.x, self.ctx, self.z)
        self.over_y = (self.x, lax.rem(self.ctx + 2, 4), self.z)
        self.part = width // 4
        self.middle = width // 8

        self.neighbours = (self.sibling, self.over_x, self.over_y)


NT = (((1,), (1,)), ((), ()))


def masked(keys, queries, bias, block, y_at):
    scores = jnp.dot(keys, queries, preferred_element_type=jnp.float32) * HEAD ** (-0.5)
    rows, columns = scores.shape
    key_slots = block * rows + lax.broadcasted_iota(jnp.int32, scores.shape, 0)
    query_slots = y_at * columns + lax.broadcasted_iota(jnp.int32, scores.shape, 1)
    scores = jnp.where(key_slots <= query_slots, scores, NEG)
    return scores + bias[block * rows : (block + 1) * rows]


def start_kernel(
    hidden,
    gains,
    keep,
    give,
    gate,
    up,
    down,
    output,
    cotangent,
    valid,
    bias,
    cos,
    sin,
    branch,
    h1_t,
    w,
    gains_all,
    out_w,
    wide,
    dm,
    inputs_own,
    q_t,
    kv,
    lse,
    o_t,
    down_t,
    out_t,
    qkv,
    h1,
    core_sem,
    gain_sem,
    x_sem,
    y_sem,
    far_sem,
    out_x_sem,
    out_y_sem,
    out_far_sem,
    local_sem,
    wide_sem,
    out_sem,
    h1_sem,
    dm_sem,
    kv_sem,
):
    x_at, ctx_at, z_at = (lax.axis_index(name) for name in ("dp", "ctx", "mp"))
    core = lax.rem(ctx_at, 2)
    y_at = (ctx_at - core) // 2
    rows, part = hidden.shape[0], keep.shape[0]
    chip_part = 2 * part
    ff = gate.shape[1] // 2
    groups = ff // 128

    def device(turn, flip):
        x_to = 1 - x_at if turn >= 2 else x_at
        y_to = 1 - y_at if turn % 2 else y_at
        core_to = 1 - core if flip else core
        return (x_to, 2 * y_to + core_to, z_at)

    def half_rows(which):
        return pl.ds(pl.multiple_of(which * part, 16), part)

    sibling, over_x, over_y = device(0, 1), device(2, 0), device(1, 0)
    barrier = pltpu.get_barrier_semaphore()
    others = [(turn, flip) for turn in range(4) for flip in range(2) if turn or flip]
    for turn, flip in others:
        pl.semaphore_signal(
            barrier, inc=1, device_id=device(turn, flip), device_id_type=pl.DeviceIdType.MESH
        )
    w[0, half_rows(core)] = keep[...]
    gains_all[core] = gains[...]
    pl.semaphore_wait(barrier, len(others))

    mine = half_rows(core)
    swap = remote(give, w.at[0, mine], core_sem.at[0], core_sem.at[1], sibling)
    swap.start()

    def gain_copy(turn, flip):
        slot = 2 * turn + core
        index = 2 * turn + flip
        return remote(
            gains, gains_all.at[slot], gain_sem.at[0, index], gain_sem.at[1, index], device(turn, flip)
        )

    for turn, flip in others:
        gain_copy(turn, flip).start()

    def cross(ref, sems, which, to_x):
        sem = sems[0] if to_x else sems[1]
        rows_of = half_rows(which)
        return remote(
            ref.at[0, rows_of],
            ref.at[2 if to_x else 1, rows_of],
            sem.at[0, which],
            sem.at[1, which],
            over_x if to_x else over_y,
        )

    def relay(ref, sems, to_x):
        which = 1 if to_x else 0
        rows_of = half_rows(which)
        return remote(
            ref.at[1 if to_x else 2, rows_of],
            ref.at[3, rows_of],
            sems[2].at[0, which],
            sems[2].at[1, which],
            over_x if to_x else over_y,
        )

    qkv_way = (w, (x_sem, y_sem, far_sem))
    out_way = (out_w, (out_x_sem, out_y_sem, out_far_sem))
    cross(*qkv_way, core, True).start()
    cross(*qkv_way, core, False).start()

    def wide_copies(group, kind, source):
        from_here = pl.ds(pl.multiple_of(core * ff + group * 128, 128), 128)
        from_there = pl.ds(pl.multiple_of((1 - core) * ff + group * 128, 128), 128)
        to = pl.ds(pl.multiple_of(group * GROUP + kind * 128, 128), 128)
        here = pltpu.make_async_copy(
            source.at[:, from_here], wide.at[mine, to], local_sem.at[kind, group]
        )
        there = remote(
            source.at[:, from_there],
            wide.at[mine, to],
            wide_sem.at[0, kind, group],
            wide_sem.at[1, kind, group],
            sibling,
        )
        return here, there

    def each_wide(kind, source, act):
        def body(group, carry):
            for copy in wide_copies(group, kind, source):
                act(copy)
            return carry

        lax.fori_loop(0, groups, body, 0)

    each_wide(0, gate, lambda copy: copy.start())
    each_wide(1, up, lambda copy: copy.start())
    swap.wait_recv()
    cross(*qkv_way, 1 - core, True).start()
    cross(*qkv_way, 1 - core, False).start()

    down_t[...] = down[...].T
    each_wide(2, down_t, lambda copy: copy.start())
    q_rows = output.shape[0] // 2
    out_cols = out_w.shape[2]
    out_w[0, mine, q_rows:] = jnp.zeros((part, out_cols - q_rows), out_w.dtype)
    out_t[:, q_rows:] = jnp.zeros((part, out_cols - q_rows), out_w.dtype)
    out_w[0, mine, :q_rows] = output[pl.ds(pl.multiple_of(core * q_rows, 16), q_rows), :].T
    out_t[:, :q_rows] = output[pl.ds(pl.multiple_of((1 - core) * q_rows, 16), q_rows), :].T
    out_copy = remote(out_t, out_w.at[0, mine], out_sem.at[0], out_sem.at[1], sibling)
    out_copy.start()

    def source_cols(turn):
        at = (x_at if turn < 2 else 1 - x_at) * 2 + (1 - y_at if turn % 2 else y_at)
        return pl.ds(pl.multiple_of(at * chip_part, 128), chip_part)

    def cut(turn):
        return slice(turn * chip_part, (turn + 1) * chip_part)

    my_rows = pl.ds(pl.multiple_of(core * rows, 16), rows)
    owned = inputs_own.shape[0]
    own_rows = pl.ds(pl.multiple_of(z_at * owned, 16), owned)
    for turn in range(4):
        block = cotangent[:, source_cols(turn)].astype(jnp.float32)
        dm[my_rows, cut(turn)] = (valid[...] * block).astype(dm.dtype)
        inputs_own[:, cut(turn)] = hidden[own_rows, source_cols(turn)].astype(jnp.float32)
    dm_copy = remote(dm.at[my_rows], dm.at[my_rows], dm_sem.at[0], dm_sem.at[1], sibling)
    dm_copy.start()

    for turn, flip in others:
        gain_copy(turn, flip).wait_recv()
    squares = hidden[...].astype(jnp.float32)
    scale = lax.rsqrt(jnp.mean(squares * squares, axis=-1, keepdims=True) + EPS)
    for turn in range(4):
        block = hidden[:, source_cols(turn)]
        gain = gains_all[2 * turn] + gains_all[2 * turn + 1]
        h1[my_rows, cut(turn)] = (block.astype(jnp.float32) * scale * gain[:1]).astype(h1.dtype)
    h1_copy = remote(h1.at[my_rows], h1.at[my_rows], h1_sem.at[0], h1_sem.at[1], sibling)
    h1_copy.start()

    def block_dot(turn):
        return jnp.dot(h1[:, cut(turn)], w[turn], preferred_element_type=jnp.float32)

    cross(*qkv_way, 0, True).wait_recv()
    relay(*qkv_way, False).start()
    cross(*qkv_way, 1, False).wait_recv()
    relay(*qkv_way, True).start()
    out_copy.wait_recv()
    for which in range(2):
        cross(*out_way, which, True).start()
        cross(*out_way, which, False).start()
    h1_copy.wait_recv()
    for turn in range(4):
        h1_t[cut(turn)] = h1[:, cut(turn)].T
    qkv[...] = block_dot(0)
    cross(*qkv_way, 1, True).wait_recv()
    qkv[...] += block_dot(2)
    cross(*qkv_way, 0, False).wait_recv()
    qkv[...] += block_dot(1)
    relay(*qkv_way, False).wait_recv()
    relay(*qkv_way, True).wait_recv()
    qkv[...] += block_dot(3)
    qkv[...] = qkv[...].T

    heads = q_t.shape[0] // HEAD
    k_row = heads * HEAD
    q_cols = k_row

    def turned(row):
        first, second = qkv[row : row + HEAD // 2], qkv[row + HEAD // 2 : row + HEAD]
        return jnp.concatenate(
            [first * cos[...] - second * sin[...], second * cos[...] + first * sin[...]], axis=0
        )

    kv[y_at, :HEAD] = turned(k_row).astype(kv.dtype)
    kv[y_at, HEAD:] = qkv[k_row + HEAD : k_row + 2 * HEAD].astype(kv.dtype)
    kv_copy = remote(kv.at[y_at], kv.at[y_at], kv_sem.at[0], kv_sem.at[1], over_y)
    kv_copy.start()
    for head in range(heads):
        q_t[head * HEAD : (head + 1) * HEAD] = turned(head * HEAD).astype(q_t.dtype)
    o_t[q_cols:] = jnp.zeros((o_t.shape[0] - q_cols, o_t.shape[1]), o_t.dtype)
    cross(*out_way, 0, True).wait_recv()
    relay(*out_way, False).start()
    cross(*out_way, 1, False).wait_recv()
    relay(*out_way, True).start()
    kv_copy.wait_recv()

    keys = [kv[block, :HEAD].T for block in range(2)]
    for head in range(heads):
        head_rows = slice(head * HEAD, (head + 1) * HEAD)
        scores = [
            masked(keys[block], q_t[head_rows], bias, block, y_at) for block in range(2)
        ]
        top = jnp.maximum(*(jnp.max(score, axis=0, keepdims=True) for score in scores))
        exponents = [jnp.exp(score - top) for score in scores]
        total = sum(jnp.sum(exponent, axis=0, keepdims=True) for exponent in exponents)
        mixed = jnp.zeros((HEAD, o_t.shape[1]), jnp.float32)
        for block in range(2):
            weights = (exponents[block] / total).astype(kv.dtype)
            mixed += jnp.dot(kv[block, HEAD:], weights, preferred_element_type=jnp.float32)
        o_t[head_rows] = mixed.astype(o_t.dtype)
        lse[head : head + 1] = top + jnp.log(total)

    cross(*out_way, 1, True).wait_recv()
    cross(*out_way, 0, False).wait_recv()
    relay(*out_way, False).wait_recv()
    relay(*out_way, True).wait_recv()
    mixed_all = o_t[...].T
    for turn in range(4):
        branch[:, cut(turn)] = lax.dot_general(
            mixed_all, out_w[turn], NT, preferred_element_type=jnp.float32
        ).astype(branch.dtype)

    for kind, source in enumerate((gate, up, down_t)):
        each_wide(kind, source, lambda copy: copy.wait())
    swap.wait_send()
    out_copy.wait_send()
    h1_copy.wait_send()
    dm_copy.wait()
    kv_copy.wait_send()
    for turn, flip in others:
        gain_copy(turn, flip).wait_send()
    for way in (qkv_way, out_way):
        for which in range(2):
            for to_x in (True, False):
                cross(*way, which, to_x).wait_send()
        relay(*way, True).wait_send()
        relay(*way, False).wait_send()


class Gather:
    def __init__(self, plane, own, w, x_sem, y_sem, far_sem, local_sem):
        self.plane, self.own, self.w = plane, own, w
        self.x_sem, self.y_sem, self.far_sem, self.local_sem = x_sem, y_sem, far_sem, local_sem
        self.groups = own.shape[1] // GROUP

    def columns(self, group):
        return pl.ds(pl.multiple_of(group * GROUP, 128), GROUP)

    def cross(self, group, to_x):
        plane, cols = self.plane, self.columns(group)
        sem = self.x_sem if to_x else self.y_sem
        return remote(
            self.own.at[:, cols],
            self.w.at[2 if to_x else 1, :, cols],
            sem.at[0, group],
            sem.at[1, group],
            plane.over_x if to_x else plane.over_y,
        )

    def relay(self, group, to_x):
        plane, cols = self.plane, self.columns(group)
        rows = pl.ds(plane.middle, plane.middle) if to_x else pl.ds(0, plane.middle)
        kind = 1 if to_x else 0
        return remote(
            self.w.at[1 if to_x else 2, rows, cols],
            self.w.at[3, rows, cols],
            self.far_sem.at[0, kind, group],
            self.far_sem.at[1, kind, group],
            plane.over_x if to_x else plane.over_y,
        )

    def load(self):
        return pltpu.make_async_copy(self.own, self.w.at[0], self.local_sem.at[0])

    def send(self, group):
        self.cross(group, True).start()
        self.cross(group, False).start()

    def pump(self, group):
        self.cross(group, True).wait_recv()
        self.relay(group, False).start()
        self.cross(group, False).wait_recv()
        self.relay(group, True).start()

        @pl.when(group + 2 < self.groups)
        def _():
            self.send(group + 2)

    def arrive(self, group):
        self.relay(group, False).wait_recv()
        self.relay(group, True).wait_recv()

    def drain(self):
        def body(group, carry):
            for to_x in (True, False):
                self.cross(group, to_x).wait_send()
                self.relay(group, to_x).wait_send()
            return carry

        lax.fori_loop(0, self.groups, body, 0)


class Scatter:
    def __init__(self, plane, stage, upper, lower, x_one, y_two, sem, size=GROUP):
        self.plane, self.stage, self.sem, self.size = plane, stage, sem, size
        first, second = pl.ds(0, plane.middle), pl.ds(plane.middle, plane.middle)
        self.kinds = (
            (2, first, upper, plane.over_x),
            (2, second, lower, plane.over_y),
            (1, first, x_one, plane.over_x),
            (0, second, y_two, plane.over_y),
        )

    def copies(self, group, kinds=range(4)):
        cols = pl.ds(pl.multiple_of(group * self.size, 128), self.size)
        for kind in kinds:
            block, rows, into, device = self.kinds[kind]
            yield remote(
                self.stage.at[block, rows, cols],
                into.at[:, cols],
                self.sem.at[0, kind, group],
                self.sem.at[1, kind, group],
                device,
            )

    def send(self, group, kinds=range(4)):
        for copy in self.copies(group, kinds):
            copy.start()

    def drain(self, groups):
        def body(group, carry):
            for copy in self.copies(group):
                copy.wait()
            return carry

        lax.fori_loop(0, groups, body, 0)


def mlp_kernel(
    branch,
    inputs,
    gain,
    valid,
    dm,
    own,
    da,
    d_middle,
    layer,
    d_gain,
    own_grad,
    stage,
    upper,
    lower,
    x_one,
    y_two,
    w,
    h2,
    h2_t,
    dm_t,
    part,
    mlp_part,
    dh2,
    middle,
    mlp,
    zd,
    tile,
    tile_own,
    x_sem,
    y_sem,
    far_sem,
    local_sem,
    scatter_sem,
    *scratch,
):
    f32 = jnp.float32
    plane = Plane(inputs.shape[0], inputs.shape[1])
    size = plane.part
    gather = Gather(plane, own, w, x_sem, y_sem, far_sem, local_sem)
    groups = gather.groups
    scatter = Scatter(plane, stage, upper, lower, x_one, y_two, scatter_sem)
    total = SumChain(plane, part, *scratch[:8])
    share = ShareChain(plane, h2, *scratch[8:11])
    total_back = SumChain(plane, part, *scratch[11:19])
    second = SumChain(plane, mlp_part, *scratch[:5], *scratch[19:22])
    share_back = ShareChain(plane, da, *scratch[22:25])

    def cut(turn):
        return slice(turn * size, (turn + 1) * size)

    load_part = pltpu.make_async_copy(branch, part, local_sem.at[1])
    load_part.start()
    gather.load().start()
    load_part.wait()
    plane.enter()
    total.open()
    gather.send(0)
    gather.send(1)
    for step in range(plane.last):
        total.step(step)
        if step == 0:
            for turn in range(4):
                dm_t[cut(turn)] = dm[:, cut(turn)].T
    total.close(middle)
    middle[...] += inputs[...]
    h2[plane.place(plane.core, plane.z)] = normed(middle[...], gain[...]).astype(h2.dtype)
    gather.pump(0)
    for step in range(plane.last + 1):
        share.step(step)
        if step == 1:
            gather.pump(1)
        if step == plane.last:
            gather.pump(2)
    total.drain()
    share.drain()
    for turn in range(4):
        h2_t[cut(turn)] = h2[:, cut(turn)].T
    dh2[...] = jnp.zeros_like(dh2)
    gather.load().wait()

    def group_body(group, carry):
        start = pl.multiple_of(group * GROUP, 128)
        gu_cols, down_cols = pl.ds(start, 256), pl.ds(start + 256, 128)
        cols = pl.ds(start, GROUP)
        gather.arrive(group)
        gu = jnp.zeros((dm.shape[0], 256), f32)
        d_hidden = jnp.zeros((dm.shape[0], 128), f32)
        for turn in range(4):
            gu += jnp.dot(h2[:, cut(turn)], w[turn, :, gu_cols], preferred_element_type=f32)
            d_hidden += jnp.dot(dm[:, cut(turn)], w[turn, :, down_cols], preferred_element_type=f32)
        gate, up = gu[:, :128], gu[:, 128:]
        sigma = jax.nn.sigmoid(gate)
        silu = gate * sigma
        zd[:, pl.ds(start, 128)] = (
            d_hidden * up * sigma * (1.0 + gate * (1.0 - sigma))
        ).astype(zd.dtype)
        zd[:, pl.ds(start + 128, 128)] = (d_hidden * silu).astype(zd.dtype)
        zd[:, down_cols] = (silu * up).astype(zd.dtype)
        d_gu, hidden = zd[:, gu_cols], zd[:, down_cols]
        for turn in range(4):
            dh2[:, cut(turn)] += lax.dot_general(
                d_gu, w[turn, :, gu_cols], NT, preferred_element_type=f32
            )
            grad_gu = jnp.dot(h2_t[cut(turn)], d_gu, preferred_element_type=f32)
            grad_down = jnp.dot(dm_t[cut(turn)], hidden, preferred_element_type=f32)
            if turn:
                tile[turn - 1, :, :256] = grad_gu.astype(tile.dtype)
                tile[turn - 1, :, 256:] = grad_down.astype(tile.dtype)
            else:
                tile_own[:, :256] = grad_gu
                tile_own[:, 256:] = grad_down
        keep = pltpu.make_async_copy(tile, stage.at[:, :, cols], local_sem.at[2])
        keep_own = pltpu.make_async_copy(tile_own, own_grad.at[:, cols], local_sem.at[3])
        keep.start()
        keep_own.start()

        @pl.when(group + 3 < groups)
        def _():
            gather.pump(group + 3)

        keep.wait()
        keep_own.wait()

        @pl.when(group == 3)
        def _():
            for before in range(3):
                scatter.send(before)

        @pl.when(group >= 3)
        def _():
            scatter.send(group)

        return carry

    lax.fori_loop(0, groups, group_body, 0)
    for turn in range(4):
        part[:, cut(turn)] = dh2[:, cut(turn)].astype(part.dtype)
    total_back.open()
    for step in range(plane.last):
        total_back.step(step)
        for turn in range(4):
            if turn % plane.last == step:
                out = jnp.zeros((dm.shape[0], size), f32)
                for group in range(groups):
                    cols = slice(group * GROUP + 256, group * GROUP + 384)
                    out += lax.dot_general(
                        zd[:, cols], w[turn, :, cols], NT, preferred_element_type=f32
                    )
                mlp_part[:, cut(turn)] = out.astype(mlp_part.dtype)
    second.open()
    total_back.close(d_middle)
    d_norm, d_gain_row = norm_back(middle[...], gain[...], d_middle[...])
    d_gain[...] = d_gain_row[None]
    d_middle[...] = dm[plane.place(plane.core, plane.z)].astype(f32) + d_norm
    da[plane.place(plane.core, plane.z)] = d_middle[...].astype(da.dtype)
    for step in range(plane.last + 1):
        share_back.step(step)
        if step < plane.last:
            second.step(step)
    second.close(mlp)
    layer[...] = (valid[...] * (middle[...] + mlp[...])).astype(layer.dtype)
    total_back.drain()
    second.drain()
    share_back.drain()
    gather.drain()
    scatter.drain(groups)


class Home:
    def __init__(self, plane, y_part, x_part, y_one, x_two, sem, size):
        self.plane, self.size, self.sem = plane, size, sem
        self.ways = (
            (y_part, y_one, plane.over_y),
            (x_part, x_two, plane.over_x),
        )

    def copies(self, group):
        cols = pl.ds(pl.multiple_of(group * self.size, 128), self.size)
        for kind, (part, into, device) in enumerate(self.ways):
            yield remote(
                part.at[:, cols],
                into.at[:, cols],
                self.sem.at[0, kind, group],
                self.sem.at[1, kind, group],
                device,
            )

    def send(self, group):
        for copy in self.copies(group):
            copy.start()

    def arrive(self, group):
        for copy in self.copies(group):
            copy.wait_recv()

    def left(self, group):
        for copy in self.copies(group):
            copy.wait_send()


def end_kernel(
    da,
    out_w,
    q_t,
    kv,
    lse,
    o_t,
    bias,
    cos,
    sin,
    h1_t,
    w,
    d_middle,
    layer,
    inputs,
    gain,
    d_gain_two,
    stage,
    upper,
    lower,
    x_one,
    y_two,
    own_grad,
    layer_all,
    grad_all,
    gain_out,
    grad_gate,
    grad_up,
    grad_down,
    grad_out,
    grad_qkv,
    do_t,
    d_t,
    dk,
    dv,
    kv_give,
    kv_take,
    part,
    d_normed,
    y_part,
    x_part,
    y_add,
    x_add,
    total,
    y_last,
    x_last,
    turned_down,
    attn_stage,
    attn_own,
    attn_upper,
    attn_lower,
    attn_x_one,
    attn_y_two,
    attn_y_one,
    attn_x_two,
    out_turned,
    gain_part,
    gain_in,
    gain_sum,
    gain_all,
    load_sem,
    wide_home_sem,
    attn_sem,
    attn_home_sem,
    kv_sem,
    final_sem,
    swap_sem,
    plane_gain_sem,
    column_gain_sem,
    *scratch,
):
    f32, low = jnp.float32, part.dtype
    plane = Plane(inputs.shape[0], inputs.shape[1])
    size, middle = plane.part, plane.middle
    core, y_at = plane.core, (plane.ctx - plane.core) // 2
    diagonal = (1 - plane.x, lax.rem(plane.ctx + 2, 4), plane.z)
    z_count = plane.last + 1
    column = [
        (plane.x, plane.ctx + flip * (1 - 2 * core), lax.rem(plane.z + turn, z_count))
        for turn in range(z_count)
        for flip in range(2)
        if turn or flip
    ]
    sums = SumChain(plane, part, *scratch[:8])
    first = ShareChain(plane, layer_all, *scratch[8:10])
    share = ShareChain(plane, grad_all, *scratch[10:12])
    groups = own_grad.shape[1] // GROUP
    attn_cols = attn_own.shape[1]
    qkv_cols = w.shape[2]
    home = Home(plane, y_part, x_part, y_last, x_last, wide_home_sem, GROUP)
    attn = Scatter(
        plane, attn_stage, attn_upper, attn_lower, attn_x_one, attn_y_two, attn_sem, attn_cols
    )
    top, bottom = pl.ds(0, middle), pl.ds(middle, middle)
    attn_home = Home(
        plane,
        attn_stage.at[0, top],
        attn_stage.at[1, bottom],
        attn_y_one,
        attn_x_two,
        attn_home_sem,
        attn_cols,
    )

    def cut(turn):
        return slice(turn * size, (turn + 1) * size)

    loads = [
        pltpu.make_async_copy(source, into, load_sem.at[index])
        for index, (source, into) in enumerate(
            (
                (stage.at[0, top], y_part),
                (stage.at[1, bottom], x_part),
                (upper, y_add),
                (lower, x_add),
                (own_grad, total),
                (x_one, y_add),
                (y_two, x_add),
            )
        )
    ]
    for load in loads[:5]:
        load.start()
    layer_all[plane.block(plane.z)] = layer[...]

    barrier = pltpu.get_barrier_semaphore()
    peers = [plane.over_x, plane.over_y, diagonal] + column
    for device in peers:
        pl.semaphore_signal(barrier, inc=1, device_id=device, device_id_type=pl.DeviceIdType.MESH)
    pl.semaphore_wait(barrier, len(peers))

    def send_home(group):
        cols = pl.ds(pl.multiple_of(group * GROUP, 128), GROUP)
        for mine, add in ((y_part, y_add), (x_part, x_add)):
            mine[:, cols] = (mine[:, cols].astype(f32) + add[:, cols].astype(f32)).astype(low)
        home.send(group)

    first.step(0)
    for load in loads[:4]:
        load.wait()
    send_home(0)
    send_home(1)

    d_out = jnp.zeros((da.shape[0], out_w.shape[2]), f32)
    for turn in range(4):
        d_out += jnp.dot(da[:, cut(turn)], out_w[turn], preferred_element_type=f32)
    do_t[...] = d_out.T.astype(low)
    heads = q_t.shape[0] // HEAD
    k_row = heads * HEAD
    keys = [kv[block, :HEAD].T for block in range(2)]
    values = [kv[block, HEAD:].T for block in range(2)]
    scale = HEAD ** (-0.5)
    dk[...] = jnp.zeros_like(dk)
    dv[...] = jnp.zeros_like(dv)

    def turned_back(tensor):
        ahead, behind = tensor[: HEAD // 2], tensor[HEAD // 2 :]
        return jnp.concatenate(
            [ahead * cos[...] + behind * sin[...], behind * cos[...] - ahead * sin[...]], axis=0
        )

    for head in range(heads):
        head_rows = slice(head * HEAD, (head + 1) * HEAD)
        queries, d_head = q_t[head_rows], do_t[head_rows]
        probs, d_probs = [], []
        inner = jnp.zeros((1, queries.shape[1]), f32)
        for block in range(2):
            scores = masked(keys[block], queries, bias, block, y_at)
            prob = jnp.exp(scores - lse[head : head + 1])
            d_prob = jnp.dot(values[block], d_head, preferred_element_type=f32)
            inner += jnp.sum(prob * d_prob, axis=0, keepdims=True)
            probs.append(prob)
            d_probs.append(d_prob)
        d_query = jnp.zeros((HEAD, queries.shape[1]), f32)
        for block in range(2):
            d_scores = (probs[block] * (d_probs[block] - inner)).astype(low)
            dk[block] += lax.dot_general(d_scores, queries, NT, preferred_element_type=f32) * scale
            dv[block] += lax.dot_general(
                probs[block].astype(low), d_head, NT, preferred_element_type=f32
            )
            d_query += jnp.dot(kv[block, :HEAD], d_scores, preferred_element_type=f32) * scale
        d_t[head_rows] = turned_back(d_query).astype(low)

    kv_give[:HEAD] = dk[1 - y_at].T.astype(low)
    kv_give[HEAD:] = dv[1 - y_at].T.astype(low)
    kv_copy = remote(kv_give, kv_take, kv_sem.at[0], kv_sem.at[1], plane.over_y)
    kv_copy.start()
    d_key, d_value = dk[y_at].T, dv[y_at].T
    d_t[k_row + 2 * HEAD :] = jnp.zeros((qkv_cols - k_row - 2 * HEAD, d_t.shape[1]), low)
    first.step(1)
    kv_copy.wait_recv()
    d_t[k_row : k_row + HEAD] = turned_back(d_key + kv_take[:HEAD].astype(f32)).astype(low)
    d_t[k_row + HEAD : k_row + 2 * HEAD] = (d_value + kv_take[HEAD:].astype(f32)).astype(low)
    d_qkv = d_t[...].T
    for turn in range(4):
        part[:, cut(turn)] = lax.dot_general(
            d_qkv, w[turn], NT, preferred_element_type=f32
        ).astype(low)
    sums.open()
    send_home(2)
    sums.step(0)
    first.step(2)

    for turn in (3, 2, 1, 0):
        grad = jnp.dot(h1_t[cut(turn)], d_qkv, preferred_element_type=f32)
        grad_o = lax.dot_general(da[:, cut(turn)].T, o_t[...], NT, preferred_element_type=f32)
        if turn:
            attn_stage[turn - 1, :, :qkv_cols] = grad.astype(low)
            attn_stage[turn - 1, :, qkv_cols:] = grad_o.astype(low)
        else:
            attn_own[:, :qkv_cols] = grad
            attn_own[:, qkv_cols:] = grad_o
        if turn == 3:
            attn.send(0, (0, 1))
            send_home(3)
    sums.step(1)
    first.step(3)
    send_home(4)
    send_home(5)
    attn.send(0, (2, 3))
    send_home(6)
    x_came, y_came = y_add, x_add
    for load in loads[5:]:
        load.start()
    sums.step(2)
    sums.close(d_normed)
    d_norm, d_gain_row = norm_back(inputs[...], gain[...], d_normed[...])
    grad_all[plane.block(plane.z)] = (d_middle[...] + d_norm).astype(low)
    share.step(0)

    gain_part[...] = jnp.zeros_like(gain_part)
    gain_part[0:1] = d_gain_row[None]
    gain_part[1:2] = d_gain_two[...]
    plane_gains = [
        remote(
            gain_part.at[:, pl.ds(turn * size, size)],
            gain_in.at[turn - 1],
            plane_gain_sem.at[0, turn - 1],
            plane_gain_sem.at[1, turn - 1],
            device,
        )
        for turn, device in ((1, plane.over_y), (2, plane.over_x), (3, diagonal))
    ]
    for copy in plane_gains:
        copy.start()

    for load in loads[4:]:
        load.wait()

    def finish_wide(group, carry):
        start = pl.multiple_of(group * GROUP, 128)
        cols = pl.ds(start, GROUP)
        home.arrive(group)
        total[:middle, cols] += x_came[:, cols].astype(f32) + y_last[:, cols].astype(f32)
        total[middle:, cols] += x_last[:, cols].astype(f32) + y_came[:, cols].astype(f32)
        down_cols = pl.ds(start + 256, 128)
        turned_down[group, 0] = total[:middle, down_cols].T
        turned_down[group, 1] = total[middle:, down_cols].T
        for copy in wide_out(group):
            copy.start()
        return carry

    def wide_out(group):
        ff = groups * 128
        start = pl.multiple_of(group * GROUP, 128)
        to = pl.ds(pl.multiple_of(core * ff + group * 128, 128), 128)
        keep = pl.ds(pl.multiple_of(core * middle, 16), middle)
        give = pl.ds(pl.multiple_of((1 - core) * middle, 16), middle)
        for kind, into in enumerate((grad_gate, grad_up)):
            cols = pl.ds(start + kind * 128, 128)
            yield pltpu.make_async_copy(
                total.at[keep, cols], into.at[:, to], final_sem.at[kind, group]
            )
            yield remote(
                total.at[give, cols],
                into.at[:, to],
                swap_sem.at[0, kind, group],
                swap_sem.at[1, kind, group],
                plane.sibling,
            )
        yield pltpu.make_async_copy(
            turned_down.at[group, core], grad_down.at[to], final_sem.at[2, group]
        )
        yield remote(
            turned_down.at[group, 1 - core],
            grad_down.at[to],
            swap_sem.at[0, 2, group],
            swap_sem.at[1, 2, group],
            plane.sibling,
        )

    share.step(1)
    lax.fori_loop(0, 3, finish_wide, 0)
    for copy in attn.copies(0, (0, 1)):
        copy.wait_recv()
    attn_stage[0, top] = (attn_stage[0, top].astype(f32) + attn_upper[...].astype(f32)).astype(low)
    attn_stage[1, bottom] = (
        attn_stage[1, bottom].astype(f32) + attn_lower[...].astype(f32)
    ).astype(low)
    attn_home.send(0)
    share.step(2)
    for copy in plane_gains:
        copy.wait_recv()
    gain_sum[...] = gain_part[:, :size] + gain_in[0] + gain_in[1] + gain_in[2]
    column_gains = [
        remote(
            gain_sum,
            gain_all.at[index],
            column_gain_sem.at[0, index],
            column_gain_sem.at[1, index],
            device,
        )
        for index, device in enumerate(column)
    ]
    for copy in column_gains:
        copy.start()
    lax.fori_loop(3, groups, finish_wide, 0)
    share.step(3)

    for copy in attn.copies(0, (2, 3)):
        copy.wait_recv()
    attn_home.arrive(0)
    attn_own[:middle] += attn_x_one[...].astype(f32) + attn_y_one[...].astype(f32)
    attn_own[middle:] += attn_x_two[...].astype(f32) + attn_y_two[...].astype(f32)
    q_rows = k_row
    for which in range(2):
        out_turned[which] = attn_own[which * middle : (which + 1) * middle, qkv_cols:].T
    out_rows = pl.ds(pl.multiple_of(core * q_rows, 16), q_rows)
    keep = pl.ds(pl.multiple_of(core * middle, 16), middle)
    give = pl.ds(pl.multiple_of((1 - core) * middle, 16), middle)
    take = pl.ds(0, q_rows)
    attn_out = [
        pltpu.make_async_copy(
            out_turned.at[core, take], grad_out.at[out_rows], final_sem.at[3, 0]
        ),
        remote(
            out_turned.at[1 - core, take],
            grad_out.at[out_rows],
            swap_sem.at[0, 3, 0],
            swap_sem.at[1, 3, 0],
            plane.sibling,
        ),
        pltpu.make_async_copy(
            attn_own.at[keep, pl.ds(0, qkv_cols)], grad_qkv.at[core], final_sem.at[3, 1]
        ),
        remote(
            attn_own.at[give, pl.ds(0, qkv_cols)],
            grad_qkv.at[core],
            swap_sem.at[0, 3, 1],
            swap_sem.at[1, 3, 1],
            plane.sibling,
        ),
    ]
    for copy in attn_out:
        copy.start()
    gain_total = gain_sum[...]
    for index, copy in enumerate(column_gains):
        copy.wait_recv()
        gain_total += gain_all[index]
    gain_out[...] = gain_total

    def drain_wide(group, carry):
        for copy in wide_out(group):
            copy.wait()
        home.left(group)
        return carry

    lax.fori_loop(0, groups, drain_wide, 0)
    for copy in attn_out:
        copy.wait()
    for copy in attn.copies(0):
        copy.wait_send()
    attn_home.left(0)
    kv_copy.wait_send()
    for copy in plane_gains + column_gains:
        copy.wait_send()
    sums.drain()
    first.drain()
    share.drain()


def on_plane(
    hidden_in,
    cotangent,
    lengths,
    norm_attn,
    w_query,
    w_key,
    w_value,
    w_output,
    norm_mlp,
    w_gate,
    w_up,
    w_down,
):
    low = jnp.bfloat16
    f32 = jnp.float32
    _, rows, width = hidden_in.shape
    part = w_query.shape[0]
    chip_part, chip_rows = 2 * part, 2 * rows
    x_at, ctx_at = lax.axis_index("dp"), lax.axis_index("ctx")
    y_at, core = ctx_at // 2, ctx_at % 2
    place = 2 * x_at + y_at
    z_count = lax.axis_size("mp")
    owned = rows // z_count
    q_cols = w_query.shape[1] // 2
    heads = q_cols // HEAD
    ff = w_gate.shape[1] // 2
    wide_cols = 3 * ff
    groups = wide_cols // GROUP

    def lanes(count):
        return -(-count // 128) * 128

    qkv_used, out_cols = q_cols + 2 * HEAD, lanes(q_cols)
    qkv_cols = lanes(qkv_used)
    attn_cols = qkv_cols + out_cols

    def half(tensor, which, axis):
        size = tensor.shape[axis] // 2
        return lax.dynamic_slice_in_dim(tensor, which * size, size, axis=axis)

    def qkv_half(which):
        pieces = [half(weight, which, 1) for weight in (w_query, w_key, w_value)]
        pad = jnp.zeros((part, qkv_cols - qkv_used), low)
        return jnp.concatenate(pieces + [pad], axis=1)

    def absolute(tensor):
        return jnp.concatenate(
            [
                lax.dynamic_slice_in_dim(tensor, (place ^ turn) * chip_part, chip_part, axis=-1)
                for turn in range(4)
            ],
            axis=-1,
        )

    gain_rows = jnp.stack([norm_attn, norm_mlp]).astype(f32)
    gains = lax.dynamic_update_slice(jnp.zeros((8, chip_part), f32), gain_rows, (0, core * part))
    length = lengths[0]
    my_slots = ctx_at * rows + jnp.arange(rows, dtype=jnp.int32)
    valid = (my_slots < length).astype(f32)[:, None]
    valid_own = lax.dynamic_slice_in_dim(
        valid, lax.axis_index("mp") * owned, owned, axis=0
    )
    key_slots = jnp.arange(2 * chip_rows, dtype=jnp.int32)
    bias = jnp.where(key_slots < length, 0.0, NEG).astype(f32)[:, None]
    slots = y_at * chip_rows + jnp.arange(chip_rows, dtype=jnp.int32)
    cosine, sine = (table.T for table in rope_tables(slots.astype(f32), HEAD))

    hbm = pl.BlockSpec(memory_space=pl.ANY)
    vmem = pl.BlockSpec(memory_space=pltpu.VMEM)
    dma, vm = pltpu.SemaphoreType.DMA, pltpu.VMEM
    whole, half_rows, own = (chip_rows, width), (rows, width), (owned, width)
    half_part = chip_part // 2

    def call(body, ins, outs, scratch, collective_id, limit, name):
        return pl.pallas_call(
            body,
            out_shape=[jax.ShapeDtypeStruct(shape, dtype) for shape, dtype, _ in outs],
            in_specs=[spec for _, spec in ins],
            out_specs=[spec for _, _, spec in outs],
            scratch_shapes=scratch,
            name=name,
            cost_estimate=pl.CostEstimate(
                flops=0, bytes_accessed=300_000_000, transcendentals=0
            ),
            compiler_params=pltpu.CompilerParams(
                collective_id=collective_id,
                has_side_effects=True,
                vmem_limit_bytes=limit * 2**20,
            ),
        )(*(value for value, _ in ins))

    branch, h1_t, qkv_w, gains_all, out_w, wide, dm, inputs_own, q_t, kv, lse, o_t = call(
        start_kernel,
        [
            (hidden_in[0], vmem),
            (gains, vmem),
            (qkv_half(core), vmem),
            (qkv_half(1 - core), vmem),
            (w_gate, hbm),
            (w_up, hbm),
            (w_down, vmem),
            (w_output, vmem),
            (cotangent[0], vmem),
            (valid, vmem),
            (bias, vmem),
            (cosine, vmem),
            (sine, vmem),
        ],
        [
            (whole, low, vmem),
            ((width, chip_rows), low, vmem),
            ((4, chip_part, qkv_cols), low, vmem),
            ((8, 8, chip_part), f32, vmem),
            ((4, chip_part, out_cols), low, vmem),
            ((chip_part, wide_cols), low, hbm),
            (whole, low, vmem),
            (own, f32, vmem),
            ((q_cols, chip_rows), low, vmem),
            ((2, 2 * HEAD, chip_rows), low, vmem),
            ((8, chip_rows), f32, vmem),
            ((out_cols, chip_rows), low, vmem),
        ],
        [
            vm((part, 2 * ff), low),
            vm((part, out_cols), low),
            vm((chip_rows, qkv_cols), f32),
            vm(whole, low),
            dma((2,)),
            dma((2, 8)),
        ]
        + [dma((2, 2))] * 6
        + [dma((3, groups)), dma((2, 3, groups))]
        + [dma((2,))] * 4,
        1,
        48,
        "start",
    )
    gains_rel = (gains_all[0::2] + gains_all[1::2])[:, :2]
    gain_one, gain_two = (gains_rel[:, row].reshape(1, width) for row in range(2))

    wide_half = ((half_part, wide_cols), low, hbm)
    da, d_middle, layer_own, d_gain_two, own_grad, stage, upper, lower, x_one, y_two = call(
        mlp_kernel,
        [
            (branch, hbm),
            (inputs_own, vmem),
            (gain_two, vmem),
            (valid_own, vmem),
            (dm, vmem),
            (wide, hbm),
        ],
        [
            (whole, low, vmem),
            (own, f32, vmem),
            (own, low, vmem),
            ((1, width), f32, vmem),
            ((chip_part, wide_cols), f32, hbm),
            ((3, chip_part, wide_cols), low, hbm),
        ]
        + [wide_half] * 4,
        [
            vm((4, chip_part, wide_cols), low),
            vm(whole, low),
            vm((width, chip_rows), low),
            vm((width, chip_rows), low),
            vm(whole, low),
            vm(whole, low),
            vm(whole, f32),
            vm(own, f32),
            vm(own, f32),
            vm((chip_rows, wide_cols), low),
            vm((3, chip_part, GROUP), low),
            vm((chip_part, GROUP), f32),
            dma((2, groups)),
            dma((2, groups)),
            dma((2, 2, groups)),
            dma((4,)),
            dma((2, 4, groups)),
        ]
        + sum_scratch(owned, z_count, width)
        + share_scratch(z_count, True)
        + sum_scratch(owned, z_count, width)
        + sum_scratch(owned, z_count, width)[5:]
        + share_scratch(z_count, True),
        2,
        63,
        "mlp",
    )

    attn_half = vm((half_part, attn_cols), low)
    wide_low = vm((half_part, wide_cols), low)
    others = 2 * z_count - 1
    layer_all, grad_all, gain_sums, grad_gate, grad_up, grad_down, grad_out, grad_qkv = call(
        end_kernel,
        [
            (value, vmem)
            for value in (
                da,
                out_w,
                q_t,
                kv,
                lse,
                o_t,
                bias,
                cosine,
                sine,
                h1_t,
                qkv_w,
                d_middle,
                layer_own,
                inputs_own,
                gain_one,
                d_gain_two,
            )
        ]
        + [(value, hbm) for value in (stage, upper, lower, x_one, y_two, own_grad)],
        [
            (half_rows, low, vmem),
            (half_rows, low, vmem),
            ((8, chip_part), f32, vmem),
            (w_gate.shape, f32, hbm),
            (w_up.shape, f32, hbm),
            (w_down.shape, f32, hbm),
            (w_output.shape, f32, hbm),
            ((2, part, qkv_cols), f32, hbm),
        ],
        [
            vm((out_cols, chip_rows), low),
            vm((qkv_cols, chip_rows), low),
            vm((2, chip_rows, HEAD), f32),
            vm((2, chip_rows, HEAD), f32),
            vm((2 * HEAD, chip_rows), low),
            vm((2 * HEAD, chip_rows), low),
            vm(whole, low),
            vm(own, f32),
            wide_low,
            wide_low,
            wide_low,
            wide_low,
            vm((chip_part, wide_cols), f32),
            wide_low,
            wide_low,
            vm((groups, 2, 128, half_part), f32),
            vm((3, chip_part, attn_cols), low),
            vm((chip_part, attn_cols), f32),
        ]
        + [attn_half] * 6
        + [
            vm((2, out_cols, half_part), f32),
            vm((8, width), f32),
            vm((3, 8, chip_part), f32),
            vm((8, chip_part), f32),
            vm((others, 8, chip_part), f32),
            dma((7,)),
            dma((2, 2, groups)),
            dma((2, 4, 1)),
            dma((2, 2, 1)),
            dma((2,)),
            dma((4, groups)),
            dma((2, 4, groups)),
            dma((2, 3)),
            dma((2, others)),
        ]
        + sum_scratch(owned, z_count, width)
        + share_scratch(z_count, False) * 2,
        3,
        63,
        "end",
    )
    gain_mine = lax.dynamic_slice_in_dim(gain_sums, core * part, part, axis=1)

    def joined(start, size):
        return jnp.concatenate([grad_qkv[which, :, start : start + size] for which in (0, 1)], 1)

    return (
        absolute(layer_all)[None],
        absolute(grad_all)[None],
        gain_mine[0],
        joined(0, q_cols),
        joined(q_cols, HEAD),
        joined(q_cols + HEAD, HEAD),
        grad_out,
        gain_mine[1],
        grad_gate,
        grad_up,
        grad_down,
    )


def solution(mesh):
    plane = dict(mesh.shape) == {"dp": 2, "ctx": 4, "mp": 4}
    return jax.shard_map(
        on_plane if plane else any_mesh,
        mesh=mesh,
        in_specs=(
            P("dp", "ctx", None),
            P("dp", "ctx", None),
            P("dp"),
            P(("dp", "ctx")),
            P(("dp", "ctx"), "mp"),
            P(("dp", "ctx"), "mp"),
            P(("dp", "ctx"), "mp"),
            P("mp", ("dp", "ctx")),
            P(("dp", "ctx")),
            P(("dp", "ctx"), "mp"),
            P(("dp", "ctx"), "mp"),
            P("mp", ("dp", "ctx")),
        ),
        out_specs=(
            P("dp", "ctx", None),
            P("dp", "ctx", None),
            P(("dp", "ctx")),
            P(("dp", "ctx"), "mp"),
            P(("dp", "ctx"), "mp"),
            P(("dp", "ctx"), "mp"),
            P("mp", ("dp", "ctx")),
            P(("dp", "ctx")),
            P(("dp", "ctx"), "mp"),
            P(("dp", "ctx"), "mp"),
            P("mp", ("dp", "ctx")),
        ),
        check_vma=False,
    )
```

```python
import functools

import jax
import jax.numpy as jnp
import numpy as np
from jax import lax
from jax.experimental import pallas as pl
from jax.experimental.pallas import tpu as pltpu
from jax.sharding import PartitionSpec as P

HEAD = 80


EPS = 1e-05
THETA = 1000000.0
NEG = -1e30


def rope_tables(places, head_size):
    half = head_size // 2
    freq = THETA ** (-(jnp.arange(half, dtype=jnp.float32) * 2.0 / head_size))
    angle = places[:, None] * freq[None, :]
    return (jnp.cos(angle), jnp.sin(angle))


def rotate(tensor, cosine, sine_table):
    half = tensor.shape[-1] // 2
    first_half = tensor[..., :half]
    second_half = tensor[..., half:]
    cos_b = cosine[:, None, :]
    sin_b = sine_table[:, None, :]
    return jnp.concatenate(
        [first_half * cos_b - second_half * sin_b, second_half * cos_b + first_half * sin_b],
        axis=-1,
    )


def rotate_back(tensor, cosine, sine_table):
    half = tensor.shape[-1] // 2
    first_half = tensor[..., :half]
    second_half = tensor[..., half:]
    cos_b = cosine[:, None, :]
    sin_b = sine_table[:, None, :]
    return jnp.concatenate(
        [first_half * cos_b + second_half * sin_b, second_half * cos_b - first_half * sin_b],
        axis=-1,
    )


def normed(tensor, gain_row):
    return tensor * lax.rsqrt(jnp.mean(tensor * tensor, axis=-1, keepdims=True) + EPS) * gain_row


def norm_back(tensor, gain_row, grad_normed):
    scale_row = lax.rsqrt(jnp.mean(tensor * tensor, axis=-1, keepdims=True) + EPS)
    grad_scaled = grad_normed * gain_row
    grad_tensor = scale_row * grad_scaled - tensor * scale_row**3 * jnp.mean(
        grad_scaled * tensor, axis=-1, keepdims=True
    )
    grad_gain = jnp.sum(grad_normed * tensor * scale_row, axis=0)
    return (grad_tensor, grad_gain)


def masked_scores(query_seq, key_seq, length, places, kv_heads, group_size):
    query_grp = query_seq.reshape(query_seq.shape[0], kv_heads, group_size, HEAD)
    key_grp = key_seq.reshape(key_seq.shape[0], kv_heads, HEAD)
    raw_scores = jnp.einsum(
        "bkgh,tkh->kgbt", query_grp, key_grp, preferred_element_type=jnp.float32
    ) * HEAD ** (-0.5)
    key_places = jnp.arange(key_grp.shape[0], dtype=jnp.int32)
    allowed = (key_places[None, :] <= places[:, None]) & (key_places[None, :] < length)
    return jnp.where(allowed[None, None], raw_scores, NEG)


def any_mesh(
    hidden_in,
    cotangent,
    lengths,
    norm_attn,
    w_query,
    w_key,
    w_value,
    w_output,
    norm_mlp,
    w_gate,
    w_up,
    w_down,
):
    seq_count, slot_count, width_all = hidden_in.shape
    tok_rows = seq_count * slot_count
    attn_set = (
        lax.all_gather(w_query, ("dp", "ctx"), axis=0, tiled=True),
        lax.all_gather(w_key, ("dp", "ctx"), axis=0, tiled=True),
        lax.all_gather(w_value, ("dp", "ctx"), axis=0, tiled=True),
        lax.all_gather(w_output, ("dp", "ctx"), axis=1, tiled=True),
        lax.all_gather(norm_attn, ("dp", "ctx"), axis=0, tiled=True),
    )
    query_w, key_w, value_w, output_w, gain_attn = attn_set
    q_heads = query_w.shape[1] // HEAD
    kv_heads = key_w.shape[1] // HEAD
    group_size = q_heads // kv_heads
    first_slot = lax.axis_index("ctx") * slot_count
    places = first_slot + jnp.arange(slot_count, dtype=jnp.int32)
    valid_mask = (places[None, :] < lengths[:, None]).astype(jnp.float32).reshape(tok_rows, 1)
    cosine, sine_table = rope_tables(places.astype(jnp.float32), HEAD)
    inputs = hidden_in.reshape(tok_rows, width_all).astype(jnp.float32)
    gain_one = gain_attn.astype(jnp.float32)
    normed_one = normed(inputs, gain_one).astype(jnp.bfloat16)
    query_proj = jnp.dot(normed_one, query_w, preferred_element_type=jnp.float32).reshape(
        seq_count, slot_count, q_heads, HEAD
    )
    key_proj = jnp.dot(normed_one, key_w, preferred_element_type=jnp.float32).reshape(
        seq_count, slot_count, kv_heads, HEAD
    )
    value_low = (
        jnp.dot(normed_one, value_w, preferred_element_type=jnp.float32)
        .astype(jnp.bfloat16)
        .reshape(seq_count, slot_count, kv_heads * HEAD)
    )
    query_low = rotate(query_proj, cosine, sine_table).astype(jnp.bfloat16)
    key_low = (
        rotate(key_proj, cosine, sine_table)
        .astype(jnp.bfloat16)
        .reshape(seq_count, slot_count, kv_heads * HEAD)
    )
    key_all, value_all = (
        lax.all_gather(key_low, "ctx", axis=1, tiled=True),
        lax.all_gather(value_low, "ctx", axis=1, tiled=True),
    )

    def attend(members):
        query_seq, key_seq, value_seq, length = members
        scores = masked_scores(query_seq, key_seq, length, places, kv_heads, group_size)
        row_max = jnp.max(scores, axis=-1, keepdims=True)
        exponent = jnp.exp(scores - row_max)
        total = jnp.sum(exponent, axis=-1, keepdims=True)
        attention = (exponent / total).astype(jnp.bfloat16)
        value_grp = value_seq.reshape(value_seq.shape[0], kv_heads, HEAD)
        mixed_heads = jnp.einsum(
            "kgbt,tkh->bkgh", attention, value_grp, preferred_element_type=jnp.float32
        )
        return (mixed_heads.reshape(slot_count, q_heads * HEAD), (row_max + jnp.log(total))[..., 0])

    mixed_all, log_total = lax.map(attend, (query_low, key_all, value_all, lengths))
    attn_low = mixed_all.reshape(tok_rows, q_heads * HEAD).astype(jnp.bfloat16)
    branch = lax.psum(jnp.dot(attn_low, output_w, preferred_element_type=jnp.float32), "mp")
    middle = inputs + branch
    mlp_set = (
        lax.all_gather(w_gate, ("dp", "ctx"), axis=0, tiled=True),
        lax.all_gather(w_up, ("dp", "ctx"), axis=0, tiled=True),
        lax.all_gather(w_down, ("dp", "ctx"), axis=1, tiled=True),
        lax.all_gather(norm_mlp, ("dp", "ctx"), axis=0, tiled=True),
    )
    gate_w, up_w, down_w, gain_mlp = mlp_set
    gain_two = gain_mlp.astype(jnp.float32)
    normed_two = normed(middle, gain_two).astype(jnp.bfloat16)
    gate_proj = jnp.dot(normed_two, gate_w, preferred_element_type=jnp.float32)
    up_proj = jnp.dot(normed_two, up_w, preferred_element_type=jnp.float32)
    hidden = (jax.nn.silu(gate_proj) * up_proj).astype(jnp.bfloat16)
    mlp_out = lax.psum(
        jnp.dot(hidden, down_w, preferred_element_type=jnp.float32).astype(jnp.bfloat16), "mp"
    ).astype(jnp.float32)
    layer_out = (
        (valid_mask * (middle + mlp_out))
        .astype(jnp.bfloat16)
        .reshape(seq_count, slot_count, width_all)
    )
    grad_out = valid_mask * cotangent.reshape(tok_rows, width_all).astype(jnp.float32)
    grad_mlp = grad_out.astype(jnp.bfloat16)
    gate_back, up_back, down_back, gain_mlp_back = (
        lax.all_gather(w_gate, ("dp", "ctx"), axis=0, tiled=True),
        lax.all_gather(w_up, ("dp", "ctx"), axis=0, tiled=True),
        lax.all_gather(w_down, ("dp", "ctx"), axis=1, tiled=True),
        lax.all_gather(norm_mlp, ("dp", "ctx"), axis=0, tiled=True),
    )
    grad_hidden = jnp.einsum("tm,fm->tf", grad_mlp, down_back, preferred_element_type=jnp.float32)
    grad_down = jnp.einsum("tf,tm->fm", hidden, grad_mlp, preferred_element_type=jnp.float32)
    sigmoid_gate = jax.nn.sigmoid(gate_proj)
    grad_gate_low = (
        grad_hidden * up_proj * sigmoid_gate * (1.0 + gate_proj * (1.0 - sigmoid_gate))
    ).astype(jnp.bfloat16)
    grad_up_low = (grad_hidden * gate_proj * sigmoid_gate).astype(jnp.bfloat16)
    grad_gate = jnp.einsum(
        "td,tf->df", normed_two, grad_gate_low, preferred_element_type=jnp.float32
    )
    grad_up = jnp.einsum("td,tf->df", normed_two, grad_up_low, preferred_element_type=jnp.float32)
    partial_two = jnp.einsum(
        "tf,df->td", grad_gate_low, gate_back, preferred_element_type=jnp.float32
    ) + jnp.einsum("tf,df->td", grad_up_low, up_back, preferred_element_type=jnp.float32)
    grad_normed_two = lax.psum(partial_two, "mp")
    grad_middle_norm, grad_gain_two = norm_back(
        middle, gain_mlp_back.astype(jnp.float32), grad_normed_two
    )
    mlp_grads = (
        lax.psum_scatter(grad_gate, ("dp", "ctx"), scatter_dimension=0, tiled=True),
        lax.psum_scatter(grad_up, ("dp", "ctx"), scatter_dimension=0, tiled=True),
        lax.psum_scatter(grad_down, ("dp", "ctx"), scatter_dimension=1, tiled=True),
        lax.psum_scatter(grad_gain_two, ("dp", "ctx"), scatter_dimension=0, tiled=True),
    )
    grad_middle = grad_out + grad_middle_norm
    grad_branch = grad_middle.astype(jnp.bfloat16)
    query_back, key_back, value_back, output_back, gain_attn_back = (
        lax.all_gather(w_query, ("dp", "ctx"), axis=0, tiled=True),
        lax.all_gather(w_key, ("dp", "ctx"), axis=0, tiled=True),
        lax.all_gather(w_value, ("dp", "ctx"), axis=0, tiled=True),
        lax.all_gather(w_output, ("dp", "ctx"), axis=1, tiled=True),
        lax.all_gather(norm_attn, ("dp", "ctx"), axis=0, tiled=True),
    )
    grad_output = jnp.einsum("tq,td->qd", attn_low, grad_branch, preferred_element_type=jnp.float32)
    grad_attn_low = (
        jnp.einsum("td,qd->tq", grad_branch, output_back, preferred_element_type=jnp.float32)
        .astype(jnp.bfloat16)
        .reshape(seq_count, slot_count, q_heads, HEAD)
    )

    def attend_back(members):
        query_seq, key_seq, value_seq, length, log_seq, grad_seq = members
        scores = masked_scores(query_seq, key_seq, length, places, kv_heads, group_size)
        attention = jnp.exp(scores - log_seq[..., None])
        query_grp = query_seq.reshape(slot_count, kv_heads, group_size, HEAD)
        key_grp = key_seq.reshape(key_seq.shape[0], kv_heads, HEAD)
        value_grp = value_seq.reshape(value_seq.shape[0], kv_heads, HEAD)
        grad_grp = grad_seq.reshape(slot_count, kv_heads, group_size, HEAD)
        grad_attention = jnp.einsum(
            "bkgh,tkh->kgbt", grad_grp, value_grp, preferred_element_type=jnp.float32
        )
        inner = jnp.sum(attention * grad_attention, axis=-1, keepdims=True)
        grad_scores = (attention * (grad_attention - inner)).astype(jnp.bfloat16)
        scale_qk = HEAD ** (-0.5)
        grad_query_seq = (
            jnp.einsum("kgbt,tkh->bkgh", grad_scores, key_grp, preferred_element_type=jnp.float32)
            * scale_qk
        )
        grad_key_seq = (
            jnp.einsum("kgbt,bkgh->tkh", grad_scores, query_grp, preferred_element_type=jnp.float32)
            * scale_qk
        )
        grad_value_seq = jnp.einsum(
            "kgbt,bkgh->tkh",
            attention.astype(jnp.bfloat16),
            grad_grp,
            preferred_element_type=jnp.float32,
        )
        key_rows = key_grp.shape[0]
        return (
            grad_query_seq.reshape(slot_count, q_heads, HEAD),
            grad_key_seq.reshape(key_rows, kv_heads * HEAD),
            grad_value_seq.reshape(key_rows, kv_heads * HEAD),
        )

    grad_query_rot, grad_key_all, grad_value_all = lax.map(
        attend_back, (query_low, key_all, value_all, lengths, log_total, grad_attn_low)
    )
    grad_key_rot, grad_value_rot = (
        lax.psum_scatter(grad_key_all, "ctx", scatter_dimension=1, tiled=True),
        lax.psum_scatter(grad_value_all, "ctx", scatter_dimension=1, tiled=True),
    )
    grad_query_low = (
        rotate_back(grad_query_rot, cosine, sine_table)
        .astype(jnp.bfloat16)
        .reshape(tok_rows, q_heads * HEAD)
    )
    grad_key_low = (
        rotate_back(grad_key_rot.reshape(seq_count, slot_count, kv_heads, HEAD), cosine, sine_table)
        .astype(jnp.bfloat16)
        .reshape(tok_rows, kv_heads * HEAD)
    )
    grad_value_low = grad_value_rot.astype(jnp.bfloat16).reshape(tok_rows, kv_heads * HEAD)
    grad_query = jnp.einsum(
        "td,tq->dq", normed_one, grad_query_low, preferred_element_type=jnp.float32
    )
    grad_key = jnp.einsum("td,tq->dq", normed_one, grad_key_low, preferred_element_type=jnp.float32)
    grad_value = jnp.einsum(
        "td,tq->dq", normed_one, grad_value_low, preferred_element_type=jnp.float32
    )
    partial_one = jnp.einsum(
        "tq,dq->td", grad_query_low, query_back, preferred_element_type=jnp.float32
    )
    partial_one = partial_one + jnp.einsum(
        "tq,dq->td", grad_key_low, key_back, preferred_element_type=jnp.float32
    )
    partial_one = partial_one + jnp.einsum(
        "tq,dq->td", grad_value_low, value_back, preferred_element_type=jnp.float32
    )
    grad_normed_one = lax.psum(partial_one, "mp")
    grad_inputs_norm, grad_gain_one = norm_back(
        inputs, gain_attn_back.astype(jnp.float32), grad_normed_one
    )
    input_grad = (
        (grad_middle + grad_inputs_norm)
        .astype(jnp.bfloat16)
        .reshape(seq_count, slot_count, width_all)
    )
    attn_grads = (
        lax.psum_scatter(grad_query, ("dp", "ctx"), scatter_dimension=0, tiled=True),
        lax.psum_scatter(grad_key, ("dp", "ctx"), scatter_dimension=0, tiled=True),
        lax.psum_scatter(grad_value, ("dp", "ctx"), scatter_dimension=0, tiled=True),
        lax.psum_scatter(grad_output, ("dp", "ctx"), scatter_dimension=1, tiled=True),
        lax.psum_scatter(grad_gain_one, ("dp", "ctx"), scatter_dimension=0, tiled=True),
    )
    return (
        layer_out,
        input_grad,
        attn_grads[4],
        attn_grads[0],
        attn_grads[1],
        attn_grads[2],
        attn_grads[3],
        mlp_grads[3],
        mlp_grads[0],
        mlp_grads[1],
        mlp_grads[2],
    )


SPLIT = 4
GROUP = 384
NT = (((1,), (1,)), ((), ()))
TN = (((0,), (0,)), ((), ()))
MESH = pl.DeviceIdType.MESH


def remote(src, dst, sems, index, device):
    return pltpu.make_async_remote_copy(
        src_ref=src,
        dst_ref=dst,
        send_sem=sems.at[(0, *index)],
        recv_sem=sems.at[(1, *index)],
        device_id=device,
        device_id_type=MESH,
    )


def rows_at(start, size):
    return pl.ds(pl.multiple_of(start, 16), size)


def lanes_at(start, size):
    return pl.ds(pl.multiple_of(start, 128), size)


def chosen(rows, columns, first_column):
    row = lax.broadcasted_iota(jnp.int32, (rows, columns), 0)
    column = lax.broadcasted_iota(jnp.int32, (rows, columns), 1)
    return (row == column - first_column).astype(jnp.bfloat16)


def masked(keys, queries, length, block, y_at):
    scores = jnp.dot(keys, queries, preferred_element_type=jnp.float32) * HEAD ** (-0.5)
    rows, columns = scores.shape
    key_slots = block * rows + lax.broadcasted_iota(jnp.int32, scores.shape, 0)
    query_slots = y_at * columns + lax.broadcasted_iota(jnp.int32, scores.shape, 1)
    return jnp.where((key_slots <= query_slots) & (key_slots < length), scores, NEG)


class Place:
    def __init__(self, owned, width):
        self.x, self.ctx, self.z = (lax.axis_index(name) for name in ("dp", "ctx", "mp"))
        self.core = lax.rem(self.ctx, 2)
        self.y = (self.ctx - self.core) // 2
        self.last = lax.axis_size("mp") - 1
        self.owned, self.rows, self.width = owned, owned * (self.last + 1), width
        self.step = width // SPLIT
        self.size, self.middle = width // 4, width // 8
        self.above, self.below = (self.x, self.ctx, self.z + 1), (self.x, self.ctx, self.z - 1)
        self.plane = {
            (turn, flip): self.turned(turn, flip)
            for turn in range(4)
            for flip in range(2)
            if turn or flip
        }
        self.sibling, self.over_x, self.over_y = (
            self.plane[key] for key in ((0, 1), (2, 0), (1, 0))
        )
        self.diagonal = self.plane[3, 0]
        self.column = [
            (self.x, self.other_core(flip), lax.rem(self.z + turn, self.last + 1))
            for turn in range(self.last + 1)
            for flip in range(2)
            if turn or flip
        ]

    def other_core(self, flip):
        return self.ctx + 1 - 2 * self.core if flip else self.ctx

    def turned(self, turn, flip):
        x_to = 1 - self.x if turn >= 2 else self.x
        y_to = 1 - self.y if turn % 2 else self.y
        core_to = 1 - self.core if flip else self.core
        return (x_to, 2 * y_to + core_to, self.z)

    def enter(self):
        barrier = pltpu.get_barrier_semaphore()
        peers = list(self.plane.values()) + self.column[1:]
        for device in peers:
            pl.semaphore_signal(barrier, inc=1, device_id=device, device_id_type=MESH)
        pl.semaphore_wait(barrier, len(peers))

    def block_of(self, core, block):
        return rows_at(core * self.rows + block * self.owned, self.owned)

    def block(self, at):
        return rows_at(at * self.owned, self.owned)

    def mine(self):
        return self.block_of(self.core, self.z)

    def columns(self, piece):
        return pl.ds(piece * self.step, self.step)

    def cut(self, turn):
        return slice(turn * self.size, (turn + 1) * self.size)

    def source(self, turn):
        x_to = 1 - self.x if turn >= 2 else self.x
        y_to = 1 - self.y if turn % 2 else self.y
        return lanes_at((2 * x_to + y_to) * self.size, self.size)


class SumChain:
    def __init__(self, place, part, held, up_in, down_in, core_sem, up_sem, down_sem):
        self.place, self.part, self.held = place, part, held
        self.ways = ((place.above, up_in, up_sem, 1), (place.below, down_in, down_sem, -1))
        self.core_sem = core_sem

    def across(self, block):
        place = self.place
        return remote(
            self.part.at[place.block_of(1 - place.core, block)],
            self.held.at[place.block(block)],
            self.core_sem,
            (block,),
            place.sibling,
        )

    def open(self):
        for block in range(self.place.last + 1):
            self.across(block).start()

    def own(self, at, cols):
        place = self.place
        mine = self.part[place.block_of(place.core, at), cols].astype(jnp.float32)
        return mine + self.held[place.block(at), cols].astype(jnp.float32)

    def hop(self, way, step, piece, at):
        place = self.place
        cols = place.columns(piece)
        return remote(
            self.part.at[place.block_of(place.core, at), cols],
            way[1].at[step, :, cols],
            way[2],
            (step, piece),
            way[0],
        )

    def far(self, way):
        return self.place.z if way[3] == 1 else self.place.last - self.place.z

    def target(self, way, step):
        return self.place.z + way[3] * (self.place.last - step)

    def step(self, step):
        place = self.place
        for way in self.ways:

            @pl.when(self.far(way) <= step)
            def _(way=way):
                at = self.target(way, step)
                rows = place.block_of(place.core, at)
                self.across(at).wait_recv()
                for piece in range(SPLIT):
                    cols = place.columns(piece)
                    total = self.own(at, cols)
                    if step:

                        @pl.when(self.far(way) > 0)
                        def _(total=total, cols=cols, piece=piece):
                            self.hop(way, step - 1, piece, at).wait_recv()
                            got = way[1][step - 1, :, cols].astype(jnp.float32)
                            self.part[rows, cols] = (total + got).astype(self.part.dtype)

                        @pl.when(self.far(way) == 0)
                        def _(total=total, cols=cols):
                            self.part[rows, cols] = total.astype(self.part.dtype)

                    else:
                        self.part[rows, cols] = total.astype(self.part.dtype)
                    self.hop(way, step, piece, at).start()

    def close(self, result):
        place = self.place
        final = place.last - 1
        self.across(place.z).wait_recv()
        result[...] = self.own(place.z, slice(None))
        for way in self.ways:

            @pl.when(self.far(way) > 0)
            def _(way=way):
                for piece in range(SPLIT):
                    self.hop(way, final, piece, place.z).wait_recv()
                result[...] += way[1][final].astype(jnp.float32)

    def drain(self):
        place = self.place
        for block in range(place.last + 1):
            self.across(block).wait_send()
        for step in range(place.last):
            for way in self.ways:

                @pl.when(self.far(way) <= step)
                def _(way=way, step=step):
                    for piece in range(SPLIT):
                        self.hop(way, step, piece, self.target(way, step)).wait_send()


class ShareChain:
    def __init__(self, place, whole, up_sem, down_sem, core_sem=None):
        self.place, self.whole, self.core_sem = place, whole, core_sem
        self.ways = ((place.above, up_sem, 1), (place.below, down_sem, -1))

    def rows(self, at):
        place = self.place
        return place.block(at) if self.core_sem is None else place.block_of(place.core, at)

    def far(self, way):
        return self.place.z if way[2] == 1 else self.place.last - self.place.z

    def hop(self, way, step, piece, origin):
        ref = self.whole.at[self.rows(origin), self.place.columns(piece)]
        return remote(ref, ref, way[1], (step, piece), way[0])

    def across(self, origin, core):
        ref = self.whole.at[self.place.block_of(core, origin)]
        return remote(ref, ref, self.core_sem, (origin,), self.place.sibling)

    def step(self, step):
        place = self.place
        for way in self.ways:
            origin = place.z - way[2] * step

            @pl.when(self.far(way) >= step)
            def _(way=way, origin=origin):
                for piece in range(SPLIT):
                    if step:
                        self.hop(way, step - 1, piece, origin).wait_recv()
                    if step < place.last:

                        @pl.when(self.far(way) < place.last)
                        def _(piece=piece):
                            self.hop(way, step, piece, origin).start()

                if step and self.core_sem is not None:
                    self.across(origin, place.core).start()

        if step == 0 and self.core_sem is not None:
            self.across(place.z, place.core).start()

    def arrive(self):
        if self.core_sem is not None:
            for origin in range(self.place.last + 1):
                self.across(origin, 1 - self.place.core).wait_recv()

    def drain(self):
        place = self.place
        for step in range(place.last):
            for way in self.ways:

                @pl.when((self.far(way) >= step) & (self.far(way) < place.last))
                def _(way=way, step=step):
                    for piece in range(SPLIT):
                        self.hop(way, step, piece, place.z - way[2] * step).wait_send()

        if self.core_sem is not None:
            for origin in range(place.last + 1):
                self.across(origin, place.core).wait_send()


class AttnGather:
    def __init__(self, place, w, first, rows, x_sem, y_sem, far_sem, index):
        self.place, self.w, self.index = place, w, index
        self.sems = (x_sem, y_sem, far_sem)
        self.halves = tuple(pl.ds(first + half * rows // 2, rows // 2) for half in range(2))

    def cross(self, half, to_x):
        place, rows = self.place, self.halves[half]
        return remote(
            self.w.at[0, rows],
            self.w.at[2 if to_x else 1, rows],
            self.sems[0] if to_x else self.sems[1],
            (self.index + half,),
            place.over_x if to_x else place.over_y,
        )

    def relay(self, to_x):
        place, half = self.place, 1 if to_x else 0
        rows = self.halves[half]
        return remote(
            self.w.at[1 if to_x else 2, rows],
            self.w.at[3, rows],
            self.sems[2],
            (self.index + half,),
            place.over_x if to_x else place.over_y,
        )

    def send(self, which):
        self.cross(which, True).start()
        self.cross(1 - which, False).start()

    def pass_on(self):
        self.cross(0, True).wait_recv()
        self.relay(False).start()
        self.cross(1, False).wait_recv()
        self.relay(True).start()

    def drain(self):
        for half in range(2):
            for to_x in (True, False):
                self.cross(half, to_x).wait_send()
        self.relay(True).wait_send()
        self.relay(False).wait_send()


class WideGather:
    def __init__(self, place, w, x_sem, y_sem, far_sem):
        self.place, self.w = place, w
        self.x_sem, self.y_sem, self.far_sem = x_sem, y_sem, far_sem
        self.groups = w.shape[2] // GROUP

    def columns(self, group):
        return lanes_at(group * GROUP, GROUP)

    def cross(self, group, to_x):
        place, cols = self.place, self.columns(group)
        return remote(
            self.w.at[0, :, cols],
            self.w.at[2 if to_x else 1, :, cols],
            self.x_sem if to_x else self.y_sem,
            (group,),
            place.over_x if to_x else place.over_y,
        )

    def relay(self, group, to_x):
        place, cols = self.place, self.columns(group)
        rows = pl.ds(place.middle, place.middle) if to_x else pl.ds(0, place.middle)
        return remote(
            self.w.at[1 if to_x else 2, rows, cols],
            self.w.at[3, rows, cols],
            self.far_sem,
            (1 if to_x else 0, group),
            place.over_x if to_x else place.over_y,
        )

    def send(self, group):
        self.cross(group, True).start()
        self.cross(group, False).start()

    def pump(self, group):
        self.cross(group, True).wait_recv()
        self.relay(group, False).start()
        self.cross(group, False).wait_recv()
        self.relay(group, True).start()

        @pl.when(group + 2 < self.groups)
        def _():
            self.send(group + 2)

    def arrive(self, group):
        self.relay(group, False).wait_recv()
        self.relay(group, True).wait_recv()

    def drain(self):
        def body(group, carry):
            for to_x in (True, False):
                self.cross(group, to_x).wait_send()
                self.relay(group, to_x).wait_send()
            return carry

        lax.fori_loop(0, self.groups, body, 0)


class Home:
    kinds = ("upper", "lower", "x_one", "y_two", "y_one", "x_two")

    def __init__(self, place, sources, targets, sem, cut):
        self.place, self.sem, self.cut = place, sem, cut
        self.sources, self.targets = sources, targets

    def copy(self, kind, group):
        place, index = self.place, self.kinds.index(kind)
        to_x = kind in ("upper", "x_one", "x_two")
        return remote(
            self.cut(self.sources[kind], group),
            self.cut(self.targets[kind], group),
            self.sem,
            (index, group),
            place.over_x if to_x else place.over_y,
        )

    def send(self, kinds, group):
        for kind in kinds:
            self.copy(kind, group).start()

    def arrive(self, kinds, group):
        for kind in kinds:
            self.copy(kind, group).wait_recv()

    def drain(self, group):
        for kind in self.kinds:
            self.copy(kind, group).wait_send()


class Refs:
    def __init__(self, names, refs):
        for name, ref in zip(names, refs, strict=True):
            setattr(self, name, ref)


def layer_kernel(names, *refs):
    r = Refs(names, refs)
    f32, low = jnp.float32, jnp.bfloat16
    z_count = lax.axis_size("mp")
    rows, width = r.hidden.shape
    place = Place(rows // z_count, width)
    size, middle, core = place.size, place.middle, place.core
    cut = place.cut
    part_rows = r.query.shape[0]
    q_rows = r.query.shape[1] // 2
    heads = q_rows // HEAD
    qkv_rows = q_rows + 2 * HEAD
    attn_rows = qkv_rows + q_rows
    attn_half = attn_rows // 2
    chip_rows = 2 * rows
    length = r.length[0, 0]
    cos_at, sin_at = r.cos[place.y], r.sin[place.y]
    w, aw = r.w, r.aw
    ff = r.gate.shape[1] // 2
    groups = ff // 128

    branch_sum = SumChain(place, r.part, *r.chain_one, *r.branch_sems)
    h2_share = ShareChain(place, r.h2, *r.h2_sems)
    back_sum = SumChain(place, r.part, *r.chain_two, *r.back_sems)
    mlp_sum = SumChain(place, r.mlp_part, *r.chain_one, *r.mlp_sems)
    da_share = ShareChain(place, r.da, *r.da_sems)
    input_sum = SumChain(place, r.part, *r.chain_two, *r.input_sems)
    layer_share = ShareChain(place, r.layer_all, *r.layer_sems)
    grad_share = ShareChain(place, r.grad_all, *r.grad_sems)
    qkv_gather = AttnGather(place, aw, 0, qkv_rows, r.attn_x, r.attn_y, r.attn_far, 0)
    out_gather = AttnGather(place, aw, qkv_rows, q_rows, r.attn_x, r.attn_y, r.attn_far, 2)
    gather = WideGather(place, w, r.wide_x, r.wide_y, r.wide_far)

    my_rows = rows_at(core * rows, rows)
    loads = [
        pltpu.make_async_copy(r.hidden, r.da.at[pl.ds(0, rows)], r.load_sem.at[0]),
        pltpu.make_async_copy(r.cotangent, r.da.at[pl.ds(rows, rows)], r.load_sem.at[1]),
    ]
    for load in loads:
        load.start()
    to_lanes = chosen(part_rows, size, core * part_rows)

    def split(total):
        half = total.shape[0] // 2
        one, two = total[:half], total[half:]
        return jnp.where(core == 0, one, two), jnp.where(core == 0, two, one)

    def spread(tensor, dims):
        return split(lax.dot_general(tensor, to_lanes, dims, preferred_element_type=f32))

    plain = (((1,), (0,)), ((), ()))
    q_pair, k_pair, v_pair = (
        spread(r.query[...], TN),
        spread(r.key_t[...], plain),
        spread(r.value_t[...], plain),
    )
    qkv_give = r.part.at[pl.ds(0, qkv_rows), pl.ds(0, size)]
    qkv_take = r.mlp_part.at[pl.ds(0, qkv_rows), pl.ds(0, size)]
    out_give = r.part.at[pl.ds(0, q_rows), pl.ds(size, size)]
    out_take = r.mlp_part.at[pl.ds(0, q_rows), pl.ds(size, size)]
    qkv_give[...] = jnp.concatenate([q_pair[1], k_pair[1], v_pair[1]], axis=0).astype(low)
    place.enter()
    qkv_swap = remote(qkv_give, qkv_take, r.core_sem, (0,), place.sibling)
    qkv_swap.start()

    row = lax.broadcasted_iota(jnp.int32, r.gains.shape, 0)
    gain_pair = [
        jnp.dot(jnp.broadcast_to(norm[...], (8, part_rows)), to_lanes, preferred_element_type=f32)
        for norm in (r.norm_one, r.norm_two)
    ]
    r.gains[...] = jnp.where(row == 0, gain_pair[0], jnp.where(row == 1, gain_pair[1], 0.0))
    r.gains_all[core] = r.gains[...]

    def gain_copy(turn, flip):
        slot = 2 * turn + core
        return remote(
            r.gains, r.gains_all.at[slot], r.gain_sem, (2 * turn + flip,), place.plane[turn, flip]
        )

    for turn, flip in place.plane:
        gain_copy(turn, flip).start()

    qkv_keep = jnp.concatenate([q_pair[0], k_pair[0], v_pair[0]], axis=0).astype(low)
    qkv_swap.wait_recv()
    aw[0, :qkv_rows] = qkv_keep + qkv_take[...]
    qkv_gather.send(0)
    qkv_gather.send(1)
    out_pair = spread(r.output_t[...], TN)
    out_give[...] = out_pair[1].astype(low)
    out_swap = remote(out_give, out_take, r.core_sem, (1,), place.sibling)
    out_swap.start()

    def wide_copies(group, kind, source):
        from_here = lanes_at(core * ff + group * 128, 128)
        from_there = lanes_at((1 - core) * ff + group * 128, 128)
        to = lanes_at(group * GROUP + kind * 128, 128)
        owner_rows = rows_at(core * part_rows, part_rows)
        here = pltpu.make_async_copy(
            source.at[:, from_here], w.at[0, owner_rows, to], r.wide_here.at[kind, group]
        )
        there = remote(
            source.at[:, from_there],
            w.at[0, owner_rows, to],
            r.wide_there,
            (kind, group),
            place.sibling,
        )
        return here, there

    sources = (r.gate, r.up, r.down_t)

    def start_wide(group, carry):
        for kind, source in enumerate(sources):
            for copy in wide_copies(group, kind, source):
                copy.start()
        return carry

    def own_wide(group, carry):
        for kind, source in enumerate(sources):
            here, there = wide_copies(group, kind, source)
            here.wait()
            there.wait_recv()
        return carry

    lax.fori_loop(0, groups, start_wide, 0)

    for load in loads:
        load.wait()
    hidden, cotangent = r.da.at[pl.ds(0, rows)], r.da.at[pl.ds(rows, rows)]
    slot = place.ctx * rows + lax.broadcasted_iota(jnp.int32, (rows, size), 0)
    for turn in range(4):
        block = cotangent[:, place.source(turn)].astype(f32)
        r.dm[my_rows, cut(turn)] = jnp.where(slot < length, block, 0.0).astype(low)
        r.inputs_own[:, cut(turn)] = r.da[place.block(place.z), place.source(turn)].astype(f32)
    dm_copy = remote(r.dm.at[my_rows], r.dm.at[my_rows], r.dm_sem, (0,), place.sibling)
    dm_copy.start()
    out_swap.wait_recv()
    aw[0, qkv_rows:] = out_pair[0].astype(low) + out_take[...]
    squares = hidden[...].astype(f32)
    scale = lax.rsqrt(jnp.mean(squares * squares, axis=-1, keepdims=True) + EPS)
    for turn, flip in place.plane:
        gain_copy(turn, flip).wait_recv()
    for turn in range(4):
        gain = r.gains_all[2 * turn] + r.gains_all[2 * turn + 1]
        r.gain_rows[:, cut(turn)] = gain
        block = hidden[:, place.source(turn)].astype(f32)
        r.h1[my_rows, cut(turn)] = (block * scale * gain[:1]).astype(low)
    h1_copy = remote(r.h1.at[my_rows], r.h1.at[my_rows], r.h1_sem, (0,), place.sibling)
    h1_copy.start()

    qkv = r.dh2.at[pl.ds(0, qkv_rows), pl.ds(0, chip_rows)]

    def qkv_dot(turn):
        return lax.dot_general(
            aw[turn, :qkv_rows], r.h1[:, cut(turn)], NT, preferred_element_type=f32
        )

    h1_copy.wait_recv()
    qkv[...] = qkv_dot(0)
    qkv_gather.pass_on()
    out_gather.send(0)
    qkv_gather.cross(1, True).wait_recv()
    qkv[...] += qkv_dot(2)
    qkv_gather.cross(0, False).wait_recv()
    qkv[...] += qkv_dot(1)
    qkv_gather.relay(False).wait_recv()
    qkv_gather.relay(True).wait_recv()
    qkv[...] += qkv_dot(3)

    def turned(first_row):
        ahead = qkv[first_row : first_row + HEAD // 2]
        behind = qkv[first_row + HEAD // 2 : first_row + HEAD]
        return jnp.concatenate(
            [ahead * cos_at - behind * sin_at, behind * cos_at + ahead * sin_at], axis=0
        )

    r.kv[place.y, :HEAD] = turned(q_rows).astype(low)
    r.kv[place.y, HEAD:] = qkv[q_rows + HEAD : qkv_rows].astype(low)
    kv_copy = remote(r.kv.at[place.y], r.kv.at[place.y], r.kv_sem, (0,), place.over_y)
    kv_copy.start()
    out_gather.send(1)
    head_rows = [slice(head * HEAD, (head + 1) * HEAD) for head in range(heads)]
    for head in range(heads):
        r.q_t[head_rows[head]] = turned(head * HEAD).astype(low)
    lax.fori_loop(0, groups, own_wide, 0)
    kv_copy.wait_recv()
    out_gather.pass_on()
    gather.send(0)

    keys = [r.kv[block, :HEAD].T for block in range(2)]
    for head in range(heads):
        scores = [
            masked(keys[block], r.q_t[head_rows[head]], length, block, place.y)
            for block in range(2)
        ]
        top = jnp.maximum(*(jnp.max(score, axis=0, keepdims=True) for score in scores))
        exponents = [jnp.exp(score - top) for score in scores]
        total = sum(jnp.sum(exponent, axis=0, keepdims=True) for exponent in exponents)
        mixed = jnp.zeros((HEAD, chip_rows), f32)
        for block in range(2):
            weights = (exponents[block] / total).astype(low)
            mixed += jnp.dot(r.kv[block, HEAD:], weights, preferred_element_type=f32)
        r.o_t[head_rows[head]] = mixed.astype(low)
        r.lse[head : head + 1] = top + jnp.log(total)
    out_gather.cross(1, True).wait_recv()
    out_gather.cross(0, False).wait_recv()
    out_gather.relay(False).wait_recv()
    out_gather.relay(True).wait_recv()
    qkv_swap.wait_send()
    out_swap.wait_send()
    mixed_all = r.o_t[...].T
    for turn in range(4):
        r.part[:, cut(turn)] = jnp.dot(
            mixed_all, aw[turn, qkv_rows:], preferred_element_type=f32
        ).astype(low)

    branch_sum.open()
    gather.send(1)
    branch_sum.step(0)
    branch_sum.step(1)
    gather.pump(0)
    branch_sum.step(2)
    branch_sum.close(r.middle)
    r.middle[...] += r.inputs_own[...]
    gain_two = r.gain_rows[1:2]
    r.h2[place.mine()] = normed(r.middle[...], gain_two).astype(low)
    h2_share.step(0)
    gather.pump(1)
    h2_share.step(1)
    h2_share.step(2)
    gather.pump(2)
    h2_share.step(3)
    h2_share.arrive()
    branch_sum.drain()
    dm_copy.wait()
    r.dh2[...] = jnp.zeros_like(r.dh2)

    def wide_cut(ref, group):
        return ref.at[:, lanes_at(group * GROUP, GROUP)]

    top_half, low_half = pl.ds(0, middle), pl.ds(middle, middle)
    home = Home(
        place,
        {
            "upper": r.stage.at[2, top_half],
            "lower": r.stage.at[2, low_half],
            "x_one": r.stage.at[1, top_half],
            "y_two": r.stage.at[0, low_half],
            "y_one": w.at[0, top_half],
            "x_two": w.at[0, low_half],
        },
        {
            "upper": r.upper,
            "lower": r.lower,
            "x_one": r.x_one,
            "y_two": r.y_two,
            "y_one": w.at[3, top_half],
            "x_two": w.at[3, low_half],
        },
        r.home_sem,
        wide_cut,
    )
    far_kinds, straight_kinds, last_kinds = (
        ("upper", "lower"),
        ("x_one", "y_two"),
        ("y_one", "x_two"),
    )

    def group_body(group, carry):
        start = group * GROUP
        gu_cols, down_cols = lanes_at(start, 256), lanes_at(start + 256, 128)
        gather.arrive(group)
        gu = jnp.zeros((chip_rows, 256), f32)
        d_hidden = jnp.zeros((chip_rows, 128), f32)
        for turn in range(4):
            gu += jnp.dot(r.h2[:, cut(turn)], w[turn, :, gu_cols], preferred_element_type=f32)
            d_hidden += jnp.dot(
                r.dm[:, cut(turn)], w[turn, :, down_cols], preferred_element_type=f32
            )
        gate, up = gu[:, :128], gu[:, 128:]
        sigma = jax.nn.sigmoid(gate)
        silu = gate * sigma
        d_gate = d_hidden * up * sigma * (1.0 + gate * (1.0 - sigma))
        r.zd[:, lanes_at(start, 128)] = d_gate.astype(low)
        r.zd[:, lanes_at(start + 128, 128)] = (d_hidden * silu).astype(low)
        r.zd[:, down_cols] = (silu * up).astype(low)
        d_gu, hidden_low = r.zd[:, gu_cols], r.zd[:, down_cols]
        for turn in range(4):
            r.dh2[:, cut(turn)] += lax.dot_general(
                d_gu, w[turn, :, gu_cols], NT, preferred_element_type=f32
            )
        for turn in range(4):
            grad_gu = lax.dot_general(r.h2[:, cut(turn)], d_gu, TN, preferred_element_type=f32)
            grad_down = lax.dot_general(
                r.dm[:, cut(turn)], hidden_low, TN, preferred_element_type=f32
            )
            if turn:
                r.tile[turn - 1, :, :256] = grad_gu.astype(low)
                r.tile[turn - 1, :, 256:] = grad_down.astype(low)
            else:
                r.tile_own[:, :256] = grad_gu
                r.tile_own[:, 256:] = grad_down
        cols = lanes_at(start, GROUP)
        keep = pltpu.make_async_copy(r.tile, r.stage.at[:, :, cols], r.keep_sem.at[0])
        keep_own = pltpu.make_async_copy(r.tile_own, r.own_grad.at[:, cols], r.keep_sem.at[1])
        keep.start()
        keep_own.start()

        @pl.when(group + 3 < groups)
        def _():
            gather.pump(group + 3)

        keep.wait()
        keep_own.wait()

        @pl.when(group == 3)
        def _():
            for before in range(3):
                home.send(far_kinds, before)

        @pl.when(group >= 3)
        def _():
            home.send(far_kinds, group)

        return carry

    lax.fori_loop(0, groups, group_body, 0)
    h2_share.drain()

    for turn in range(4):
        r.part[:, cut(turn)] = r.dh2[:, cut(turn)].astype(low)
    back_sum.open()
    for step in range(place.last):
        back_sum.step(step)
        for turn in range(4):
            if turn % place.last == step:
                out = jnp.zeros((chip_rows, size), f32)
                for group in range(groups):
                    cols = slice(group * GROUP + 256, group * GROUP + 384)
                    out += lax.dot_general(
                        r.zd[:, cols], w[turn, :, cols], NT, preferred_element_type=f32
                    )
                r.mlp_part[:, cut(turn)] = out.astype(low)
        if step == 0:
            for group in range(4):
                home.send(straight_kinds, group)
    mlp_sum.open()
    back_sum.close(r.d_middle)
    d_norm, d_gain_two = norm_back(r.middle[...], gain_two, r.d_middle[...])
    r.d_middle[...] = r.dm[place.mine()].astype(f32) + d_norm
    r.da[place.mine()] = r.d_middle[...].astype(low)
    da_share.step(0)
    mlp_sum.step(0)

    gather.drain()
    for device in (place.over_x, place.over_y):
        pl.semaphore_signal(r.free_sem, inc=1, device_id=device, device_id_type=MESH)
    y_part, x_part = w.at[0, top_half], w.at[0, low_half]
    y_add, x_add = w.at[1, top_half], w.at[1, low_half]
    x_came, y_came = w.at[2, top_half], w.at[2, low_half]
    part_loads = [
        pltpu.make_async_copy(source, into, r.load_sem.at[2 + index])
        for index, (source, into) in enumerate(
            ((r.stage.at[0, top_half], y_part), (r.stage.at[1, low_half], x_part))
        )
    ]
    for load in part_loads:
        load.start()
    da_share.step(1)
    mlp_sum.step(1)
    for group in range(4, groups):
        home.send(straight_kinds, group)
    da_share.step(2)
    mlp_sum.step(2)
    da_share.step(3)
    mlp_sum.close(r.mlp)
    slot = place.ctx * place.rows + place.z * place.owned
    slot += lax.broadcasted_iota(jnp.int32, r.middle.shape, 0)
    r.layer_all[place.block(place.z)] = jnp.where(
        slot < length, r.middle[...] + r.mlp[...], 0.0
    ).astype(low)
    layer_share.step(0)
    da_share.arrive()
    back_sum.drain()
    mlp_sum.drain()
    do_t, d_t, kv_give = (
        r.mlp_part.at[pl.ds(0, count), pl.ds(at * chip_rows, chip_rows)]
        for at, count in enumerate((q_rows, qkv_rows, 2 * HEAD))
    )
    dk, dv = (
        [r.dh2.at[:, pl.ds(3 * 256 + 128 * at + 256 * which, HEAD)] for at in range(2)]
        for which in range(2)
    )

    d_out = jnp.zeros((q_rows, chip_rows), f32)
    for turn in range(4):
        d_out += lax.dot_general(
            aw[turn, qkv_rows:], r.da[:, cut(turn)], NT, preferred_element_type=f32
        )
    do_t[...] = d_out.astype(low)
    values = [r.kv[block, HEAD:].T for block in range(2)]
    keys = [r.kv[block, :HEAD].T for block in range(2)]
    scale = HEAD ** (-0.5)
    for ref in dk + dv:
        ref[...] = jnp.zeros(ref.shape, f32)

    def turned_back(tensor):
        ahead, behind = tensor[: HEAD // 2], tensor[HEAD // 2 :]
        return jnp.concatenate(
            [ahead * cos_at + behind * sin_at, behind * cos_at - ahead * sin_at], axis=0
        )

    for head in range(heads):
        queries, d_head = r.q_t[head_rows[head]], do_t[head_rows[head]]
        probs, d_probs = [], []
        inner = jnp.zeros((1, chip_rows), f32)
        for block in range(2):
            scores = masked(keys[block], queries, length, block, place.y)
            prob = jnp.exp(scores - r.lse[head : head + 1])
            d_prob = jnp.dot(values[block], d_head, preferred_element_type=f32)
            inner += jnp.sum(prob * d_prob, axis=0, keepdims=True)
            probs.append(prob)
            d_probs.append(d_prob)
        d_query = jnp.zeros((HEAD, chip_rows), f32)
        for block in range(2):
            d_scores = (probs[block] * (d_probs[block] - inner)).astype(low)
            dk[block][...] += (
                lax.dot_general(d_scores, queries, NT, preferred_element_type=f32) * scale
            )
            dv[block][...] += lax.dot_general(
                probs[block].astype(low), d_head, NT, preferred_element_type=f32
            )
            d_query += jnp.dot(r.kv[block, :HEAD], d_scores, preferred_element_type=f32) * scale
        d_t[head_rows[head]] = turned_back(d_query).astype(low)

    def of_half(pair, which):
        return jnp.where(which == 0, pair[0][...], pair[1][...]).T

    kv_give[:HEAD] = of_half(dk, 1 - place.y).astype(low)
    kv_give[HEAD:] = of_half(dv, 1 - place.y).astype(low)
    kv_back = remote(kv_give, r.kv_take, r.kv_sem, (1,), place.over_y)
    kv_back.start()
    d_key, d_value = of_half(dk, place.y), of_half(dv, place.y)

    pl.semaphore_wait(r.free_sem, 2)
    for load in part_loads:
        load.wait()
    add_loads = {}
    for kind, source, into in (("upper", r.upper, y_add), ("lower", r.lower, x_add)):
        add_loads[kind] = lambda group, kind=kind, source=source, into=into: (
            pltpu.make_async_copy(
                wide_cut(source, group),
                wide_cut(into, group),
                r.add_sem.at[far_kinds.index(kind), group],
            )
        )

    def fetch_far(group, carry):
        home.arrive(far_kinds, group)
        for kind in far_kinds:
            add_loads[kind](group).start()
        return carry

    def send_last(group, carry):
        cols = lanes_at(group * GROUP, GROUP)
        for kind, mine, add in (("upper", y_part, y_add), ("lower", x_part, x_add)):
            add_loads[kind](group).wait()
            mine[:, cols] = (mine[:, cols].astype(f32) + add[:, cols].astype(f32)).astype(low)
        home.send(last_kinds, group)
        return carry

    lax.fori_loop(0, groups, fetch_far, 0)
    lax.fori_loop(0, 1, send_last, 0)
    layer_share.step(1)
    kv_back.wait_recv()
    d_t[q_rows : q_rows + HEAD] = turned_back(d_key + r.kv_take[:HEAD].astype(f32)).astype(low)
    d_t[q_rows + HEAD :] = (d_value + r.kv_take[HEAD:].astype(f32)).astype(low)
    d_qkv = d_t[...].T
    for turn in range(4):
        r.part[:, cut(turn)] = jnp.dot(
            d_qkv, aw[turn, :qkv_rows], preferred_element_type=f32
        ).astype(low)

    input_sum.open()
    lax.fori_loop(1, 3, send_last, 0)
    input_sum.step(0)
    layer_share.step(2)

    def view(ref, at):
        return ref.at[pl.ds(0, attn_half), pl.ds(at * size, size)]

    stage = {
        (turn, half): view(r.h2, 2 * (turn - 1) + half) if turn < 3 else view(r.dm, half)
        for turn in (1, 2, 3)
        for half in range(2)
    }
    attn_own = [view(r.dh2, 2 + half) for half in range(2)]
    attn_home = Home(
        place,
        {
            "upper": stage[3, 0],
            "lower": stage[3, 1],
            "x_one": stage[2, 0],
            "y_two": stage[1, 1],
            "y_one": stage[1, 0],
            "x_two": stage[2, 1],
        },
        {
            "upper": view(r.zd, 0),
            "lower": view(r.zd, 1),
            "x_one": view(r.zd, 2),
            "y_two": view(r.zd, 3),
            "y_one": view(r.dm, 2),
            "x_two": view(r.dm, 3),
        },
        r.attn_home_sem,
        lambda ref, group: ref,
    )
    for turn in (3, 2, 1, 0):
        grad = jnp.concatenate(
            [
                jnp.dot(left, right[:, cut(turn)], preferred_element_type=f32)
                for left, right in ((d_t[...], r.h1), (r.o_t[...], r.da))
            ],
            axis=0,
        )
        for half in range(2):
            piece = grad[half * attn_half : (half + 1) * attn_half]
            if turn:
                stage[turn, half][...] = piece.astype(low)
            else:
                attn_own[half][...] = piece
        if turn == 3:
            attn_home.send(far_kinds, 0)
    lax.fori_loop(3, 5, send_last, 0)
    input_sum.step(1)
    layer_share.step(3)
    attn_home.send(straight_kinds, 0)
    lax.fori_loop(5, groups, send_last, 0)
    input_sum.step(2)
    input_sum.close(r.mlp)
    d_norm, d_gain_one = norm_back(r.inputs_own[...], r.gain_rows[0:1], r.mlp[...])
    r.grad_all[place.block(place.z)] = (r.d_middle[...] + d_norm).astype(low)
    grad_share.step(0)

    row = lax.broadcasted_iota(jnp.int32, r.gain_part.shape, 0)
    r.gain_part[...] = jnp.where(
        row == 0, d_gain_one[None], jnp.where(row == 1, d_gain_two[None], 0.0)
    )
    plane_gains = [
        remote(
            r.gain_part.at[:, pl.ds(turn * size, size)],
            r.gain_in.at[turn - 1],
            r.plane_gain_sem,
            (turn - 1,),
            place.plane[turn, 0],
        )
        for turn in (1, 2, 3)
    ]
    for copy in plane_gains:
        copy.start()

    slots = (
        (r.tile_own.at[top_half], r.tile_own.at[low_half]),
        (r.dh2.at[top_half, pl.ds(0, GROUP)], r.dh2.at[top_half, pl.ds(GROUP, GROUP)]),
    )

    def final_loads(group):
        cols = lanes_at(group * GROUP, GROUP)
        parity = group % 2
        yield pltpu.make_async_copy(
            r.own_grad.at[top_half, cols], slots[parity][0], r.final_sem.at[0, group]
        )
        yield pltpu.make_async_copy(
            r.own_grad.at[low_half, cols], slots[parity][1], r.final_sem.at[1, group]
        )
        yield pltpu.make_async_copy(
            r.x_one.at[:, cols], x_came.at[:, cols], r.final_sem.at[2, group]
        )
        yield pltpu.make_async_copy(
            r.y_two.at[:, cols], y_came.at[:, cols], r.final_sem.at[3, group]
        )

    def final_out(group):
        parity = group % 2
        to = lanes_at(core * ff + group * 128, 128)
        for kind, into in enumerate((r.grad_gate, r.grad_up, r.grad_down)):
            cols = pl.ds(kind * 128, 128)
            for half in range(2):
                source = slots[parity][half].at[:, cols]
                yield (
                    half,
                    pltpu.make_async_copy(source, into.at[:, to], r.out_here.at[kind, group]),
                    remote(source, into.at[:, to], r.out_there, (kind, group), place.sibling),
                )

    def final_start(group):
        home.arrive(straight_kinds, group)
        for load in final_loads(group):
            load.start()

    def final_sum(group):
        cols = lanes_at(group * GROUP, GROUP)
        upper, lower = slots[group % 2]
        home.arrive(last_kinds, group)
        for load in final_loads(group):
            load.wait()
        y_last, x_last = w.at[3, top_half, cols], w.at[3, low_half, cols]
        upper[...] += x_came[:, cols].astype(f32) + y_last[...].astype(f32)
        lower[...] += x_last[...].astype(f32) + y_came[:, cols].astype(f32)
        for half, here, there in final_out(group):

            @pl.when(core == half)
            def _(here=here):
                here.start()

            @pl.when(core != half)
            def _(there=there):
                there.start()

    def final_free(group):
        for half, here, there in final_out(group):

            @pl.when(core == half)
            def _(here=here):
                here.wait()

            @pl.when(core != half)
            def _(there=there):
                there.wait_send()

    def finish(group):
        final_sum(group)
        if group:
            final_free(group - 1)
        if group + 1 < groups:
            final_start(group + 1)

    final_start(0)
    grad_share.step(1)
    finish(0)
    finish(1)
    attn_home.arrive(far_kinds, 0)
    for turn, half, kind in ((1, 0, "upper"), (2, 1, "lower")):
        mine = stage[turn, half]
        mine[...] = (
            mine[...].astype(f32) + attn_home.targets[kind][...].astype(f32)
        ).astype(low)
    attn_home.send(last_kinds, 0)
    finish(2)
    grad_share.step(2)
    for copy in plane_gains:
        copy.wait_recv()
    r.gain_sum[...] = r.gain_part[:, :size] + r.gain_in[0] + r.gain_in[1] + r.gain_in[2]
    column_gains = [
        remote(r.gain_sum, r.gain_all.at[index], r.column_gain_sem, (index,), device)
        for index, device in enumerate(place.column)
    ]
    for copy in column_gains:
        copy.start()
    finish(3)
    finish(4)
    grad_share.step(3)
    for group in range(5, groups):
        finish(group)
    attn_home.arrive(straight_kinds + last_kinds, 0)
    attn_own[0][...] += attn_home.targets["x_one"][...].astype(f32) + attn_home.targets["y_one"][
        ...
    ].astype(f32)
    attn_own[1][...] += attn_home.targets["x_two"][...].astype(f32) + attn_home.targets["y_two"][
        ...
    ].astype(f32)
    attn_out = []
    for half in range(2):
        to = pl.ds(half * attn_half, attn_half)
        attn_out.append(
            pltpu.make_async_copy(attn_own[half], r.grad_attn.at[core, to], r.out_attn.at[half])
        )
        attn_out.append(
            remote(
                attn_own[half], r.grad_attn.at[core, to], r.swap_attn, (half,), place.sibling
            )
        )
    for copy in attn_out:
        copy.start()
    gain_total = r.gain_sum[...]
    for index, copy in enumerate(column_gains):
        copy.wait_recv()
        gain_total += r.gain_all[index]
    r.gain_out[...] = gain_total

    final_free(groups - 1)

    def settle(group, carry):
        for kind, source in enumerate(sources):
            wide_copies(group, kind, source)[1].wait_send()
            to = lanes_at(core * ff + group * 128, 128)
            into = (r.grad_gate, r.grad_up, r.grad_down)[kind]
            remote(
                r.tile_own.at[top_half, pl.ds(0, 128)],
                into.at[:, to],
                r.out_there,
                (kind, group),
                place.sibling,
            ).wait_recv()
        home.drain(group)
        return carry

    lax.fori_loop(0, groups, settle, 0)
    for copy in attn_out:
        copy.wait()
    attn_home.drain(0)
    for copy in (kv_copy, kv_back, h1_copy, *plane_gains, *column_gains):
        copy.wait_send()
    for turn, flip in place.plane:
        gain_copy(turn, flip).wait_send()
    for chain in (input_sum, da_share, layer_share, grad_share):
        chain.drain()
    qkv_gather.drain()
    out_gather.drain()


class Lists:
    def __init__(self):
        self.names, self.items = [], []

    def add(self, name, item):
        self.names.append(name)
        self.items.append(item)


def grouped_kernel(names, counts, *refs):
    given, at = [], 0
    for count in counts:
        given.append(refs[at] if count is None else refs[at : at + count])
        at += count or 1
    layer_kernel(names, *given)


def on_plane(
    hidden_in,
    cotangent,
    lengths,
    norm_attn,
    w_query,
    w_key,
    w_value,
    w_output,
    norm_mlp,
    w_gate,
    w_up,
    w_down,
):
    low, f32 = jnp.bfloat16, jnp.float32
    _, rows, width = hidden_in.shape
    part = w_query.shape[0]
    chip_part, chip_rows = 2 * part, 2 * rows
    place = 2 * lax.axis_index("dp") + lax.axis_index("ctx") // 2
    core = lax.axis_index("ctx") % 2
    z_count = lax.axis_size("mp")
    owned, hops = rows // z_count, z_count - 1
    q_rows = w_query.shape[1] // 2
    qkv_rows = q_rows + 2 * HEAD
    attn_rows = qkv_rows + q_rows
    ff = w_gate.shape[1] // 2
    wide_cols = 3 * ff
    groups = wide_cols // GROUP
    half_part = chip_part // 2
    others = 2 * z_count - 1

    slots = np.arange(2 * chip_rows, dtype=np.float32)
    freq = np.float32(THETA) ** -(np.arange(HEAD // 2, dtype=np.float32) * 2.0 / HEAD)
    angle = (freq.astype(np.float32)[:, None] * slots[None]).reshape(HEAD // 2, 2, chip_rows)
    angle = angle.astype(np.float32).swapaxes(0, 1)
    cosine, sine = (jnp.asarray(table(angle), f32) for table in (np.cos, np.sin))

    hbm = pl.BlockSpec(memory_space=pl.ANY)
    smem = pl.BlockSpec(memory_space=pltpu.SMEM)
    vmem = pl.BlockSpec(memory_space=pltpu.VMEM)
    dma, vm = pltpu.SemaphoreType.DMA, pltpu.VMEM
    whole, own = (chip_rows, width), (owned, width)

    ins, outs, scratch = Lists(), Lists(), Lists()
    for name, value, spec in (
        ("hidden", hidden_in[0], hbm),
        ("cotangent", cotangent[0], hbm),
        ("length", lengths.reshape(1, 1), smem),
        ("norm_one", norm_attn.reshape(1, part), vmem),
        ("norm_two", norm_mlp.reshape(1, part), vmem),
        ("query", w_query, vmem),
        ("key_t", w_key.T, vmem),
        ("value_t", w_value.T, vmem),
        ("output_t", w_output.T, vmem),
        ("gate", w_gate, hbm),
        ("up", w_up, hbm),
        ("down_t", w_down.T, hbm),
        ("cos", cosine, vmem),
        ("sin", sine, vmem),
    ):
        ins.add(name, (value, spec))
    for name, shape, dtype, spec in (
        ("layer_all", (rows, width), low, vmem),
        ("grad_all", (rows, width), low, vmem),
        ("gain_out", (8, chip_part), f32, vmem),
        ("grad_gate", w_gate.shape, f32, hbm),
        ("grad_up", w_up.shape, f32, hbm),
        ("grad_down", w_gate.shape, f32, hbm),
        ("grad_attn", (2, attn_rows, chip_part), f32, hbm),
        ("own_grad", (chip_part, wide_cols), f32, hbm),
        ("stage", (3, chip_part, wide_cols), low, hbm),
        ("upper", (half_part, wide_cols), low, hbm),
        ("lower", (half_part, wide_cols), low, hbm),
        ("x_one", (half_part, wide_cols), low, hbm),
        ("y_two", (half_part, wide_cols), low, hbm),
    ):
        outs.add(name, (jax.ShapeDtypeStruct(shape, dtype), spec))
    chain = [vm((rows, width), low), vm((hops, *own), low), vm((hops, *own), low)]
    ways = [dma((2, hops, SPLIT))] * 2
    cores = dma((2, z_count))
    for name, item in (
        ("w", vm((4, chip_part, wide_cols), low)),
        ("aw", vm((4, attn_rows, chip_part), low)),
        ("h1", vm(whole, low)),
        ("h2", vm(whole, low)),
        ("dm", vm(whole, low)),
        ("da", vm(whole, low)),
        ("part", vm(whole, low)),
        ("mlp_part", vm(whole, low)),
        ("dh2", vm(whole, f32)),
        ("zd", vm((chip_rows, wide_cols), low)),
        ("tile", vm((3, chip_part, GROUP), low)),
        ("tile_own", vm((chip_part, GROUP), f32)),
        ("chain_one", chain),
        ("chain_two", chain),
        ("inputs_own", vm(own, f32)),
        ("middle", vm(own, f32)),
        ("mlp", vm(own, f32)),
        ("d_middle", vm(own, f32)),
        ("gains", vm((8, chip_part), f32)),
        ("gains_all", vm((8, 8, chip_part), f32)),
        ("gain_rows", vm((8, width), f32)),
        ("kv", vm((2, 2 * HEAD, chip_rows), low)),
        ("q_t", vm((q_rows, chip_rows), low)),
        ("o_t", vm((q_rows, chip_rows), low)),
        ("lse", vm((8, chip_rows), f32)),
        ("kv_take", vm((2 * HEAD, chip_rows), low)),
        ("gain_part", vm((8, width), f32)),
        ("gain_in", vm((3, 8, chip_part), f32)),
        ("gain_sum", vm((8, chip_part), f32)),
        ("gain_all", vm((others, 8, chip_part), f32)),
        ("load_sem", dma((4,))),
        ("core_sem", dma((2, 2))),
        ("gain_sem", dma((2, 8))),
        ("attn_x", dma((2, 4))),
        ("attn_y", dma((2, 4))),
        ("attn_far", dma((2, 4))),
        ("wide_here", dma((3, groups))),
        ("wide_there", dma((2, 3, groups))),
        ("dm_sem", dma((2, 1))),
        ("h1_sem", dma((2, 1))),
        ("kv_sem", dma((2, 2))),
        ("wide_x", dma((2, groups))),
        ("wide_y", dma((2, groups))),
        ("wide_far", dma((2, 2, groups))),
        ("keep_sem", dma((2,))),
        ("home_sem", dma((2, 6, groups))),
        ("add_sem", dma((2, groups))),
        ("attn_home_sem", dma((2, 6, 1))),
        ("final_sem", dma((4, groups))),
        ("out_here", dma((3, groups))),
        ("out_there", dma((2, 3, groups))),
        ("out_attn", dma((2,))),
        ("swap_attn", dma((2, 2))),
        ("plane_gain_sem", dma((2, 3))),
        ("column_gain_sem", dma((2, others))),
        ("free_sem", pltpu.SemaphoreType.REGULAR),
        ("branch_sems", [cores] + ways),
        ("back_sems", [cores] + ways),
        ("mlp_sems", [cores] + ways),
        ("input_sems", [cores] + ways),
        ("h2_sems", ways + [cores]),
        ("da_sems", ways + [cores]),
        ("layer_sems", ways),
        ("grad_sems", ways),
    ):
        scratch.add(name, item)

    counts = [None] * (len(ins.items) + len(outs.items))
    flat = []
    for item in scratch.items:
        counts.append(len(item) if isinstance(item, list) else None)
        flat += item if isinstance(item, list) else [item]
    names = ins.names + outs.names + scratch.names
    results = pl.pallas_call(
        functools.partial(grouped_kernel, names, counts),
        out_shape=[shape for shape, _ in outs.items],
        in_specs=[spec for _, spec in ins.items],
        out_specs=[spec for _, spec in outs.items],
        scratch_shapes=flat,
        name="layer",
        compiler_params=pltpu.CompilerParams(
            collective_id=1, has_side_effects=True, vmem_limit_bytes=65_400 * 2**10
        ),
    )(*(value for value, _ in ins.items))
    layer_all, grad_all, gain_sums, grad_gate, grad_up, grad_down, grad_attn = results[:7]
    gain_mine = lax.dynamic_slice_in_dim(gain_sums, core * part, part, axis=1)

    def absolute(tensor):
        return jnp.concatenate(
            [
                lax.dynamic_slice_in_dim(tensor, (place ^ turn) * chip_part, chip_part, axis=-1)
                for turn in range(4)
            ],
            axis=-1,
        )

    attn_mine = lax.dynamic_slice_in_dim(grad_attn, core * part, part, axis=2)

    def joined(start, size):
        return attn_mine[:, start : start + size].reshape(2 * size, part)

    return (
        absolute(layer_all)[None],
        absolute(grad_all)[None],
        gain_mine[0],
        joined(0, q_rows).T,
        joined(q_rows, HEAD).T,
        joined(q_rows + HEAD, HEAD).T,
        joined(qkv_rows, q_rows),
        gain_mine[1],
        grad_gate,
        grad_up,
        grad_down.T,
    )


def solution(mesh):
    plane = dict(mesh.shape) == {"dp": 2, "ctx": 4, "mp": 4}
    return jax.shard_map(
        on_plane if plane else any_mesh,
        mesh=mesh,
        in_specs=(
            P("dp", "ctx", None),
            P("dp", "ctx", None),
            P("dp"),
            P(("dp", "ctx")),
            P(("dp", "ctx"), "mp"),
            P(("dp", "ctx"), "mp"),
            P(("dp", "ctx"), "mp"),
            P("mp", ("dp", "ctx")),
            P(("dp", "ctx")),
            P(("dp", "ctx"), "mp"),
            P(("dp", "ctx"), "mp"),
            P("mp", ("dp", "ctx")),
        ),
        out_specs=(
            P("dp", "ctx", None),
            P("dp", "ctx", None),
            P(("dp", "ctx")),
            P(("dp", "ctx"), "mp"),
            P(("dp", "ctx"), "mp"),
            P(("dp", "ctx"), "mp"),
            P("mp", ("dp", "ctx")),
            P(("dp", "ctx")),
            P(("dp", "ctx"), "mp"),
            P(("dp", "ctx"), "mp"),
            P("mp", ("dp", "ctx")),
        ),
        check_vma=False,
    )
```

```python
import functools

import jax
import jax.numpy as jnp
import numpy as np
from jax import lax
from jax.experimental import pallas as pl
from jax.experimental.pallas import tpu as pltpu
from jax.sharding import PartitionSpec as P

HEAD = 80


EPS = 1e-05
THETA = 1000000.0
NEG = -1e30


def rope_tables(places, head_size):
    half = head_size // 2
    freq = THETA ** (-(jnp.arange(half, dtype=jnp.float32) * 2.0 / head_size))
    angle = places[:, None] * freq[None, :]
    return (jnp.cos(angle), jnp.sin(angle))


def rotate(tensor, cosine, sine_table):
    half = tensor.shape[-1] // 2
    first_half = tensor[..., :half]
    second_half = tensor[..., half:]
    cos_b = cosine[:, None, :]
    sin_b = sine_table[:, None, :]
    return jnp.concatenate(
        [first_half * cos_b - second_half * sin_b, second_half * cos_b + first_half * sin_b],
        axis=-1,
    )


def rotate_back(tensor, cosine, sine_table):
    half = tensor.shape[-1] // 2
    first_half = tensor[..., :half]
    second_half = tensor[..., half:]
    cos_b = cosine[:, None, :]
    sin_b = sine_table[:, None, :]
    return jnp.concatenate(
        [first_half * cos_b + second_half * sin_b, second_half * cos_b - first_half * sin_b],
        axis=-1,
    )


def normed(tensor, gain_row):
    return tensor * lax.rsqrt(jnp.mean(tensor * tensor, axis=-1, keepdims=True) + EPS) * gain_row


def norm_back(tensor, gain_row, grad_normed):
    scale_row = lax.rsqrt(jnp.mean(tensor * tensor, axis=-1, keepdims=True) + EPS)
    grad_scaled = grad_normed * gain_row
    grad_tensor = scale_row * grad_scaled - tensor * scale_row**3 * jnp.mean(
        grad_scaled * tensor, axis=-1, keepdims=True
    )
    grad_gain = jnp.sum(grad_normed * tensor * scale_row, axis=0)
    return (grad_tensor, grad_gain)


def masked_scores(query_seq, key_seq, length, places, kv_heads, group_size):
    query_grp = query_seq.reshape(query_seq.shape[0], kv_heads, group_size, HEAD)
    key_grp = key_seq.reshape(key_seq.shape[0], kv_heads, HEAD)
    raw_scores = jnp.einsum(
        "bkgh,tkh->kgbt", query_grp, key_grp, preferred_element_type=jnp.float32
    ) * HEAD ** (-0.5)
    key_places = jnp.arange(key_grp.shape[0], dtype=jnp.int32)
    allowed = (key_places[None, :] <= places[:, None]) & (key_places[None, :] < length)
    return jnp.where(allowed[None, None], raw_scores, NEG)


def any_mesh(
    hidden_in,
    cotangent,
    lengths,
    norm_attn,
    w_query,
    w_key,
    w_value,
    w_output,
    norm_mlp,
    w_gate,
    w_up,
    w_down,
):
    seq_count, slot_count, width_all = hidden_in.shape
    tok_rows = seq_count * slot_count
    attn_set = (
        lax.all_gather(w_query, ("dp", "ctx"), axis=0, tiled=True),
        lax.all_gather(w_key, ("dp", "ctx"), axis=0, tiled=True),
        lax.all_gather(w_value, ("dp", "ctx"), axis=0, tiled=True),
        lax.all_gather(w_output, ("dp", "ctx"), axis=1, tiled=True),
        lax.all_gather(norm_attn, ("dp", "ctx"), axis=0, tiled=True),
    )
    query_w, key_w, value_w, output_w, gain_attn = attn_set
    q_heads = query_w.shape[1] // HEAD
    kv_heads = key_w.shape[1] // HEAD
    group_size = q_heads // kv_heads
    first_slot = lax.axis_index("ctx") * slot_count
    places = first_slot + jnp.arange(slot_count, dtype=jnp.int32)
    valid_mask = (places[None, :] < lengths[:, None]).astype(jnp.float32).reshape(tok_rows, 1)
    cosine, sine_table = rope_tables(places.astype(jnp.float32), HEAD)
    inputs = hidden_in.reshape(tok_rows, width_all).astype(jnp.float32)
    gain_one = gain_attn.astype(jnp.float32)
    normed_one = normed(inputs, gain_one).astype(jnp.bfloat16)
    query_proj = jnp.dot(normed_one, query_w, preferred_element_type=jnp.float32).reshape(
        seq_count, slot_count, q_heads, HEAD
    )
    key_proj = jnp.dot(normed_one, key_w, preferred_element_type=jnp.float32).reshape(
        seq_count, slot_count, kv_heads, HEAD
    )
    value_low = (
        jnp.dot(normed_one, value_w, preferred_element_type=jnp.float32)
        .astype(jnp.bfloat16)
        .reshape(seq_count, slot_count, kv_heads * HEAD)
    )
    query_low = rotate(query_proj, cosine, sine_table).astype(jnp.bfloat16)
    key_low = (
        rotate(key_proj, cosine, sine_table)
        .astype(jnp.bfloat16)
        .reshape(seq_count, slot_count, kv_heads * HEAD)
    )
    key_all, value_all = (
        lax.all_gather(key_low, "ctx", axis=1, tiled=True),
        lax.all_gather(value_low, "ctx", axis=1, tiled=True),
    )

    def attend(members):
        query_seq, key_seq, value_seq, length = members
        scores = masked_scores(query_seq, key_seq, length, places, kv_heads, group_size)
        row_max = jnp.max(scores, axis=-1, keepdims=True)
        exponent = jnp.exp(scores - row_max)
        total = jnp.sum(exponent, axis=-1, keepdims=True)
        attention = (exponent / total).astype(jnp.bfloat16)
        value_grp = value_seq.reshape(value_seq.shape[0], kv_heads, HEAD)
        mixed_heads = jnp.einsum(
            "kgbt,tkh->bkgh", attention, value_grp, preferred_element_type=jnp.float32
        )
        return (mixed_heads.reshape(slot_count, q_heads * HEAD), (row_max + jnp.log(total))[..., 0])

    mixed_all, log_total = lax.map(attend, (query_low, key_all, value_all, lengths))
    attn_low = mixed_all.reshape(tok_rows, q_heads * HEAD).astype(jnp.bfloat16)
    branch = lax.psum(jnp.dot(attn_low, output_w, preferred_element_type=jnp.float32), "mp")
    middle = inputs + branch
    mlp_set = (
        lax.all_gather(w_gate, ("dp", "ctx"), axis=0, tiled=True),
        lax.all_gather(w_up, ("dp", "ctx"), axis=0, tiled=True),
        lax.all_gather(w_down, ("dp", "ctx"), axis=1, tiled=True),
        lax.all_gather(norm_mlp, ("dp", "ctx"), axis=0, tiled=True),
    )
    gate_w, up_w, down_w, gain_mlp = mlp_set
    gain_two = gain_mlp.astype(jnp.float32)
    normed_two = normed(middle, gain_two).astype(jnp.bfloat16)
    gate_proj = jnp.dot(normed_two, gate_w, preferred_element_type=jnp.float32)
    up_proj = jnp.dot(normed_two, up_w, preferred_element_type=jnp.float32)
    hidden = (jax.nn.silu(gate_proj) * up_proj).astype(jnp.bfloat16)
    mlp_out = lax.psum(
        jnp.dot(hidden, down_w, preferred_element_type=jnp.float32).astype(jnp.bfloat16), "mp"
    ).astype(jnp.float32)
    layer_out = (
        (valid_mask * (middle + mlp_out))
        .astype(jnp.bfloat16)
        .reshape(seq_count, slot_count, width_all)
    )
    grad_out = valid_mask * cotangent.reshape(tok_rows, width_all).astype(jnp.float32)
    grad_mlp = grad_out.astype(jnp.bfloat16)
    gate_back, up_back, down_back, gain_mlp_back = (
        lax.all_gather(w_gate, ("dp", "ctx"), axis=0, tiled=True),
        lax.all_gather(w_up, ("dp", "ctx"), axis=0, tiled=True),
        lax.all_gather(w_down, ("dp", "ctx"), axis=1, tiled=True),
        lax.all_gather(norm_mlp, ("dp", "ctx"), axis=0, tiled=True),
    )
    grad_hidden = jnp.einsum("tm,fm->tf", grad_mlp, down_back, preferred_element_type=jnp.float32)
    grad_down = jnp.einsum("tf,tm->fm", hidden, grad_mlp, preferred_element_type=jnp.float32)
    sigmoid_gate = jax.nn.sigmoid(gate_proj)
    grad_gate_low = (
        grad_hidden * up_proj * sigmoid_gate * (1.0 + gate_proj * (1.0 - sigmoid_gate))
    ).astype(jnp.bfloat16)
    grad_up_low = (grad_hidden * gate_proj * sigmoid_gate).astype(jnp.bfloat16)
    grad_gate = jnp.einsum(
        "td,tf->df", normed_two, grad_gate_low, preferred_element_type=jnp.float32
    )
    grad_up = jnp.einsum("td,tf->df", normed_two, grad_up_low, preferred_element_type=jnp.float32)
    partial_two = jnp.einsum(
        "tf,df->td", grad_gate_low, gate_back, preferred_element_type=jnp.float32
    ) + jnp.einsum("tf,df->td", grad_up_low, up_back, preferred_element_type=jnp.float32)
    grad_normed_two = lax.psum(partial_two, "mp")
    grad_middle_norm, grad_gain_two = norm_back(
        middle, gain_mlp_back.astype(jnp.float32), grad_normed_two
    )
    mlp_grads = (
        lax.psum_scatter(grad_gate, ("dp", "ctx"), scatter_dimension=0, tiled=True),
        lax.psum_scatter(grad_up, ("dp", "ctx"), scatter_dimension=0, tiled=True),
        lax.psum_scatter(grad_down, ("dp", "ctx"), scatter_dimension=1, tiled=True),
        lax.psum_scatter(grad_gain_two, ("dp", "ctx"), scatter_dimension=0, tiled=True),
    )
    grad_middle = grad_out + grad_middle_norm
    grad_branch = grad_middle.astype(jnp.bfloat16)
    query_back, key_back, value_back, output_back, gain_attn_back = (
        lax.all_gather(w_query, ("dp", "ctx"), axis=0, tiled=True),
        lax.all_gather(w_key, ("dp", "ctx"), axis=0, tiled=True),
        lax.all_gather(w_value, ("dp", "ctx"), axis=0, tiled=True),
        lax.all_gather(w_output, ("dp", "ctx"), axis=1, tiled=True),
        lax.all_gather(norm_attn, ("dp", "ctx"), axis=0, tiled=True),
    )
    grad_output = jnp.einsum("tq,td->qd", attn_low, grad_branch, preferred_element_type=jnp.float32)
    grad_attn_low = (
        jnp.einsum("td,qd->tq", grad_branch, output_back, preferred_element_type=jnp.float32)
        .astype(jnp.bfloat16)
        .reshape(seq_count, slot_count, q_heads, HEAD)
    )

    def attend_back(members):
        query_seq, key_seq, value_seq, length, log_seq, grad_seq = members
        scores = masked_scores(query_seq, key_seq, length, places, kv_heads, group_size)
        attention = jnp.exp(scores - log_seq[..., None])
        query_grp = query_seq.reshape(slot_count, kv_heads, group_size, HEAD)
        key_grp = key_seq.reshape(key_seq.shape[0], kv_heads, HEAD)
        value_grp = value_seq.reshape(value_seq.shape[0], kv_heads, HEAD)
        grad_grp = grad_seq.reshape(slot_count, kv_heads, group_size, HEAD)
        grad_attention = jnp.einsum(
            "bkgh,tkh->kgbt", grad_grp, value_grp, preferred_element_type=jnp.float32
        )
        inner = jnp.sum(attention * grad_attention, axis=-1, keepdims=True)
        grad_scores = (attention * (grad_attention - inner)).astype(jnp.bfloat16)
        scale_qk = HEAD ** (-0.5)
        grad_query_seq = (
            jnp.einsum("kgbt,tkh->bkgh", grad_scores, key_grp, preferred_element_type=jnp.float32)
            * scale_qk
        )
        grad_key_seq = (
            jnp.einsum("kgbt,bkgh->tkh", grad_scores, query_grp, preferred_element_type=jnp.float32)
            * scale_qk
        )
        grad_value_seq = jnp.einsum(
            "kgbt,bkgh->tkh",
            attention.astype(jnp.bfloat16),
            grad_grp,
            preferred_element_type=jnp.float32,
        )
        key_rows = key_grp.shape[0]
        return (
            grad_query_seq.reshape(slot_count, q_heads, HEAD),
            grad_key_seq.reshape(key_rows, kv_heads * HEAD),
            grad_value_seq.reshape(key_rows, kv_heads * HEAD),
        )

    grad_query_rot, grad_key_all, grad_value_all = lax.map(
        attend_back, (query_low, key_all, value_all, lengths, log_total, grad_attn_low)
    )
    grad_key_rot, grad_value_rot = (
        lax.psum_scatter(grad_key_all, "ctx", scatter_dimension=1, tiled=True),
        lax.psum_scatter(grad_value_all, "ctx", scatter_dimension=1, tiled=True),
    )
    grad_query_low = (
        rotate_back(grad_query_rot, cosine, sine_table)
        .astype(jnp.bfloat16)
        .reshape(tok_rows, q_heads * HEAD)
    )
    grad_key_low = (
        rotate_back(grad_key_rot.reshape(seq_count, slot_count, kv_heads, HEAD), cosine, sine_table)
        .astype(jnp.bfloat16)
        .reshape(tok_rows, kv_heads * HEAD)
    )
    grad_value_low = grad_value_rot.astype(jnp.bfloat16).reshape(tok_rows, kv_heads * HEAD)
    grad_query = jnp.einsum(
        "td,tq->dq", normed_one, grad_query_low, preferred_element_type=jnp.float32
    )
    grad_key = jnp.einsum("td,tq->dq", normed_one, grad_key_low, preferred_element_type=jnp.float32)
    grad_value = jnp.einsum(
        "td,tq->dq", normed_one, grad_value_low, preferred_element_type=jnp.float32
    )
    partial_one = jnp.einsum(
        "tq,dq->td", grad_query_low, query_back, preferred_element_type=jnp.float32
    )
    partial_one = partial_one + jnp.einsum(
        "tq,dq->td", grad_key_low, key_back, preferred_element_type=jnp.float32
    )
    partial_one = partial_one + jnp.einsum(
        "tq,dq->td", grad_value_low, value_back, preferred_element_type=jnp.float32
    )
    grad_normed_one = lax.psum(partial_one, "mp")
    grad_inputs_norm, grad_gain_one = norm_back(
        inputs, gain_attn_back.astype(jnp.float32), grad_normed_one
    )
    input_grad = (
        (grad_middle + grad_inputs_norm)
        .astype(jnp.bfloat16)
        .reshape(seq_count, slot_count, width_all)
    )
    attn_grads = (
        lax.psum_scatter(grad_query, ("dp", "ctx"), scatter_dimension=0, tiled=True),
        lax.psum_scatter(grad_key, ("dp", "ctx"), scatter_dimension=0, tiled=True),
        lax.psum_scatter(grad_value, ("dp", "ctx"), scatter_dimension=0, tiled=True),
        lax.psum_scatter(grad_output, ("dp", "ctx"), scatter_dimension=1, tiled=True),
        lax.psum_scatter(grad_gain_one, ("dp", "ctx"), scatter_dimension=0, tiled=True),
    )
    return (
        layer_out,
        input_grad,
        attn_grads[4],
        attn_grads[0],
        attn_grads[1],
        attn_grads[2],
        attn_grads[3],
        mlp_grads[3],
        mlp_grads[0],
        mlp_grads[1],
        mlp_grads[2],
    )


SPLIT = 4
GROUP = 384
NT = (((1,), (1,)), ((), ()))
TN = (((0,), (0,)), ((), ()))
MESH = pl.DeviceIdType.MESH


def remote(src, dst, sems, index, device):
    return pltpu.make_async_remote_copy(
        src_ref=src,
        dst_ref=dst,
        send_sem=sems.at[(0, *index)],
        recv_sem=sems.at[(1, *index)],
        device_id=device,
        device_id_type=MESH,
    )


def rows_at(start, size):
    return pl.ds(pl.multiple_of(start, 16), size)


def lanes_at(start, size):
    return pl.ds(pl.multiple_of(start, 128), size)


def chosen(rows, columns, first_column):
    row = lax.broadcasted_iota(jnp.int32, (rows, columns), 0)
    column = lax.broadcasted_iota(jnp.int32, (rows, columns), 1)
    return (row == column - first_column).astype(jnp.bfloat16)


def masked(keys, queries, length, block, y_at):
    scores = jnp.dot(keys, queries, preferred_element_type=jnp.float32) * HEAD ** (-0.5)
    rows, columns = scores.shape
    key_slots = block * rows + lax.broadcasted_iota(jnp.int32, scores.shape, 0)
    query_slots = y_at * columns + lax.broadcasted_iota(jnp.int32, scores.shape, 1)
    return jnp.where((key_slots <= query_slots) & (key_slots < length), scores, NEG)


class Place:
    def __init__(self, owned, width):
        self.x, self.ctx, self.z = (lax.axis_index(name) for name in ("dp", "ctx", "mp"))
        self.core = lax.rem(self.ctx, 2)
        self.y = (self.ctx - self.core) // 2
        self.last = lax.axis_size("mp") - 1
        self.owned, self.rows, self.width = owned, owned * (self.last + 1), width
        self.step = width // SPLIT
        self.size, self.middle = width // 4, width // 8
        self.above, self.below = (self.x, self.ctx, self.z + 1), (self.x, self.ctx, self.z - 1)
        self.plane = {
            (turn, flip): self.turned(turn, flip)
            for turn in range(4)
            for flip in range(2)
            if turn or flip
        }
        self.sibling, self.over_x, self.over_y = (
            self.plane[key] for key in ((0, 1), (2, 0), (1, 0))
        )
        self.diagonal = self.plane[3, 0]
        self.column = [
            (self.x, self.other_core(flip), lax.rem(self.z + turn, self.last + 1))
            for turn in range(self.last + 1)
            for flip in range(2)
            if turn or flip
        ]

    def other_core(self, flip):
        return self.ctx + 1 - 2 * self.core if flip else self.ctx

    def turned(self, turn, flip):
        x_to = 1 - self.x if turn >= 2 else self.x
        y_to = 1 - self.y if turn % 2 else self.y
        core_to = 1 - self.core if flip else self.core
        return (x_to, 2 * y_to + core_to, self.z)

    def enter(self):
        barrier = pltpu.get_barrier_semaphore()
        peers = list(self.plane.values()) + self.column[1:]
        for device in peers:
            pl.semaphore_signal(barrier, inc=1, device_id=device, device_id_type=MESH)
        pl.semaphore_wait(barrier, len(peers))

    def block_of(self, core, block):
        return rows_at(core * self.rows + block * self.owned, self.owned)

    def block(self, at):
        return rows_at(at * self.owned, self.owned)

    def mine(self):
        return self.block_of(self.core, self.z)

    def columns(self, piece):
        return pl.ds(piece * self.step, self.step)

    def cut(self, turn):
        return slice(turn * self.size, (turn + 1) * self.size)

    def source(self, turn):
        x_to = 1 - self.x if turn >= 2 else self.x
        y_to = 1 - self.y if turn % 2 else self.y
        return lanes_at((2 * x_to + y_to) * self.size, self.size)


class SumChain:
    def __init__(self, place, part, held, up_in, down_in, core_sem, up_sem, down_sem):
        self.place, self.part, self.held = place, part, held
        self.ways = ((place.above, up_in, up_sem, 1), (place.below, down_in, down_sem, -1))
        self.core_sem = core_sem

    def across(self, block):
        place = self.place
        return remote(
            self.part.at[place.block_of(1 - place.core, block)],
            self.held.at[place.block(block)],
            self.core_sem,
            (block,),
            place.sibling,
        )

    def open(self):
        for block in range(self.place.last + 1):
            self.across(block).start()

    def own(self, at, cols):
        place = self.place
        mine = self.part[place.block_of(place.core, at), cols].astype(jnp.float32)
        return mine + self.held[place.block(at), cols].astype(jnp.float32)

    def hop(self, way, step, piece, at):
        place = self.place
        cols = place.columns(piece)
        return remote(
            self.part.at[place.block_of(place.core, at), cols],
            way[1].at[step, :, cols],
            way[2],
            (step, piece),
            way[0],
        )

    def far(self, way):
        return self.place.z if way[3] == 1 else self.place.last - self.place.z

    def target(self, way, step):
        return self.place.z + way[3] * (self.place.last - step)

    def step(self, step):
        place = self.place
        for way in self.ways:

            @pl.when(self.far(way) <= step)
            def _(way=way):
                at = self.target(way, step)
                rows = place.block_of(place.core, at)
                self.across(at).wait_recv()
                for piece in range(SPLIT):
                    cols = place.columns(piece)
                    total = self.own(at, cols)
                    if step:

                        @pl.when(self.far(way) > 0)
                        def _(total=total, cols=cols, piece=piece):
                            self.hop(way, step - 1, piece, at).wait_recv()
                            got = way[1][step - 1, :, cols].astype(jnp.float32)
                            self.part[rows, cols] = (total + got).astype(self.part.dtype)

                        @pl.when(self.far(way) == 0)
                        def _(total=total, cols=cols):
                            self.part[rows, cols] = total.astype(self.part.dtype)

                    else:
                        self.part[rows, cols] = total.astype(self.part.dtype)
                    self.hop(way, step, piece, at).start()

    def close(self, result):
        place = self.place
        final = place.last - 1
        self.across(place.z).wait_recv()
        result[...] = self.own(place.z, slice(None))
        for way in self.ways:

            @pl.when(self.far(way) > 0)
            def _(way=way):
                for piece in range(SPLIT):
                    self.hop(way, final, piece, place.z).wait_recv()
                result[...] += way[1][final].astype(jnp.float32)

    def drain(self):
        place = self.place
        for block in range(place.last + 1):
            self.across(block).wait_send()
        for step in range(place.last):
            for way in self.ways:

                @pl.when(self.far(way) <= step)
                def _(way=way, step=step):
                    for piece in range(SPLIT):
                        self.hop(way, step, piece, self.target(way, step)).wait_send()


class ShareChain:
    def __init__(self, place, whole, up_sem, down_sem, core_sem=None):
        self.place, self.whole, self.core_sem = place, whole, core_sem
        self.ways = ((place.above, up_sem, 1), (place.below, down_sem, -1))

    def rows(self, at):
        place = self.place
        return place.block(at) if self.core_sem is None else place.block_of(place.core, at)

    def far(self, way):
        return self.place.z if way[2] == 1 else self.place.last - self.place.z

    def hop(self, way, step, piece, origin):
        ref = self.whole.at[self.rows(origin), self.place.columns(piece)]
        return remote(ref, ref, way[1], (step, piece), way[0])

    def across(self, origin, core):
        ref = self.whole.at[self.place.block_of(core, origin)]
        return remote(ref, ref, self.core_sem, (origin,), self.place.sibling)

    def step(self, step):
        place = self.place
        for way in self.ways:
            origin = place.z - way[2] * step

            @pl.when(self.far(way) >= step)
            def _(way=way, origin=origin):
                for piece in range(SPLIT):
                    if step:
                        self.hop(way, step - 1, piece, origin).wait_recv()
                    if step < place.last:

                        @pl.when(self.far(way) < place.last)
                        def _(piece=piece):
                            self.hop(way, step, piece, origin).start()

                if step and self.core_sem is not None:
                    self.across(origin, place.core).start()

        if step == 0 and self.core_sem is not None:
            self.across(place.z, place.core).start()

    def arrive(self):
        if self.core_sem is not None:
            for origin in range(self.place.last + 1):
                self.across(origin, 1 - self.place.core).wait_recv()

    def drain(self):
        place = self.place
        for step in range(place.last):
            for way in self.ways:

                @pl.when((self.far(way) >= step) & (self.far(way) < place.last))
                def _(way=way, step=step):
                    for piece in range(SPLIT):
                        self.hop(way, step, piece, place.z - way[2] * step).wait_send()

        if self.core_sem is not None:
            for origin in range(place.last + 1):
                self.across(origin, place.core).wait_send()


class AttnGather:
    def __init__(self, place, w, first, rows, x_sem, y_sem, far_sem, index):
        self.place, self.w, self.index = place, w, index
        self.sems = (x_sem, y_sem, far_sem)
        self.halves = tuple(pl.ds(first + half * rows // 2, rows // 2) for half in range(2))

    def cross(self, half, to_x):
        place, rows = self.place, self.halves[half]
        return remote(
            self.w.at[0, rows],
            self.w.at[2 if to_x else 1, rows],
            self.sems[0] if to_x else self.sems[1],
            (self.index + half,),
            place.over_x if to_x else place.over_y,
        )

    def relay(self, to_x):
        place, half = self.place, 1 if to_x else 0
        rows = self.halves[half]
        return remote(
            self.w.at[1 if to_x else 2, rows],
            self.w.at[3, rows],
            self.sems[2],
            (self.index + half,),
            place.over_x if to_x else place.over_y,
        )

    def send(self, which):
        self.cross(which, True).start()
        self.cross(1 - which, False).start()

    def pass_on(self):
        self.cross(0, True).wait_recv()
        self.relay(False).start()
        self.cross(1, False).wait_recv()
        self.relay(True).start()

    def drain(self):
        for half in range(2):
            for to_x in (True, False):
                self.cross(half, to_x).wait_send()
        self.relay(True).wait_send()
        self.relay(False).wait_send()


class WideGather:
    def __init__(self, place, w, x_sem, y_sem, far_sem):
        self.place, self.w = place, w
        self.x_sem, self.y_sem, self.far_sem = x_sem, y_sem, far_sem
        self.groups = w.shape[2] // GROUP

    def columns(self, group):
        return lanes_at(group * GROUP, GROUP)

    def cross(self, group, to_x):
        place, cols = self.place, self.columns(group)
        return remote(
            self.w.at[0, :, cols],
            self.w.at[2 if to_x else 1, :, cols],
            self.x_sem if to_x else self.y_sem,
            (group,),
            place.over_x if to_x else place.over_y,
        )

    def relay(self, group, to_x):
        place, cols = self.place, self.columns(group)
        rows = pl.ds(place.middle, place.middle) if to_x else pl.ds(0, place.middle)
        return remote(
            self.w.at[1 if to_x else 2, rows, cols],
            self.w.at[3, rows, cols],
            self.far_sem,
            (1 if to_x else 0, group),
            place.over_x if to_x else place.over_y,
        )

    def send(self, group):
        self.cross(group, True).start()
        self.cross(group, False).start()

    def pump(self, group):
        self.cross(group, True).wait_recv()
        self.relay(group, False).start()
        self.cross(group, False).wait_recv()
        self.relay(group, True).start()

        @pl.when(group + 2 < self.groups)
        def _():
            self.send(group + 2)

    def arrive(self, group):
        self.relay(group, False).wait_recv()
        self.relay(group, True).wait_recv()

    def drain(self):
        def body(group, carry):
            for to_x in (True, False):
                self.cross(group, to_x).wait_send()
                self.relay(group, to_x).wait_send()
            return carry

        lax.fori_loop(0, self.groups, body, 0)


class Home:
    kinds = ("upper", "lower", "x_one", "y_two", "y_one", "x_two")

    def __init__(self, place, sources, targets, sem, cut):
        self.place, self.sem, self.cut = place, sem, cut
        self.sources, self.targets = sources, targets

    def copy(self, kind, group):
        place, index = self.place, self.kinds.index(kind)
        to_x = kind in ("upper", "x_one", "x_two")
        return remote(
            self.cut(self.sources[kind], group),
            self.cut(self.targets[kind], group),
            self.sem,
            (index, group),
            place.over_x if to_x else place.over_y,
        )

    def send(self, kinds, group):
        for kind in kinds:
            self.copy(kind, group).start()

    def arrive(self, kinds, group):
        for kind in kinds:
            self.copy(kind, group).wait_recv()

    def drain(self, group):
        for kind in self.kinds:
            self.copy(kind, group).wait_send()


class Refs:
    def __init__(self, names, refs):
        for name, ref in zip(names, refs, strict=True):
            setattr(self, name, ref)


def layer_kernel(names, *refs):
    r = Refs(names, refs)
    f32, low = jnp.float32, jnp.bfloat16
    z_count = lax.axis_size("mp")
    rows, width = r.hidden.shape
    place = Place(rows // z_count, width)
    size, middle, core = place.size, place.middle, place.core
    cut = place.cut
    part_rows = r.query.shape[0]
    q_rows = r.query.shape[1] // 2
    heads = q_rows // HEAD
    qkv_rows = q_rows + 2 * HEAD
    attn_rows = qkv_rows + q_rows
    attn_half = attn_rows // 2
    chip_rows = 2 * rows
    length = r.length[0, 0]
    cos_at, sin_at = r.cos[place.y], r.sin[place.y]
    w, aw = r.w, r.aw
    ff = r.gate.shape[1] // 2
    groups = ff // 128

    branch_sum = SumChain(place, r.part, *r.chain_one, *r.branch_sems)
    h2_share = ShareChain(place, r.h2, *r.h2_sems)
    back_sum = SumChain(place, r.part, *r.chain_two, *r.back_sems)
    mlp_sum = SumChain(place, r.mlp_part, *r.chain_one, *r.mlp_sems)
    da_share = ShareChain(place, r.da, *r.da_sems)
    input_sum = SumChain(place, r.part, *r.chain_two, *r.input_sems)
    layer_share = ShareChain(place, r.layer_all, *r.layer_sems)
    grad_share = ShareChain(place, r.grad_all, *r.grad_sems)
    qkv_gather = AttnGather(place, aw, 0, qkv_rows, r.attn_x, r.attn_y, r.attn_far, 0)
    out_gather = AttnGather(place, aw, qkv_rows, q_rows, r.attn_x, r.attn_y, r.attn_far, 2)
    gather = WideGather(place, w, r.wide_x, r.wide_y, r.wide_far)

    my_rows = rows_at(core * rows, rows)
    loads = [
        pltpu.make_async_copy(r.hidden, r.da.at[pl.ds(0, rows)], r.load_sem.at[0]),
        pltpu.make_async_copy(r.cotangent, r.da.at[pl.ds(rows, rows)], r.load_sem.at[1]),
    ]
    for load in loads:
        load.start()
    to_lanes = chosen(part_rows, size, core * part_rows)

    def split(total):
        half = total.shape[0] // 2
        one, two = total[:half], total[half:]
        return jnp.where(core == 0, one, two), jnp.where(core == 0, two, one)

    def spread(tensor, dims):
        return split(lax.dot_general(tensor, to_lanes, dims, preferred_element_type=f32))

    plain = (((1,), (0,)), ((), ()))
    q_pair, k_pair, v_pair = (
        spread(r.query[...], TN),
        spread(r.key_t[...], plain),
        spread(r.value_t[...], plain),
    )
    qkv_give = r.part.at[pl.ds(0, qkv_rows), pl.ds(0, size)]
    qkv_take = r.mlp_part.at[pl.ds(0, qkv_rows), pl.ds(0, size)]
    out_give = r.part.at[pl.ds(0, q_rows), pl.ds(size, size)]
    out_take = r.mlp_part.at[pl.ds(0, q_rows), pl.ds(size, size)]
    qkv_give[...] = jnp.concatenate([q_pair[1], k_pair[1], v_pair[1]], axis=0).astype(low)
    place.enter()
    qkv_swap = remote(qkv_give, qkv_take, r.core_sem, (0,), place.sibling)
    qkv_swap.start()

    row = lax.broadcasted_iota(jnp.int32, r.gains.shape, 0)
    gain_pair = [
        jnp.dot(jnp.broadcast_to(norm[...][None], (8, part_rows)), to_lanes, preferred_element_type=f32)
        for norm in (r.norm_one, r.norm_two)
    ]
    r.gains[...] = jnp.where(row == 0, gain_pair[0], jnp.where(row == 1, gain_pair[1], 0.0))
    r.gains_all[core] = r.gains[...]

    def gain_copy(turn, flip):
        slot = 2 * turn + core
        return remote(
            r.gains, r.gains_all.at[slot], r.gain_sem, (2 * turn + flip,), place.plane[turn, flip]
        )

    for turn, flip in place.plane:
        gain_copy(turn, flip).start()

    qkv_keep = jnp.concatenate([q_pair[0], k_pair[0], v_pair[0]], axis=0).astype(low)
    qkv_swap.wait_recv()
    aw[0, :qkv_rows] = qkv_keep + qkv_take[...]
    qkv_gather.send(0)
    qkv_gather.send(1)
    out_pair = spread(r.output_t[...], TN)
    out_give[...] = out_pair[1].astype(low)
    out_swap = remote(out_give, out_take, r.core_sem, (1,), place.sibling)
    out_swap.start()

    def wide_copies(group, kind, source):
        from_here = lanes_at(core * ff + group * 128, 128)
        from_there = lanes_at((1 - core) * ff + group * 128, 128)
        to = lanes_at(group * GROUP + kind * 128, 128)
        owner_rows = rows_at(core * part_rows, part_rows)
        here = pltpu.make_async_copy(
            source.at[:, from_here], w.at[0, owner_rows, to], r.wide_here.at[kind, group]
        )
        there = remote(
            source.at[:, from_there],
            w.at[0, owner_rows, to],
            r.wide_there,
            (kind, group),
            place.sibling,
        )
        return here, there

    sources = (r.gate, r.up, r.down_t)

    def start_wide(group, carry):
        for kind, source in enumerate(sources):
            for copy in wide_copies(group, kind, source):
                copy.start()
        return carry

    def own_wide(group, carry):
        for kind, source in enumerate(sources):
            here, there = wide_copies(group, kind, source)
            here.wait()
            there.wait_recv()
        return carry

    lax.fori_loop(0, groups, start_wide, 0)

    for load in loads:
        load.wait()
    hidden, cotangent = r.da.at[pl.ds(0, rows)], r.da.at[pl.ds(rows, rows)]
    slot = place.ctx * rows + lax.broadcasted_iota(jnp.int32, (rows, size), 0)
    for turn in range(4):
        block = cotangent[:, place.source(turn)].astype(f32)
        r.dm[my_rows, cut(turn)] = jnp.where(slot < length, block, 0.0).astype(low)
        r.inputs_own[:, cut(turn)] = r.da[place.block(place.z), place.source(turn)].astype(f32)
    dm_copy = remote(r.dm.at[my_rows], r.dm.at[my_rows], r.dm_sem, (0,), place.sibling)
    dm_copy.start()
    out_swap.wait_recv()
    aw[0, qkv_rows:] = out_pair[0].astype(low) + out_take[...]
    squares = hidden[...].astype(f32)
    scale = lax.rsqrt(jnp.mean(squares * squares, axis=-1, keepdims=True) + EPS)
    for turn, flip in place.plane:
        gain_copy(turn, flip).wait_recv()
    for turn in range(4):
        gain = r.gains_all[2 * turn] + r.gains_all[2 * turn + 1]
        r.gain_rows[:, cut(turn)] = gain
        block = hidden[:, place.source(turn)].astype(f32)
        r.h1[my_rows, cut(turn)] = (block * scale * gain[:1]).astype(low)
    h1_copy = remote(r.h1.at[my_rows], r.h1.at[my_rows], r.h1_sem, (0,), place.sibling)
    h1_copy.start()

    qkv = r.dh2.at[pl.ds(0, qkv_rows), pl.ds(0, chip_rows)]

    def qkv_dot(turn):
        return lax.dot_general(
            aw[turn, :qkv_rows], r.h1[:, cut(turn)], NT, preferred_element_type=f32
        )

    h1_copy.wait_recv()
    qkv[...] = qkv_dot(0)
    qkv_gather.pass_on()
    out_gather.send(0)
    qkv_gather.cross(1, True).wait_recv()
    qkv[...] += qkv_dot(2)
    qkv_gather.cross(0, False).wait_recv()
    qkv[...] += qkv_dot(1)
    qkv_gather.relay(False).wait_recv()
    qkv_gather.relay(True).wait_recv()
    qkv[...] += qkv_dot(3)

    def turned(first_row):
        ahead = qkv[first_row : first_row + HEAD // 2]
        behind = qkv[first_row + HEAD // 2 : first_row + HEAD]
        return jnp.concatenate(
            [ahead * cos_at - behind * sin_at, behind * cos_at + ahead * sin_at], axis=0
        )

    r.kv[place.y, :HEAD] = turned(q_rows).astype(low)
    r.kv[place.y, HEAD:] = qkv[q_rows + HEAD : qkv_rows].astype(low)
    kv_copy = remote(r.kv.at[place.y], r.kv.at[place.y], r.kv_sem, (0,), place.over_y)
    kv_copy.start()
    out_gather.send(1)
    head_rows = [slice(head * HEAD, (head + 1) * HEAD) for head in range(heads)]
    for head in range(heads):
        r.q_t[head_rows[head]] = turned(head * HEAD).astype(low)
    lax.fori_loop(0, groups, own_wide, 0)
    kv_copy.wait_recv()
    out_gather.pass_on()
    gather.send(0)

    keys = [r.kv[block, :HEAD].T for block in range(2)]
    for head in range(heads):
        scores = [
            masked(keys[block], r.q_t[head_rows[head]], length, block, place.y)
            for block in range(2)
        ]
        top = jnp.maximum(*(jnp.max(score, axis=0, keepdims=True) for score in scores))
        exponents = [jnp.exp(score - top) for score in scores]
        total = sum(jnp.sum(exponent, axis=0, keepdims=True) for exponent in exponents)
        mixed = jnp.zeros((HEAD, chip_rows), f32)
        for block in range(2):
            weights = (exponents[block] / total).astype(low)
            mixed += jnp.dot(r.kv[block, HEAD:], weights, preferred_element_type=f32)
        r.o_t[head_rows[head]] = mixed.astype(low)
        r.lse[head : head + 1] = top + jnp.log(total)
    out_gather.cross(1, True).wait_recv()
    out_gather.cross(0, False).wait_recv()
    out_gather.relay(False).wait_recv()
    out_gather.relay(True).wait_recv()
    qkv_swap.wait_send()
    out_swap.wait_send()
    mixed_all = r.o_t[...].T
    for turn in range(4):
        r.part[:, cut(turn)] = jnp.dot(
            mixed_all, aw[turn, qkv_rows:], preferred_element_type=f32
        ).astype(low)

    branch_sum.open()
    gather.send(1)
    branch_sum.step(0)
    branch_sum.step(1)
    gather.pump(0)
    branch_sum.step(2)
    branch_sum.close(r.middle)
    r.middle[...] += r.inputs_own[...]
    gain_two = r.gain_rows[1:2]
    r.h2[place.mine()] = normed(r.middle[...], gain_two).astype(low)
    h2_share.step(0)
    gather.pump(1)
    h2_share.step(1)
    h2_share.step(2)
    gather.pump(2)
    h2_share.step(3)
    h2_share.arrive()
    branch_sum.drain()
    dm_copy.wait()
    r.dh2[...] = jnp.zeros_like(r.dh2)

    def wide_cut(ref, group):
        return ref.at[:, lanes_at(group * GROUP, GROUP)]

    top_half, low_half = pl.ds(0, middle), pl.ds(middle, middle)
    home = Home(
        place,
        {
            "upper": r.stage.at[2, top_half],
            "lower": r.stage.at[2, low_half],
            "x_one": r.stage.at[1, top_half],
            "y_two": r.stage.at[0, low_half],
            "y_one": w.at[0, top_half],
            "x_two": w.at[0, low_half],
        },
        {
            "upper": r.upper,
            "lower": r.lower,
            "x_one": r.x_one,
            "y_two": r.y_two,
            "y_one": w.at[3, top_half],
            "x_two": w.at[3, low_half],
        },
        r.home_sem,
        wide_cut,
    )
    far_kinds, straight_kinds, last_kinds = (
        ("upper", "lower"),
        ("x_one", "y_two"),
        ("y_one", "x_two"),
    )

    def group_body(group, carry):
        start = group * GROUP
        gu_cols, down_cols = lanes_at(start, 256), lanes_at(start + 256, 128)
        gather.arrive(group)
        gu = jnp.zeros((chip_rows, 256), f32)
        d_hidden = jnp.zeros((chip_rows, 128), f32)
        for turn in range(4):
            gu += jnp.dot(r.h2[:, cut(turn)], w[turn, :, gu_cols], preferred_element_type=f32)
            d_hidden += jnp.dot(
                r.dm[:, cut(turn)], w[turn, :, down_cols], preferred_element_type=f32
            )
        gate, up = gu[:, :128], gu[:, 128:]
        sigma = jax.nn.sigmoid(gate)
        silu = gate * sigma
        d_gate = d_hidden * up * sigma * (1.0 + gate * (1.0 - sigma))
        r.zd[:, lanes_at(start, 128)] = d_gate.astype(low)
        r.zd[:, lanes_at(start + 128, 128)] = (d_hidden * silu).astype(low)
        r.zd[:, down_cols] = (silu * up).astype(low)
        d_gu, hidden_low = r.zd[:, gu_cols], r.zd[:, down_cols]
        for turn in range(4):
            r.dh2[:, cut(turn)] += lax.dot_general(
                d_gu, w[turn, :, gu_cols], NT, preferred_element_type=f32
            )
        for turn in range(4):
            grad_gu = lax.dot_general(r.h2[:, cut(turn)], d_gu, TN, preferred_element_type=f32)
            grad_down = lax.dot_general(
                r.dm[:, cut(turn)], hidden_low, TN, preferred_element_type=f32
            )
            if turn:
                r.tile[turn - 1, :, :256] = grad_gu.astype(low)
                r.tile[turn - 1, :, 256:] = grad_down.astype(low)
            else:
                r.tile_own[:, :256] = grad_gu
                r.tile_own[:, 256:] = grad_down
        cols = lanes_at(start, GROUP)
        keep = pltpu.make_async_copy(r.tile, r.stage.at[:, :, cols], r.keep_sem.at[0])
        keep_own = pltpu.make_async_copy(r.tile_own, r.own_grad.at[:, cols], r.keep_sem.at[1])
        keep.start()
        keep_own.start()

        @pl.when(group + 3 < groups)
        def _():
            gather.pump(group + 3)

        keep.wait()
        keep_own.wait()

        @pl.when(group == 3)
        def _():
            for before in range(3):
                home.send(far_kinds, before)

        @pl.when(group >= 3)
        def _():
            home.send(far_kinds, group)

        return carry

    lax.fori_loop(0, groups, group_body, 0)
    h2_share.drain()

    for turn in range(4):
        r.part[:, cut(turn)] = r.dh2[:, cut(turn)].astype(low)
    back_sum.open()
    for step in range(place.last):
        back_sum.step(step)
        for turn in range(4):
            if turn % place.last == step:
                out = jnp.zeros((chip_rows, size), f32)
                for group in range(groups):
                    cols = slice(group * GROUP + 256, group * GROUP + 384)
                    out += lax.dot_general(
                        r.zd[:, cols], w[turn, :, cols], NT, preferred_element_type=f32
                    )
                r.mlp_part[:, cut(turn)] = out.astype(low)
        if step == 0:
            for group in range(4):
                home.send(straight_kinds, group)
    mlp_sum.open()
    back_sum.close(r.d_middle)
    d_norm, d_gain_two = norm_back(r.middle[...], gain_two, r.d_middle[...])
    r.d_middle[...] = r.dm[place.mine()].astype(f32) + d_norm
    r.da[place.mine()] = r.d_middle[...].astype(low)
    da_share.step(0)
    mlp_sum.step(0)

    gather.drain()
    for device in (place.over_x, place.over_y):
        pl.semaphore_signal(r.free_sem, inc=1, device_id=device, device_id_type=MESH)
    y_part, x_part = w.at[0, top_half], w.at[0, low_half]
    y_add, x_add = w.at[1, top_half], w.at[1, low_half]
    x_came, y_came = w.at[2, top_half], w.at[2, low_half]
    part_loads = [
        pltpu.make_async_copy(source, into, r.load_sem.at[2 + index])
        for index, (source, into) in enumerate(
            ((r.stage.at[0, top_half], y_part), (r.stage.at[1, low_half], x_part))
        )
    ]
    for load in part_loads:
        load.start()
    da_share.step(1)
    mlp_sum.step(1)
    for group in range(4, groups):
        home.send(straight_kinds, group)
    da_share.step(2)
    mlp_sum.step(2)
    da_share.step(3)
    mlp_sum.close(r.mlp)
    slot = place.ctx * place.rows + place.z * place.owned
    slot += lax.broadcasted_iota(jnp.int32, r.middle.shape, 0)
    r.layer_all[place.block(place.z)] = jnp.where(
        slot < length, r.middle[...] + r.mlp[...], 0.0
    ).astype(low)
    layer_share.step(0)
    da_share.arrive()
    back_sum.drain()
    mlp_sum.drain()
    do_t, d_t, kv_give = (
        r.mlp_part.at[pl.ds(0, count), pl.ds(at * chip_rows, chip_rows)]
        for at, count in enumerate((q_rows, qkv_rows, 2 * HEAD))
    )
    dk, dv = (
        [r.dh2.at[:, pl.ds(3 * 256 + 128 * at + 256 * which, HEAD)] for at in range(2)]
        for which in range(2)
    )

    d_out = jnp.zeros((q_rows, chip_rows), f32)
    for turn in range(4):
        d_out += lax.dot_general(
            aw[turn, qkv_rows:], r.da[:, cut(turn)], NT, preferred_element_type=f32
        )
    do_t[...] = d_out.astype(low)
    values = [r.kv[block, HEAD:].T for block in range(2)]
    keys = [r.kv[block, :HEAD].T for block in range(2)]
    scale = HEAD ** (-0.5)
    for ref in dk + dv:
        ref[...] = jnp.zeros(ref.shape, f32)

    def turned_back(tensor):
        ahead, behind = tensor[: HEAD // 2], tensor[HEAD // 2 :]
        return jnp.concatenate(
            [ahead * cos_at + behind * sin_at, behind * cos_at - ahead * sin_at], axis=0
        )

    for head in range(heads):
        queries, d_head = r.q_t[head_rows[head]], do_t[head_rows[head]]
        probs, d_probs = [], []
        inner = jnp.zeros((1, chip_rows), f32)
        for block in range(2):
            scores = masked(keys[block], queries, length, block, place.y)
            prob = jnp.exp(scores - r.lse[head : head + 1])
            d_prob = jnp.dot(values[block], d_head, preferred_element_type=f32)
            inner += jnp.sum(prob * d_prob, axis=0, keepdims=True)
            probs.append(prob)
            d_probs.append(d_prob)
        d_query = jnp.zeros((HEAD, chip_rows), f32)
        for block in range(2):
            d_scores = (probs[block] * (d_probs[block] - inner)).astype(low)
            dk[block][...] += (
                lax.dot_general(d_scores, queries, NT, preferred_element_type=f32) * scale
            )
            dv[block][...] += lax.dot_general(
                probs[block].astype(low), d_head, NT, preferred_element_type=f32
            )
            d_query += jnp.dot(r.kv[block, :HEAD], d_scores, preferred_element_type=f32) * scale
        d_t[head_rows[head]] = turned_back(d_query).astype(low)

    def of_half(pair, which):
        return jnp.where(which == 0, pair[0][...], pair[1][...]).T

    kv_give[:HEAD] = of_half(dk, 1 - place.y).astype(low)
    kv_give[HEAD:] = of_half(dv, 1 - place.y).astype(low)
    kv_back = remote(kv_give, r.kv_take, r.kv_sem, (1,), place.over_y)
    kv_back.start()
    d_key, d_value = of_half(dk, place.y), of_half(dv, place.y)

    pl.semaphore_wait(r.free_sem, 2)
    for load in part_loads:
        load.wait()
    add_loads = {}
    for kind, source, into in (("upper", r.upper, y_add), ("lower", r.lower, x_add)):
        add_loads[kind] = lambda group, kind=kind, source=source, into=into: (
            pltpu.make_async_copy(
                wide_cut(source, group),
                wide_cut(into, group),
                r.add_sem.at[far_kinds.index(kind), group],
            )
        )

    def fetch_far(group, carry):
        home.arrive(far_kinds, group)
        for kind in far_kinds:
            add_loads[kind](group).start()
        return carry

    def send_last(group, carry):
        cols = lanes_at(group * GROUP, GROUP)
        for kind, mine, add in (("upper", y_part, y_add), ("lower", x_part, x_add)):
            add_loads[kind](group).wait()
            mine[:, cols] = (mine[:, cols].astype(f32) + add[:, cols].astype(f32)).astype(low)
        home.send(last_kinds, group)
        return carry

    lax.fori_loop(0, groups, fetch_far, 0)
    lax.fori_loop(0, 1, send_last, 0)
    layer_share.step(1)
    kv_back.wait_recv()
    d_t[q_rows : q_rows + HEAD] = turned_back(d_key + r.kv_take[:HEAD].astype(f32)).astype(low)
    d_t[q_rows + HEAD :] = (d_value + r.kv_take[HEAD:].astype(f32)).astype(low)
    d_qkv = d_t[...].T
    for turn in range(4):
        r.part[:, cut(turn)] = jnp.dot(
            d_qkv, aw[turn, :qkv_rows], preferred_element_type=f32
        ).astype(low)

    input_sum.open()
    lax.fori_loop(1, 3, send_last, 0)
    input_sum.step(0)
    layer_share.step(2)

    def view(ref, at):
        return ref.at[pl.ds(0, attn_half), pl.ds(at * size, size)]

    stage = {
        (turn, half): view(r.h2, 2 * (turn - 1) + half) if turn < 3 else view(r.dm, half)
        for turn in (1, 2, 3)
        for half in range(2)
    }
    attn_own = [view(r.dh2, 2 + half) for half in range(2)]
    attn_home = Home(
        place,
        {
            "upper": stage[3, 0],
            "lower": stage[3, 1],
            "x_one": stage[2, 0],
            "y_two": stage[1, 1],
            "y_one": stage[1, 0],
            "x_two": stage[2, 1],
        },
        {
            "upper": view(r.zd, 0),
            "lower": view(r.zd, 1),
            "x_one": view(r.zd, 2),
            "y_two": view(r.zd, 3),
            "y_one": view(r.dm, 2),
            "x_two": view(r.dm, 3),
        },
        r.attn_home_sem,
        lambda ref, group: ref,
    )
    for turn in (3, 2, 1, 0):
        grad = jnp.concatenate(
            [
                jnp.dot(left, right[:, cut(turn)], preferred_element_type=f32)
                for left, right in ((d_t[...], r.h1), (r.o_t[...], r.da))
            ],
            axis=0,
        )
        for half in range(2):
            piece = grad[half * attn_half : (half + 1) * attn_half]
            if turn:
                stage[turn, half][...] = piece.astype(low)
            else:
                attn_own[half][...] = piece
        if turn == 3:
            attn_home.send(far_kinds, 0)
    lax.fori_loop(3, 5, send_last, 0)
    input_sum.step(1)
    layer_share.step(3)
    attn_home.send(straight_kinds, 0)
    lax.fori_loop(5, groups, send_last, 0)
    input_sum.step(2)
    input_sum.close(r.mlp)
    d_norm, d_gain_one = norm_back(r.inputs_own[...], r.gain_rows[0:1], r.mlp[...])
    r.grad_all[place.block(place.z)] = (r.d_middle[...] + d_norm).astype(low)
    grad_share.step(0)

    row = lax.broadcasted_iota(jnp.int32, r.gain_part.shape, 0)
    r.gain_part[...] = jnp.where(
        row == 0, d_gain_one[None], jnp.where(row == 1, d_gain_two[None], 0.0)
    )
    plane_gains = [
        remote(
            r.gain_part.at[:, pl.ds(turn * size, size)],
            r.gain_in.at[turn - 1],
            r.plane_gain_sem,
            (turn - 1,),
            place.plane[turn, 0],
        )
        for turn in (1, 2, 3)
    ]
    for copy in plane_gains:
        copy.start()

    slots = (
        (r.tile_own.at[top_half], r.tile_own.at[low_half]),
        (r.dh2.at[top_half, pl.ds(0, GROUP)], r.dh2.at[top_half, pl.ds(GROUP, GROUP)]),
    )

    def final_loads(group):
        cols = lanes_at(group * GROUP, GROUP)
        parity = group % 2
        yield pltpu.make_async_copy(
            r.own_grad.at[top_half, cols], slots[parity][0], r.final_sem.at[0, group]
        )
        yield pltpu.make_async_copy(
            r.own_grad.at[low_half, cols], slots[parity][1], r.final_sem.at[1, group]
        )
        yield pltpu.make_async_copy(
            r.x_one.at[:, cols], x_came.at[:, cols], r.final_sem.at[2, group]
        )
        yield pltpu.make_async_copy(
            r.y_two.at[:, cols], y_came.at[:, cols], r.final_sem.at[3, group]
        )

    def final_out(group):
        parity = group % 2
        to = lanes_at(core * ff + group * 128, 128)
        for kind, into in enumerate((r.grad_gate, r.grad_up, r.grad_down)):
            cols = pl.ds(kind * 128, 128)
            for half in range(2):
                source = slots[parity][half].at[:, cols]
                yield (
                    half,
                    pltpu.make_async_copy(source, into.at[:, to], r.out_here.at[kind, group]),
                    remote(source, into.at[:, to], r.out_there, (kind, group), place.sibling),
                )

    def final_start(group):
        home.arrive(straight_kinds, group)
        for load in final_loads(group):
            load.start()

    def final_sum(group):
        cols = lanes_at(group * GROUP, GROUP)
        upper, lower = slots[group % 2]
        home.arrive(last_kinds, group)
        for load in final_loads(group):
            load.wait()
        y_last, x_last = w.at[3, top_half, cols], w.at[3, low_half, cols]
        upper[...] += x_came[:, cols].astype(f32) + y_last[...].astype(f32)
        lower[...] += x_last[...].astype(f32) + y_came[:, cols].astype(f32)
        for half, here, there in final_out(group):

            @pl.when(core == half)
            def _(here=here):
                here.start()

            @pl.when(core != half)
            def _(there=there):
                there.start()

    def final_free(group):
        for half, here, there in final_out(group):

            @pl.when(core == half)
            def _(here=here):
                here.wait()

            @pl.when(core != half)
            def _(there=there):
                there.wait_send()

    def finish(group):
        final_sum(group)
        if group:
            final_free(group - 1)
        if group + 1 < groups:
            final_start(group + 1)

    final_start(0)
    grad_share.step(1)
    finish(0)
    finish(1)
    attn_home.arrive(far_kinds, 0)
    for turn, half, kind in ((1, 0, "upper"), (2, 1, "lower")):
        mine = stage[turn, half]
        mine[...] = (
            mine[...].astype(f32) + attn_home.targets[kind][...].astype(f32)
        ).astype(low)
    attn_home.send(last_kinds, 0)
    finish(2)
    grad_share.step(2)
    for copy in plane_gains:
        copy.wait_recv()
    r.gain_sum[...] = r.gain_part[:, :size] + r.gain_in[0] + r.gain_in[1] + r.gain_in[2]
    column_gains = [
        remote(r.gain_sum, r.gain_all.at[index], r.column_gain_sem, (index,), device)
        for index, device in enumerate(place.column)
    ]
    for copy in column_gains:
        copy.start()
    finish(3)
    finish(4)
    grad_share.step(3)
    for group in range(5, groups):
        finish(group)
    attn_home.arrive(straight_kinds + last_kinds, 0)
    attn_own[0][...] += attn_home.targets["x_one"][...].astype(f32) + attn_home.targets["y_one"][
        ...
    ].astype(f32)
    attn_own[1][...] += attn_home.targets["x_two"][...].astype(f32) + attn_home.targets["y_two"][
        ...
    ].astype(f32)
    attn_out = []
    for half in range(2):
        to = pl.ds(half * attn_half, attn_half)
        attn_out.append(
            pltpu.make_async_copy(attn_own[half], r.grad_attn.at[core, to], r.out_attn.at[half])
        )
        attn_out.append(
            remote(
                attn_own[half], r.grad_attn.at[core, to], r.swap_attn, (half,), place.sibling
            )
        )
    for copy in attn_out:
        copy.start()
    gain_total = r.gain_sum[...]
    for index, copy in enumerate(column_gains):
        copy.wait_recv()
        gain_total += r.gain_all[index]
    r.gain_out[...] = gain_total

    final_free(groups - 1)

    def settle(group, carry):
        for kind, source in enumerate(sources):
            wide_copies(group, kind, source)[1].wait_send()
            to = lanes_at(core * ff + group * 128, 128)
            into = (r.grad_gate, r.grad_up, r.grad_down)[kind]
            remote(
                r.tile_own.at[top_half, pl.ds(0, 128)],
                into.at[:, to],
                r.out_there,
                (kind, group),
                place.sibling,
            ).wait_recv()
        home.drain(group)
        return carry

    lax.fori_loop(0, groups, settle, 0)
    for copy in attn_out:
        copy.wait()
    attn_home.drain(0)
    for copy in (kv_copy, kv_back, h1_copy, *plane_gains, *column_gains):
        copy.wait_send()
    for turn, flip in place.plane:
        gain_copy(turn, flip).wait_send()
    for chain in (input_sum, da_share, layer_share, grad_share):
        chain.drain()
    qkv_gather.drain()
    out_gather.drain()


class Lists:
    def __init__(self):
        self.names, self.items = [], []

    def add(self, name, item):
        self.names.append(name)
        self.items.append(item)


def grouped_kernel(names, counts, *refs):
    given, at = [], 0
    for count in counts:
        given.append(refs[at] if count is None else refs[at : at + count])
        at += count or 1
    layer_kernel(names, *given)


def finish_kernel(
    layer_all,
    grad_all,
    gains,
    gate,
    up,
    down,
    attn,
    layer_out,
    input_grad,
    gain_one,
    gain_two,
    query,
    key_t,
    value_t,
    output_t,
    gate_out,
    up_out,
    down_out,
    attn_here,
    layer_here,
    grad_here,
    gate_here,
    up_here,
    down_here,
    in_sem,
    out_sem,
):
    part = key_t.shape[1]
    place = 2 * lax.axis_index("dp") + lax.axis_index("ctx") // 2
    first = lax.rem(lax.axis_index("ctx"), 2) == 0
    size = 2 * part
    here = (attn_here, layer_here, grad_here, gate_here, up_here, down_here)
    loads = [
        pltpu.make_async_copy(source, into, in_sem.at[index])
        for index, (source, into) in enumerate(
            zip((attn, layer_all, grad_all, gate, up, down), here, strict=True)
        )
    ]
    for load in loads:
        load.start()
    stores = []

    def store(source, into):
        stores.append(pltpu.make_async_copy(source, into, out_sem.at[len(stores)]))
        stores[-1].start()

    def own(tensor):
        return jnp.where(first, tensor[:, :part], tensor[:, part:])

    mine = own(gains[...])
    gain_one[...], gain_two[...] = mine[0], mine[1]
    loads[0].wait()
    q_rows = query.shape[1] // 2
    start = 0
    for into, size_of in ((query, q_rows), (key_t, HEAD), (value_t, HEAD), (output_t, q_rows)):
        rows = slice(start, start + size_of)
        start += size_of
        both = jnp.concatenate([own(attn_here[which, rows]) for which in range(2)], axis=0)
        into[...] = both if size_of == HEAD else both.T
    for index, into in ((1, layer_out), (2, input_grad)):
        loads[index].wait()
        for turn in range(4):
            at = lanes_at((place ^ turn) * size, size)
            store(here[index].at[:, turn * size : (turn + 1) * size], into.at[:, at])
    for index, into in ((3, gate_out), (4, up_out), (5, down_out)):
        loads[index].wait()
        store(here[index], into)
    for copy in stores:
        copy.wait()


def on_plane(
    hidden_in,
    cotangent,
    lengths,
    norm_attn,
    w_query,
    w_key,
    w_value,
    w_output,
    norm_mlp,
    w_gate,
    w_up,
    w_down,
):
    low, f32 = jnp.bfloat16, jnp.float32
    _, rows, width = hidden_in.shape
    part = w_query.shape[0]
    chip_part, chip_rows = 2 * part, 2 * rows
    z_count = lax.axis_size("mp")
    owned, hops = rows // z_count, z_count - 1
    q_rows = w_query.shape[1] // 2
    qkv_rows = q_rows + 2 * HEAD
    attn_rows = qkv_rows + q_rows
    ff = w_gate.shape[1] // 2
    wide_cols = 3 * ff
    groups = wide_cols // GROUP
    half_part = chip_part // 2
    others = 2 * z_count - 1

    slots = np.arange(2 * chip_rows, dtype=np.float32)
    freq = np.float32(THETA) ** -(np.arange(HEAD // 2, dtype=np.float32) * 2.0 / HEAD)
    angle = (freq.astype(np.float32)[:, None] * slots[None]).reshape(HEAD // 2, 2, chip_rows)
    angle = angle.astype(np.float32).swapaxes(0, 1)
    cosine, sine = (jnp.asarray(table(angle), f32) for table in (np.cos, np.sin))

    hbm = pl.BlockSpec(memory_space=pl.ANY)
    smem = pl.BlockSpec(memory_space=pltpu.SMEM)
    vmem = pl.BlockSpec(memory_space=pltpu.VMEM)
    dma, vm = pltpu.SemaphoreType.DMA, pltpu.VMEM
    whole, own = (chip_rows, width), (owned, width)

    ins, outs, scratch = Lists(), Lists(), Lists()
    for name, value, spec in (
        ("hidden", hidden_in[0], hbm),
        ("cotangent", cotangent[0], hbm),
        ("length", lengths.reshape(1, 1), smem),
        ("norm_one", norm_attn, vmem),
        ("norm_two", norm_mlp, vmem),
        ("query", w_query, vmem),
        ("key_t", w_key.T, vmem),
        ("value_t", w_value.T, vmem),
        ("output_t", w_output.T, vmem),
        ("gate", w_gate, hbm),
        ("up", w_up, hbm),
        ("down_t", w_down.T, hbm),
        ("cos", cosine, vmem),
        ("sin", sine, vmem),
    ):
        ins.add(name, (value, spec))
    for name, shape, dtype, spec in (
        ("layer_all", (rows, width), low, vmem),
        ("grad_all", (rows, width), low, vmem),
        ("gain_out", (8, chip_part), f32, vmem),
        ("grad_gate", w_gate.shape, f32, hbm),
        ("grad_up", w_up.shape, f32, hbm),
        ("grad_down", w_gate.shape, f32, hbm),
        ("grad_attn", (2, attn_rows, chip_part), f32, hbm),
        ("own_grad", (chip_part, wide_cols), f32, hbm),
        ("stage", (3, chip_part, wide_cols), low, hbm),
        ("upper", (half_part, wide_cols), low, hbm),
        ("lower", (half_part, wide_cols), low, hbm),
        ("x_one", (half_part, wide_cols), low, hbm),
        ("y_two", (half_part, wide_cols), low, hbm),
    ):
        outs.add(name, (jax.ShapeDtypeStruct(shape, dtype), spec))
    chain = [vm((rows, width), low), vm((hops, *own), low), vm((hops, *own), low)]
    ways = [dma((2, hops, SPLIT))] * 2
    cores = dma((2, z_count))
    for name, item in (
        ("w", vm((4, chip_part, wide_cols), low)),
        ("aw", vm((4, attn_rows, chip_part), low)),
        ("h1", vm(whole, low)),
        ("h2", vm(whole, low)),
        ("dm", vm(whole, low)),
        ("da", vm(whole, low)),
        ("part", vm(whole, low)),
        ("mlp_part", vm(whole, low)),
        ("dh2", vm(whole, f32)),
        ("zd", vm((chip_rows, wide_cols), low)),
        ("tile", vm((3, chip_part, GROUP), low)),
        ("tile_own", vm((chip_part, GROUP), f32)),
        ("chain_one", chain),
        ("chain_two", chain),
        ("inputs_own", vm(own, f32)),
        ("middle", vm(own, f32)),
        ("mlp", vm(own, f32)),
        ("d_middle", vm(own, f32)),
        ("gains", vm((8, chip_part), f32)),
        ("gains_all", vm((8, 8, chip_part), f32)),
        ("gain_rows", vm((8, width), f32)),
        ("kv", vm((2, 2 * HEAD, chip_rows), low)),
        ("q_t", vm((q_rows, chip_rows), low)),
        ("o_t", vm((q_rows, chip_rows), low)),
        ("lse", vm((8, chip_rows), f32)),
        ("kv_take", vm((2 * HEAD, chip_rows), low)),
        ("gain_part", vm((8, width), f32)),
        ("gain_in", vm((3, 8, chip_part), f32)),
        ("gain_sum", vm((8, chip_part), f32)),
        ("gain_all", vm((others, 8, chip_part), f32)),
        ("load_sem", dma((4,))),
        ("core_sem", dma((2, 2))),
        ("gain_sem", dma((2, 8))),
        ("attn_x", dma((2, 4))),
        ("attn_y", dma((2, 4))),
        ("attn_far", dma((2, 4))),
        ("wide_here", dma((3, groups))),
        ("wide_there", dma((2, 3, groups))),
        ("dm_sem", dma((2, 1))),
        ("h1_sem", dma((2, 1))),
        ("kv_sem", dma((2, 2))),
        ("wide_x", dma((2, groups))),
        ("wide_y", dma((2, groups))),
        ("wide_far", dma((2, 2, groups))),
        ("keep_sem", dma((2,))),
        ("home_sem", dma((2, 6, groups))),
        ("add_sem", dma((2, groups))),
        ("attn_home_sem", dma((2, 6, 1))),
        ("final_sem", dma((4, groups))),
        ("out_here", dma((3, groups))),
        ("out_there", dma((2, 3, groups))),
        ("out_attn", dma((2,))),
        ("swap_attn", dma((2, 2))),
        ("plane_gain_sem", dma((2, 3))),
        ("column_gain_sem", dma((2, others))),
        ("free_sem", pltpu.SemaphoreType.REGULAR),
        ("branch_sems", [cores] + ways),
        ("back_sems", [cores] + ways),
        ("mlp_sems", [cores] + ways),
        ("input_sems", [cores] + ways),
        ("h2_sems", ways + [cores]),
        ("da_sems", ways + [cores]),
        ("layer_sems", ways),
        ("grad_sems", ways),
    ):
        scratch.add(name, item)

    counts = [None] * (len(ins.items) + len(outs.items))
    flat = []
    for item in scratch.items:
        counts.append(len(item) if isinstance(item, list) else None)
        flat += item if isinstance(item, list) else [item]
    names = ins.names + outs.names + scratch.names
    results = pl.pallas_call(
        functools.partial(grouped_kernel, names, counts),
        out_shape=[shape for shape, _ in outs.items],
        in_specs=[spec for _, spec in ins.items],
        out_specs=[spec for _, spec in outs.items],
        scratch_shapes=flat,
        name="layer",
        compiler_params=pltpu.CompilerParams(
            collective_id=1, has_side_effects=True, vmem_limit_bytes=65_400 * 2**10
        ),
    )(*(value for value, _ in ins.items))
    layer_all, grad_all, gain_sums, grad_gate, grad_up, grad_down, grad_attn = results[:7]
    gate_like = jax.ShapeDtypeStruct(w_gate.shape, f32)
    tokens = jax.ShapeDtypeStruct((rows, width), low)
    gain_like = jax.ShapeDtypeStruct((part,), f32)
    square = jax.ShapeDtypeStruct((part, 2 * q_rows), f32)
    flat_heads = jax.ShapeDtypeStruct((2 * HEAD, part), f32)
    (
        layer_out,
        input_grad,
        gain_one,
        gain_two,
        grad_query,
        grad_key_t,
        grad_value_t,
        grad_output_t,
        grad_gate,
        grad_up,
        grad_down_t,
    ) = pl.pallas_call(
        finish_kernel,
        out_shape=[tokens] * 2
        + [gain_like] * 2
        + [square, flat_heads, flat_heads, square]
        + [gate_like] * 3,
        in_specs=[hbm, hbm, vmem, hbm, hbm, hbm, hbm],
        out_specs=[hbm] * 2 + [vmem] * 6 + [hbm] * 3,
        scratch_shapes=[vm((2, attn_rows, chip_part), f32)]
        + [vm((rows, width), low)] * 2
        + [vm(w_gate.shape, f32)] * 3
        + [dma((6,)), dma((11,))],
        name="finish",
        compiler_params=pltpu.CompilerParams(vmem_limit_bytes=65_400 * 2**10),
    )(layer_all, grad_all, gain_sums, grad_gate, grad_up, grad_down, grad_attn)
    return (
        layer_out[None],
        input_grad[None],
        gain_one,
        grad_query,
        grad_key_t.T,
        grad_value_t.T,
        grad_output_t.T,
        gain_two,
        grad_gate,
        grad_up,
        grad_down_t.T,
    )


def solution(mesh):
    plane = dict(mesh.shape) == {"dp": 2, "ctx": 4, "mp": 4}
    return jax.shard_map(
        on_plane if plane else any_mesh,
        mesh=mesh,
        in_specs=(
            P("dp", "ctx", None),
            P("dp", "ctx", None),
            P("dp"),
            P(("dp", "ctx")),
            P(("dp", "ctx"), "mp"),
            P(("dp", "ctx"), "mp"),
            P(("dp", "ctx"), "mp"),
            P("mp", ("dp", "ctx")),
            P(("dp", "ctx")),
            P(("dp", "ctx"), "mp"),
            P(("dp", "ctx"), "mp"),
            P("mp", ("dp", "ctx")),
        ),
        out_specs=(
            P("dp", "ctx", None),
            P("dp", "ctx", None),
            P(("dp", "ctx")),
            P(("dp", "ctx"), "mp"),
            P(("dp", "ctx"), "mp"),
            P(("dp", "ctx"), "mp"),
            P("mp", ("dp", "ctx")),
            P(("dp", "ctx")),
            P(("dp", "ctx"), "mp"),
            P(("dp", "ctx"), "mp"),
            P("mp", ("dp", "ctx")),
        ),
        check_vma=False,
    )
```

```python
import functools

import jax
import jax.numpy as jnp
import numpy as np
from jax import lax
from jax.experimental import pallas as pl
from jax.experimental.pallas import tpu as pltpu
from jax.sharding import PartitionSpec as P

HEAD = 80


EPS = 1e-05
THETA = 1000000.0
NEG = -1e30


def rope_tables(places, head_size):
    half = head_size // 2
    freq = THETA ** (-(jnp.arange(half, dtype=jnp.float32) * 2.0 / head_size))
    angle = places[:, None] * freq[None, :]
    return (jnp.cos(angle), jnp.sin(angle))


def rotate(tensor, cosine, sine_table):
    half = tensor.shape[-1] // 2
    first_half = tensor[..., :half]
    second_half = tensor[..., half:]
    cos_b = cosine[:, None, :]
    sin_b = sine_table[:, None, :]
    return jnp.concatenate(
        [first_half * cos_b - second_half * sin_b, second_half * cos_b + first_half * sin_b],
        axis=-1,
    )


def rotate_back(tensor, cosine, sine_table):
    half = tensor.shape[-1] // 2
    first_half = tensor[..., :half]
    second_half = tensor[..., half:]
    cos_b = cosine[:, None, :]
    sin_b = sine_table[:, None, :]
    return jnp.concatenate(
        [first_half * cos_b + second_half * sin_b, second_half * cos_b - first_half * sin_b],
        axis=-1,
    )


def normed(tensor, gain_row):
    return tensor * lax.rsqrt(jnp.mean(tensor * tensor, axis=-1, keepdims=True) + EPS) * gain_row


def norm_back(tensor, gain_row, grad_normed):
    scale_row = lax.rsqrt(jnp.mean(tensor * tensor, axis=-1, keepdims=True) + EPS)
    grad_scaled = grad_normed * gain_row
    grad_tensor = scale_row * grad_scaled - tensor * scale_row**3 * jnp.mean(
        grad_scaled * tensor, axis=-1, keepdims=True
    )
    grad_gain = jnp.sum(grad_normed * tensor * scale_row, axis=0)
    return (grad_tensor, grad_gain)


def masked_scores(query_seq, key_seq, length, places, kv_heads, group_size):
    query_grp = query_seq.reshape(query_seq.shape[0], kv_heads, group_size, HEAD)
    key_grp = key_seq.reshape(key_seq.shape[0], kv_heads, HEAD)
    raw_scores = jnp.einsum(
        "bkgh,tkh->kgbt", query_grp, key_grp, preferred_element_type=jnp.float32
    ) * HEAD ** (-0.5)
    key_places = jnp.arange(key_grp.shape[0], dtype=jnp.int32)
    allowed = (key_places[None, :] <= places[:, None]) & (key_places[None, :] < length)
    return jnp.where(allowed[None, None], raw_scores, NEG)


def any_mesh(
    hidden_in,
    cotangent,
    lengths,
    norm_attn,
    w_query,
    w_key,
    w_value,
    w_output,
    norm_mlp,
    w_gate,
    w_up,
    w_down,
):
    seq_count, slot_count, width_all = hidden_in.shape
    tok_rows = seq_count * slot_count
    attn_set = (
        lax.all_gather(w_query, ("dp", "ctx"), axis=0, tiled=True),
        lax.all_gather(w_key, ("dp", "ctx"), axis=0, tiled=True),
        lax.all_gather(w_value, ("dp", "ctx"), axis=0, tiled=True),
        lax.all_gather(w_output, ("dp", "ctx"), axis=1, tiled=True),
        lax.all_gather(norm_attn, ("dp", "ctx"), axis=0, tiled=True),
    )
    query_w, key_w, value_w, output_w, gain_attn = attn_set
    q_heads = query_w.shape[1] // HEAD
    kv_heads = key_w.shape[1] // HEAD
    group_size = q_heads // kv_heads
    first_slot = lax.axis_index("ctx") * slot_count
    places = first_slot + jnp.arange(slot_count, dtype=jnp.int32)
    valid_mask = (places[None, :] < lengths[:, None]).astype(jnp.float32).reshape(tok_rows, 1)
    cosine, sine_table = rope_tables(places.astype(jnp.float32), HEAD)
    inputs = hidden_in.reshape(tok_rows, width_all).astype(jnp.float32)
    gain_one = gain_attn.astype(jnp.float32)
    normed_one = normed(inputs, gain_one).astype(jnp.bfloat16)
    query_proj = jnp.dot(normed_one, query_w, preferred_element_type=jnp.float32).reshape(
        seq_count, slot_count, q_heads, HEAD
    )
    key_proj = jnp.dot(normed_one, key_w, preferred_element_type=jnp.float32).reshape(
        seq_count, slot_count, kv_heads, HEAD
    )
    value_low = (
        jnp.dot(normed_one, value_w, preferred_element_type=jnp.float32)
        .astype(jnp.bfloat16)
        .reshape(seq_count, slot_count, kv_heads * HEAD)
    )
    query_low = rotate(query_proj, cosine, sine_table).astype(jnp.bfloat16)
    key_low = (
        rotate(key_proj, cosine, sine_table)
        .astype(jnp.bfloat16)
        .reshape(seq_count, slot_count, kv_heads * HEAD)
    )
    key_all, value_all = (
        lax.all_gather(key_low, "ctx", axis=1, tiled=True),
        lax.all_gather(value_low, "ctx", axis=1, tiled=True),
    )

    def attend(members):
        query_seq, key_seq, value_seq, length = members
        scores = masked_scores(query_seq, key_seq, length, places, kv_heads, group_size)
        row_max = jnp.max(scores, axis=-1, keepdims=True)
        exponent = jnp.exp(scores - row_max)
        total = jnp.sum(exponent, axis=-1, keepdims=True)
        attention = (exponent / total).astype(jnp.bfloat16)
        value_grp = value_seq.reshape(value_seq.shape[0], kv_heads, HEAD)
        mixed_heads = jnp.einsum(
            "kgbt,tkh->bkgh", attention, value_grp, preferred_element_type=jnp.float32
        )
        return (mixed_heads.reshape(slot_count, q_heads * HEAD), (row_max + jnp.log(total))[..., 0])

    mixed_all, log_total = lax.map(attend, (query_low, key_all, value_all, lengths))
    attn_low = mixed_all.reshape(tok_rows, q_heads * HEAD).astype(jnp.bfloat16)
    branch = lax.psum(jnp.dot(attn_low, output_w, preferred_element_type=jnp.float32), "mp")
    middle = inputs + branch
    mlp_set = (
        lax.all_gather(w_gate, ("dp", "ctx"), axis=0, tiled=True),
        lax.all_gather(w_up, ("dp", "ctx"), axis=0, tiled=True),
        lax.all_gather(w_down, ("dp", "ctx"), axis=1, tiled=True),
        lax.all_gather(norm_mlp, ("dp", "ctx"), axis=0, tiled=True),
    )
    gate_w, up_w, down_w, gain_mlp = mlp_set
    gain_two = gain_mlp.astype(jnp.float32)
    normed_two = normed(middle, gain_two).astype(jnp.bfloat16)
    gate_proj = jnp.dot(normed_two, gate_w, preferred_element_type=jnp.float32)
    up_proj = jnp.dot(normed_two, up_w, preferred_element_type=jnp.float32)
    hidden = (jax.nn.silu(gate_proj) * up_proj).astype(jnp.bfloat16)
    mlp_out = lax.psum(
        jnp.dot(hidden, down_w, preferred_element_type=jnp.float32).astype(jnp.bfloat16), "mp"
    ).astype(jnp.float32)
    layer_out = (
        (valid_mask * (middle + mlp_out))
        .astype(jnp.bfloat16)
        .reshape(seq_count, slot_count, width_all)
    )
    grad_out = valid_mask * cotangent.reshape(tok_rows, width_all).astype(jnp.float32)
    grad_mlp = grad_out.astype(jnp.bfloat16)
    gate_back, up_back, down_back, gain_mlp_back = (
        lax.all_gather(w_gate, ("dp", "ctx"), axis=0, tiled=True),
        lax.all_gather(w_up, ("dp", "ctx"), axis=0, tiled=True),
        lax.all_gather(w_down, ("dp", "ctx"), axis=1, tiled=True),
        lax.all_gather(norm_mlp, ("dp", "ctx"), axis=0, tiled=True),
    )
    grad_hidden = jnp.einsum("tm,fm->tf", grad_mlp, down_back, preferred_element_type=jnp.float32)
    grad_down = jnp.einsum("tf,tm->fm", hidden, grad_mlp, preferred_element_type=jnp.float32)
    sigmoid_gate = jax.nn.sigmoid(gate_proj)
    grad_gate_low = (
        grad_hidden * up_proj * sigmoid_gate * (1.0 + gate_proj * (1.0 - sigmoid_gate))
    ).astype(jnp.bfloat16)
    grad_up_low = (grad_hidden * gate_proj * sigmoid_gate).astype(jnp.bfloat16)
    grad_gate = jnp.einsum(
        "td,tf->df", normed_two, grad_gate_low, preferred_element_type=jnp.float32
    )
    grad_up = jnp.einsum("td,tf->df", normed_two, grad_up_low, preferred_element_type=jnp.float32)
    partial_two = jnp.einsum(
        "tf,df->td", grad_gate_low, gate_back, preferred_element_type=jnp.float32
    ) + jnp.einsum("tf,df->td", grad_up_low, up_back, preferred_element_type=jnp.float32)
    grad_normed_two = lax.psum(partial_two, "mp")
    grad_middle_norm, grad_gain_two = norm_back(
        middle, gain_mlp_back.astype(jnp.float32), grad_normed_two
    )
    mlp_grads = (
        lax.psum_scatter(grad_gate, ("dp", "ctx"), scatter_dimension=0, tiled=True),
        lax.psum_scatter(grad_up, ("dp", "ctx"), scatter_dimension=0, tiled=True),
        lax.psum_scatter(grad_down, ("dp", "ctx"), scatter_dimension=1, tiled=True),
        lax.psum_scatter(grad_gain_two, ("dp", "ctx"), scatter_dimension=0, tiled=True),
    )
    grad_middle = grad_out + grad_middle_norm
    grad_branch = grad_middle.astype(jnp.bfloat16)
    query_back, key_back, value_back, output_back, gain_attn_back = (
        lax.all_gather(w_query, ("dp", "ctx"), axis=0, tiled=True),
        lax.all_gather(w_key, ("dp", "ctx"), axis=0, tiled=True),
        lax.all_gather(w_value, ("dp", "ctx"), axis=0, tiled=True),
        lax.all_gather(w_output, ("dp", "ctx"), axis=1, tiled=True),
        lax.all_gather(norm_attn, ("dp", "ctx"), axis=0, tiled=True),
    )
    grad_output = jnp.einsum("tq,td->qd", attn_low, grad_branch, preferred_element_type=jnp.float32)
    grad_attn_low = (
        jnp.einsum("td,qd->tq", grad_branch, output_back, preferred_element_type=jnp.float32)
        .astype(jnp.bfloat16)
        .reshape(seq_count, slot_count, q_heads, HEAD)
    )

    def attend_back(members):
        query_seq, key_seq, value_seq, length, log_seq, grad_seq = members
        scores = masked_scores(query_seq, key_seq, length, places, kv_heads, group_size)
        attention = jnp.exp(scores - log_seq[..., None])
        query_grp = query_seq.reshape(slot_count, kv_heads, group_size, HEAD)
        key_grp = key_seq.reshape(key_seq.shape[0], kv_heads, HEAD)
        value_grp = value_seq.reshape(value_seq.shape[0], kv_heads, HEAD)
        grad_grp = grad_seq.reshape(slot_count, kv_heads, group_size, HEAD)
        grad_attention = jnp.einsum(
            "bkgh,tkh->kgbt", grad_grp, value_grp, preferred_element_type=jnp.float32
        )
        inner = jnp.sum(attention * grad_attention, axis=-1, keepdims=True)
        grad_scores = (attention * (grad_attention - inner)).astype(jnp.bfloat16)
        scale_qk = HEAD ** (-0.5)
        grad_query_seq = (
            jnp.einsum("kgbt,tkh->bkgh", grad_scores, key_grp, preferred_element_type=jnp.float32)
            * scale_qk
        )
        grad_key_seq = (
            jnp.einsum("kgbt,bkgh->tkh", grad_scores, query_grp, preferred_element_type=jnp.float32)
            * scale_qk
        )
        grad_value_seq = jnp.einsum(
            "kgbt,bkgh->tkh",
            attention.astype(jnp.bfloat16),
            grad_grp,
            preferred_element_type=jnp.float32,
        )
        key_rows = key_grp.shape[0]
        return (
            grad_query_seq.reshape(slot_count, q_heads, HEAD),
            grad_key_seq.reshape(key_rows, kv_heads * HEAD),
            grad_value_seq.reshape(key_rows, kv_heads * HEAD),
        )

    grad_query_rot, grad_key_all, grad_value_all = lax.map(
        attend_back, (query_low, key_all, value_all, lengths, log_total, grad_attn_low)
    )
    grad_key_rot, grad_value_rot = (
        lax.psum_scatter(grad_key_all, "ctx", scatter_dimension=1, tiled=True),
        lax.psum_scatter(grad_value_all, "ctx", scatter_dimension=1, tiled=True),
    )
    grad_query_low = (
        rotate_back(grad_query_rot, cosine, sine_table)
        .astype(jnp.bfloat16)
        .reshape(tok_rows, q_heads * HEAD)
    )
    grad_key_low = (
        rotate_back(grad_key_rot.reshape(seq_count, slot_count, kv_heads, HEAD), cosine, sine_table)
        .astype(jnp.bfloat16)
        .reshape(tok_rows, kv_heads * HEAD)
    )
    grad_value_low = grad_value_rot.astype(jnp.bfloat16).reshape(tok_rows, kv_heads * HEAD)
    grad_query = jnp.einsum(
        "td,tq->dq", normed_one, grad_query_low, preferred_element_type=jnp.float32
    )
    grad_key = jnp.einsum("td,tq->dq", normed_one, grad_key_low, preferred_element_type=jnp.float32)
    grad_value = jnp.einsum(
        "td,tq->dq", normed_one, grad_value_low, preferred_element_type=jnp.float32
    )
    partial_one = jnp.einsum(
        "tq,dq->td", grad_query_low, query_back, preferred_element_type=jnp.float32
    )
    partial_one = partial_one + jnp.einsum(
        "tq,dq->td", grad_key_low, key_back, preferred_element_type=jnp.float32
    )
    partial_one = partial_one + jnp.einsum(
        "tq,dq->td", grad_value_low, value_back, preferred_element_type=jnp.float32
    )
    grad_normed_one = lax.psum(partial_one, "mp")
    grad_inputs_norm, grad_gain_one = norm_back(
        inputs, gain_attn_back.astype(jnp.float32), grad_normed_one
    )
    input_grad = (
        (grad_middle + grad_inputs_norm)
        .astype(jnp.bfloat16)
        .reshape(seq_count, slot_count, width_all)
    )
    attn_grads = (
        lax.psum_scatter(grad_query, ("dp", "ctx"), scatter_dimension=0, tiled=True),
        lax.psum_scatter(grad_key, ("dp", "ctx"), scatter_dimension=0, tiled=True),
        lax.psum_scatter(grad_value, ("dp", "ctx"), scatter_dimension=0, tiled=True),
        lax.psum_scatter(grad_output, ("dp", "ctx"), scatter_dimension=1, tiled=True),
        lax.psum_scatter(grad_gain_one, ("dp", "ctx"), scatter_dimension=0, tiled=True),
    )
    return (
        layer_out,
        input_grad,
        attn_grads[4],
        attn_grads[0],
        attn_grads[1],
        attn_grads[2],
        attn_grads[3],
        mlp_grads[3],
        mlp_grads[0],
        mlp_grads[1],
        mlp_grads[2],
    )


SPLIT = 2
GROUP = 384
NT = (((1,), (1,)), ((), ()))
TN = (((0,), (0,)), ((), ()))
MESH = pl.DeviceIdType.MESH


def remote(src, dst, sems, index, device):
    return pltpu.make_async_remote_copy(
        src_ref=src,
        dst_ref=dst,
        send_sem=sems.at[(0, *index)],
        recv_sem=sems.at[(1, *index)],
        device_id=device,
        device_id_type=MESH,
    )


def rows_at(start, size):
    return pl.ds(pl.multiple_of(start, 16), size)


def lanes_at(start, size):
    return pl.ds(pl.multiple_of(start, 128), size)


def chosen(rows, columns, first_column):
    row = lax.broadcasted_iota(jnp.int32, (rows, columns), 0)
    column = lax.broadcasted_iota(jnp.int32, (rows, columns), 1)
    return (row == column - first_column).astype(jnp.bfloat16)


def masked(keys, queries, length, block, first_query):
    scores = jnp.dot(keys, queries, preferred_element_type=jnp.float32) * HEAD ** (-0.5)
    rows, columns = scores.shape
    key_slots = block * rows + lax.broadcasted_iota(jnp.int32, scores.shape, 0)
    query_slots = first_query + lax.broadcasted_iota(jnp.int32, scores.shape, 1)
    return jnp.where((key_slots <= query_slots) & (key_slots < length), scores, NEG)


class Place:
    def __init__(self, owned, width):
        self.x, self.ctx, self.z = (lax.axis_index(name) for name in ("dp", "ctx", "mp"))
        self.core = lax.rem(self.ctx, 2)
        self.y = (self.ctx - self.core) // 2
        self.last = lax.axis_size("mp") - 1
        self.owned, self.rows, self.width = owned, owned * (self.last + 1), width
        self.step = width // SPLIT
        self.size, self.middle = width // 4, width // 8
        self.above, self.below = (self.x, self.ctx, self.z + 1), (self.x, self.ctx, self.z - 1)
        self.plane = {
            (turn, flip): self.turned(turn, flip)
            for turn in range(4)
            for flip in range(2)
            if turn or flip
        }
        self.sibling, self.over_x, self.over_y = (
            self.plane[key] for key in ((0, 1), (2, 0), (1, 0))
        )
        self.diagonal = self.plane[3, 0]
        self.column = [
            (self.x, self.other_core(flip), lax.rem(self.z + turn, self.last + 1))
            for turn in range(self.last + 1)
            for flip in range(2)
            if turn or flip
        ]

    def other_core(self, flip):
        return self.ctx + 1 - 2 * self.core if flip else self.ctx

    def turned(self, turn, flip):
        x_to = 1 - self.x if turn >= 2 else self.x
        y_to = 1 - self.y if turn % 2 else self.y
        core_to = 1 - self.core if flip else self.core
        return (x_to, 2 * y_to + core_to, self.z)

    def greet(self):
        for device in list(self.plane.values()) + self.column[1:]:
            pl.semaphore_signal(
                pltpu.get_barrier_semaphore(), inc=1, device_id=device, device_id_type=MESH
            )

    def enter(self):
        pl.semaphore_wait(pltpu.get_barrier_semaphore(), len(self.plane) + len(self.column) - 1)

    def span(self, half):
        size = self.owned if half is None else self.owned // 2
        return (half or 0) * size, size

    def block_of(self, core, block, half=None):
        first, size = self.span(half)
        return rows_at(core * self.rows + block * self.owned + first, size)

    def block(self, at, half=None):
        first, size = self.span(half)
        return rows_at(at * self.owned + first, size)

    def inner(self, half):
        return pl.ds(*self.span(half))

    def mine(self, half=None):
        return self.block_of(self.core, self.z, half)

    def columns(self, piece):
        return pl.ds(piece * self.step, self.step)

    def far(self, sign):
        return self.z if sign == 1 else self.last - self.z

    def target(self, sign, step):
        return self.z + sign * (self.last - step)

    def held_groups(self, core, x, groups):
        count = jnp.where(core == x, (groups + 1) // 2, groups // 2)
        return count, jnp.where(x == 1, groups - count, 0)

    def cut(self, turn):
        return slice(turn * self.size, (turn + 1) * self.size)

    def source(self, turn):
        x_to = 1 - self.x if turn >= 2 else self.x
        y_to = 1 - self.y if turn % 2 else self.y
        return lanes_at((2 * x_to + y_to) * self.size, self.size)


class SumChain:
    def __init__(
        self, place, part, held, ins, core_sem, up_sem, down_sem, extra=None, half=None
    ):
        self.place, self.part, self.held, self.ins, self.extra = place, part, held, ins, extra
        self.half, self.inner = half, place.inner(half)
        self.ways = ((place.above, 0, up_sem, 1), (place.below, place.last, down_sem, -1))
        self.core_sem = core_sem

    def across(self, block):
        place = self.place
        return remote(
            self.part.at[place.block_of(1 - place.core, block, self.half)],
            self.held.at[place.block(block, self.half)],
            self.core_sem,
            (block,),
            place.sibling,
        )

    def open(self):
        for block in range(self.place.last + 1):
            self.across(block).start()

    def wait(self, at):
        self.across(at).wait_recv()
        if self.extra is not None:
            self.extra.cross(at).wait_recv()

    def own(self, at, cols):
        place = self.place
        mine = self.part[place.block_of(place.core, at, self.half), cols].astype(jnp.float32)
        mine = mine + self.held[place.block(at, self.half), cols].astype(jnp.float32)
        if self.extra is not None:
            mine = mine + self.extra.came(at)[:, cols].astype(jnp.float32)
        return mine

    def hop(self, way, step, piece, at):
        place = self.place
        cols = place.columns(piece)
        return remote(
            self.part.at[place.block_of(place.core, at, self.half), cols],
            self.ins.at[way[1] + step, self.inner, cols],
            way[2],
            (step, piece),
            way[0],
        )

    def step(self, step):
        place = self.place
        for way in self.ways:

            @pl.when(place.far(way[3]) <= step)
            def _(way=way):
                at = place.target(way[3], step)
                rows = place.block_of(place.core, at, self.half)
                self.wait(at)
                for piece in range(SPLIT):
                    cols = place.columns(piece)
                    total = self.own(at, cols)
                    if step:

                        @pl.when(place.far(way[3]) > 0)
                        def _(total=total, cols=cols, piece=piece):
                            self.hop(way, step - 1, piece, at).wait_recv()
                            got = self.ins[way[1] + step - 1, self.inner, cols].astype(jnp.float32)
                            self.part[rows, cols] = (total + got).astype(self.part.dtype)

                        @pl.when(place.far(way[3]) == 0)
                        def _(total=total, cols=cols):
                            self.part[rows, cols] = total.astype(self.part.dtype)

                    else:
                        self.part[rows, cols] = total.astype(self.part.dtype)
                    self.hop(way, step, piece, at).start()

    def close(self, result):
        place = self.place
        final = place.last - 1
        self.wait(place.z)
        result = result.at[self.inner]
        result[...] = self.own(place.z, slice(None))
        for way in self.ways:

            @pl.when(place.far(way[3]) > 0)
            def _(way=way):
                for piece in range(SPLIT):
                    self.hop(way, final, piece, place.z).wait_recv()
                result[...] += self.ins[way[1] + final, self.inner].astype(jnp.float32)

    def drain(self):
        place = self.place
        for block in range(place.last + 1):
            self.across(block).wait_send()
        for step in range(place.last):
            for way in self.ways:

                @pl.when(place.far(way[3]) <= step)
                def _(way=way, step=step):
                    for piece in range(SPLIT):
                        self.hop(way, step, piece, place.target(way[3], step)).wait_send()


class CrossSum:
    def __init__(self, place, part, held, came, core_sem, x_sem, half=None):
        self.place, self.part, self.held = place, part, held
        self.came = lambda at: came(at, place.inner(half))
        self.core_sem, self.x_sem, self.half = core_sem, x_sem, half

    def across(self, block):
        place = self.place
        return remote(
            self.part.at[place.block_of(1 - place.core, block, self.half)],
            self.held.at[place.block(block, self.half)],
            self.core_sem,
            (block,),
            place.sibling,
        )

    def cross(self, at):
        place = self.place
        return remote(
            self.part.at[place.block_of(place.core, at, self.half)],
            self.came(at),
            self.x_sem,
            (at,),
            place.over_x,
        )

    def open(self):
        for block in range(self.place.last + 1):
            self.across(block).start()

    def send(self):
        place = self.place

        def one(at):
            self.across(at).wait_recv()
            rows = place.block_of(place.core, at, self.half)
            total = self.part[rows].astype(jnp.float32)
            total = total + self.held[place.block(at, self.half)].astype(jnp.float32)
            self.part[rows] = total.astype(self.part.dtype)
            self.cross(at).start()

        for step in range(place.last):
            for sign in (1, -1):

                @pl.when(place.far(sign) <= step)
                def _(sign=sign):
                    one(place.target(sign, step))

        one(place.z)

    def drain(self):
        for block in range(self.place.last + 1):
            self.across(block).wait_send()
            self.cross(block).wait_send()


class ShareChain:
    def __init__(self, place, whole, up_sem, down_sem, core_sem=None, half=None):
        self.place, self.whole, self.core_sem, self.half = place, whole, core_sem, half
        self.ways = ((place.above, up_sem, 1), (place.below, down_sem, -1))

    def rows(self, at):
        place = self.place
        if self.core_sem is None:
            return place.block(at, self.half)
        return place.block_of(place.core, at, self.half)

    def hop(self, way, step, piece, origin):
        ref = self.whole.at[self.rows(origin), self.place.columns(piece)]
        return remote(ref, ref, way[1], (step, piece), way[0])

    def across(self, origin, core):
        ref = self.whole.at[self.place.block_of(core, origin, self.half)]
        return remote(ref, ref, self.core_sem, (origin,), self.place.sibling)

    def step(self, step):
        place = self.place
        for way in self.ways:
            origin = place.z - way[2] * step

            @pl.when(place.far(way[2]) >= step)
            def _(way=way, origin=origin):
                for piece in range(SPLIT):
                    if step:
                        self.hop(way, step - 1, piece, origin).wait_recv()
                    if step < place.last:

                        @pl.when(place.far(way[2]) < place.last)
                        def _(piece=piece):
                            self.hop(way, step, piece, origin).start()

                if step and self.core_sem is not None:
                    self.across(origin, place.core).start()

        if step == 0 and self.core_sem is not None:
            self.across(place.z, place.core).start()

    def reached(self, step):
        place = self.place
        if step == 0:
            return [(place.z >= 0, place.z)]
        return [(place.far(sign) >= step, place.z - sign * step) for sign in (1, -1)]

    def arrive(self):
        if self.core_sem is not None:
            for origin in range(self.place.last + 1):
                self.across(origin, 1 - self.place.core).wait_recv()

    def drain(self):
        place = self.place
        for step in range(place.last):
            for way in self.ways:

                @pl.when((place.far(way[2]) >= step) & (place.far(way[2]) < place.last))
                def _(way=way, step=step):
                    for piece in range(SPLIT):
                        self.hop(way, step, piece, place.z - way[2] * step).wait_send()

        if self.core_sem is not None:
            for origin in range(place.last + 1):
                self.across(origin, place.core).wait_send()


class AttnGather:
    def __init__(self, place, w, first, by_y, by_x, x_sem, y_sem, far_sem, index):
        self.place, self.w, self.index = place, w, index
        self.sems = (x_sem, y_sem, far_sem)
        self.halves = (pl.ds(first, by_y), pl.ds(first + by_y, by_x))

    def cross(self, half, to_x):
        place, rows = self.place, self.halves[half]
        return remote(
            self.w.at[0, rows],
            self.w.at[2 if to_x else 1, rows],
            self.sems[0] if to_x else self.sems[1],
            (self.index + half,),
            place.over_x if to_x else place.over_y,
        )

    def relay(self, to_x):
        place, half = self.place, 1 if to_x else 0
        rows = self.halves[half]
        return remote(
            self.w.at[1 if to_x else 2, rows],
            self.w.at[3, rows],
            self.sems[2],
            (self.index + half,),
            place.over_x if to_x else place.over_y,
        )

    def send(self, which):
        self.cross(which, True).start()
        self.cross(1 - which, False).start()

    def pass_on(self):
        self.cross(0, True).wait_recv()
        self.relay(False).start()
        self.cross(1, False).wait_recv()
        self.relay(True).start()

    def drain(self):
        for half in range(2):
            for to_x in (True, False):
                self.cross(half, to_x).wait_send()
        self.relay(True).wait_send()
        self.relay(False).wait_send()


class WideGather:
    def __init__(self, place, block, w, x_sem, y_sem, far_sem):
        self.place, self.block, self.w = place, block, w
        self.x_sem, self.y_sem, self.far_sem = x_sem, y_sem, far_sem
        self.groups = block.shape[1] // GROUP
        self.most = (self.groups + 1) // 2
        self.count, self.base = place.held_groups(place.core, place.x, self.groups)
        self.other_count, self.other_base = place.held_groups(
            place.core, 1 - place.x, self.groups
        )

    def cross_x(self, group):
        return remote(
            self.block.at[:, lanes_at((self.other_base + group) * GROUP, GROUP)],
            self.w.at[1, :, lanes_at(group * GROUP, GROUP)],
            self.x_sem,
            (group,),
            self.place.over_x,
        )

    def came_x(self, group):
        here = self.w.at[1, :, lanes_at(group * GROUP, GROUP)]
        return remote(here, here, self.x_sem, (group,), self.place.over_x)

    def cross_y(self, group):
        return remote(
            self.block.at[:, lanes_at((self.base + group) * GROUP, GROUP)],
            self.w.at[0, :, lanes_at(group * GROUP, GROUP)],
            self.y_sem,
            (group,),
            self.place.over_y,
        )

    def pass_on(self, group):
        cols = lanes_at(group * GROUP, GROUP)
        return remote(
            self.w.at[1, :, cols], self.w.at[2, :, cols], self.far_sem, (group,), self.place.over_y
        )

    def start(self):
        def body(group, carry):
            self.cross_x(group).start()
            return carry

        lax.fori_loop(0, self.other_count, body, 0)

        self.cross_y(0).start()
        self.cross_y(1).start()

    def pump(self, group):
        @pl.when(group < self.count)
        def _():
            self.came_x(group).wait_recv()
            self.pass_on(group).start()

        @pl.when(group + 2 < self.count)
        def _():
            self.cross_y(group + 2).start()

    def arrive(self, group):
        self.cross_y(group).wait_recv()
        self.pass_on(group).wait_recv()

    def rows(self, turn, group, first, size):
        if turn == 0:
            return self.block[:, lanes_at((self.base + group) * GROUP + first, size)]
        return self.w[turn - 1, :, lanes_at(group * GROUP + first, size)]

    def drain(self):
        def sent_x(group, carry):
            self.cross_x(group).wait_send()
            return carry

        def sent_y(group, carry):
            self.cross_y(group).wait_send()
            self.pass_on(group).wait_send()
            return carry

        lax.fori_loop(0, self.other_count, sent_x, 0)
        lax.fori_loop(0, self.count, sent_y, 0)


class Home:
    kinds = ("upper", "lower", "x_one", "y_two", "y_one", "x_two")

    def __init__(self, place, sources, targets, sem, cut):
        self.place, self.sem, self.cut = place, sem, cut
        self.sources, self.targets = sources, targets

    def copy(self, kind, group):
        place, index = self.place, self.kinds.index(kind)
        to_x = kind in ("upper", "x_one", "x_two")
        return remote(
            self.cut(self.sources[kind], group),
            self.cut(self.targets[kind], group),
            self.sem,
            (index, group),
            place.over_x if to_x else place.over_y,
        )

    def send(self, kinds, group):
        for kind in kinds:
            self.copy(kind, group).start()

    def arrive(self, kinds, group):
        for kind in kinds:
            self.copy(kind, group).wait_recv()

    def drain(self, group):
        for kind in self.kinds:
            self.copy(kind, group).wait_send()


class WideHome:
    kinds = ("near", "far", "cross")

    def __init__(self, place, sources, targets, sem):
        self.place, self.sources, self.targets, self.sem = place, sources, targets, sem

    def copy(self, kind, group):
        cols = lanes_at(group * GROUP, GROUP)
        return remote(
            self.sources[kind].at[:, cols],
            self.targets[kind].at[:, cols],
            self.sem,
            (self.kinds.index(kind), group),
            self.place.over_x if kind == "cross" else self.place.over_y,
        )


class Refs:
    def __init__(self, names, refs):
        for name, ref in zip(names, refs, strict=True):
            setattr(self, name, ref)


def layer_kernel(names, *refs):
    r = Refs(names, refs)
    f32, low = jnp.float32, jnp.bfloat16
    z_count = lax.axis_size("mp")
    rows, width = r.hidden.shape
    place = Place(rows // z_count, width)
    size, middle, core = place.size, place.middle, place.core
    cut = place.cut
    part_rows = r.query.shape[0]
    q_rows = r.query.shape[1] // 2
    heads = q_rows // HEAD
    qkv_rows = q_rows + 2 * HEAD
    attn_rows = qkv_rows + q_rows
    chip_rows = 2 * rows
    attn_halves = (attn_rows - chip_rows, chip_rows)
    length = r.length[0, 0]
    cos_at, sin_at = r.cos[place.y], r.sin[place.y]
    w, aw = r.w, r.aw
    ff = r.gate.shape[1] // 2
    groups = ff // 128

    both_halves = range(2)
    branch_sum = [
        SumChain(place, r.part, *r.chain_one, *r.branch_sems[3 * k : 3 * k + 3], half=k)
        for k in both_halves
    ]
    h2_share = [
        ShareChain(place, r.h2, *r.h2_sems[3 * k : 3 * k + 3], half=k) for k in both_halves
    ]
    dm_share = ShareChain(place, r.dm_x, *r.dm_x_sems)
    back_cross = [
        CrossSum(
            place,
            r.mlp_part,
            r.chain_one[0],
            lambda at, inner: r.chain_one[1].at[at, inner],
            *r.back_cross_sems[2 * k : 2 * k + 2],
            half=k,
        )
        for k in both_halves
    ]
    mlp_cross = CrossSum(
        place,
        r.h2_x,
        r.h2.at[pl.ds(0, rows)],
        lambda at, inner: r.h2.at[rows_at(rows + at * place.owned, place.owned)],
        *r.mlp_cross_sems,
    )
    back_sum = [
        SumChain(
            place,
            r.part,
            *r.chain_two,
            *r.back_sems[3 * k : 3 * k + 3],
            extra=back_cross[k],
            half=k,
        )
        for k in both_halves
    ]
    mlp_sum = SumChain(place, r.dm_x, *r.chain_one, *r.mlp_sems, mlp_cross)
    da_share = [
        ShareChain(place, r.da, *r.da_sems[3 * k : 3 * k + 3], half=k) for k in both_halves
    ]
    input_sum = [
        SumChain(place, r.part, *r.chain_two, *r.input_sems[3 * k : 3 * k + 3], half=k)
        for k in both_halves
    ]
    layer_share = ShareChain(place, r.layer_all, *r.layer_sems)
    grad_share = [
        ShareChain(place, r.grad_all, *r.grad_sems[2 * k : 2 * k + 2], half=k)
        for k in both_halves
    ]

    def each(pair, name, *args):
        for member in pair:
            getattr(member, name)(*args)

    def chained(sums, shares, end, between, late):
        ahead, behind = sums
        first, second = shares
        ahead.step(0)
        if not late:
            behind.step(0)
        between(0)
        ahead.step(1)
        if not late:
            behind.step(1)
        between(1)
        ahead.step(2)
        end(0)
        first.step(0)
        if late:
            behind.step(0)
            between(2)
            behind.step(1)
        behind.step(2)
        if not late:
            between(2)
        first.step(1)
        between(3)
        end(1)
        second.step(0)
        first.step(2)
        between(4)
        second.step(1)
        first.step(3)
        between(5)
        second.step(2)
        between(6)
        second.step(3)
        between(7)
    sems = (r.attn_x, r.attn_y, r.attn_far)
    half_q = q_rows // 32 * 16
    q_gather = AttnGather(place, aw, 0, half_q, q_rows - half_q, *sems, 0)
    out_gather = AttnGather(place, aw, qkv_rows, half_q, q_rows - half_q, *sems, 2)
    kv_gather = AttnGather(place, aw, q_rows, 2 * HEAD - 16, 16, *sems, 4)
    gather = WideGather(place, r.block, w, r.wide_x, r.wide_y, r.wide_far)
    count, base = gather.count, gather.base

    my_rows = rows_at(core * rows, rows)
    loads = [
        pltpu.make_async_copy(r.hidden, r.da.at[pl.ds(0, rows)], r.load_sem.at[0]),
        pltpu.make_async_copy(r.cotangent, r.da.at[pl.ds(rows, rows)], r.load_sem.at[1]),
    ]
    place.greet()
    for load in loads:
        load.start()
    to_lanes = chosen(part_rows, size, core * part_rows)

    def split(total):
        half = total.shape[0] // 2
        one, two = total[:half], total[half:]
        pair = jnp.where(core == 0, one, two), jnp.where(core == 0, two, one)
        return tuple(member.astype(low) for member in pair)

    def spread(tensor, dims):
        return split(lax.dot_general(tensor, to_lanes, dims, preferred_element_type=f32))

    plain = (((1,), (0,)), ((), ()))
    q_pair, k_pair, v_pair = (
        spread(r.query[...], TN),
        spread(r.key_t[...], plain),
        spread(r.value_t[...], plain),
    )
    qkv_give = r.part.at[pl.ds(0, qkv_rows), pl.ds(0, size)]
    qkv_take = r.mlp_part.at[pl.ds(0, qkv_rows), pl.ds(0, size)]
    out_give = r.part.at[pl.ds(0, q_rows), pl.ds(size, size)]
    out_take = r.mlp_part.at[pl.ds(0, q_rows), pl.ds(size, size)]
    qkv_give[...] = jnp.concatenate([q_pair[1], k_pair[1], v_pair[1]], axis=0)
    for load in loads:
        load.wait()
    hidden, cotangent = r.da.at[pl.ds(0, rows)], r.da.at[pl.ds(rows, rows)]
    slot = place.ctx * rows + lax.broadcasted_iota(jnp.int32, (rows, size), 0)
    for turn in range(4):
        block = cotangent[:, place.source(turn)].astype(f32)
        r.dm[my_rows, cut(turn)] = jnp.where(slot < length, block, 0.0).astype(low)
    row = lax.broadcasted_iota(jnp.int32, r.gains.shape, 0)
    gain_pair = [
        jnp.dot(jnp.broadcast_to(norm[...][None], (8, part_rows)), to_lanes, preferred_element_type=f32)
        for norm in (r.norm_one, r.norm_two)
    ]
    r.gains[...] = jnp.where(row == 0, gain_pair[0], jnp.where(row == 1, gain_pair[1], 0.0))
    r.gains_all[core] = r.gains[...]
    r.gain_part[...] = jnp.zeros_like(r.gain_part)

    def gain_copy(turn, flip):
        slot = 2 * turn + core
        return remote(
            r.gains, r.gains_all.at[slot], r.gain_sem, (2 * turn + flip,), place.plane[turn, flip]
        )

    place.enter()
    for turn, flip in place.plane:
        gain_copy(turn, flip).start()
    qkv_swap = remote(qkv_give, qkv_take, r.core_sem, (0,), place.sibling)
    qkv_swap.start()
    dm_cross = remote(
        r.dm.at[place.mine()], r.dm_x.at[place.mine()], r.dm_cross_sem, (0,), place.over_x
    )
    dm_cross.start()
    dm_copy = remote(r.dm.at[my_rows], r.dm.at[my_rows], r.dm_sem, (0,), place.sibling)
    dm_copy.start()

    qkv_keep = jnp.concatenate([q_pair[0], k_pair[0], v_pair[0]], axis=0)
    qkv_swap.wait_recv()
    aw[0, :qkv_rows] = qkv_keep + qkv_take[...]
    kv_gather.send(0)
    kv_gather.send(1)
    q_gather.send(0)
    q_gather.send(1)
    out_pair = spread(r.output_t[...], TN)
    out_give[...] = out_pair[1]
    out_swap = remote(out_give, out_take, r.core_sem, (1,), place.sibling)
    out_swap.start()

    def wide_copies(group, kind, source):
        from_here = lanes_at(core * ff + group * 128, 128)
        from_there = lanes_at((1 - core) * ff + group * 128, 128)
        to = lanes_at(group * GROUP + kind * 128, 128)
        owner_rows = rows_at(core * part_rows, part_rows)
        here = pltpu.make_async_copy(
            source.at[:, from_here], r.block.at[owner_rows, to], r.wide_here.at[kind, group]
        )
        there = remote(
            source.at[:, from_there],
            r.block.at[owner_rows, to],
            r.wide_there,
            (kind, group),
            place.sibling,
        )
        return here, there

    sources = (r.gate, r.up, r.down_t)

    def start_wide(group, carry):
        for kind, source in enumerate(sources):
            for copy in wide_copies(group, kind, source):
                copy.start()
        return carry

    def own_wide(group, carry):
        for kind, source in enumerate(sources):
            here, there = wide_copies(group, kind, source)
            here.wait()
            there.wait_recv()
        return carry

    for turn in range(4):
        r.inputs_own[:, cut(turn)] = r.da[place.block(place.z), place.source(turn)].astype(f32)
    out_swap.wait_recv()
    aw[0, qkv_rows:] = out_pair[0] + out_take[...]
    squares = jnp.zeros((rows, 1), f32)
    for turn in range(4):
        block = hidden[:, cut(turn)].astype(f32)
        squares += jnp.sum(block * block, axis=-1, keepdims=True)
    scale = lax.rsqrt(squares / width + EPS)
    for turn, flip in place.plane:
        gain_copy(turn, flip).wait_recv()
    for turn in range(4):
        gain = r.gains_all[2 * turn] + r.gains_all[2 * turn + 1]
        r.gain_rows[:, cut(turn)] = gain
        block = hidden[:, place.source(turn)].astype(f32)
        r.h1[my_rows, cut(turn)] = (block * scale * gain[:1]).astype(low)
    h1_copy = remote(r.h1.at[my_rows], r.h1.at[my_rows], r.h1_sem, (0,), place.sibling)
    h1_copy.start()

    qkv = r.dh2.at[pl.ds(0, qkv_rows), pl.ds(0, chip_rows)]
    q_part, kv_part = slice(0, q_rows), slice(q_rows, qkv_rows)

    def qkv_dot(turn, part):
        return lax.dot_general(
            aw[turn, part], r.h1[:, cut(turn)], NT, preferred_element_type=f32
        )

    def gathered_dot(group, part):
        group.cross(1, True).wait_recv()
        qkv[part] += qkv_dot(2, part)
        group.cross(0, False).wait_recv()
        qkv[part] += qkv_dot(1, part)
        group.relay(False).wait_recv()
        group.relay(True).wait_recv()
        qkv[part] += qkv_dot(3, part)

    h1_copy.wait_recv()
    qkv[...] = qkv_dot(0, slice(0, qkv_rows))
    kv_gather.pass_on()
    lax.fori_loop(0, groups, start_wide, 0)

    def sent_wide(group, carry):
        for kind, source in enumerate(sources):
            wide_copies(group, kind, source)[1].wait_send()
        return carry

    q_gather.pass_on()
    dm_cross.wait_recv()
    dm_share.step(0)
    gathered_dot(kv_gather, kv_part)

    def turned(first_row):
        ahead = qkv[first_row : first_row + HEAD // 2]
        behind = qkv[first_row + HEAD // 2 : first_row + HEAD]
        return jnp.concatenate(
            [ahead * cos_at - behind * sin_at, behind * cos_at + ahead * sin_at], axis=0
        )

    r.kv[place.y, :HEAD] = turned(q_rows).astype(low)
    r.kv[place.y, HEAD:] = qkv[q_rows + HEAD : qkv_rows].astype(low)
    kv_copy = remote(r.kv.at[place.y], r.kv.at[place.y], r.kv_sem, (0,), place.over_y)
    kv_copy.start()
    out_gather.send(0)
    out_gather.send(1)
    gathered_dot(q_gather, q_part)
    head_rows = [slice(head * HEAD, (head + 1) * HEAD) for head in range(heads)]
    for head in range(heads):
        r.q_t[head_rows[head]] = turned(head * HEAD).astype(low)
    dm_share.step(1)
    kv_copy.wait_recv()

    keys = [r.kv[block, :HEAD].T for block in range(2)]
    half_slots = chip_rows // 2
    query_halves = [
        (slice(half * half_slots, (half + 1) * half_slots), place.y * chip_rows + half * half_slots)
        for half in range(2)
    ]
    def head_forward(head, carry):
        at = rows_at(head * HEAD, HEAD)
        for lanes, first_query in query_halves:
            queries = r.q_t[at, lanes]
            scores = [
                masked(keys[block], queries, length, block, first_query) for block in range(2)
            ]
            top = jnp.maximum(*(jnp.max(score, axis=0, keepdims=True) for score in scores))
            exponents = [jnp.exp(score - top) for score in scores]
            total = sum(jnp.sum(exponent, axis=0, keepdims=True) for exponent in exponents)
            mixed = jnp.zeros((HEAD, half_slots), f32)
            for block in range(2):
                weights = (exponents[block] / total).astype(low)
                mixed += jnp.dot(r.kv[block, HEAD:], weights, preferred_element_type=f32)
            r.o_t[at, lanes] = mixed.astype(low)
            r.lse[pl.ds(head, 1), lanes] = top + jnp.log(total)
        return carry

    lax.fori_loop(0, heads, head_forward, 0)
    out_gather.pass_on()
    lax.fori_loop(0, groups, own_wide, 0)
    gather.start()
    dm_share.step(2)
    out_gather.cross(1, True).wait_recv()
    out_gather.cross(0, False).wait_recv()
    out_gather.relay(False).wait_recv()
    out_gather.relay(True).wait_recv()
    qkv_swap.wait_send()
    out_swap.wait_send()
    mixed_all = r.o_t[...].T
    for turn in range(4):
        r.part[:, cut(turn)] = jnp.dot(
            mixed_all, aw[turn, qkv_rows:], preferred_element_type=f32
        ).astype(low)

    each(branch_sum, "open")
    gain_two = r.gain_rows[1:2]

    def h2_cross(origin, half):
        block = place.block_of(core, origin, half)
        return remote(
            r.h2.at[block], r.h2_x.at[block], r.h2_cross_sem, (half, origin), place.over_x
        )

    def h2_across(origin, of_core, half):
        block = place.block_of(of_core, origin, half)
        return remote(
            r.h2_x.at[block], r.h2_x.at[block], r.h2_across_sem, (half, origin), place.sibling
        )

    def branch_end(half):
        inner = place.inner(half)
        branch_sum[half].close(r.middle)
        r.middle[inner] += r.inputs_own[inner]
        r.h2[place.mine(half)] = normed(r.middle[inner], gain_two).astype(low)
        h2_cross(place.z, half).start()

    def h2_on(half, step):
        for here, origin in h2_share[half].reached(step):

            @pl.when(here)
            def _(origin=origin):
                h2_cross(origin, half).start()

    def beside_branch(when):
        if when == 0:
            dm_share.step(3)
        if when == 2:
            gather.pump(0)
        if when == 3:
            h2_on(0, 1)
            gather.pump(1)
        if when == 4:
            h2_on(0, 2)
            gather.pump(2)
        if when == 5:
            h2_on(1, 1)
            h2_on(0, 3)
            gather.pump(3)
        if when == 6:
            h2_on(1, 2)
        if when == 7:
            h2_on(1, 3)

    chained(branch_sum, h2_share, branch_end, beside_branch, False)
    each(h2_share, "arrive")
    each(branch_sum, "drain")
    dm_copy.wait()
    dm_share.arrive()

    zd_rows = (slice(0, chip_rows), slice(chip_rows, 2 * chip_rows))
    tokens = ((r.h2, r.dm), (r.h2_x, r.dm_x))

    def cut_of(turn, which):
        return cut(turn ^ 2 if which else turn)

    def activate(group, which):
        left, d_left = tokens[which]
        gu = jnp.zeros((chip_rows, 256), f32)
        d_hidden = jnp.zeros((chip_rows, 128), f32)
        for turn in range(4):
            gu += jnp.dot(
                left[:, cut_of(turn, which)], gather.rows(turn, group, 0, 256), preferred_element_type=f32
            )
            d_hidden += jnp.dot(
                d_left[:, cut_of(turn, which)],
                gather.rows(turn, group, 256, 128),
                preferred_element_type=f32,
            )
        gate, up = gu[:, :128], gu[:, 128:]
        sigma = jax.nn.sigmoid(gate)
        silu = gate * sigma
        d_gate = d_hidden * up * sigma * (1.0 + gate * (1.0 - sigma))
        at = zd_rows[which]
        start = group * GROUP
        r.zd[at, lanes_at(start, 128)] = d_gate.astype(low)
        r.zd[at, lanes_at(start + 128, 128)] = (d_hidden * silu).astype(low)
        r.zd[at, lanes_at(start + 256, 128)] = (silu * up).astype(low)

    def gradients(group):
        cols = lanes_at(group * GROUP, GROUP)
        for turn in range(4):
            grad_gu = jnp.zeros((size, 256), f32)
            grad_down = jnp.zeros((size, 128), f32)
            for which, (left, d_left) in enumerate(tokens):
                at = zd_rows[which]
                grad_gu += lax.dot_general(
                    left[:, cut_of(turn, which)],
                    r.zd[at, lanes_at(group * GROUP, 256)],
                    TN,
                    preferred_element_type=f32,
                )
                grad_down += lax.dot_general(
                    d_left[:, cut_of(turn, which)],
                    r.zd[at, lanes_at(group * GROUP + 256, 128)],
                    TN,
                    preferred_element_type=f32,
                )
            if turn:
                r.tile[turn - 1, :, :256] = grad_gu.astype(low)
                r.tile[turn - 1, :, 256:] = grad_down.astype(low)
            else:
                r.tile_own[:, :256] = grad_gu
                r.tile_own[:, 256:] = grad_down
        keep = pltpu.make_async_copy(r.tile, r.stage.at[:, :, cols], r.keep_sem.at[0])
        keep_own = pltpu.make_async_copy(r.tile_own, r.own_grad.at[:, cols], r.keep_sem.at[1])
        keep.start()
        keep_own.start()
        keep.wait()
        keep_own.wait()

    def each_count(act):
        for number in sorted({groups // 2, (groups + 1) // 2}):

            @pl.when(count == number)
            def _(number=number):
                act(number)

    def summed(into, which, first, width_of, turns):
        def act(number):
            for turn in turns:
                out = jnp.zeros((chip_rows, size), f32)
                for group in range(number):
                    out += lax.dot_general(
                        r.zd[zd_rows[which], lanes_at(group * GROUP + first, width_of)],
                        gather.rows(turn, group, first, width_of),
                        NT,
                        preferred_element_type=f32,
                    )
                into[:, cut_of(turn, which)] = out.astype(low)

        each_count(act)

    home = WideHome(
        place,
        {"near": r.stage.at[0], "far": r.stage.at[2], "cross": w.at[0]},
        {"near": r.near, "far": r.far, "cross": r.crossed},
        r.home_sem,
    )

    def send_grads(group, kinds):
        for kind in kinds:
            home.copy(kind, group).start()

    def if_last(act):
        pl.when(count > least)(act)

    least = groups // 2
    gather.arrive(0)
    activate(0, 0)
    for half in both_halves:
        for origin in range(z_count):
            h2_cross(origin, half).wait_recv()
            h2_across(origin, core, half).start()
    gather.arrive(1)
    activate(1, 0)
    for half in both_halves:
        for origin in range(z_count):
            h2_across(origin, 1 - core, half).wait_recv()
    for group in range(least):
        if group > 1:
            gather.arrive(group)
            activate(group, 0)
        activate(group, 1)
    gradients(0)
    send_grads(0, ("far",))

    @if_last
    def _():
        gather.arrive(least)
        activate(least, 1)
        activate(least, 0)

    summed(r.mlp_part, 1, 0, 256, range(4))
    each(back_cross, "open")
    summed(r.part, 0, 0, 256, range(2))
    back_cross[0].send()
    summed(r.part, 0, 0, 256, range(2, 4))
    back_cross[1].send()
    each(back_sum, "open")

    def back_end(half):
        inner = place.inner(half)
        back_sum[half].close(r.d_middle)
        d_norm, d_gain = norm_back(r.middle[inner], gain_two, r.d_middle[inner])
        if half:
            d_gain = d_gain + r.gain_part[1]
        r.gain_part[1:2] = d_gain[None]
        r.d_middle[inner] = r.dm[place.mine(half)].astype(f32) + d_norm
        r.da[place.mine(half)] = r.d_middle[inner].astype(low)

    def beside_back(when):
        if when in (0, 1):
            gradients(when + 1)
            send_grads(when + 1, ("far",))
        if when == 2:

            @if_last
            def _():
                gradients(least)
                send_grads(least, ("far",))

            send_grads(0, ("near",))
            each(h2_share, "drain")
            dm_share.drain()
            lax.fori_loop(0, groups, sent_wide, 0)
            for half in both_halves:
                for origin in range(z_count):
                    h2_cross(origin, half).wait_send()
                    h2_across(origin, core, half).wait_send()
            for device in (place.sibling, place.over_x):
                quiet(r.quiet_sem, device)
            summed(r.h2_x, 1, 256, 128, range(4))
        if when == 3:
            pl.semaphore_wait(r.quiet_sem, 2)
            mlp_cross.open()
            summed(r.dm_x, 0, 256, 128, range(4))
            mlp_cross.send()
            send_grads(1, ("near",))
        if when == 4:
            quiet(r.chain_sem, place.sibling)

            @pl.when(place.z < place.last)
            def _():
                quiet(r.chain_sem, place.above)

            @pl.when(place.z > 0)
            def _():
                quiet(r.chain_sem, place.below)

        if when == 5:
            ends = jnp.where(place.z == 0, 1, 0) + jnp.where(place.z == place.last, 1, 0)
            pl.semaphore_wait(r.chain_sem, 3 - ends)
            mlp_sum.open()
            mlp_sum.step(0)
        if when == 7:
            mlp_sum.step(1)

    def quiet(sem, device):
        pl.semaphore_signal(sem, inc=1, device_id=device, device_id_type=MESH)

    chained(back_sum, da_share, back_end, beside_back, True)

    dm_cross.wait_send()
    for device in (place.over_x, place.over_y):
        pl.semaphore_signal(r.free_sem, inc=1, device_id=device, device_id_type=MESH)
    gather.drain()
    part_load = pltpu.make_async_copy(r.stage.at[1], w.at[0], r.load_sem.at[2])
    part_load.start()
    each(da_share, "arrive")
    each(back_sum, "drain")
    each(back_cross, "drain")
    do_t, d_t, kv_give = (
        r.mlp_part.at[pl.ds(0, number), pl.ds(at * chip_rows, chip_rows)]
        for at, number in enumerate((q_rows, qkv_rows, 2 * HEAD))
    )
    dk, dv = (
        [r.dh2.at[:, pl.ds(3 * 256 + 128 * at + 256 * which, HEAD)] for at in range(2)]
        for which in range(2)
    )

    d_out = jnp.zeros((q_rows, chip_rows), f32)
    for turn in range(4):
        d_out += lax.dot_general(
            aw[turn, qkv_rows:], r.da[:, cut(turn)], NT, preferred_element_type=f32
        )
    do_t[...] = d_out.astype(low)
    values = [r.kv[block, HEAD:].T for block in range(2)]
    keys = [r.kv[block, :HEAD].T for block in range(2)]
    scale = HEAD ** (-0.5)
    for ref in dk + dv:
        ref[...] = jnp.zeros(ref.shape, f32)

    def turned_back(tensor, cosine, sine):
        ahead, behind = tensor[: HEAD // 2], tensor[HEAD // 2 :]
        return jnp.concatenate(
            [ahead * cosine + behind * sine, behind * cosine - ahead * sine], axis=0
        )

    def far_load(group):
        cols = lanes_at(group * GROUP, GROUP)
        return pltpu.make_async_copy(r.far.at[:, cols], w.at[1, :, cols], r.add_sem.at[group])

    def fetch_far(group, carry):
        home.copy("far", group).wait_recv()
        far_load(group).start()
        return carry

    def send_cross(group, carry):
        cols = lanes_at(group * GROUP, GROUP)
        far_load(group).wait()
        mine = w[0, :, cols].astype(f32) + w[1, :, cols].astype(f32)
        w[0, :, cols] = mine.astype(low)
        home.copy("cross", group).start()
        return carry

    lax.fori_loop(0, count, fetch_far, 0)
    part_load.wait()
    def finish_layer():
        mlp_sum.close(r.mlp)
        slot = place.ctx * place.rows + place.z * place.owned
        slot += lax.broadcasted_iota(jnp.int32, r.middle.shape, 0)
        r.layer_all[place.block(place.z)] = jnp.where(
            slot < length, r.middle[...] + r.mlp[...], 0.0
        ).astype(low)
        layer_share.step(0)

    def head_back(head, carry):
        at = rows_at(head * HEAD, HEAD)
        for lanes, first_query in query_halves:
            queries, d_head = r.q_t[at, lanes], do_t[at, lanes]
            probs, d_probs = [], []
            inner = jnp.zeros((1, half_slots), f32)
            for block in range(2):
                scores = masked(keys[block], queries, length, block, first_query)
                prob = jnp.exp(scores - r.lse[pl.ds(head, 1), lanes])
                d_prob = jnp.dot(values[block], d_head, preferred_element_type=f32)
                inner += jnp.sum(prob * d_prob, axis=0, keepdims=True)
                probs.append(prob)
                d_probs.append(d_prob)
            d_query = jnp.zeros((HEAD, half_slots), f32)
            for block in range(2):
                d_scores = (probs[block] * (d_probs[block] - inner)).astype(low)
                dk[block][...] += (
                    lax.dot_general(d_scores, queries, NT, preferred_element_type=f32) * scale
                )
                dv[block][...] += lax.dot_general(
                    probs[block].astype(low), d_head, NT, preferred_element_type=f32
                )
                d_query += (
                    jnp.dot(r.kv[block, :HEAD], d_scores, preferred_element_type=f32) * scale
                )
            d_t[at, lanes] = turned_back(d_query, cos_at[:, lanes], sin_at[:, lanes]).astype(low)
        return carry

    mlp_sum.step(2)
    send_cross(0, 0)
    lax.fori_loop(0, heads // 2, head_back, 0)
    send_cross(1, 0)
    lax.fori_loop(heads // 2, heads, head_back, 0)

    def of_half(pair, which):
        return jnp.where(which == 0, pair[0][...], pair[1][...]).T

    kv_give[:HEAD] = of_half(dk, 1 - place.y).astype(low)
    kv_give[HEAD:] = of_half(dv, 1 - place.y).astype(low)
    kv_back = remote(kv_give, r.kv_take, r.kv_sem, (1,), place.over_y)
    kv_back.start()
    send_grads(2, ("near",))
    finish_layer()
    d_key, d_value = of_half(dk, place.y), of_half(dv, place.y)

    lax.fori_loop(2, count, send_cross, 0)
    kv_back.wait_recv()
    d_t[q_rows : q_rows + HEAD] = turned_back(
        d_key + r.kv_take[:HEAD].astype(f32), cos_at, sin_at
    ).astype(low)
    d_t[q_rows + HEAD :] = (d_value + r.kv_take[HEAD:].astype(f32)).astype(low)
    d_qkv = d_t[...].T
    for turn in range(4):
        r.part[:, cut(turn)] = jnp.dot(
            d_qkv, aw[turn, :qkv_rows], preferred_element_type=f32
        ).astype(low)

    each(input_sum, "open")

    def view(ref, at, half):
        return ref.at[pl.ds(0, attn_halves[half]), pl.ds(at * size, size)]

    def zd_view(at, half):
        return r.zd.at[pl.ds(at // 2 * chip_rows, attn_halves[half]), pl.ds(at % 2 * size, size)]

    far_kinds, straight_kinds, last_kinds = (
        ("upper", "lower"),
        ("x_one", "y_two"),
        ("y_one", "x_two"),
    )
    stage = {
        (turn, half): view(*((r.h2, 2 * (turn - 1) + half) if turn < 3 else (r.dm, half)), half)
        for turn in (1, 2, 3)
        for half in range(2)
    }
    attn_own = [view(r.dh2, 2 + half, half) for half in range(2)]
    attn_home = Home(
        place,
        {
            "upper": stage[3, 0],
            "lower": stage[3, 1],
            "x_one": stage[2, 0],
            "y_two": stage[1, 1],
            "y_one": stage[1, 0],
            "x_two": stage[2, 1],
        },
        {
            "upper": zd_view(0, 0),
            "lower": zd_view(1, 1),
            "x_one": zd_view(2, 0),
            "y_two": zd_view(3, 1),
            "y_one": view(r.dm, 2, 0),
            "x_two": view(r.dm, 3, 1),
        },
        r.attn_home_sem,
        lambda ref, group: ref,
    )
    def attn_gradients(turn):
        grad = jnp.dot(d_t[...], r.h1[:, cut(turn)], preferred_element_type=f32)
        grad_o = jnp.dot(r.o_t[...], r.da[:, cut(turn)], preferred_element_type=f32)
        top, bottom = (stage[turn, 0], stage[turn, 1]) if turn else attn_own
        first_rows = attn_halves[0]
        left_over = qkv_rows - first_rows
        top[...] = grad[:first_rows].astype(top.dtype)
        bottom[:left_over] = grad[first_rows:].astype(top.dtype)
        bottom[left_over:] = grad_o.astype(top.dtype)

    def input_end(half):
        inner = place.inner(half)
        input_sum[half].close(r.middle)
        d_norm, d_gain = norm_back(r.inputs_own[inner], r.gain_rows[0:1], r.middle[inner])
        if half:
            d_gain = d_gain + r.gain_part[0]
        r.gain_part[0:1] = d_gain[None]
        r.grad_all[place.block(place.z, half)] = (r.d_middle[inner] + d_norm).astype(low)

    def beside_input(when):
        if when == 0:
            pl.semaphore_wait(r.free_sem, 2)
            attn_gradients(3)
            attn_home.send(far_kinds, 0)
            attn_gradients(2)
            attn_gradients(1)
            layer_share.step(1)
        if when == 1:
            attn_gradients(0)
            attn_home.send(straight_kinds, 0)

            @if_last
            def _():
                send_grads(least, ("near",))

        if when == 2:
            final_start(0)
            layer_share.step(2)
        if when == 3:
            finish(0)
            finish(1)
            finish(2)
        if when == 4:
            start_gains()
            layer_share.step(3)
            finish(3)
        if when == 5:
            finish(4)
            attn_second()
        if when == 6:
            finish(5)
            for group in range(least):
                home.copy("far", group).wait_send()
                home.copy("near", group).wait_send()

            @if_last
            def _():
                home.copy("far", least).wait_send()
                home.copy("near", least).wait_send()

            q_gather.drain()
            kv_gather.drain()
            out_gather.drain()
        if when == 7:
            finish(6)
            finish(7)

    plane_gains = [
        remote(
            r.gain_part.at[:, pl.ds(turn * size, size)],
            r.gain_in.at[turn - 1],
            r.plane_gain_sem,
            (turn - 1,),
            place.plane[turn, 0],
        )
        for turn in (1, 2, 3)
    ]

    def start_gains():
        for copy in plane_gains:
            copy.start()

    top_half, low_half = pl.ds(0, middle), pl.ds(middle, middle)
    slots = (
        (r.tile_own.at[top_half], r.tile_own.at[low_half]),
        (r.dh2.at[top_half, pl.ds(0, GROUP)], r.dh2.at[top_half, pl.ds(GROUP, GROUP)]),
    )
    halves = (top_half, low_half)
    items = [("own", 0), ("own", 1), ("cross", 0), ("cross", 1)]
    items += [("cross", 2), ("own", 2), ("cross", 3), ("own", 3)]

    def guarded(index, act):
        kind, group = items[index]
        limit = count if kind == "own" else gather.other_count
        if group < groups // 2:
            act()
        else:
            pl.when(group < limit)(act)

    def final_loads(index):
        kind, group = items[index]
        cols = pl.ds(group * GROUP, GROUP)
        if kind == "own":
            for half in range(2):
                yield pltpu.make_async_copy(
                    r.own_grad.at[halves[half], cols],
                    slots[index % 2][half],
                    r.final_sem.at[half, index],
                )
            yield pltpu.make_async_copy(
                r.near.at[:, cols], w.at[2, :, cols], r.final_sem.at[2, index]
            )
        else:
            yield pltpu.make_async_copy(
                r.crossed.at[:, cols], w.at[1, :, cols], r.final_sem.at[2, index]
            )

    def final_out(index):
        kind, group = items[index]
        first = base if kind == "own" else gather.other_base
        to = lanes_at(core * ff + (first + group) * 128, 128)
        for which, into in enumerate((r.grad_gate, r.grad_up, r.grad_down)):
            cols = pl.ds(which * 128, 128)
            for half in range(2):
                source = slots[index % 2][half].at[:, cols]
                yield (
                    half,
                    pltpu.make_async_copy(
                        source, into.at[:, to], r.out_here.at[which, first + group]
                    ),
                    remote(
                        source, into.at[:, to], r.out_there, (which, first + group), place.sibling
                    ),
                )

    def final_start(index):
        def act():
            kind, group = items[index]
            home.copy("near" if kind == "own" else "cross", group).wait_recv()
            for load in final_loads(index):
                load.start()

        guarded(index, act)

    def final_sum(index):
        def act():
            kind, group = items[index]
            cols = pl.ds(group * GROUP, GROUP)
            for load in final_loads(index):
                load.wait()
            for half in range(2):
                if kind == "own":
                    slots[index % 2][half][...] += w[2, halves[half], cols].astype(f32)
                else:
                    slots[index % 2][half][...] = w[1, halves[half], cols].astype(f32)
            for half, here, there in final_out(index):

                @pl.when(core == half)
                def _(here=here):
                    here.start()

                @pl.when(core != half)
                def _(there=there):
                    there.start()

        guarded(index, act)

    def final_free(index):
        def act():
            for half, here, there in final_out(index):

                @pl.when(core == half)
                def _(here=here):
                    here.wait()

                @pl.when(core != half)
                def _(there=there):
                    there.wait_send()

        guarded(index, act)

    def finish(index):
        final_sum(index)
        if index:
            final_free(index - 1)
        if index + 1 < len(items):
            final_start(index + 1)

    def attn_second():
        attn_home.arrive(far_kinds, 0)
        for turn, half, kind in ((1, 0, "upper"), (2, 1, "lower")):
            mine = stage[turn, half]
            mine[...] = (
                mine[...].astype(f32) + attn_home.targets[kind][...].astype(f32)
            ).astype(low)
        attn_home.send(last_kinds, 0)

    chained(input_sum, grad_share, input_end, beside_input, False)
    for copy in plane_gains:
        copy.wait_recv()
    r.gain_sum[...] = r.gain_part[:, :size] + r.gain_in[0] + r.gain_in[1] + r.gain_in[2]
    column_gains = [
        remote(r.gain_sum, r.gain_all.at[index], r.column_gain_sem, (index,), device)
        for index, device in enumerate(place.column)
    ]
    for copy in column_gains:
        copy.start()
    attn_home.arrive(straight_kinds + last_kinds, 0)
    attn_own[0][...] += attn_home.targets["x_one"][...].astype(f32) + attn_home.targets["y_one"][
        ...
    ].astype(f32)
    attn_own[1][...] += attn_home.targets["x_two"][...].astype(f32) + attn_home.targets["y_two"][
        ...
    ].astype(f32)
    attn_out = []
    for half in range(2):
        to = pl.ds(half * attn_halves[0], attn_halves[half])
        attn_out.append(
            pltpu.make_async_copy(attn_own[half], r.grad_attn.at[core, to], r.out_attn.at[half])
        )
        attn_out.append(
            remote(
                attn_own[half], r.grad_attn.at[core, to], r.swap_attn, (half,), place.sibling
            )
        )
    for copy in attn_out:
        copy.start()
    gain_total = r.gain_sum[...]
    for index, copy in enumerate(column_gains):
        copy.wait_recv()
        gain_total += r.gain_all[index]
    r.gain_out[...] = gain_total

    final_free(len(items) - 1)

    def settle(group, carry):
        for kind in range(len(sources)):
            to = lanes_at(core * ff + group * 128, 128)
            into = (r.grad_gate, r.grad_up, r.grad_down)[kind]
            remote(
                r.tile_own.at[top_half, pl.ds(0, 128)],
                into.at[:, to],
                r.out_there,
                (kind, group),
                place.sibling,
            ).wait_recv()
        return carry

    def sent_home(group, carry):
        home.copy("cross", group).wait_send()
        return carry

    lax.fori_loop(0, groups, settle, 0)
    lax.fori_loop(0, count, sent_home, 0)
    for copy in attn_out:
        copy.wait()
    attn_home.drain(0)
    for copy in (kv_copy, kv_back, h1_copy, *plane_gains, *column_gains):
        copy.wait_send()
    for turn, flip in place.plane:
        gain_copy(turn, flip).wait_send()
    for chain in (*input_sum, mlp_sum, mlp_cross, *da_share, layer_share, *grad_share):
        chain.drain()


class Lists:
    def __init__(self):
        self.names, self.items = [], []

    def add(self, name, item):
        self.names.append(name)
        self.items.append(item)


def grouped_kernel(names, counts, *refs):
    given, at = [], 0
    for count in counts:
        given.append(refs[at] if count is None else refs[at : at + count])
        at += count or 1
    layer_kernel(names, *given)


def finish_kernel(
    layer_all,
    grad_all,
    gains,
    gate,
    up,
    down,
    attn,
    layer_out,
    input_grad,
    gain_one,
    gain_two,
    query,
    key_t,
    value_t,
    output_t,
    gate_out,
    up_out,
    down_out,
    attn_here,
    layer_here,
    grad_here,
    gate_here,
    up_here,
    down_here,
    in_sem,
    out_sem,
):
    part = key_t.shape[1]
    place = 2 * lax.axis_index("dp") + lax.axis_index("ctx") // 2
    first = lax.rem(lax.axis_index("ctx"), 2) == 0
    size = 2 * part
    here = (attn_here, layer_here, grad_here, gate_here, up_here, down_here)
    loads = [
        pltpu.make_async_copy(source, into, in_sem.at[index])
        for index, (source, into) in enumerate(
            zip((attn, layer_all, grad_all, gate, up, down), here, strict=True)
        )
    ]
    for load in loads:
        load.start()
    stores = []

    def store(source, into):
        stores.append(pltpu.make_async_copy(source, into, out_sem.at[len(stores)]))
        stores[-1].start()

    def own(tensor):
        return jnp.where(first, tensor[:, :part], tensor[:, part:])

    mine = own(gains[...])
    gain_one[...], gain_two[...] = mine[0], mine[1]
    loads[0].wait()
    q_rows = query.shape[1] // 2
    start = 0
    for into, size_of in ((query, q_rows), (key_t, HEAD), (value_t, HEAD), (output_t, q_rows)):
        rows = slice(start, start + size_of)
        start += size_of
        both = jnp.concatenate([own(attn_here[which, rows]) for which in range(2)], axis=0)
        into[...] = both if size_of == HEAD else both.T
    for index, into in ((1, layer_out), (2, input_grad)):
        loads[index].wait()
        for turn in range(4):
            at = lanes_at((place ^ turn) * size, size)
            store(here[index].at[:, turn * size : (turn + 1) * size], into.at[:, at])
    for index, into in ((3, gate_out), (4, up_out), (5, down_out)):
        loads[index].wait()
        store(here[index], into)
    for copy in stores:
        copy.wait()


def on_plane(
    hidden_in,
    cotangent,
    lengths,
    norm_attn,
    w_query,
    w_key,
    w_value,
    w_output,
    norm_mlp,
    w_gate,
    w_up,
    w_down,
):
    low, f32 = jnp.bfloat16, jnp.float32
    _, rows, width = hidden_in.shape
    part = w_query.shape[0]
    chip_part, chip_rows = 2 * part, 2 * rows
    z_count = lax.axis_size("mp")
    owned, hops = rows // z_count, z_count - 1
    q_rows = w_query.shape[1] // 2
    qkv_rows = q_rows + 2 * HEAD
    attn_rows = qkv_rows + q_rows
    ff = w_gate.shape[1] // 2
    wide_cols = 3 * ff
    groups = wide_cols // GROUP
    most = (groups + 1) // 2
    held_cols = most * GROUP
    others = 2 * z_count - 1

    slots = np.arange(2 * chip_rows, dtype=np.float32)
    freq = np.float32(THETA) ** -(np.arange(HEAD // 2, dtype=np.float32) * 2.0 / HEAD)
    angle = (freq.astype(np.float32)[:, None] * slots[None]).reshape(HEAD // 2, 2, chip_rows)
    angle = angle.astype(np.float32).swapaxes(0, 1)
    cosine, sine = (jnp.asarray(table(angle), f32) for table in (np.cos, np.sin))

    hbm = pl.BlockSpec(memory_space=pl.ANY)
    smem = pl.BlockSpec(memory_space=pltpu.SMEM)
    vmem = pl.BlockSpec(memory_space=pltpu.VMEM)
    dma, vm = pltpu.SemaphoreType.DMA, pltpu.VMEM
    whole, own = (chip_rows, width), (owned, width)

    ins, outs, scratch = Lists(), Lists(), Lists()
    for name, value, spec in (
        ("hidden", hidden_in[0], hbm),
        ("cotangent", cotangent[0], hbm),
        ("length", lengths.reshape(1, 1), smem),
        ("norm_one", norm_attn, vmem),
        ("norm_two", norm_mlp, vmem),
        ("query", w_query, vmem),
        ("key_t", w_key.T, vmem),
        ("value_t", w_value.T, vmem),
        ("output_t", w_output.T, vmem),
        ("gate", w_gate, hbm),
        ("up", w_up, hbm),
        ("down_t", w_down.T, hbm),
        ("cos", cosine, vmem),
        ("sin", sine, vmem),
    ):
        ins.add(name, (value, spec))
    for name, shape, dtype, spec in (
        ("layer_all", (rows, width), low, vmem),
        ("grad_all", (rows, width), low, vmem),
        ("gain_out", (8, chip_part), f32, vmem),
        ("grad_gate", w_gate.shape, f32, hbm),
        ("grad_up", w_up.shape, f32, hbm),
        ("grad_down", w_gate.shape, f32, hbm),
        ("grad_attn", (2, attn_rows, chip_part), f32, hbm),
        ("own_grad", (chip_part, held_cols), f32, hbm),
        ("stage", (3, chip_part, held_cols), low, hbm),
        ("near", (chip_part, held_cols), low, hbm),
        ("far", (chip_part, held_cols), low, hbm),
        ("crossed", (chip_part, held_cols), low, hbm),
    ):
        outs.add(name, (jax.ShapeDtypeStruct(shape, dtype), spec))
    chain = [vm((rows, width), low), vm((2 * hops, *own), low)]
    ways = [dma((2, hops, SPLIT))] * 2
    cores = dma((2, z_count))
    for name, item in (
        ("block", vm((chip_part, wide_cols), low)),
        ("w", vm((3, chip_part, held_cols), low)),
        ("aw", vm((4, attn_rows, chip_part), low)),
        ("h1", vm(whole, low)),
        ("h2", vm(whole, low)),
        ("h2_x", vm(whole, low)),
        ("dm", vm(whole, low)),
        ("dm_x", vm(whole, low)),
        ("da", vm(whole, low)),
        ("part", vm(whole, low)),
        ("mlp_part", vm(whole, low)),
        ("dh2", vm(whole, f32)),
        ("zd", vm((2 * chip_rows, held_cols), low)),
        ("tile", vm((3, chip_part, GROUP), low)),
        ("tile_own", vm((chip_part, GROUP), f32)),
        ("chain_one", chain),
        ("chain_two", chain),
        ("inputs_own", vm(own, f32)),
        ("middle", vm(own, f32)),
        ("mlp", vm(own, f32)),
        ("d_middle", vm(own, f32)),
        ("gains", vm((8, chip_part), f32)),
        ("gains_all", vm((8, 8, chip_part), f32)),
        ("gain_rows", vm((8, width), f32)),
        ("kv", vm((2, 2 * HEAD, chip_rows), low)),
        ("q_t", vm((q_rows, chip_rows), low)),
        ("o_t", vm((q_rows, chip_rows), low)),
        ("lse", vm((8, chip_rows), f32)),
        ("kv_take", vm((2 * HEAD, chip_rows), low)),
        ("gain_part", vm((8, width), f32)),
        ("gain_in", vm((3, 8, chip_part), f32)),
        ("gain_sum", vm((8, chip_part), f32)),
        ("gain_all", vm((others, 8, chip_part), f32)),
        ("load_sem", dma((4,))),
        ("core_sem", dma((2, 2))),
        ("gain_sem", dma((2, 8))),
        ("attn_x", dma((2, 6))),
        ("attn_y", dma((2, 6))),
        ("attn_far", dma((2, 6))),
        ("wide_here", dma((3, groups))),
        ("wide_there", dma((2, 3, groups))),
        ("dm_sem", dma((2, 1))),
        ("h1_sem", dma((2, 1))),
        ("kv_sem", dma((2, 2))),
        ("wide_x", dma((2, most))),
        ("wide_y", dma((2, most))),
        ("wide_far", dma((2, most))),
        ("dm_cross_sem", dma((2, 1))),
        ("h2_cross_sem", dma((2, 2, z_count))),
        ("h2_across_sem", dma((2, 2, z_count))),
        ("keep_sem", dma((2,))),
        ("home_sem", dma((2, 3, most))),
        ("add_sem", dma((most,))),
        ("attn_home_sem", dma((2, 6, 1))),
        ("final_sem", dma((3, 2 * most))),
        ("out_here", dma((3, groups))),
        ("out_there", dma((2, 3, groups))),
        ("out_attn", dma((2,))),
        ("swap_attn", dma((2, 2))),
        ("plane_gain_sem", dma((2, 3))),
        ("column_gain_sem", dma((2, others))),
        ("free_sem", pltpu.SemaphoreType.REGULAR),
        ("quiet_sem", pltpu.SemaphoreType.REGULAR),
        ("chain_sem", pltpu.SemaphoreType.REGULAR),
        ("branch_sems", ([cores] + ways) * 2),
        ("back_sems", ([cores] + ways) * 2),
        ("mlp_sems", [cores] + ways),
        ("input_sems", ([cores] + ways) * 2),
        ("h2_sems", (ways + [cores]) * 2),
        ("dm_x_sems", ways + [cores]),
        ("back_cross_sems", [cores] * 4),
        ("mlp_cross_sems", [cores, cores]),
        ("da_sems", (ways + [cores]) * 2),
        ("layer_sems", ways),
        ("grad_sems", ways * 2),
    ):
        scratch.add(name, item)

    counts = [None] * (len(ins.items) + len(outs.items))
    flat = []
    for item in scratch.items:
        counts.append(len(item) if isinstance(item, list) else None)
        flat += item if isinstance(item, list) else [item]
    names = ins.names + outs.names + scratch.names
    results = pl.pallas_call(
        functools.partial(grouped_kernel, names, counts),
        out_shape=[shape for shape, _ in outs.items],
        in_specs=[spec for _, spec in ins.items],
        out_specs=[spec for _, spec in outs.items],
        scratch_shapes=flat,
        name="layer",
        compiler_params=pltpu.CompilerParams(
            collective_id=1, has_side_effects=True, vmem_limit_bytes=65_400 * 2**10
        ),
    )(*(value for value, _ in ins.items))
    layer_all, grad_all, gain_sums, grad_gate, grad_up, grad_down, grad_attn = results[:7]
    gate_like = jax.ShapeDtypeStruct(w_gate.shape, f32)
    tokens = jax.ShapeDtypeStruct((rows, width), low)
    gain_like = jax.ShapeDtypeStruct((part,), f32)
    square = jax.ShapeDtypeStruct((part, 2 * q_rows), f32)
    flat_heads = jax.ShapeDtypeStruct((2 * HEAD, part), f32)
    (
        layer_out,
        input_grad,
        gain_one,
        gain_two,
        grad_query,
        grad_key_t,
        grad_value_t,
        grad_output_t,
        grad_gate,
        grad_up,
        grad_down_t,
    ) = pl.pallas_call(
        finish_kernel,
        out_shape=[tokens] * 2
        + [gain_like] * 2
        + [square, flat_heads, flat_heads, square]
        + [gate_like] * 3,
        in_specs=[hbm, hbm, vmem, hbm, hbm, hbm, hbm],
        out_specs=[hbm] * 2 + [vmem] * 6 + [hbm] * 3,
        scratch_shapes=[vm((2, attn_rows, chip_part), f32)]
        + [vm((rows, width), low)] * 2
        + [vm(w_gate.shape, f32)] * 3
        + [dma((6,)), dma((11,))],
        name="finish",
        compiler_params=pltpu.CompilerParams(vmem_limit_bytes=65_400 * 2**10),
    )(layer_all, grad_all, gain_sums, grad_gate, grad_up, grad_down, grad_attn)
    return (
        layer_out[None],
        input_grad[None],
        gain_one,
        grad_query,
        grad_key_t.T,
        grad_value_t.T,
        grad_output_t.T,
        gain_two,
        grad_gate,
        grad_up,
        grad_down_t.T,
    )


def solution(mesh):
    plane = dict(mesh.shape) == {"dp": 2, "ctx": 4, "mp": 4}
    return jax.shard_map(
        on_plane if plane else any_mesh,
        mesh=mesh,
        in_specs=(
            P("dp", "ctx", None),
            P("dp", "ctx", None),
            P("dp"),
            P(("dp", "ctx")),
            P(("dp", "ctx"), "mp"),
            P(("dp", "ctx"), "mp"),
            P(("dp", "ctx"), "mp"),
            P("mp", ("dp", "ctx")),
            P(("dp", "ctx")),
            P(("dp", "ctx"), "mp"),
            P(("dp", "ctx"), "mp"),
            P("mp", ("dp", "ctx")),
        ),
        out_specs=(
            P("dp", "ctx", None),
            P("dp", "ctx", None),
            P(("dp", "ctx")),
            P(("dp", "ctx"), "mp"),
            P(("dp", "ctx"), "mp"),
            P(("dp", "ctx"), "mp"),
            P("mp", ("dp", "ctx")),
            P(("dp", "ctx")),
            P(("dp", "ctx"), "mp"),
            P(("dp", "ctx"), "mp"),
            P("mp", ("dp", "ctx")),
        ),
        check_vma=False,
    )
```

```python
import functools

import jax
import jax.numpy as jnp
import numpy as np
from jax import lax
from jax.experimental import pallas as pl
from jax.experimental.pallas import tpu as pltpu
from jax.sharding import PartitionSpec as P

HEAD = 80


EPS = 1e-05
THETA = 1000000.0
NEG = -1e30


def rope_tables(places, head_size):
    half = head_size // 2
    freq = THETA ** (-(jnp.arange(half, dtype=jnp.float32) * 2.0 / head_size))
    angle = places[:, None] * freq[None, :]
    return (jnp.cos(angle), jnp.sin(angle))


def rotate(tensor, cosine, sine_table):
    half = tensor.shape[-1] // 2
    first_half = tensor[..., :half]
    second_half = tensor[..., half:]
    cos_b = cosine[:, None, :]
    sin_b = sine_table[:, None, :]
    return jnp.concatenate(
        [first_half * cos_b - second_half * sin_b, second_half * cos_b + first_half * sin_b],
        axis=-1,
    )


def rotate_back(tensor, cosine, sine_table):
    half = tensor.shape[-1] // 2
    first_half = tensor[..., :half]
    second_half = tensor[..., half:]
    cos_b = cosine[:, None, :]
    sin_b = sine_table[:, None, :]
    return jnp.concatenate(
        [first_half * cos_b + second_half * sin_b, second_half * cos_b - first_half * sin_b],
        axis=-1,
    )


def normed(tensor, gain_row):
    return tensor * lax.rsqrt(jnp.mean(tensor * tensor, axis=-1, keepdims=True) + EPS) * gain_row


def norm_back(tensor, gain_row, grad_normed):
    scale_row = lax.rsqrt(jnp.mean(tensor * tensor, axis=-1, keepdims=True) + EPS)
    grad_scaled = grad_normed * gain_row
    grad_tensor = scale_row * grad_scaled - tensor * scale_row**3 * jnp.mean(
        grad_scaled * tensor, axis=-1, keepdims=True
    )
    grad_gain = jnp.sum(grad_normed * tensor * scale_row, axis=0)
    return (grad_tensor, grad_gain)


def masked_scores(query_seq, key_seq, length, places, kv_heads, group_size):
    query_grp = query_seq.reshape(query_seq.shape[0], kv_heads, group_size, HEAD)
    key_grp = key_seq.reshape(key_seq.shape[0], kv_heads, HEAD)
    raw_scores = jnp.einsum(
        "bkgh,tkh->kgbt", query_grp, key_grp, preferred_element_type=jnp.float32
    ) * HEAD ** (-0.5)
    key_places = jnp.arange(key_grp.shape[0], dtype=jnp.int32)
    allowed = (key_places[None, :] <= places[:, None]) & (key_places[None, :] < length)
    return jnp.where(allowed[None, None], raw_scores, NEG)


def any_mesh(
    hidden_in,
    cotangent,
    lengths,
    norm_attn,
    w_query,
    w_key,
    w_value,
    w_output,
    norm_mlp,
    w_gate,
    w_up,
    w_down,
):
    seq_count, slot_count, width_all = hidden_in.shape
    tok_rows = seq_count * slot_count
    attn_set = (
        lax.all_gather(w_query, ("dp", "ctx"), axis=0, tiled=True),
        lax.all_gather(w_key, ("dp", "ctx"), axis=0, tiled=True),
        lax.all_gather(w_value, ("dp", "ctx"), axis=0, tiled=True),
        lax.all_gather(w_output, ("dp", "ctx"), axis=1, tiled=True),
        lax.all_gather(norm_attn, ("dp", "ctx"), axis=0, tiled=True),
    )
    query_w, key_w, value_w, output_w, gain_attn = attn_set
    q_heads = query_w.shape[1] // HEAD
    kv_heads = key_w.shape[1] // HEAD
    group_size = q_heads // kv_heads
    first_slot = lax.axis_index("ctx") * slot_count
    places = first_slot + jnp.arange(slot_count, dtype=jnp.int32)
    valid_mask = (places[None, :] < lengths[:, None]).astype(jnp.float32).reshape(tok_rows, 1)
    cosine, sine_table = rope_tables(places.astype(jnp.float32), HEAD)
    inputs = hidden_in.reshape(tok_rows, width_all).astype(jnp.float32)
    gain_one = gain_attn.astype(jnp.float32)
    normed_one = normed(inputs, gain_one).astype(jnp.bfloat16)
    query_proj = jnp.dot(normed_one, query_w, preferred_element_type=jnp.float32).reshape(
        seq_count, slot_count, q_heads, HEAD
    )
    key_proj = jnp.dot(normed_one, key_w, preferred_element_type=jnp.float32).reshape(
        seq_count, slot_count, kv_heads, HEAD
    )
    value_low = (
        jnp.dot(normed_one, value_w, preferred_element_type=jnp.float32)
        .astype(jnp.bfloat16)
        .reshape(seq_count, slot_count, kv_heads * HEAD)
    )
    query_low = rotate(query_proj, cosine, sine_table).astype(jnp.bfloat16)
    key_low = (
        rotate(key_proj, cosine, sine_table)
        .astype(jnp.bfloat16)
        .reshape(seq_count, slot_count, kv_heads * HEAD)
    )
    key_all, value_all = (
        lax.all_gather(key_low, "ctx", axis=1, tiled=True),
        lax.all_gather(value_low, "ctx", axis=1, tiled=True),
    )

    def attend(members):
        query_seq, key_seq, value_seq, length = members
        scores = masked_scores(query_seq, key_seq, length, places, kv_heads, group_size)
        row_max = jnp.max(scores, axis=-1, keepdims=True)
        exponent = jnp.exp(scores - row_max)
        total = jnp.sum(exponent, axis=-1, keepdims=True)
        attention = (exponent / total).astype(jnp.bfloat16)
        value_grp = value_seq.reshape(value_seq.shape[0], kv_heads, HEAD)
        mixed_heads = jnp.einsum(
            "kgbt,tkh->bkgh", attention, value_grp, preferred_element_type=jnp.float32
        )
        return (mixed_heads.reshape(slot_count, q_heads * HEAD), (row_max + jnp.log(total))[..., 0])

    mixed_all, log_total = lax.map(attend, (query_low, key_all, value_all, lengths))
    attn_low = mixed_all.reshape(tok_rows, q_heads * HEAD).astype(jnp.bfloat16)
    branch = lax.psum(jnp.dot(attn_low, output_w, preferred_element_type=jnp.float32), "mp")
    middle = inputs + branch
    mlp_set = (
        lax.all_gather(w_gate, ("dp", "ctx"), axis=0, tiled=True),
        lax.all_gather(w_up, ("dp", "ctx"), axis=0, tiled=True),
        lax.all_gather(w_down, ("dp", "ctx"), axis=1, tiled=True),
        lax.all_gather(norm_mlp, ("dp", "ctx"), axis=0, tiled=True),
    )
    gate_w, up_w, down_w, gain_mlp = mlp_set
    gain_two = gain_mlp.astype(jnp.float32)
    normed_two = normed(middle, gain_two).astype(jnp.bfloat16)
    gate_proj = jnp.dot(normed_two, gate_w, preferred_element_type=jnp.float32)
    up_proj = jnp.dot(normed_two, up_w, preferred_element_type=jnp.float32)
    hidden = (jax.nn.silu(gate_proj) * up_proj).astype(jnp.bfloat16)
    mlp_out = lax.psum(
        jnp.dot(hidden, down_w, preferred_element_type=jnp.float32).astype(jnp.bfloat16), "mp"
    ).astype(jnp.float32)
    layer_out = (
        (valid_mask * (middle + mlp_out))
        .astype(jnp.bfloat16)
        .reshape(seq_count, slot_count, width_all)
    )
    grad_out = valid_mask * cotangent.reshape(tok_rows, width_all).astype(jnp.float32)
    grad_mlp = grad_out.astype(jnp.bfloat16)
    gate_back, up_back, down_back, gain_mlp_back = (
        lax.all_gather(w_gate, ("dp", "ctx"), axis=0, tiled=True),
        lax.all_gather(w_up, ("dp", "ctx"), axis=0, tiled=True),
        lax.all_gather(w_down, ("dp", "ctx"), axis=1, tiled=True),
        lax.all_gather(norm_mlp, ("dp", "ctx"), axis=0, tiled=True),
    )
    grad_hidden = jnp.einsum("tm,fm->tf", grad_mlp, down_back, preferred_element_type=jnp.float32)
    grad_down = jnp.einsum("tf,tm->fm", hidden, grad_mlp, preferred_element_type=jnp.float32)
    sigmoid_gate = jax.nn.sigmoid(gate_proj)
    grad_gate_low = (
        grad_hidden * up_proj * sigmoid_gate * (1.0 + gate_proj * (1.0 - sigmoid_gate))
    ).astype(jnp.bfloat16)
    grad_up_low = (grad_hidden * gate_proj * sigmoid_gate).astype(jnp.bfloat16)
    grad_gate = jnp.einsum(
        "td,tf->df", normed_two, grad_gate_low, preferred_element_type=jnp.float32
    )
    grad_up = jnp.einsum("td,tf->df", normed_two, grad_up_low, preferred_element_type=jnp.float32)
    partial_two = jnp.einsum(
        "tf,df->td", grad_gate_low, gate_back, preferred_element_type=jnp.float32
    ) + jnp.einsum("tf,df->td", grad_up_low, up_back, preferred_element_type=jnp.float32)
    grad_normed_two = lax.psum(partial_two, "mp")
    grad_middle_norm, grad_gain_two = norm_back(
        middle, gain_mlp_back.astype(jnp.float32), grad_normed_two
    )
    mlp_grads = (
        lax.psum_scatter(grad_gate, ("dp", "ctx"), scatter_dimension=0, tiled=True),
        lax.psum_scatter(grad_up, ("dp", "ctx"), scatter_dimension=0, tiled=True),
        lax.psum_scatter(grad_down, ("dp", "ctx"), scatter_dimension=1, tiled=True),
        lax.psum_scatter(grad_gain_two, ("dp", "ctx"), scatter_dimension=0, tiled=True),
    )
    grad_middle = grad_out + grad_middle_norm
    grad_branch = grad_middle.astype(jnp.bfloat16)
    query_back, key_back, value_back, output_back, gain_attn_back = (
        lax.all_gather(w_query, ("dp", "ctx"), axis=0, tiled=True),
        lax.all_gather(w_key, ("dp", "ctx"), axis=0, tiled=True),
        lax.all_gather(w_value, ("dp", "ctx"), axis=0, tiled=True),
        lax.all_gather(w_output, ("dp", "ctx"), axis=1, tiled=True),
        lax.all_gather(norm_attn, ("dp", "ctx"), axis=0, tiled=True),
    )
    grad_output = jnp.einsum("tq,td->qd", attn_low, grad_branch, preferred_element_type=jnp.float32)
    grad_attn_low = (
        jnp.einsum("td,qd->tq", grad_branch, output_back, preferred_element_type=jnp.float32)
        .astype(jnp.bfloat16)
        .reshape(seq_count, slot_count, q_heads, HEAD)
    )

    def attend_back(members):
        query_seq, key_seq, value_seq, length, log_seq, grad_seq = members
        scores = masked_scores(query_seq, key_seq, length, places, kv_heads, group_size)
        attention = jnp.exp(scores - log_seq[..., None])
        query_grp = query_seq.reshape(slot_count, kv_heads, group_size, HEAD)
        key_grp = key_seq.reshape(key_seq.shape[0], kv_heads, HEAD)
        value_grp = value_seq.reshape(value_seq.shape[0], kv_heads, HEAD)
        grad_grp = grad_seq.reshape(slot_count, kv_heads, group_size, HEAD)
        grad_attention = jnp.einsum(
            "bkgh,tkh->kgbt", grad_grp, value_grp, preferred_element_type=jnp.float32
        )
        inner = jnp.sum(attention * grad_attention, axis=-1, keepdims=True)
        grad_scores = (attention * (grad_attention - inner)).astype(jnp.bfloat16)
        scale_qk = HEAD ** (-0.5)
        grad_query_seq = (
            jnp.einsum("kgbt,tkh->bkgh", grad_scores, key_grp, preferred_element_type=jnp.float32)
            * scale_qk
        )
        grad_key_seq = (
            jnp.einsum("kgbt,bkgh->tkh", grad_scores, query_grp, preferred_element_type=jnp.float32)
            * scale_qk
        )
        grad_value_seq = jnp.einsum(
            "kgbt,bkgh->tkh",
            attention.astype(jnp.bfloat16),
            grad_grp,
            preferred_element_type=jnp.float32,
        )
        key_rows = key_grp.shape[0]
        return (
            grad_query_seq.reshape(slot_count, q_heads, HEAD),
            grad_key_seq.reshape(key_rows, kv_heads * HEAD),
            grad_value_seq.reshape(key_rows, kv_heads * HEAD),
        )

    grad_query_rot, grad_key_all, grad_value_all = lax.map(
        attend_back, (query_low, key_all, value_all, lengths, log_total, grad_attn_low)
    )
    grad_key_rot, grad_value_rot = (
        lax.psum_scatter(grad_key_all, "ctx", scatter_dimension=1, tiled=True),
        lax.psum_scatter(grad_value_all, "ctx", scatter_dimension=1, tiled=True),
    )
    grad_query_low = (
        rotate_back(grad_query_rot, cosine, sine_table)
        .astype(jnp.bfloat16)
        .reshape(tok_rows, q_heads * HEAD)
    )
    grad_key_low = (
        rotate_back(grad_key_rot.reshape(seq_count, slot_count, kv_heads, HEAD), cosine, sine_table)
        .astype(jnp.bfloat16)
        .reshape(tok_rows, kv_heads * HEAD)
    )
    grad_value_low = grad_value_rot.astype(jnp.bfloat16).reshape(tok_rows, kv_heads * HEAD)
    grad_query = jnp.einsum(
        "td,tq->dq", normed_one, grad_query_low, preferred_element_type=jnp.float32
    )
    grad_key = jnp.einsum("td,tq->dq", normed_one, grad_key_low, preferred_element_type=jnp.float32)
    grad_value = jnp.einsum(
        "td,tq->dq", normed_one, grad_value_low, preferred_element_type=jnp.float32
    )
    partial_one = jnp.einsum(
        "tq,dq->td", grad_query_low, query_back, preferred_element_type=jnp.float32
    )
    partial_one = partial_one + jnp.einsum(
        "tq,dq->td", grad_key_low, key_back, preferred_element_type=jnp.float32
    )
    partial_one = partial_one + jnp.einsum(
        "tq,dq->td", grad_value_low, value_back, preferred_element_type=jnp.float32
    )
    grad_normed_one = lax.psum(partial_one, "mp")
    grad_inputs_norm, grad_gain_one = norm_back(
        inputs, gain_attn_back.astype(jnp.float32), grad_normed_one
    )
    input_grad = (
        (grad_middle + grad_inputs_norm)
        .astype(jnp.bfloat16)
        .reshape(seq_count, slot_count, width_all)
    )
    attn_grads = (
        lax.psum_scatter(grad_query, ("dp", "ctx"), scatter_dimension=0, tiled=True),
        lax.psum_scatter(grad_key, ("dp", "ctx"), scatter_dimension=0, tiled=True),
        lax.psum_scatter(grad_value, ("dp", "ctx"), scatter_dimension=0, tiled=True),
        lax.psum_scatter(grad_output, ("dp", "ctx"), scatter_dimension=1, tiled=True),
        lax.psum_scatter(grad_gain_one, ("dp", "ctx"), scatter_dimension=0, tiled=True),
    )
    return (
        layer_out,
        input_grad,
        attn_grads[4],
        attn_grads[0],
        attn_grads[1],
        attn_grads[2],
        attn_grads[3],
        mlp_grads[3],
        mlp_grads[0],
        mlp_grads[1],
        mlp_grads[2],
    )


SPLIT = 2
GROUP = 384
NT = (((1,), (1,)), ((), ()))
TN = (((0,), (0,)), ((), ()))
MESH = pl.DeviceIdType.MESH


def remote(src, dst, sems, index, device):
    return pltpu.make_async_remote_copy(
        src_ref=src,
        dst_ref=dst,
        send_sem=sems.at[(0, *index)],
        recv_sem=sems.at[(1, *index)],
        device_id=device,
        device_id_type=MESH,
    )


def rows_at(start, size):
    return pl.ds(pl.multiple_of(start, 16), size)


def lanes_at(start, size):
    return pl.ds(pl.multiple_of(start, 128), size)


def chosen(rows, columns, first_column):
    row = lax.broadcasted_iota(jnp.int32, (rows, columns), 0)
    column = lax.broadcasted_iota(jnp.int32, (rows, columns), 1)
    return (row == column - first_column).astype(jnp.bfloat16)


def masked(keys, queries, length, block, first_query):
    scores = jnp.dot(keys, queries, preferred_element_type=jnp.float32) * HEAD ** (-0.5)
    rows, columns = scores.shape
    key_slots = block * rows + lax.broadcasted_iota(jnp.int32, scores.shape, 0)
    query_slots = first_query + lax.broadcasted_iota(jnp.int32, scores.shape, 1)
    return jnp.where((key_slots <= query_slots) & (key_slots < length), scores, NEG)


class Place:
    def __init__(self, owned, width):
        self.x, self.ctx, self.z = (lax.axis_index(name) for name in ("dp", "ctx", "mp"))
        self.core = lax.rem(self.ctx, 2)
        self.y = (self.ctx - self.core) // 2
        self.last = lax.axis_size("mp") - 1
        self.owned, self.rows, self.width = owned, owned * (self.last + 1), width
        self.step = width // SPLIT
        self.size, self.middle = width // 4, width // 8
        self.above, self.below = (self.x, self.ctx, self.z + 1), (self.x, self.ctx, self.z - 1)
        self.plane = {
            (turn, flip): self.turned(turn, flip)
            for turn in range(4)
            for flip in range(2)
            if turn or flip
        }
        self.sibling, self.over_x, self.over_y = (
            self.plane[key] for key in ((0, 1), (2, 0), (1, 0))
        )
        self.diagonal = self.plane[3, 0]
        self.column = [
            (self.x, self.other_core(flip), lax.rem(self.z + turn, self.last + 1))
            for turn in range(self.last + 1)
            for flip in range(2)
            if turn or flip
        ]

    def other_core(self, flip):
        return self.ctx + 1 - 2 * self.core if flip else self.ctx

    def turned(self, turn, flip):
        x_to = 1 - self.x if turn >= 2 else self.x
        y_to = 1 - self.y if turn % 2 else self.y
        core_to = 1 - self.core if flip else self.core
        return (x_to, 2 * y_to + core_to, self.z)

    def greet(self):
        for device in list(self.plane.values()) + self.column[1:]:
            pl.semaphore_signal(
                pltpu.get_barrier_semaphore(), inc=1, device_id=device, device_id_type=MESH
            )

    def enter(self):
        pl.semaphore_wait(pltpu.get_barrier_semaphore(), len(self.plane) + len(self.column) - 1)

    def span(self, half):
        size = self.owned if half is None else self.owned // 2
        return (half or 0) * size, size

    def block_of(self, core, block, half=None):
        first, size = self.span(half)
        return rows_at(core * self.rows + block * self.owned + first, size)

    def block(self, at, half=None):
        first, size = self.span(half)
        return rows_at(at * self.owned + first, size)

    def inner(self, half):
        return pl.ds(*self.span(half))

    def mine(self, half=None):
        return self.block_of(self.core, self.z, half)

    def columns(self, piece):
        return pl.ds(piece * self.step, self.step)

    def far(self, sign):
        return self.z if sign == 1 else self.last - self.z

    def target(self, sign, step):
        return self.z + sign * (self.last - step)

    def held_groups(self, core, x, groups):
        count = jnp.where(core == x, (groups + 1) // 2, groups // 2)
        return count, jnp.where(x == 1, groups - count, 0)

    def cut(self, turn):
        return slice(turn * self.size, (turn + 1) * self.size)

    def source(self, turn):
        x_to = 1 - self.x if turn >= 2 else self.x
        y_to = 1 - self.y if turn % 2 else self.y
        return lanes_at((2 * x_to + y_to) * self.size, self.size)


class SumChain:
    def __init__(
        self, place, part, held, ins, core_sem, up_sem, down_sem, extra=None, half=None
    ):
        self.place, self.part, self.held, self.ins, self.extra = place, part, held, ins, extra
        self.half, self.inner = half, place.inner(half)
        self.ways = ((place.above, 0, up_sem, 1), (place.below, place.last, down_sem, -1))
        self.core_sem = core_sem

    def across(self, block):
        place = self.place
        return remote(
            self.part.at[place.block_of(1 - place.core, block, self.half)],
            self.held.at[place.block(block, self.half)],
            self.core_sem,
            (block,),
            place.sibling,
        )

    def open(self):
        for block in range(self.place.last + 1):
            self.across(block).start()

    def wait(self, at):
        self.across(at).wait_recv()
        if self.extra is not None:
            self.extra.cross(at).wait_recv()

    def own(self, at, cols):
        place = self.place
        mine = self.part[place.block_of(place.core, at, self.half), cols].astype(jnp.float32)
        mine = mine + self.held[place.block(at, self.half), cols].astype(jnp.float32)
        if self.extra is not None:
            mine = mine + self.extra.came(at)[:, cols].astype(jnp.float32)
        return mine

    def hop(self, way, step, piece, at):
        place = self.place
        cols = place.columns(piece)
        return remote(
            self.part.at[place.block_of(place.core, at, self.half), cols],
            self.ins.at[way[1] + step, self.inner, cols],
            way[2],
            (step, piece),
            way[0],
        )

    def step(self, step):
        place = self.place
        for way in self.ways:

            @pl.when(place.far(way[3]) <= step)
            def _(way=way):
                at = place.target(way[3], step)
                rows = place.block_of(place.core, at, self.half)
                self.wait(at)
                for piece in range(SPLIT):
                    cols = place.columns(piece)
                    total = self.own(at, cols)
                    if step:

                        @pl.when(place.far(way[3]) > 0)
                        def _(total=total, cols=cols, piece=piece):
                            self.hop(way, step - 1, piece, at).wait_recv()
                            got = self.ins[way[1] + step - 1, self.inner, cols].astype(jnp.float32)
                            self.part[rows, cols] = (total + got).astype(self.part.dtype)

                        @pl.when(place.far(way[3]) == 0)
                        def _(total=total, cols=cols):
                            self.part[rows, cols] = total.astype(self.part.dtype)

                    else:
                        self.part[rows, cols] = total.astype(self.part.dtype)
                    self.hop(way, step, piece, at).start()

    def close(self, result):
        place = self.place
        final = place.last - 1
        self.wait(place.z)
        result = result.at[self.inner]
        result[...] = self.own(place.z, slice(None))
        for way in self.ways:

            @pl.when(place.far(way[3]) > 0)
            def _(way=way):
                for piece in range(SPLIT):
                    self.hop(way, final, piece, place.z).wait_recv()
                result[...] += self.ins[way[1] + final, self.inner].astype(jnp.float32)

    def drain(self):
        place = self.place
        for block in range(place.last + 1):
            self.across(block).wait_send()
        for step in range(place.last):
            for way in self.ways:

                @pl.when(place.far(way[3]) <= step)
                def _(way=way, step=step):
                    for piece in range(SPLIT):
                        self.hop(way, step, piece, place.target(way[3], step)).wait_send()


class CrossSum:
    def __init__(self, place, part, held, came, core_sem, x_sem, half=None):
        self.place, self.part, self.held = place, part, held
        self.came = lambda at: came(at, place.inner(half))
        self.core_sem, self.x_sem, self.half = core_sem, x_sem, half

    def across(self, block):
        place = self.place
        return remote(
            self.part.at[place.block_of(1 - place.core, block, self.half)],
            self.held.at[place.block(block, self.half)],
            self.core_sem,
            (block,),
            place.sibling,
        )

    def cross(self, at):
        place = self.place
        return remote(
            self.part.at[place.block_of(place.core, at, self.half)],
            self.came(at),
            self.x_sem,
            (at,),
            place.over_x,
        )

    def open(self):
        for block in range(self.place.last + 1):
            self.across(block).start()

    def send(self):
        place = self.place

        def one(at):
            self.across(at).wait_recv()
            rows = place.block_of(place.core, at, self.half)
            total = self.part[rows].astype(jnp.float32)
            total = total + self.held[place.block(at, self.half)].astype(jnp.float32)
            self.part[rows] = total.astype(self.part.dtype)
            self.cross(at).start()

        for step in range(place.last):
            for sign in (1, -1):

                @pl.when(place.far(sign) <= step)
                def _(sign=sign):
                    one(place.target(sign, step))

        one(place.z)

    def drain(self):
        for block in range(self.place.last + 1):
            self.across(block).wait_send()
            self.cross(block).wait_send()


class ShareChain:
    def __init__(self, place, whole, up_sem, down_sem, core_sem=None, half=None):
        self.place, self.whole, self.core_sem, self.half = place, whole, core_sem, half
        self.ways = ((place.above, up_sem, 1), (place.below, down_sem, -1))

    def rows(self, at):
        place = self.place
        if self.core_sem is None:
            return place.block(at, self.half)
        return place.block_of(place.core, at, self.half)

    def hop(self, way, step, piece, origin):
        ref = self.whole.at[self.rows(origin), self.place.columns(piece)]
        return remote(ref, ref, way[1], (step, piece), way[0])

    def across(self, origin, core):
        ref = self.whole.at[self.place.block_of(core, origin, self.half)]
        return remote(ref, ref, self.core_sem, (origin,), self.place.sibling)

    def step(self, step):
        place = self.place
        for way in self.ways:
            origin = place.z - way[2] * step

            @pl.when(place.far(way[2]) >= step)
            def _(way=way, origin=origin):
                for piece in range(SPLIT):
                    if step:
                        self.hop(way, step - 1, piece, origin).wait_recv()
                    if step < place.last:

                        @pl.when(place.far(way[2]) < place.last)
                        def _(piece=piece):
                            self.hop(way, step, piece, origin).start()

                if step and self.core_sem is not None:
                    self.across(origin, place.core).start()

        if step == 0 and self.core_sem is not None:
            self.across(place.z, place.core).start()

    def reached(self, step):
        place = self.place
        if step == 0:
            return [(place.z >= 0, place.z)]
        return [(place.far(sign) >= step, place.z - sign * step) for sign in (1, -1)]

    def arrive(self):
        if self.core_sem is not None:
            for origin in range(self.place.last + 1):
                self.across(origin, 1 - self.place.core).wait_recv()

    def drain(self):
        place = self.place
        for step in range(place.last):
            for way in self.ways:

                @pl.when((place.far(way[2]) >= step) & (place.far(way[2]) < place.last))
                def _(way=way, step=step):
                    for piece in range(SPLIT):
                        self.hop(way, step, piece, place.z - way[2] * step).wait_send()

        if self.core_sem is not None:
            for origin in range(place.last + 1):
                self.across(origin, place.core).wait_send()


class AttnGather:
    def __init__(self, place, w, first, by_y, by_x, x_sem, y_sem, far_sem, index):
        self.place, self.w, self.index = place, w, index
        self.sems = (x_sem, y_sem, far_sem)
        self.halves = (pl.ds(first, by_y), pl.ds(first + by_y, by_x))

    def cross(self, half, to_x):
        place, rows = self.place, self.halves[half]
        return remote(
            self.w.at[0, rows],
            self.w.at[2 if to_x else 1, rows],
            self.sems[0] if to_x else self.sems[1],
            (self.index + half,),
            place.over_x if to_x else place.over_y,
        )

    def relay(self, to_x):
        place, half = self.place, 1 if to_x else 0
        rows = self.halves[half]
        return remote(
            self.w.at[1 if to_x else 2, rows],
            self.w.at[3, rows],
            self.sems[2],
            (self.index + half,),
            place.over_x if to_x else place.over_y,
        )

    def send(self, which):
        self.cross(which, True).start()
        self.cross(1 - which, False).start()

    def pass_on(self):
        self.cross(0, True).wait_recv()
        self.relay(False).start()
        self.cross(1, False).wait_recv()
        self.relay(True).start()

    def drain(self):
        for half in range(2):
            for to_x in (True, False):
                self.cross(half, to_x).wait_send()
        self.relay(True).wait_send()
        self.relay(False).wait_send()


class WideGather:
    def __init__(self, place, block, w, x_sem, y_sem, far_sem):
        self.place, self.block, self.w = place, block, w
        self.x_sem, self.y_sem, self.far_sem = x_sem, y_sem, far_sem
        self.groups = block.shape[1] // GROUP
        self.most = (self.groups + 1) // 2
        self.count, self.base = place.held_groups(place.core, place.x, self.groups)
        self.other_count, self.other_base = place.held_groups(
            place.core, 1 - place.x, self.groups
        )

    def cross_x(self, group):
        return remote(
            self.block.at[:, lanes_at((self.other_base + group) * GROUP, GROUP)],
            self.w.at[1, :, lanes_at(group * GROUP, GROUP)],
            self.x_sem,
            (group,),
            self.place.over_x,
        )

    def came_x(self, group):
        here = self.w.at[1, :, lanes_at(group * GROUP, GROUP)]
        return remote(here, here, self.x_sem, (group,), self.place.over_x)

    def cross_y(self, group):
        return remote(
            self.block.at[:, lanes_at((self.base + group) * GROUP, GROUP)],
            self.w.at[0, :, lanes_at(group * GROUP, GROUP)],
            self.y_sem,
            (group,),
            self.place.over_y,
        )

    def pass_on(self, group):
        cols = lanes_at(group * GROUP, GROUP)
        return remote(
            self.w.at[1, :, cols], self.w.at[2, :, cols], self.far_sem, (group,), self.place.over_y
        )

    def start(self):
        def body(group, carry):
            self.cross_x(group).start()
            return carry

        lax.fori_loop(0, self.other_count, body, 0)

        self.cross_y(0).start()
        self.cross_y(1).start()

    def pump(self, group):
        @pl.when(group < self.count)
        def _():
            self.came_x(group).wait_recv()
            self.pass_on(group).start()

        @pl.when(group + 2 < self.count)
        def _():
            self.cross_y(group + 2).start()

    def arrive(self, group):
        self.cross_y(group).wait_recv()
        self.pass_on(group).wait_recv()

    def rows(self, turn, group, first, size):
        if turn == 0:
            return self.block[:, lanes_at((self.base + group) * GROUP + first, size)]
        return self.w[turn - 1, :, lanes_at(group * GROUP + first, size)]

    def drain(self):
        def sent_x(group, carry):
            self.cross_x(group).wait_send()
            return carry

        def sent_y(group, carry):
            self.cross_y(group).wait_send()
            self.pass_on(group).wait_send()
            return carry

        lax.fori_loop(0, self.other_count, sent_x, 0)
        lax.fori_loop(0, self.count, sent_y, 0)


class Home:
    kinds = ("upper", "lower", "x_one", "y_two", "y_one", "x_two")

    def __init__(self, place, sources, targets, sem, cut):
        self.place, self.sem, self.cut = place, sem, cut
        self.sources, self.targets = sources, targets

    def copy(self, kind, group):
        place, index = self.place, self.kinds.index(kind)
        to_x = kind in ("upper", "x_one", "x_two")
        return remote(
            self.cut(self.sources[kind], group),
            self.cut(self.targets[kind], group),
            self.sem,
            (index, group),
            place.over_x if to_x else place.over_y,
        )

    def send(self, kinds, group):
        for kind in kinds:
            self.copy(kind, group).start()

    def arrive(self, kinds, group):
        for kind in kinds:
            self.copy(kind, group).wait_recv()

    def drain(self, group):
        for kind in self.kinds:
            self.copy(kind, group).wait_send()


class WideHome:
    kinds = ("near", "far", "cross")

    def __init__(self, place, sources, targets, sem):
        self.place, self.sources, self.targets, self.sem = place, sources, targets, sem

    def copy(self, kind, group):
        cols = lanes_at(group * GROUP, GROUP)
        return remote(
            self.sources[kind].at[:, cols],
            self.targets[kind].at[:, cols],
            self.sem,
            (self.kinds.index(kind), group),
            self.place.over_x if kind == "cross" else self.place.over_y,
        )


class Refs:
    def __init__(self, names, refs):
        for name, ref in zip(names, refs, strict=True):
            setattr(self, name, ref)


def layer_kernel(names, *refs):
    r = Refs(names, refs)
    f32, low = jnp.float32, jnp.bfloat16
    z_count = lax.axis_size("mp")
    rows, width = r.hidden.shape
    place = Place(rows // z_count, width)
    size, middle, core = place.size, place.middle, place.core
    cut = place.cut
    part_rows = r.query.shape[0]
    q_rows = r.query.shape[1] // 2
    heads = q_rows // HEAD
    qkv_rows = q_rows + 2 * HEAD
    attn_rows = qkv_rows + q_rows
    chip_rows = 2 * rows
    attn_halves = (attn_rows - chip_rows, chip_rows)
    length = r.length[0, 0]
    cos_at, sin_at = r.cos[place.y], r.sin[place.y]
    w, aw = r.w, r.aw
    ff = r.gate.shape[1] // 2
    groups = ff // 128

    both_halves = range(2)
    branch_sum = [
        SumChain(place, r.part, *r.chain_one, *r.branch_sems[3 * k : 3 * k + 3], half=k)
        for k in both_halves
    ]
    h2_share = [
        ShareChain(place, r.h2, *r.h2_sems[3 * k : 3 * k + 3], half=k) for k in both_halves
    ]
    dm_share = ShareChain(place, r.dm_x, *r.dm_x_sems)
    back_cross = [
        CrossSum(
            place,
            r.mlp_part,
            r.chain_one[0],
            lambda at, inner: r.chain_one[1].at[at, inner],
            *r.back_cross_sems[2 * k : 2 * k + 2],
            half=k,
        )
        for k in both_halves
    ]
    mlp_cross = CrossSum(
        place,
        r.h2_x,
        r.h2.at[pl.ds(0, rows)],
        lambda at, inner: r.h2.at[rows_at(rows + at * place.owned, place.owned)],
        *r.mlp_cross_sems,
    )
    back_sum = [
        SumChain(
            place,
            r.part,
            *r.chain_two,
            *r.back_sems[3 * k : 3 * k + 3],
            extra=back_cross[k],
            half=k,
        )
        for k in both_halves
    ]
    mlp_sum = SumChain(place, r.dm_x, *r.chain_one, *r.mlp_sems, mlp_cross)
    da_share = [
        ShareChain(place, r.da, *r.da_sems[3 * k : 3 * k + 3], half=k) for k in both_halves
    ]
    input_sum = [
        SumChain(place, r.part, *r.chain_two, *r.input_sems[3 * k : 3 * k + 3], half=k)
        for k in both_halves
    ]
    layer_share = ShareChain(place, r.layer_all, *r.layer_sems)
    grad_share = [
        ShareChain(place, r.grad_all, *r.grad_sems[2 * k : 2 * k + 2], half=k)
        for k in both_halves
    ]

    def each(pair, name, *args):
        for member in pair:
            getattr(member, name)(*args)

    def chained(sums, shares, end, between, late):
        ahead, behind = sums
        first, second = shares
        ahead.step(0)
        if not late:
            behind.step(0)
        between(0)
        ahead.step(1)
        if not late:
            behind.step(1)
        between(1)
        ahead.step(2)
        between("ahead")
        end(0)
        first.step(0)
        if late:
            behind.step(0)
            between(2)
            behind.step(1)
        behind.step(2)
        if not late:
            between(2)
        first.step(1)
        between(3)
        end(1)
        second.step(0)
        first.step(2)
        between(4)
        second.step(1)
        first.step(3)
        between(5)
        second.step(2)
        between(6)
        second.step(3)
        between(7)
    sems = (r.attn_x, r.attn_y, r.attn_far)
    half_q = q_rows // 32 * 16
    q_gather = AttnGather(place, aw, 0, half_q, q_rows - half_q, *sems, 0)
    out_gather = AttnGather(place, aw, qkv_rows, half_q, q_rows - half_q, *sems, 2)
    kv_gather = AttnGather(place, aw, q_rows, 2 * HEAD - 16, 16, *sems, 4)
    gather = WideGather(place, r.block, w, r.wide_x, r.wide_y, r.wide_far)
    count, base = gather.count, gather.base

    my_rows = rows_at(core * rows, rows)
    loads = [
        pltpu.make_async_copy(r.hidden, r.da.at[pl.ds(0, rows)], r.load_sem.at[0]),
        pltpu.make_async_copy(r.cotangent, r.da.at[pl.ds(rows, rows)], r.load_sem.at[1]),
    ]
    place.greet()
    for load in loads:
        load.start()
    to_lanes = chosen(part_rows, size, core * part_rows)

    def split(total):
        half = total.shape[0] // 2
        one, two = total[:half], total[half:]
        pair = jnp.where(core == 0, one, two), jnp.where(core == 0, two, one)
        return tuple(member.astype(low) for member in pair)

    def spread(tensor, dims):
        return split(lax.dot_general(tensor, to_lanes, dims, preferred_element_type=f32))

    plain = (((1,), (0,)), ((), ()))
    q_pair, k_pair, v_pair = (
        spread(r.query[...], TN),
        spread(r.key_t[...], plain),
        spread(r.value_t[...], plain),
    )
    qkv_give = r.part.at[pl.ds(0, qkv_rows), pl.ds(0, size)]
    qkv_take = r.mlp_part.at[pl.ds(0, qkv_rows), pl.ds(0, size)]
    out_give = r.part.at[pl.ds(0, q_rows), pl.ds(size, size)]
    out_take = r.mlp_part.at[pl.ds(0, q_rows), pl.ds(size, size)]
    qkv_give[...] = jnp.concatenate([q_pair[1], k_pair[1], v_pair[1]], axis=0)
    for load in loads:
        load.wait()
    hidden, cotangent = r.da.at[pl.ds(0, rows)], r.da.at[pl.ds(rows, rows)]
    slot = place.ctx * rows + lax.broadcasted_iota(jnp.int32, (rows, size), 0)
    for turn in range(4):
        block = cotangent[:, place.source(turn)].astype(f32)
        r.dm[my_rows, cut(turn)] = jnp.where(slot < length, block, 0.0).astype(low)
    row = lax.broadcasted_iota(jnp.int32, r.gains.shape, 0)
    gain_pair = [
        jnp.dot(jnp.broadcast_to(norm[...][None], (8, part_rows)), to_lanes, preferred_element_type=f32)
        for norm in (r.norm_one, r.norm_two)
    ]
    r.gains[...] = jnp.where(row == 0, gain_pair[0], jnp.where(row == 1, gain_pair[1], 0.0))
    r.gains_all[core] = r.gains[...]
    r.gain_part[...] = jnp.zeros_like(r.gain_part)

    def gain_copy(turn, flip):
        slot = 2 * turn + core
        return remote(
            r.gains, r.gains_all.at[slot], r.gain_sem, (2 * turn + flip,), place.plane[turn, flip]
        )

    place.enter()
    for turn, flip in place.plane:
        gain_copy(turn, flip).start()
    qkv_swap = remote(qkv_give, qkv_take, r.core_sem, (0,), place.sibling)
    qkv_swap.start()
    dm_cross = remote(
        r.dm.at[place.mine()], r.dm_x.at[place.mine()], r.dm_cross_sem, (0,), place.over_x
    )
    dm_cross.start()
    dm_copy = remote(r.dm.at[my_rows], r.dm.at[my_rows], r.dm_sem, (0,), place.sibling)
    dm_copy.start()

    qkv_keep = jnp.concatenate([q_pair[0], k_pair[0], v_pair[0]], axis=0)
    qkv_swap.wait_recv()
    aw[0, :qkv_rows] = qkv_keep + qkv_take[...]
    kv_gather.send(0)
    kv_gather.send(1)
    q_gather.send(0)
    q_gather.send(1)
    out_pair = spread(r.output_t[...], TN)
    out_give[...] = out_pair[1]
    out_swap = remote(out_give, out_take, r.core_sem, (1,), place.sibling)
    out_swap.start()

    def wide_copies(group, kind, source):
        from_here = lanes_at(core * ff + group * 128, 128)
        from_there = lanes_at((1 - core) * ff + group * 128, 128)
        to = lanes_at(group * GROUP + kind * 128, 128)
        owner_rows = rows_at(core * part_rows, part_rows)
        here = pltpu.make_async_copy(
            source.at[:, from_here], r.block.at[owner_rows, to], r.wide_here.at[kind, group]
        )
        there = remote(
            source.at[:, from_there],
            r.block.at[owner_rows, to],
            r.wide_there,
            (kind, group),
            place.sibling,
        )
        return here, there

    sources = (r.gate, r.up, r.down_t)

    def start_wide(group, carry):
        for kind, source in enumerate(sources):
            for copy in wide_copies(group, kind, source):
                copy.start()
        return carry

    def own_wide(group, carry):
        for kind, source in enumerate(sources):
            here, there = wide_copies(group, kind, source)
            here.wait()
            there.wait_recv()
        return carry

    for turn in range(4):
        r.inputs_own[:, cut(turn)] = r.da[place.block(place.z), place.source(turn)].astype(f32)
    out_swap.wait_recv()
    aw[0, qkv_rows:] = out_pair[0] + out_take[...]
    squares = jnp.zeros((rows, 1), f32)
    for turn in range(4):
        block = hidden[:, cut(turn)].astype(f32)
        squares += jnp.sum(block * block, axis=-1, keepdims=True)
    scale = lax.rsqrt(squares / width + EPS)
    for turn, flip in place.plane:
        gain_copy(turn, flip).wait_recv()
    for turn in range(4):
        gain = r.gains_all[2 * turn] + r.gains_all[2 * turn + 1]
        r.gain_rows[:, cut(turn)] = gain
        block = hidden[:, place.source(turn)].astype(f32)
        r.h1[my_rows, cut(turn)] = (block * scale * gain[:1]).astype(low)
    h1_copy = remote(r.h1.at[my_rows], r.h1.at[my_rows], r.h1_sem, (0,), place.sibling)
    h1_copy.start()

    qkv = r.dh2.at[pl.ds(0, qkv_rows), pl.ds(0, chip_rows)]
    q_part, kv_part = slice(0, q_rows), slice(q_rows, qkv_rows)

    def qkv_dot(turn, part):
        return lax.dot_general(
            aw[turn, part], r.h1[:, cut(turn)], NT, preferred_element_type=f32
        )

    def gathered_dot(group, part):
        group.cross(1, True).wait_recv()
        qkv[part] += qkv_dot(2, part)
        group.cross(0, False).wait_recv()
        qkv[part] += qkv_dot(1, part)
        group.relay(False).wait_recv()
        group.relay(True).wait_recv()
        qkv[part] += qkv_dot(3, part)

    h1_copy.wait_recv()
    qkv[...] = qkv_dot(0, slice(0, qkv_rows))
    kv_gather.pass_on()
    lax.fori_loop(0, groups, start_wide, 0)

    def sent_wide(group, carry):
        for kind, source in enumerate(sources):
            wide_copies(group, kind, source)[1].wait_send()
        return carry

    q_gather.pass_on()
    dm_cross.wait_recv()
    dm_share.step(0)
    gathered_dot(kv_gather, kv_part)

    def turned(first_row):
        ahead = qkv[first_row : first_row + HEAD // 2]
        behind = qkv[first_row + HEAD // 2 : first_row + HEAD]
        return jnp.concatenate(
            [ahead * cos_at - behind * sin_at, behind * cos_at + ahead * sin_at], axis=0
        )

    r.kv[place.y, :HEAD] = turned(q_rows).astype(low)
    r.kv[place.y, HEAD:] = qkv[q_rows + HEAD : qkv_rows].astype(low)
    kv_copy = remote(r.kv.at[place.y], r.kv.at[place.y], r.kv_sem, (0,), place.over_y)
    kv_copy.start()
    out_gather.send(0)
    out_gather.send(1)
    gathered_dot(q_gather, q_part)
    head_rows = [slice(head * HEAD, (head + 1) * HEAD) for head in range(heads)]
    for head in range(heads):
        r.q_t[head_rows[head]] = turned(head * HEAD).astype(low)
    dm_share.step(1)
    kv_copy.wait_recv()

    keys = [r.kv[block, :HEAD].T for block in range(2)]
    half_slots = chip_rows // 2
    query_halves = [
        (slice(half * half_slots, (half + 1) * half_slots), place.y * chip_rows + half * half_slots)
        for half in range(2)
    ]
    def head_forward(head, carry):
        at = rows_at(head * HEAD, HEAD)
        for lanes, first_query in query_halves:
            queries = r.q_t[at, lanes]
            scores = [
                masked(keys[block], queries, length, block, first_query) for block in range(2)
            ]
            top = jnp.maximum(*(jnp.max(score, axis=0, keepdims=True) for score in scores))
            exponents = [jnp.exp(score - top) for score in scores]
            total = sum(jnp.sum(exponent, axis=0, keepdims=True) for exponent in exponents)
            mixed = jnp.zeros((HEAD, half_slots), f32)
            for block in range(2):
                weights = (exponents[block] / total).astype(low)
                mixed += jnp.dot(r.kv[block, HEAD:], weights, preferred_element_type=f32)
            r.o_t[at, lanes] = mixed.astype(low)
            r.lse[pl.ds(head, 1), lanes] = top + jnp.log(total)
        return carry

    lax.fori_loop(0, heads, head_forward, 0)
    out_gather.pass_on()
    lax.fori_loop(0, groups, own_wide, 0)
    gather.start()
    dm_share.step(2)
    out_gather.cross(1, True).wait_recv()
    out_gather.cross(0, False).wait_recv()
    out_gather.relay(False).wait_recv()
    out_gather.relay(True).wait_recv()
    qkv_swap.wait_send()
    out_swap.wait_send()
    mixed_all = r.o_t[...].T
    for turn in range(4):
        r.part[:, cut(turn)] = jnp.dot(
            mixed_all, aw[turn, qkv_rows:], preferred_element_type=f32
        ).astype(low)

    each(branch_sum, "open")
    gain_two = r.gain_rows[1:2]

    def h2_cross(origin, half):
        block = place.block_of(core, origin, half)
        return remote(
            r.h2.at[block], r.h2_x.at[block], r.h2_cross_sem, (half, origin), place.over_x
        )

    def h2_across(origin, of_core, half):
        block = place.block_of(of_core, origin, half)
        return remote(
            r.h2_x.at[block], r.h2_x.at[block], r.h2_across_sem, (half, origin), place.sibling
        )

    def branch_end(half):
        inner = place.inner(half)
        branch_sum[half].close(r.middle)
        r.middle[inner] += r.inputs_own[inner]
        r.h2[place.mine(half)] = normed(r.middle[inner], gain_two).astype(low)
        h2_cross(place.z, half).start()

    def h2_on(half, step):
        for here, origin in h2_share[half].reached(step):

            @pl.when(here)
            def _(origin=origin):
                h2_cross(origin, half).start()

    def beside_branch(when):
        if when == 0:
            dm_share.step(3)
        if when == 2:
            gather.pump(0)
        if when == 3:
            h2_on(0, 1)
            gather.pump(1)
        if when == 4:
            h2_on(0, 2)
            gather.pump(2)
        if when == 5:
            h2_on(1, 1)
            h2_on(0, 3)
            gather.pump(3)
        if when == 6:
            h2_on(1, 2)
        if when == 7:
            h2_on(1, 3)

    chained(branch_sum, h2_share, branch_end, beside_branch, False)
    each(h2_share, "arrive")
    each(branch_sum, "drain")
    dm_copy.wait()
    dm_share.arrive()

    zd_rows = (slice(0, chip_rows), slice(chip_rows, 2 * chip_rows))
    tokens = ((r.h2, r.dm), (r.h2_x, r.dm_x))

    def cut_of(turn, which):
        return cut(turn ^ 2 if which else turn)

    def activate(group, which):
        left, d_left = tokens[which]
        gu = jnp.zeros((chip_rows, 256), f32)
        d_hidden = jnp.zeros((chip_rows, 128), f32)
        for turn in range(4):
            gu += jnp.dot(
                left[:, cut_of(turn, which)], gather.rows(turn, group, 0, 256), preferred_element_type=f32
            )
            d_hidden += jnp.dot(
                d_left[:, cut_of(turn, which)],
                gather.rows(turn, group, 256, 128),
                preferred_element_type=f32,
            )
        gate, up = gu[:, :128], gu[:, 128:]
        sigma = jax.nn.sigmoid(gate)
        silu = gate * sigma
        d_gate = d_hidden * up * sigma * (1.0 + gate * (1.0 - sigma))
        at = zd_rows[which]
        start = group * GROUP
        r.zd[at, lanes_at(start, 128)] = d_gate.astype(low)
        r.zd[at, lanes_at(start + 128, 128)] = (d_hidden * silu).astype(low)
        r.zd[at, lanes_at(start + 256, 128)] = (silu * up).astype(low)

    def gradients(group):
        cols = lanes_at(group * GROUP, GROUP)
        for turn in range(4):
            grad_gu = jnp.zeros((size, 256), f32)
            grad_down = jnp.zeros((size, 128), f32)
            for which, (left, d_left) in enumerate(tokens):
                at = zd_rows[which]
                grad_gu += lax.dot_general(
                    left[:, cut_of(turn, which)],
                    r.zd[at, lanes_at(group * GROUP, 256)],
                    TN,
                    preferred_element_type=f32,
                )
                grad_down += lax.dot_general(
                    d_left[:, cut_of(turn, which)],
                    r.zd[at, lanes_at(group * GROUP + 256, 128)],
                    TN,
                    preferred_element_type=f32,
                )
            if turn:
                r.tile[turn - 1, :, :256] = grad_gu.astype(low)
                r.tile[turn - 1, :, 256:] = grad_down.astype(low)
            else:
                r.tile_own[:, :256] = grad_gu
                r.tile_own[:, 256:] = grad_down
        keep = pltpu.make_async_copy(r.tile, r.stage.at[:, :, cols], r.keep_sem.at[0])
        keep_own = pltpu.make_async_copy(r.tile_own, r.own_grad.at[:, cols], r.keep_sem.at[1])
        keep.start()
        keep_own.start()
        keep.wait()
        keep_own.wait()

    def each_count(act):
        for number in sorted({groups // 2, (groups + 1) // 2}):

            @pl.when(count == number)
            def _(number=number):
                act(number)

    def summed(into, which, first, width_of, turns):
        def act(number):
            for turn in turns:
                out = jnp.zeros((chip_rows, size), f32)
                for group in range(number):
                    out += lax.dot_general(
                        r.zd[zd_rows[which], lanes_at(group * GROUP + first, width_of)],
                        gather.rows(turn, group, first, width_of),
                        NT,
                        preferred_element_type=f32,
                    )
                into[:, cut_of(turn, which)] = out.astype(low)

        each_count(act)

    home = WideHome(
        place,
        {"near": r.stage.at[0], "far": r.stage.at[2], "cross": w.at[0]},
        {"near": r.near, "far": r.far, "cross": r.crossed},
        r.home_sem,
    )

    def send_grads(group, kinds):
        for kind in kinds:
            home.copy(kind, group).start()

    def if_last(act):
        pl.when(count > least)(act)

    least = groups // 2
    gather.arrive(0)
    activate(0, 0)
    for half in both_halves:
        for origin in range(z_count):
            h2_cross(origin, half).wait_recv()
            h2_across(origin, core, half).start()
    gather.arrive(1)
    activate(1, 0)
    for half in both_halves:
        for origin in range(z_count):
            h2_across(origin, 1 - core, half).wait_recv()
    for group in range(least):
        if group > 1:
            gather.arrive(group)
            activate(group, 0)
        activate(group, 1)
    gradients(0)
    send_grads(0, ("far",))

    @if_last
    def _():
        gather.arrive(least)
        activate(least, 1)
        activate(least, 0)

    summed(r.mlp_part, 1, 0, 256, range(4))
    each(back_cross, "open")
    summed(r.part, 0, 0, 256, range(2))
    back_cross[0].send()
    summed(r.part, 0, 0, 256, range(2, 4))
    back_cross[1].send()
    each(back_sum, "open")

    def back_end(half):
        inner = place.inner(half)
        back_sum[half].close(r.d_middle)
        d_norm, d_gain = norm_back(r.middle[inner], gain_two, r.d_middle[inner])
        if half:
            d_gain = d_gain + r.gain_part[1]
        r.gain_part[1:2] = d_gain[None]
        r.d_middle[inner] = r.dm[place.mine(half)].astype(f32) + d_norm
        r.da[place.mine(half)] = r.d_middle[inner].astype(low)

    def beside_back(when):
        if when in (0, 1):
            gradients(when + 1)
            send_grads(when + 1, ("far",))
        if when == 2:

            @if_last
            def _():
                gradients(least)
                send_grads(least, ("far",))

            send_grads(0, ("near",))
            each(h2_share, "drain")
            dm_share.drain()
            lax.fori_loop(0, groups, sent_wide, 0)
            for half in both_halves:
                for origin in range(z_count):
                    h2_cross(origin, half).wait_send()
                    h2_across(origin, core, half).wait_send()
            for device in (place.sibling, place.over_x):
                quiet(r.quiet_sem, device)
            summed(r.h2_x, 1, 256, 128, range(4))
        if when == 3:
            pl.semaphore_wait(r.quiet_sem, 2)
            mlp_cross.open()
            summed(r.dm_x, 0, 256, 128, range(4))
            mlp_cross.send()
            send_grads(1, ("near",))
        if when == 4:
            quiet(r.chain_sem, place.sibling)

            @pl.when(place.z < place.last)
            def _():
                quiet(r.chain_sem, place.above)

            @pl.when(place.z > 0)
            def _():
                quiet(r.chain_sem, place.below)

        if when == 5:
            ends = jnp.where(place.z == 0, 1, 0) + jnp.where(place.z == place.last, 1, 0)
            pl.semaphore_wait(r.chain_sem, 3 - ends)
            mlp_sum.open()
            mlp_sum.step(0)
        if when == 7:
            mlp_sum.step(1)

    def quiet(sem, device):
        pl.semaphore_signal(sem, inc=1, device_id=device, device_id_type=MESH)

    chained(back_sum, da_share, back_end, beside_back, True)

    dm_cross.wait_send()
    for device in (place.over_x, place.over_y):
        pl.semaphore_signal(r.free_sem, inc=1, device_id=device, device_id_type=MESH)
    gather.drain()
    part_load = pltpu.make_async_copy(r.stage.at[1], w.at[0], r.load_sem.at[2])
    part_load.start()
    each(da_share, "arrive")
    each(back_sum, "drain")
    each(back_cross, "drain")
    do_t, d_t, kv_give = (
        r.mlp_part.at[pl.ds(0, number), pl.ds(at * chip_rows, chip_rows)]
        for at, number in enumerate((q_rows, qkv_rows, 2 * HEAD))
    )
    dk, dv = (
        [r.dh2.at[:, pl.ds(3 * 256 + 128 * at + 256 * which, HEAD)] for at in range(2)]
        for which in range(2)
    )

    d_out = jnp.zeros((q_rows, chip_rows), f32)
    for turn in range(4):
        d_out += lax.dot_general(
            aw[turn, qkv_rows:], r.da[:, cut(turn)], NT, preferred_element_type=f32
        )
    do_t[...] = d_out.astype(low)
    values = [r.kv[block, HEAD:].T for block in range(2)]
    keys = [r.kv[block, :HEAD].T for block in range(2)]
    scale = HEAD ** (-0.5)
    for ref in dk + dv:
        ref[...] = jnp.zeros(ref.shape, f32)

    def turned_back(tensor, cosine, sine):
        ahead, behind = tensor[: HEAD // 2], tensor[HEAD // 2 :]
        return jnp.concatenate(
            [ahead * cosine + behind * sine, behind * cosine - ahead * sine], axis=0
        )

    def far_load(group):
        cols = lanes_at(group * GROUP, GROUP)
        return pltpu.make_async_copy(r.far.at[:, cols], w.at[1, :, cols], r.add_sem.at[group])

    def fetch_far(group, carry):
        home.copy("far", group).wait_recv()
        far_load(group).start()
        return carry

    def send_cross(group, carry):
        cols = lanes_at(group * GROUP, GROUP)
        far_load(group).wait()
        mine = w[0, :, cols].astype(f32) + w[1, :, cols].astype(f32)
        w[0, :, cols] = mine.astype(low)
        home.copy("cross", group).start()
        return carry

    lax.fori_loop(0, count, fetch_far, 0)
    part_load.wait()
    def finish_layer():
        mlp_sum.close(r.mlp)
        slot = place.ctx * place.rows + place.z * place.owned
        slot += lax.broadcasted_iota(jnp.int32, r.middle.shape, 0)
        r.layer_all[place.block(place.z)] = jnp.where(
            slot < length, r.middle[...] + r.mlp[...], 0.0
        ).astype(low)
        layer_share.step(0)

    def head_back(head, carry):
        at = rows_at(head * HEAD, HEAD)
        for lanes, first_query in query_halves:
            queries, d_head = r.q_t[at, lanes], do_t[at, lanes]
            probs, d_probs = [], []
            inner = jnp.zeros((1, half_slots), f32)
            for block in range(2):
                scores = masked(keys[block], queries, length, block, first_query)
                prob = jnp.exp(scores - r.lse[pl.ds(head, 1), lanes])
                d_prob = jnp.dot(values[block], d_head, preferred_element_type=f32)
                inner += jnp.sum(prob * d_prob, axis=0, keepdims=True)
                probs.append(prob)
                d_probs.append(d_prob)
            d_query = jnp.zeros((HEAD, half_slots), f32)
            for block in range(2):
                d_scores = (probs[block] * (d_probs[block] - inner)).astype(low)
                dk[block][...] += (
                    lax.dot_general(d_scores, queries, NT, preferred_element_type=f32) * scale
                )
                dv[block][...] += lax.dot_general(
                    probs[block].astype(low), d_head, NT, preferred_element_type=f32
                )
                d_query += (
                    jnp.dot(r.kv[block, :HEAD], d_scores, preferred_element_type=f32) * scale
                )
            d_t[at, lanes] = turned_back(d_query, cos_at[:, lanes], sin_at[:, lanes]).astype(low)
        return carry

    send_cross(0, 0)
    lax.fori_loop(0, heads // 2, head_back, 0)
    mlp_sum.step(2)
    send_cross(1, 0)
    lax.fori_loop(heads // 2, heads, head_back, 0)

    def of_half(pair, which):
        return jnp.where(which == 0, pair[0][...], pair[1][...]).T

    kv_give[:HEAD] = of_half(dk, 1 - place.y).astype(low)
    kv_give[HEAD:] = of_half(dv, 1 - place.y).astype(low)
    kv_back = remote(kv_give, r.kv_take, r.kv_sem, (1,), place.over_y)
    kv_back.start()
    send_grads(2, ("near",))
    finish_layer()
    d_key, d_value = of_half(dk, place.y), of_half(dv, place.y)

    lax.fori_loop(2, count, send_cross, 0)
    kv_back.wait_recv()
    d_t[q_rows : q_rows + HEAD] = turned_back(
        d_key + r.kv_take[:HEAD].astype(f32), cos_at, sin_at
    ).astype(low)
    d_t[q_rows + HEAD :] = (d_value + r.kv_take[HEAD:].astype(f32)).astype(low)
    d_qkv = d_t[...].T
    for turn in range(4):
        r.part[:, cut(turn)] = jnp.dot(
            d_qkv, aw[turn, :qkv_rows], preferred_element_type=f32
        ).astype(low)

    each(input_sum, "open")

    def view(ref, at, half):
        return ref.at[pl.ds(0, attn_halves[half]), pl.ds(at * size, size)]

    def zd_view(at, half):
        return r.zd.at[pl.ds(at // 2 * chip_rows, attn_halves[half]), pl.ds(at % 2 * size, size)]

    far_kinds, straight_kinds, last_kinds = (
        ("upper", "lower"),
        ("x_one", "y_two"),
        ("y_one", "x_two"),
    )
    stage = {
        (turn, half): view(*((r.h2, 2 * (turn - 1) + half) if turn < 3 else (r.dm, half)), half)
        for turn in (1, 2, 3)
        for half in range(2)
    }
    attn_own = [view(r.dh2, 2 + half, half) for half in range(2)]
    attn_home = Home(
        place,
        {
            "upper": stage[3, 0],
            "lower": stage[3, 1],
            "x_one": stage[2, 0],
            "y_two": stage[1, 1],
            "y_one": stage[1, 0],
            "x_two": stage[2, 1],
        },
        {
            "upper": zd_view(0, 0),
            "lower": zd_view(1, 1),
            "x_one": zd_view(2, 0),
            "y_two": zd_view(3, 1),
            "y_one": view(r.dm, 2, 0),
            "x_two": view(r.dm, 3, 1),
        },
        r.attn_home_sem,
        lambda ref, group: ref,
    )
    def attn_gradients(turn):
        grad = jnp.dot(d_t[...], r.h1[:, cut(turn)], preferred_element_type=f32)
        grad_o = jnp.dot(r.o_t[...], r.da[:, cut(turn)], preferred_element_type=f32)
        top, bottom = (stage[turn, 0], stage[turn, 1]) if turn else attn_own
        first_rows = attn_halves[0]
        left_over = qkv_rows - first_rows
        top[...] = grad[:first_rows].astype(top.dtype)
        bottom[:left_over] = grad[first_rows:].astype(top.dtype)
        bottom[left_over:] = grad_o.astype(top.dtype)

    def input_end(half):
        inner = place.inner(half)
        input_sum[half].close(r.middle)
        d_norm, d_gain = norm_back(r.inputs_own[inner], r.gain_rows[0:1], r.middle[inner])
        if half:
            d_gain = d_gain + r.gain_part[0]
        r.gain_part[0:1] = d_gain[None]
        r.grad_all[place.block(place.z, half)] = (r.d_middle[inner] + d_norm).astype(low)

    def beside_input(when):
        if when == 0:
            pl.semaphore_wait(r.free_sem, 2)
            attn_gradients(3)
            attn_home.send(far_kinds, 0)
            attn_gradients(2)
            attn_gradients(1)
            layer_share.step(1)
        if when == 1:
            attn_gradients(0)
            attn_home.send(straight_kinds, 0)

            @if_last
            def _():
                send_grads(least, ("near",))

        if when == "ahead":
            layer_share.step(2)
        if when == 2:
            final_start(0)
            finish(0)
        if when == 3:
            layer_share.step(3)
            finish(1)
            finish(2)
        if when == 4:
            start_gains()
            finish(3)
        if when == 5:
            finish(4)
            attn_second()
        if when == 6:
            finish(5)
            for group in range(least):
                home.copy("far", group).wait_send()
                home.copy("near", group).wait_send()

            @if_last
            def _():
                home.copy("far", least).wait_send()
                home.copy("near", least).wait_send()

            q_gather.drain()
            kv_gather.drain()
            out_gather.drain()
        if when == 7:
            finish(6)
            finish(7)

    plane_gains = [
        remote(
            r.gain_part.at[:, pl.ds(turn * size, size)],
            r.gain_in.at[turn - 1],
            r.plane_gain_sem,
            (turn - 1,),
            place.plane[turn, 0],
        )
        for turn in (1, 2, 3)
    ]

    def start_gains():
        for copy in plane_gains:
            copy.start()

    top_half, low_half = pl.ds(0, middle), pl.ds(middle, middle)
    slots = (
        (r.tile_own.at[top_half], r.tile_own.at[low_half]),
        (r.dh2.at[top_half, pl.ds(0, GROUP)], r.dh2.at[top_half, pl.ds(GROUP, GROUP)]),
    )
    halves = (top_half, low_half)
    items = [("own", 0), ("own", 1), ("cross", 0), ("cross", 1)]
    items += [("cross", 2), ("own", 2), ("cross", 3), ("own", 3)]

    def guarded(index, act):
        kind, group = items[index]
        limit = count if kind == "own" else gather.other_count
        if group < groups // 2:
            act()
        else:
            pl.when(group < limit)(act)

    def final_loads(index):
        kind, group = items[index]
        cols = pl.ds(group * GROUP, GROUP)
        if kind == "own":
            for half in range(2):
                yield pltpu.make_async_copy(
                    r.own_grad.at[halves[half], cols],
                    slots[index % 2][half],
                    r.final_sem.at[half, index],
                )
            yield pltpu.make_async_copy(
                r.near.at[:, cols], w.at[2, :, cols], r.final_sem.at[2, index]
            )
        else:
            yield pltpu.make_async_copy(
                r.crossed.at[:, cols], w.at[1, :, cols], r.final_sem.at[2, index]
            )

    def final_out(index):
        kind, group = items[index]
        first = base if kind == "own" else gather.other_base
        to = lanes_at(core * ff + (first + group) * 128, 128)
        for which, into in enumerate((r.grad_gate, r.grad_up, r.grad_down)):
            cols = pl.ds(which * 128, 128)
            for half in range(2):
                source = slots[index % 2][half].at[:, cols]
                yield (
                    half,
                    pltpu.make_async_copy(
                        source, into.at[:, to], r.out_here.at[which, first + group]
                    ),
                    remote(
                        source, into.at[:, to], r.out_there, (which, first + group), place.sibling
                    ),
                )

    def final_start(index):
        def act():
            kind, group = items[index]
            home.copy("near" if kind == "own" else "cross", group).wait_recv()
            for load in final_loads(index):
                load.start()

        guarded(index, act)

    def final_sum(index):
        def act():
            kind, group = items[index]
            cols = pl.ds(group * GROUP, GROUP)
            for load in final_loads(index):
                load.wait()
            for half in range(2):
                if kind == "own":
                    slots[index % 2][half][...] += w[2, halves[half], cols].astype(f32)
                else:
                    slots[index % 2][half][...] = w[1, halves[half], cols].astype(f32)
            for half, here, there in final_out(index):

                @pl.when(core == half)
                def _(here=here):
                    here.start()

                @pl.when(core != half)
                def _(there=there):
                    there.start()

        guarded(index, act)

    def final_free(index):
        def act():
            for half, here, there in final_out(index):

                @pl.when(core == half)
                def _(here=here):
                    here.wait()

                @pl.when(core != half)
                def _(there=there):
                    there.wait_send()

        guarded(index, act)

    def finish(index):
        final_sum(index)
        if index:
            final_free(index - 1)
        if index + 1 < len(items):
            final_start(index + 1)

    def attn_second():
        attn_home.arrive(far_kinds, 0)
        for turn, half, kind in ((1, 0, "upper"), (2, 1, "lower")):
            mine = stage[turn, half]
            mine[...] = (
                mine[...].astype(f32) + attn_home.targets[kind][...].astype(f32)
            ).astype(low)
        attn_home.send(last_kinds, 0)

    chained(input_sum, grad_share, input_end, beside_input, False)
    for copy in plane_gains:
        copy.wait_recv()
    r.gain_sum[...] = r.gain_part[:, :size] + r.gain_in[0] + r.gain_in[1] + r.gain_in[2]
    column_gains = [
        remote(r.gain_sum, r.gain_all.at[index], r.column_gain_sem, (index,), device)
        for index, device in enumerate(place.column)
    ]
    for copy in column_gains:
        copy.start()
    attn_home.arrive(straight_kinds + last_kinds, 0)
    attn_own[0][...] += attn_home.targets["x_one"][...].astype(f32) + attn_home.targets["y_one"][
        ...
    ].astype(f32)
    attn_own[1][...] += attn_home.targets["x_two"][...].astype(f32) + attn_home.targets["y_two"][
        ...
    ].astype(f32)
    attn_out = []
    for half in range(2):
        to = pl.ds(half * attn_halves[0], attn_halves[half])
        attn_out.append(
            pltpu.make_async_copy(attn_own[half], r.grad_attn.at[core, to], r.out_attn.at[half])
        )
        attn_out.append(
            remote(
                attn_own[half], r.grad_attn.at[core, to], r.swap_attn, (half,), place.sibling
            )
        )
    for copy in attn_out:
        copy.start()
    gain_total = r.gain_sum[...]
    for index, copy in enumerate(column_gains):
        copy.wait_recv()
        gain_total += r.gain_all[index]
    r.gain_out[...] = gain_total

    final_free(len(items) - 1)

    def settle(group, carry):
        for kind in range(len(sources)):
            to = lanes_at(core * ff + group * 128, 128)
            into = (r.grad_gate, r.grad_up, r.grad_down)[kind]
            remote(
                r.tile_own.at[top_half, pl.ds(0, 128)],
                into.at[:, to],
                r.out_there,
                (kind, group),
                place.sibling,
            ).wait_recv()
        return carry

    def sent_home(group, carry):
        home.copy("cross", group).wait_send()
        return carry

    lax.fori_loop(0, groups, settle, 0)
    lax.fori_loop(0, count, sent_home, 0)
    for copy in attn_out:
        copy.wait()
    attn_home.drain(0)
    for copy in (kv_copy, kv_back, h1_copy, *plane_gains, *column_gains):
        copy.wait_send()
    for turn, flip in place.plane:
        gain_copy(turn, flip).wait_send()
    for chain in (*input_sum, mlp_sum, mlp_cross, *da_share, layer_share, *grad_share):
        chain.drain()


class Lists:
    def __init__(self):
        self.names, self.items = [], []

    def add(self, name, item):
        self.names.append(name)
        self.items.append(item)


def grouped_kernel(names, counts, *refs):
    given, at = [], 0
    for count in counts:
        given.append(refs[at] if count is None else refs[at : at + count])
        at += count or 1
    layer_kernel(names, *given)


def finish_kernel(
    layer_all,
    grad_all,
    gains,
    gate,
    up,
    down,
    attn,
    layer_out,
    input_grad,
    gain_one,
    gain_two,
    query,
    key_t,
    value_t,
    output_t,
    gate_out,
    up_out,
    down_out,
    attn_here,
    layer_here,
    grad_here,
    gate_here,
    up_here,
    down_here,
    in_sem,
    out_sem,
):
    part = key_t.shape[1]
    place = 2 * lax.axis_index("dp") + lax.axis_index("ctx") // 2
    first = lax.rem(lax.axis_index("ctx"), 2) == 0
    size = 2 * part
    here = (gate_here, up_here, down_here, layer_here, grad_here, attn_here)
    loads = [
        pltpu.make_async_copy(source, into, in_sem.at[index])
        for index, (source, into) in enumerate(
            zip((gate, up, down, layer_all, grad_all, attn), here, strict=True)
        )
    ]
    for load in loads:
        load.start()
    stores = []

    def store(source, into):
        stores.append(pltpu.make_async_copy(source, into, out_sem.at[len(stores)]))
        stores[-1].start()

    def own(tensor):
        return jnp.where(first, tensor[:, :part], tensor[:, part:])

    mine = own(gains[...])
    gain_one[...], gain_two[...] = mine[0], mine[1]
    for index, into in enumerate((gate_out, up_out, down_out)):
        loads[index].wait()
        store(here[index], into)
    for index, into in ((3, layer_out), (4, input_grad)):
        loads[index].wait()
        for turn in range(4):
            at = lanes_at((place ^ turn) * size, size)
            store(here[index].at[:, turn * size : (turn + 1) * size], into.at[:, at])
    loads[5].wait()
    q_rows = query.shape[1] // 2
    start = 0
    for into, size_of in ((query, q_rows), (key_t, HEAD), (value_t, HEAD), (output_t, q_rows)):
        rows = slice(start, start + size_of)
        start += size_of
        both = jnp.concatenate([own(attn_here[which, rows]) for which in range(2)], axis=0)
        into[...] = both if size_of == HEAD else both.T
    for copy in stores:
        copy.wait()


def on_plane(
    hidden_in,
    cotangent,
    lengths,
    norm_attn,
    w_query,
    w_key,
    w_value,
    w_output,
    norm_mlp,
    w_gate,
    w_up,
    w_down,
):
    low, f32 = jnp.bfloat16, jnp.float32
    _, rows, width = hidden_in.shape
    part = w_query.shape[0]
    chip_part, chip_rows = 2 * part, 2 * rows
    z_count = lax.axis_size("mp")
    owned, hops = rows // z_count, z_count - 1
    q_rows = w_query.shape[1] // 2
    qkv_rows = q_rows + 2 * HEAD
    attn_rows = qkv_rows + q_rows
    ff = w_gate.shape[1] // 2
    wide_cols = 3 * ff
    groups = wide_cols // GROUP
    most = (groups + 1) // 2
    held_cols = most * GROUP
    others = 2 * z_count - 1

    slots = np.arange(2 * chip_rows, dtype=np.float32)
    freq = np.float32(THETA) ** -(np.arange(HEAD // 2, dtype=np.float32) * 2.0 / HEAD)
    angle = (freq.astype(np.float32)[:, None] * slots[None]).reshape(HEAD // 2, 2, chip_rows)
    angle = angle.astype(np.float32).swapaxes(0, 1)
    cosine, sine = (jnp.asarray(table(angle), f32) for table in (np.cos, np.sin))

    hbm = pl.BlockSpec(memory_space=pl.ANY)
    smem = pl.BlockSpec(memory_space=pltpu.SMEM)
    vmem = pl.BlockSpec(memory_space=pltpu.VMEM)
    dma, vm = pltpu.SemaphoreType.DMA, pltpu.VMEM
    whole, own = (chip_rows, width), (owned, width)

    ins, outs, scratch = Lists(), Lists(), Lists()
    for name, value, spec in (
        ("hidden", hidden_in[0], hbm),
        ("cotangent", cotangent[0], hbm),
        ("length", lengths.reshape(1, 1), smem),
        ("norm_one", norm_attn, vmem),
        ("norm_two", norm_mlp, vmem),
        ("query", w_query, vmem),
        ("key_t", w_key.T, vmem),
        ("value_t", w_value.T, vmem),
        ("output_t", w_output.T, vmem),
        ("gate", w_gate, hbm),
        ("up", w_up, hbm),
        ("down_t", w_down.T, hbm),
        ("cos", cosine, vmem),
        ("sin", sine, vmem),
    ):
        ins.add(name, (value, spec))
    for name, shape, dtype, spec in (
        ("layer_all", (rows, width), low, vmem),
        ("grad_all", (rows, width), low, vmem),
        ("gain_out", (8, chip_part), f32, vmem),
        ("grad_gate", w_gate.shape, f32, hbm),
        ("grad_up", w_up.shape, f32, hbm),
        ("grad_down", w_gate.shape, f32, hbm),
        ("grad_attn", (2, attn_rows, chip_part), f32, hbm),
        ("own_grad", (chip_part, held_cols), f32, hbm),
        ("stage", (3, chip_part, held_cols), low, hbm),
        ("near", (chip_part, held_cols), low, hbm),
        ("far", (chip_part, held_cols), low, hbm),
        ("crossed", (chip_part, held_cols), low, hbm),
    ):
        outs.add(name, (jax.ShapeDtypeStruct(shape, dtype), spec))
    chain = [vm((rows, width), low), vm((2 * hops, *own), low)]
    ways = [dma((2, hops, SPLIT))] * 2
    cores = dma((2, z_count))
    for name, item in (
        ("block", vm((chip_part, wide_cols), low)),
        ("w", vm((3, chip_part, held_cols), low)),
        ("aw", vm((4, attn_rows, chip_part), low)),
        ("h1", vm(whole, low)),
        ("h2", vm(whole, low)),
        ("h2_x", vm(whole, low)),
        ("dm", vm(whole, low)),
        ("dm_x", vm(whole, low)),
        ("da", vm(whole, low)),
        ("part", vm(whole, low)),
        ("mlp_part", vm(whole, low)),
        ("dh2", vm(whole, f32)),
        ("zd", vm((2 * chip_rows, held_cols), low)),
        ("tile", vm((3, chip_part, GROUP), low)),
        ("tile_own", vm((chip_part, GROUP), f32)),
        ("chain_one", chain),
        ("chain_two", chain),
        ("inputs_own", vm(own, f32)),
        ("middle", vm(own, f32)),
        ("mlp", vm(own, f32)),
        ("d_middle", vm(own, f32)),
        ("gains", vm((8, chip_part), f32)),
        ("gains_all", vm((8, 8, chip_part), f32)),
        ("gain_rows", vm((8, width), f32)),
        ("kv", vm((2, 2 * HEAD, chip_rows), low)),
        ("q_t", vm((q_rows, chip_rows), low)),
        ("o_t", vm((q_rows, chip_rows), low)),
        ("lse", vm((8, chip_rows), f32)),
        ("kv_take", vm((2 * HEAD, chip_rows), low)),
        ("gain_part", vm((8, width), f32)),
        ("gain_in", vm((3, 8, chip_part), f32)),
        ("gain_sum", vm((8, chip_part), f32)),
        ("gain_all", vm((others, 8, chip_part), f32)),
        ("load_sem", dma((4,))),
        ("core_sem", dma((2, 2))),
        ("gain_sem", dma((2, 8))),
        ("attn_x", dma((2, 6))),
        ("attn_y", dma((2, 6))),
        ("attn_far", dma((2, 6))),
        ("wide_here", dma((3, groups))),
        ("wide_there", dma((2, 3, groups))),
        ("dm_sem", dma((2, 1))),
        ("h1_sem", dma((2, 1))),
        ("kv_sem", dma((2, 2))),
        ("wide_x", dma((2, most))),
        ("wide_y", dma((2, most))),
        ("wide_far", dma((2, most))),
        ("dm_cross_sem", dma((2, 1))),
        ("h2_cross_sem", dma((2, 2, z_count))),
        ("h2_across_sem", dma((2, 2, z_count))),
        ("keep_sem", dma((2,))),
        ("home_sem", dma((2, 3, most))),
        ("add_sem", dma((most,))),
        ("attn_home_sem", dma((2, 6, 1))),
        ("final_sem", dma((3, 2 * most))),
        ("out_here", dma((3, groups))),
        ("out_there", dma((2, 3, groups))),
        ("out_attn", dma((2,))),
        ("swap_attn", dma((2, 2))),
        ("plane_gain_sem", dma((2, 3))),
        ("column_gain_sem", dma((2, others))),
        ("free_sem", pltpu.SemaphoreType.REGULAR),
        ("quiet_sem", pltpu.SemaphoreType.REGULAR),
        ("chain_sem", pltpu.SemaphoreType.REGULAR),
        ("branch_sems", ([cores] + ways) * 2),
        ("back_sems", ([cores] + ways) * 2),
        ("mlp_sems", [cores] + ways),
        ("input_sems", ([cores] + ways) * 2),
        ("h2_sems", (ways + [cores]) * 2),
        ("dm_x_sems", ways + [cores]),
        ("back_cross_sems", [cores] * 4),
        ("mlp_cross_sems", [cores, cores]),
        ("da_sems", (ways + [cores]) * 2),
        ("layer_sems", ways),
        ("grad_sems", ways * 2),
    ):
        scratch.add(name, item)

    counts = [None] * (len(ins.items) + len(outs.items))
    flat = []
    for item in scratch.items:
        counts.append(len(item) if isinstance(item, list) else None)
        flat += item if isinstance(item, list) else [item]
    names = ins.names + outs.names + scratch.names
    results = pl.pallas_call(
        functools.partial(grouped_kernel, names, counts),
        out_shape=[shape for shape, _ in outs.items],
        in_specs=[spec for _, spec in ins.items],
        out_specs=[spec for _, spec in outs.items],
        scratch_shapes=flat,
        name="layer",
        compiler_params=pltpu.CompilerParams(
            collective_id=1, has_side_effects=True, vmem_limit_bytes=65_400 * 2**10
        ),
    )(*(value for value, _ in ins.items))
    layer_all, grad_all, gain_sums, grad_gate, grad_up, grad_down, grad_attn = results[:7]
    gate_like = jax.ShapeDtypeStruct(w_gate.shape, f32)
    tokens = jax.ShapeDtypeStruct((rows, width), low)
    gain_like = jax.ShapeDtypeStruct((part,), f32)
    square = jax.ShapeDtypeStruct((part, 2 * q_rows), f32)
    flat_heads = jax.ShapeDtypeStruct((2 * HEAD, part), f32)
    (
        layer_out,
        input_grad,
        gain_one,
        gain_two,
        grad_query,
        grad_key_t,
        grad_value_t,
        grad_output_t,
        grad_gate,
        grad_up,
        grad_down_t,
    ) = pl.pallas_call(
        finish_kernel,
        out_shape=[tokens] * 2
        + [gain_like] * 2
        + [square, flat_heads, flat_heads, square]
        + [gate_like] * 3,
        in_specs=[hbm, hbm, vmem, hbm, hbm, hbm, hbm],
        out_specs=[hbm] * 2 + [vmem] * 6 + [hbm] * 3,
        scratch_shapes=[vm((2, attn_rows, chip_part), f32)]
        + [vm((rows, width), low)] * 2
        + [vm(w_gate.shape, f32)] * 3
        + [dma((6,)), dma((11,))],
        name="finish",
        compiler_params=pltpu.CompilerParams(vmem_limit_bytes=65_400 * 2**10),
    )(layer_all, grad_all, gain_sums, grad_gate, grad_up, grad_down, grad_attn)
    return (
        layer_out[None],
        input_grad[None],
        gain_one,
        grad_query,
        grad_key_t.T,
        grad_value_t.T,
        grad_output_t.T,
        gain_two,
        grad_gate,
        grad_up,
        grad_down_t.T,
    )


def solution(mesh):
    plane = dict(mesh.shape) == {"dp": 2, "ctx": 4, "mp": 4}
    return jax.shard_map(
        on_plane if plane else any_mesh,
        mesh=mesh,
        in_specs=(
            P("dp", "ctx", None),
            P("dp", "ctx", None),
            P("dp"),
            P(("dp", "ctx")),
            P(("dp", "ctx"), "mp"),
            P(("dp", "ctx"), "mp"),
            P(("dp", "ctx"), "mp"),
            P("mp", ("dp", "ctx")),
            P(("dp", "ctx")),
            P(("dp", "ctx"), "mp"),
            P(("dp", "ctx"), "mp"),
            P("mp", ("dp", "ctx")),
        ),
        out_specs=(
            P("dp", "ctx", None),
            P("dp", "ctx", None),
            P(("dp", "ctx")),
            P(("dp", "ctx"), "mp"),
            P(("dp", "ctx"), "mp"),
            P(("dp", "ctx"), "mp"),
            P("mp", ("dp", "ctx")),
            P(("dp", "ctx")),
            P(("dp", "ctx"), "mp"),
            P(("dp", "ctx"), "mp"),
            P("mp", ("dp", "ctx")),
        ),
        check_vma=False,
    )
```

```python
import functools

import jax
import jax.numpy as jnp
import numpy as np
from jax import lax
from jax.experimental import pallas as pl
from jax.experimental.pallas import tpu as pltpu
from jax.sharding import PartitionSpec as P

HEAD = 80


EPS = 1e-05
THETA = 1000000.0
NEG = -1e30


def rope_tables(places, head_size):
    half = head_size // 2
    freq = THETA ** (-(jnp.arange(half, dtype=jnp.float32) * 2.0 / head_size))
    angle = places[:, None] * freq[None, :]
    return (jnp.cos(angle), jnp.sin(angle))


def rotate(tensor, cosine, sine_table):
    half = tensor.shape[-1] // 2
    first_half = tensor[..., :half]
    second_half = tensor[..., half:]
    cos_b = cosine[:, None, :]
    sin_b = sine_table[:, None, :]
    return jnp.concatenate(
        [first_half * cos_b - second_half * sin_b, second_half * cos_b + first_half * sin_b],
        axis=-1,
    )


def rotate_back(tensor, cosine, sine_table):
    half = tensor.shape[-1] // 2
    first_half = tensor[..., :half]
    second_half = tensor[..., half:]
    cos_b = cosine[:, None, :]
    sin_b = sine_table[:, None, :]
    return jnp.concatenate(
        [first_half * cos_b + second_half * sin_b, second_half * cos_b - first_half * sin_b],
        axis=-1,
    )


def normed(tensor, gain_row):
    return tensor * lax.rsqrt(jnp.mean(tensor * tensor, axis=-1, keepdims=True) + EPS) * gain_row


def norm_back(tensor, gain_row, grad_normed):
    scale_row = lax.rsqrt(jnp.mean(tensor * tensor, axis=-1, keepdims=True) + EPS)
    grad_scaled = grad_normed * gain_row
    grad_tensor = scale_row * grad_scaled - tensor * scale_row**3 * jnp.mean(
        grad_scaled * tensor, axis=-1, keepdims=True
    )
    grad_gain = jnp.sum(grad_normed * tensor * scale_row, axis=0)
    return (grad_tensor, grad_gain)


def masked_scores(query_seq, key_seq, length, places, kv_heads, group_size):
    query_grp = query_seq.reshape(query_seq.shape[0], kv_heads, group_size, HEAD)
    key_grp = key_seq.reshape(key_seq.shape[0], kv_heads, HEAD)
    raw_scores = jnp.einsum(
        "bkgh,tkh->kgbt", query_grp, key_grp, preferred_element_type=jnp.float32
    ) * HEAD ** (-0.5)
    key_places = jnp.arange(key_grp.shape[0], dtype=jnp.int32)
    allowed = (key_places[None, :] <= places[:, None]) & (key_places[None, :] < length)
    return jnp.where(allowed[None, None], raw_scores, NEG)


def any_mesh(
    hidden_in,
    cotangent,
    lengths,
    norm_attn,
    w_query,
    w_key,
    w_value,
    w_output,
    norm_mlp,
    w_gate,
    w_up,
    w_down,
):
    seq_count, slot_count, width_all = hidden_in.shape
    tok_rows = seq_count * slot_count
    attn_set = (
        lax.all_gather(w_query, ("dp", "ctx"), axis=0, tiled=True),
        lax.all_gather(w_key, ("dp", "ctx"), axis=0, tiled=True),
        lax.all_gather(w_value, ("dp", "ctx"), axis=0, tiled=True),
        lax.all_gather(w_output, ("dp", "ctx"), axis=1, tiled=True),
        lax.all_gather(norm_attn, ("dp", "ctx"), axis=0, tiled=True),
    )
    query_w, key_w, value_w, output_w, gain_attn = attn_set
    q_heads = query_w.shape[1] // HEAD
    kv_heads = key_w.shape[1] // HEAD
    group_size = q_heads // kv_heads
    first_slot = lax.axis_index("ctx") * slot_count
    places = first_slot + jnp.arange(slot_count, dtype=jnp.int32)
    valid_mask = (places[None, :] < lengths[:, None]).astype(jnp.float32).reshape(tok_rows, 1)
    cosine, sine_table = rope_tables(places.astype(jnp.float32), HEAD)
    inputs = hidden_in.reshape(tok_rows, width_all).astype(jnp.float32)
    gain_one = gain_attn.astype(jnp.float32)
    normed_one = normed(inputs, gain_one).astype(jnp.bfloat16)
    query_proj = jnp.dot(normed_one, query_w, preferred_element_type=jnp.float32).reshape(
        seq_count, slot_count, q_heads, HEAD
    )
    key_proj = jnp.dot(normed_one, key_w, preferred_element_type=jnp.float32).reshape(
        seq_count, slot_count, kv_heads, HEAD
    )
    value_low = (
        jnp.dot(normed_one, value_w, preferred_element_type=jnp.float32)
        .astype(jnp.bfloat16)
        .reshape(seq_count, slot_count, kv_heads * HEAD)
    )
    query_low = rotate(query_proj, cosine, sine_table).astype(jnp.bfloat16)
    key_low = (
        rotate(key_proj, cosine, sine_table)
        .astype(jnp.bfloat16)
        .reshape(seq_count, slot_count, kv_heads * HEAD)
    )
    key_all, value_all = (
        lax.all_gather(key_low, "ctx", axis=1, tiled=True),
        lax.all_gather(value_low, "ctx", axis=1, tiled=True),
    )

    def attend(members):
        query_seq, key_seq, value_seq, length = members
        scores = masked_scores(query_seq, key_seq, length, places, kv_heads, group_size)
        row_max = jnp.max(scores, axis=-1, keepdims=True)
        exponent = jnp.exp(scores - row_max)
        total = jnp.sum(exponent, axis=-1, keepdims=True)
        attention = (exponent / total).astype(jnp.bfloat16)
        value_grp = value_seq.reshape(value_seq.shape[0], kv_heads, HEAD)
        mixed_heads = jnp.einsum(
            "kgbt,tkh->bkgh", attention, value_grp, preferred_element_type=jnp.float32
        )
        return (mixed_heads.reshape(slot_count, q_heads * HEAD), (row_max + jnp.log(total))[..., 0])

    mixed_all, log_total = lax.map(attend, (query_low, key_all, value_all, lengths))
    attn_low = mixed_all.reshape(tok_rows, q_heads * HEAD).astype(jnp.bfloat16)
    branch = lax.psum(jnp.dot(attn_low, output_w, preferred_element_type=jnp.float32), "mp")
    middle = inputs + branch
    mlp_set = (
        lax.all_gather(w_gate, ("dp", "ctx"), axis=0, tiled=True),
        lax.all_gather(w_up, ("dp", "ctx"), axis=0, tiled=True),
        lax.all_gather(w_down, ("dp", "ctx"), axis=1, tiled=True),
        lax.all_gather(norm_mlp, ("dp", "ctx"), axis=0, tiled=True),
    )
    gate_w, up_w, down_w, gain_mlp = mlp_set
    gain_two = gain_mlp.astype(jnp.float32)
    normed_two = normed(middle, gain_two).astype(jnp.bfloat16)
    gate_proj = jnp.dot(normed_two, gate_w, preferred_element_type=jnp.float32)
    up_proj = jnp.dot(normed_two, up_w, preferred_element_type=jnp.float32)
    hidden = (jax.nn.silu(gate_proj) * up_proj).astype(jnp.bfloat16)
    mlp_out = lax.psum(
        jnp.dot(hidden, down_w, preferred_element_type=jnp.float32).astype(jnp.bfloat16), "mp"
    ).astype(jnp.float32)
    layer_out = (
        (valid_mask * (middle + mlp_out))
        .astype(jnp.bfloat16)
        .reshape(seq_count, slot_count, width_all)
    )
    grad_out = valid_mask * cotangent.reshape(tok_rows, width_all).astype(jnp.float32)
    grad_mlp = grad_out.astype(jnp.bfloat16)
    gate_back, up_back, down_back, gain_mlp_back = (
        lax.all_gather(w_gate, ("dp", "ctx"), axis=0, tiled=True),
        lax.all_gather(w_up, ("dp", "ctx"), axis=0, tiled=True),
        lax.all_gather(w_down, ("dp", "ctx"), axis=1, tiled=True),
        lax.all_gather(norm_mlp, ("dp", "ctx"), axis=0, tiled=True),
    )
    grad_hidden = jnp.einsum("tm,fm->tf", grad_mlp, down_back, preferred_element_type=jnp.float32)
    grad_down = jnp.einsum("tf,tm->fm", hidden, grad_mlp, preferred_element_type=jnp.float32)
    sigmoid_gate = jax.nn.sigmoid(gate_proj)
    grad_gate_low = (
        grad_hidden * up_proj * sigmoid_gate * (1.0 + gate_proj * (1.0 - sigmoid_gate))
    ).astype(jnp.bfloat16)
    grad_up_low = (grad_hidden * gate_proj * sigmoid_gate).astype(jnp.bfloat16)
    grad_gate = jnp.einsum(
        "td,tf->df", normed_two, grad_gate_low, preferred_element_type=jnp.float32
    )
    grad_up = jnp.einsum("td,tf->df", normed_two, grad_up_low, preferred_element_type=jnp.float32)
    partial_two = jnp.einsum(
        "tf,df->td", grad_gate_low, gate_back, preferred_element_type=jnp.float32
    ) + jnp.einsum("tf,df->td", grad_up_low, up_back, preferred_element_type=jnp.float32)
    grad_normed_two = lax.psum(partial_two, "mp")
    grad_middle_norm, grad_gain_two = norm_back(
        middle, gain_mlp_back.astype(jnp.float32), grad_normed_two
    )
    mlp_grads = (
        lax.psum_scatter(grad_gate, ("dp", "ctx"), scatter_dimension=0, tiled=True),
        lax.psum_scatter(grad_up, ("dp", "ctx"), scatter_dimension=0, tiled=True),
        lax.psum_scatter(grad_down, ("dp", "ctx"), scatter_dimension=1, tiled=True),
        lax.psum_scatter(grad_gain_two, ("dp", "ctx"), scatter_dimension=0, tiled=True),
    )
    grad_middle = grad_out + grad_middle_norm
    grad_branch = grad_middle.astype(jnp.bfloat16)
    query_back, key_back, value_back, output_back, gain_attn_back = (
        lax.all_gather(w_query, ("dp", "ctx"), axis=0, tiled=True),
        lax.all_gather(w_key, ("dp", "ctx"), axis=0, tiled=True),
        lax.all_gather(w_value, ("dp", "ctx"), axis=0, tiled=True),
        lax.all_gather(w_output, ("dp", "ctx"), axis=1, tiled=True),
        lax.all_gather(norm_attn, ("dp", "ctx"), axis=0, tiled=True),
    )
    grad_output = jnp.einsum("tq,td->qd", attn_low, grad_branch, preferred_element_type=jnp.float32)
    grad_attn_low = (
        jnp.einsum("td,qd->tq", grad_branch, output_back, preferred_element_type=jnp.float32)
        .astype(jnp.bfloat16)
        .reshape(seq_count, slot_count, q_heads, HEAD)
    )

    def attend_back(members):
        query_seq, key_seq, value_seq, length, log_seq, grad_seq = members
        scores = masked_scores(query_seq, key_seq, length, places, kv_heads, group_size)
        attention = jnp.exp(scores - log_seq[..., None])
        query_grp = query_seq.reshape(slot_count, kv_heads, group_size, HEAD)
        key_grp = key_seq.reshape(key_seq.shape[0], kv_heads, HEAD)
        value_grp = value_seq.reshape(value_seq.shape[0], kv_heads, HEAD)
        grad_grp = grad_seq.reshape(slot_count, kv_heads, group_size, HEAD)
        grad_attention = jnp.einsum(
            "bkgh,tkh->kgbt", grad_grp, value_grp, preferred_element_type=jnp.float32
        )
        inner = jnp.sum(attention * grad_attention, axis=-1, keepdims=True)
        grad_scores = (attention * (grad_attention - inner)).astype(jnp.bfloat16)
        scale_qk = HEAD ** (-0.5)
        grad_query_seq = (
            jnp.einsum("kgbt,tkh->bkgh", grad_scores, key_grp, preferred_element_type=jnp.float32)
            * scale_qk
        )
        grad_key_seq = (
            jnp.einsum("kgbt,bkgh->tkh", grad_scores, query_grp, preferred_element_type=jnp.float32)
            * scale_qk
        )
        grad_value_seq = jnp.einsum(
            "kgbt,bkgh->tkh",
            attention.astype(jnp.bfloat16),
            grad_grp,
            preferred_element_type=jnp.float32,
        )
        key_rows = key_grp.shape[0]
        return (
            grad_query_seq.reshape(slot_count, q_heads, HEAD),
            grad_key_seq.reshape(key_rows, kv_heads * HEAD),
            grad_value_seq.reshape(key_rows, kv_heads * HEAD),
        )

    grad_query_rot, grad_key_all, grad_value_all = lax.map(
        attend_back, (query_low, key_all, value_all, lengths, log_total, grad_attn_low)
    )
    grad_key_rot, grad_value_rot = (
        lax.psum_scatter(grad_key_all, "ctx", scatter_dimension=1, tiled=True),
        lax.psum_scatter(grad_value_all, "ctx", scatter_dimension=1, tiled=True),
    )
    grad_query_low = (
        rotate_back(grad_query_rot, cosine, sine_table)
        .astype(jnp.bfloat16)
        .reshape(tok_rows, q_heads * HEAD)
    )
    grad_key_low = (
        rotate_back(grad_key_rot.reshape(seq_count, slot_count, kv_heads, HEAD), cosine, sine_table)
        .astype(jnp.bfloat16)
        .reshape(tok_rows, kv_heads * HEAD)
    )
    grad_value_low = grad_value_rot.astype(jnp.bfloat16).reshape(tok_rows, kv_heads * HEAD)
    grad_query = jnp.einsum(
        "td,tq->dq", normed_one, grad_query_low, preferred_element_type=jnp.float32
    )
    grad_key = jnp.einsum("td,tq->dq", normed_one, grad_key_low, preferred_element_type=jnp.float32)
    grad_value = jnp.einsum(
        "td,tq->dq", normed_one, grad_value_low, preferred_element_type=jnp.float32
    )
    partial_one = jnp.einsum(
        "tq,dq->td", grad_query_low, query_back, preferred_element_type=jnp.float32
    )
    partial_one = partial_one + jnp.einsum(
        "tq,dq->td", grad_key_low, key_back, preferred_element_type=jnp.float32
    )
    partial_one = partial_one + jnp.einsum(
        "tq,dq->td", grad_value_low, value_back, preferred_element_type=jnp.float32
    )
    grad_normed_one = lax.psum(partial_one, "mp")
    grad_inputs_norm, grad_gain_one = norm_back(
        inputs, gain_attn_back.astype(jnp.float32), grad_normed_one
    )
    input_grad = (
        (grad_middle + grad_inputs_norm)
        .astype(jnp.bfloat16)
        .reshape(seq_count, slot_count, width_all)
    )
    attn_grads = (
        lax.psum_scatter(grad_query, ("dp", "ctx"), scatter_dimension=0, tiled=True),
        lax.psum_scatter(grad_key, ("dp", "ctx"), scatter_dimension=0, tiled=True),
        lax.psum_scatter(grad_value, ("dp", "ctx"), scatter_dimension=0, tiled=True),
        lax.psum_scatter(grad_output, ("dp", "ctx"), scatter_dimension=1, tiled=True),
        lax.psum_scatter(grad_gain_one, ("dp", "ctx"), scatter_dimension=0, tiled=True),
    )
    return (
        layer_out,
        input_grad,
        attn_grads[4],
        attn_grads[0],
        attn_grads[1],
        attn_grads[2],
        attn_grads[3],
        mlp_grads[3],
        mlp_grads[0],
        mlp_grads[1],
        mlp_grads[2],
    )


SPLIT = 2
GROUP = 384
NT = (((1,), (1,)), ((), ()))
TN = (((0,), (0,)), ((), ()))
MESH = pl.DeviceIdType.MESH


def remote(src, dst, sems, index, device):
    return pltpu.make_async_remote_copy(
        src_ref=src,
        dst_ref=dst,
        send_sem=sems.at[(0, *index)],
        recv_sem=sems.at[(1, *index)],
        device_id=device,
        device_id_type=MESH,
    )


def rows_at(start, size):
    return pl.ds(pl.multiple_of(start, 16), size)


def lanes_at(start, size):
    return pl.ds(pl.multiple_of(start, 128), size)


def chosen(rows, columns, first_column):
    row = lax.broadcasted_iota(jnp.int32, (rows, columns), 0)
    column = lax.broadcasted_iota(jnp.int32, (rows, columns), 1)
    return (row == column - first_column).astype(jnp.bfloat16)


def masked(keys, queries, length, block, first_query):
    scores = jnp.dot(keys, queries, preferred_element_type=jnp.float32) * HEAD ** (-0.5)
    rows, columns = scores.shape
    key_slots = block * rows + lax.broadcasted_iota(jnp.int32, scores.shape, 0)
    query_slots = first_query + lax.broadcasted_iota(jnp.int32, scores.shape, 1)
    return jnp.where((key_slots <= query_slots) & (key_slots < length), scores, NEG)


class Place:
    def __init__(self, owned, width):
        self.x, self.ctx, self.z = (lax.axis_index(name) for name in ("dp", "ctx", "mp"))
        self.core = lax.rem(self.ctx, 2)
        self.y = (self.ctx - self.core) // 2
        self.last = lax.axis_size("mp") - 1
        self.owned, self.rows, self.width = owned, owned * (self.last + 1), width
        self.step = width // SPLIT
        self.size, self.middle = width // 4, width // 8
        self.above, self.below = (self.x, self.ctx, self.z + 1), (self.x, self.ctx, self.z - 1)
        self.plane = {
            (turn, flip): self.turned(turn, flip)
            for turn in range(4)
            for flip in range(2)
            if turn or flip
        }
        self.sibling, self.over_x, self.over_y = (
            self.plane[key] for key in ((0, 1), (2, 0), (1, 0))
        )
        self.diagonal = self.plane[3, 0]
        self.column = [
            (self.x, self.other_core(flip), lax.rem(self.z + turn, self.last + 1))
            for turn in range(self.last + 1)
            for flip in range(2)
            if turn or flip
        ]

    def other_core(self, flip):
        return self.ctx + 1 - 2 * self.core if flip else self.ctx

    def turned(self, turn, flip):
        x_to = 1 - self.x if turn >= 2 else self.x
        y_to = 1 - self.y if turn % 2 else self.y
        core_to = 1 - self.core if flip else self.core
        return (x_to, 2 * y_to + core_to, self.z)

    def greet(self):
        for device in list(self.plane.values()) + self.column[1:]:
            pl.semaphore_signal(
                pltpu.get_barrier_semaphore(), inc=1, device_id=device, device_id_type=MESH
            )

    def enter(self):
        pl.semaphore_wait(pltpu.get_barrier_semaphore(), len(self.plane) + len(self.column) - 1)

    def span(self, half):
        size = self.owned if half is None else self.owned // 2
        return (half or 0) * size, size

    def block_of(self, core, block, half=None):
        first, size = self.span(half)
        return rows_at(core * self.rows + block * self.owned + first, size)

    def block(self, at, half=None):
        first, size = self.span(half)
        return rows_at(at * self.owned + first, size)

    def inner(self, half):
        return pl.ds(*self.span(half))

    def mine(self, half=None):
        return self.block_of(self.core, self.z, half)

    def columns(self, piece):
        return pl.ds(piece * self.step, self.step)

    def far(self, sign):
        return self.z if sign == 1 else self.last - self.z

    def target(self, sign, step):
        return self.z + sign * (self.last - step)

    def held_groups(self, core, x, groups):
        count = jnp.where(core == x, (groups + 1) // 2, groups // 2)
        return count, jnp.where(x == 1, groups - count, 0)

    def cut(self, turn):
        return slice(turn * self.size, (turn + 1) * self.size)

    def source(self, turn):
        x_to = 1 - self.x if turn >= 2 else self.x
        y_to = 1 - self.y if turn % 2 else self.y
        return lanes_at((2 * x_to + y_to) * self.size, self.size)


class SumChain:
    def __init__(
        self, place, part, held, ins, core_sem, up_sem, down_sem, extra=None, half=None
    ):
        self.place, self.part, self.held, self.ins, self.extra = place, part, held, ins, extra
        self.half, self.inner = half, place.inner(half)
        self.ways = ((place.above, 0, up_sem, 1), (place.below, place.last, down_sem, -1))
        self.core_sem = core_sem

    def across(self, block):
        place = self.place
        return remote(
            self.part.at[place.block_of(1 - place.core, block, self.half)],
            self.held.at[place.block(block, self.half)],
            self.core_sem,
            (block,),
            place.sibling,
        )

    def open(self):
        for block in range(self.place.last + 1):
            self.across(block).start()

    def wait(self, at):
        self.across(at).wait_recv()
        if self.extra is not None:
            self.extra.cross(at).wait_recv()

    def own(self, at, cols):
        place = self.place
        mine = self.part[place.block_of(place.core, at, self.half), cols].astype(jnp.float32)
        mine = mine + self.held[place.block(at, self.half), cols].astype(jnp.float32)
        if self.extra is not None:
            mine = mine + self.extra.came(at)[:, cols].astype(jnp.float32)
        return mine

    def hop(self, way, step, piece, at):
        place = self.place
        cols = place.columns(piece)
        return remote(
            self.part.at[place.block_of(place.core, at, self.half), cols],
            self.ins.at[way[1] + step, self.inner, cols],
            way[2],
            (step, piece),
            way[0],
        )

    def step(self, step):
        place = self.place
        for way in self.ways:

            @pl.when(place.far(way[3]) <= step)
            def _(way=way):
                at = place.target(way[3], step)
                rows = place.block_of(place.core, at, self.half)
                self.wait(at)
                for piece in range(SPLIT):
                    cols = place.columns(piece)
                    total = self.own(at, cols)
                    if step:

                        @pl.when(place.far(way[3]) > 0)
                        def _(total=total, cols=cols, piece=piece):
                            self.hop(way, step - 1, piece, at).wait_recv()
                            got = self.ins[way[1] + step - 1, self.inner, cols].astype(jnp.float32)
                            self.part[rows, cols] = (total + got).astype(self.part.dtype)

                        @pl.when(place.far(way[3]) == 0)
                        def _(total=total, cols=cols):
                            self.part[rows, cols] = total.astype(self.part.dtype)

                    else:
                        self.part[rows, cols] = total.astype(self.part.dtype)
                    self.hop(way, step, piece, at).start()

    def close(self, result):
        place = self.place
        final = place.last - 1
        self.wait(place.z)
        result = result.at[self.inner]
        result[...] = self.own(place.z, slice(None))
        for way in self.ways:

            @pl.when(place.far(way[3]) > 0)
            def _(way=way):
                for piece in range(SPLIT):
                    self.hop(way, final, piece, place.z).wait_recv()
                result[...] += self.ins[way[1] + final, self.inner].astype(jnp.float32)

    def drain(self):
        place = self.place
        for block in range(place.last + 1):
            self.across(block).wait_send()
        for step in range(place.last):
            for way in self.ways:

                @pl.when(place.far(way[3]) <= step)
                def _(way=way, step=step):
                    for piece in range(SPLIT):
                        self.hop(way, step, piece, place.target(way[3], step)).wait_send()


class CrossSum:
    def __init__(self, place, part, held, came, core_sem, x_sem, half=None):
        self.place, self.part, self.held = place, part, held
        self.came = lambda at: came(at, place.inner(half))
        self.core_sem, self.x_sem, self.half = core_sem, x_sem, half

    def across(self, block):
        place = self.place
        return remote(
            self.part.at[place.block_of(1 - place.core, block, self.half)],
            self.held.at[place.block(block, self.half)],
            self.core_sem,
            (block,),
            place.sibling,
        )

    def cross(self, at):
        place = self.place
        return remote(
            self.part.at[place.block_of(place.core, at, self.half)],
            self.came(at),
            self.x_sem,
            (at,),
            place.over_x,
        )

    def open(self):
        for block in range(self.place.last + 1):
            self.across(block).start()

    def send(self):
        place = self.place

        def one(at):
            self.across(at).wait_recv()
            rows = place.block_of(place.core, at, self.half)
            total = self.part[rows].astype(jnp.float32)
            total = total + self.held[place.block(at, self.half)].astype(jnp.float32)
            self.part[rows] = total.astype(self.part.dtype)
            self.cross(at).start()

        for step in range(place.last):
            for sign in (1, -1):

                @pl.when(place.far(sign) <= step)
                def _(sign=sign):
                    one(place.target(sign, step))

        one(place.z)

    def drain(self):
        for block in range(self.place.last + 1):
            self.across(block).wait_send()
            self.cross(block).wait_send()


class ShareChain:
    def __init__(self, place, whole, up_sem, down_sem, core_sem=None, half=None):
        self.place, self.whole, self.core_sem, self.half = place, whole, core_sem, half
        self.ways = ((place.above, up_sem, 1), (place.below, down_sem, -1))

    def rows(self, at):
        place = self.place
        if self.core_sem is None:
            return place.block(at, self.half)
        return place.block_of(place.core, at, self.half)

    def hop(self, way, step, piece, origin):
        ref = self.whole.at[self.rows(origin), self.place.columns(piece)]
        return remote(ref, ref, way[1], (step, piece), way[0])

    def across(self, origin, core):
        ref = self.whole.at[self.place.block_of(core, origin, self.half)]
        return remote(ref, ref, self.core_sem, (origin,), self.place.sibling)

    def step(self, step):
        place = self.place
        for way in self.ways:
            origin = place.z - way[2] * step

            @pl.when(place.far(way[2]) >= step)
            def _(way=way, origin=origin):
                for piece in range(SPLIT):
                    if step:
                        self.hop(way, step - 1, piece, origin).wait_recv()
                    if step < place.last:

                        @pl.when(place.far(way[2]) < place.last)
                        def _(piece=piece):
                            self.hop(way, step, piece, origin).start()

                if step and self.core_sem is not None:
                    self.across(origin, place.core).start()

        if step == 0 and self.core_sem is not None:
            self.across(place.z, place.core).start()

    def reached(self, step):
        place = self.place
        if step == 0:
            return [(place.z >= 0, place.z)]
        return [(place.far(sign) >= step, place.z - sign * step) for sign in (1, -1)]

    def arrive(self):
        if self.core_sem is not None:
            for origin in range(self.place.last + 1):
                self.across(origin, 1 - self.place.core).wait_recv()

    def drain(self):
        place = self.place
        for step in range(place.last):
            for way in self.ways:

                @pl.when((place.far(way[2]) >= step) & (place.far(way[2]) < place.last))
                def _(way=way, step=step):
                    for piece in range(SPLIT):
                        self.hop(way, step, piece, place.z - way[2] * step).wait_send()

        if self.core_sem is not None:
            for origin in range(place.last + 1):
                self.across(origin, place.core).wait_send()


class AttnGather:
    def __init__(self, place, w, first, by_y, by_x, x_sem, y_sem, far_sem, index):
        self.place, self.w, self.index = place, w, index
        self.sems = (x_sem, y_sem, far_sem)
        self.halves = (pl.ds(first, by_y), pl.ds(first + by_y, by_x))

    def cross(self, half, to_x):
        place, rows = self.place, self.halves[half]
        return remote(
            self.w.at[0, rows],
            self.w.at[2 if to_x else 1, rows],
            self.sems[0] if to_x else self.sems[1],
            (self.index + half,),
            place.over_x if to_x else place.over_y,
        )

    def relay(self, to_x):
        place, half = self.place, 1 if to_x else 0
        rows = self.halves[half]
        return remote(
            self.w.at[1 if to_x else 2, rows],
            self.w.at[3, rows],
            self.sems[2],
            (self.index + half,),
            place.over_x if to_x else place.over_y,
        )

    def send(self, which):
        self.cross(which, True).start()
        self.cross(1 - which, False).start()

    def pass_on(self):
        self.cross(0, True).wait_recv()
        self.relay(False).start()
        self.cross(1, False).wait_recv()
        self.relay(True).start()

    def drain(self):
        for half in range(2):
            for to_x in (True, False):
                self.cross(half, to_x).wait_send()
        self.relay(True).wait_send()
        self.relay(False).wait_send()


class WideGather:
    def __init__(self, place, block, w, x_sem, y_sem, far_sem):
        self.place, self.block, self.w = place, block, w
        self.x_sem, self.y_sem, self.far_sem = x_sem, y_sem, far_sem
        self.groups = block.shape[1] // GROUP
        self.most = (self.groups + 1) // 2
        self.count, self.base = place.held_groups(place.core, place.x, self.groups)
        self.other_count, self.other_base = place.held_groups(
            place.core, 1 - place.x, self.groups
        )

    def cross_x(self, group):
        return remote(
            self.block.at[:, lanes_at((self.other_base + group) * GROUP, GROUP)],
            self.w.at[1, :, lanes_at(group * GROUP, GROUP)],
            self.x_sem,
            (group,),
            self.place.over_x,
        )

    def came_x(self, group):
        here = self.w.at[1, :, lanes_at(group * GROUP, GROUP)]
        return remote(here, here, self.x_sem, (group,), self.place.over_x)

    def cross_y(self, group):
        return remote(
            self.block.at[:, lanes_at((self.base + group) * GROUP, GROUP)],
            self.w.at[0, :, lanes_at(group * GROUP, GROUP)],
            self.y_sem,
            (group,),
            self.place.over_y,
        )

    def pass_on(self, group):
        cols = lanes_at(group * GROUP, GROUP)
        return remote(
            self.w.at[1, :, cols], self.w.at[2, :, cols], self.far_sem, (group,), self.place.over_y
        )

    def start(self):
        def body(group, carry):
            self.cross_x(group).start()
            return carry

        lax.fori_loop(0, self.other_count, body, 0)

        self.cross_y(0).start()
        self.cross_y(1).start()

    def pump(self, group):
        @pl.when(group < self.count)
        def _():
            self.came_x(group).wait_recv()
            self.pass_on(group).start()

        @pl.when(group + 2 < self.count)
        def _():
            self.cross_y(group + 2).start()

    def arrive(self, group):
        self.cross_y(group).wait_recv()
        self.pass_on(group).wait_recv()

    def rows(self, turn, group, first, size):
        if turn == 0:
            return self.block[:, lanes_at((self.base + group) * GROUP + first, size)]
        return self.w[turn - 1, :, lanes_at(group * GROUP + first, size)]

    def drain(self):
        def sent_x(group, carry):
            self.cross_x(group).wait_send()
            return carry

        def sent_y(group, carry):
            self.cross_y(group).wait_send()
            self.pass_on(group).wait_send()
            return carry

        lax.fori_loop(0, self.other_count, sent_x, 0)
        lax.fori_loop(0, self.count, sent_y, 0)


class Home:
    kinds = ("upper", "lower", "x_one", "y_two", "y_one", "x_two")

    def __init__(self, place, sources, targets, sem, cut):
        self.place, self.sem, self.cut = place, sem, cut
        self.sources, self.targets = sources, targets

    def copy(self, kind, group):
        place, index = self.place, self.kinds.index(kind)
        to_x = kind in ("upper", "x_one", "x_two")
        return remote(
            self.cut(self.sources[kind], group),
            self.cut(self.targets[kind], group),
            self.sem,
            (index, group),
            place.over_x if to_x else place.over_y,
        )

    def send(self, kinds, group):
        for kind in kinds:
            self.copy(kind, group).start()

    def arrive(self, kinds, group):
        for kind in kinds:
            self.copy(kind, group).wait_recv()

    def drain(self, group):
        for kind in self.kinds:
            self.copy(kind, group).wait_send()


class WideHome:
    kinds = ("near", "far", "cross")

    def __init__(self, place, sources, targets, sem):
        self.place, self.sources, self.targets, self.sem = place, sources, targets, sem

    def copy(self, kind, group):
        cols = lanes_at(group * GROUP, GROUP)
        return remote(
            self.sources[kind].at[:, cols],
            self.targets[kind].at[:, cols],
            self.sem,
            (self.kinds.index(kind), group),
            self.place.over_x if kind == "cross" else self.place.over_y,
        )


class Refs:
    def __init__(self, names, refs):
        for name, ref in zip(names, refs, strict=True):
            setattr(self, name, ref)


def layer_kernel(names, *refs):
    r = Refs(names, refs)
    f32, low = jnp.float32, jnp.bfloat16
    z_count = lax.axis_size("mp")
    rows, width = r.hidden.shape
    place = Place(rows // z_count, width)
    size, middle, core = place.size, place.middle, place.core
    cut = place.cut
    part_rows = r.query.shape[0]
    q_rows = r.query.shape[1] // 2
    heads = q_rows // HEAD
    qkv_rows = q_rows + 2 * HEAD
    attn_rows = qkv_rows + q_rows
    chip_rows = 2 * rows
    attn_halves = (attn_rows - chip_rows, chip_rows)
    length = r.length[0, 0]
    cos_at, sin_at = r.cos[place.y], r.sin[place.y]
    w, aw = r.w, r.aw
    ff = r.gate.shape[1] // 2
    groups = ff // 128

    both_halves = range(2)
    branch_sum = [
        SumChain(place, r.part, *r.chain_one, *r.branch_sems[3 * k : 3 * k + 3], half=k)
        for k in both_halves
    ]
    h2_share = [
        ShareChain(place, r.h2, *r.h2_sems[3 * k : 3 * k + 3], half=k) for k in both_halves
    ]
    dm_share = ShareChain(place, r.dm_x, *r.dm_x_sems)
    back_cross = [
        CrossSum(
            place,
            r.mlp_part,
            r.chain_one[0],
            lambda at, inner: r.chain_one[1].at[at, inner],
            *r.back_cross_sems[2 * k : 2 * k + 2],
            half=k,
        )
        for k in both_halves
    ]
    mlp_cross = CrossSum(
        place,
        r.h2_x,
        r.h2.at[pl.ds(0, rows)],
        lambda at, inner: r.h2.at[rows_at(rows + at * place.owned, place.owned)],
        *r.mlp_cross_sems,
    )
    back_sum = [
        SumChain(
            place,
            r.part,
            *r.chain_two,
            *r.back_sems[3 * k : 3 * k + 3],
            extra=back_cross[k],
            half=k,
        )
        for k in both_halves
    ]
    mlp_sum = SumChain(place, r.dm_x, *r.chain_one, *r.mlp_sems, mlp_cross)
    da_share = [
        ShareChain(place, r.da, *r.da_sems[3 * k : 3 * k + 3], half=k) for k in both_halves
    ]
    input_sum = [
        SumChain(place, r.part, *r.chain_two, *r.input_sems[3 * k : 3 * k + 3], half=k)
        for k in both_halves
    ]
    layer_share = ShareChain(place, r.layer_all, *r.layer_sems)
    grad_share = [
        ShareChain(place, r.grad_all, *r.grad_sems[2 * k : 2 * k + 2], half=k)
        for k in both_halves
    ]

    def each(pair, name, *args):
        for member in pair:
            getattr(member, name)(*args)

    def chained(sums, shares, end, between, late):
        ahead, behind = sums
        first, second = shares
        ahead.step(0)
        if not late:
            behind.step(0)
        between(0)
        ahead.step(1)
        if not late:
            behind.step(1)
        between(1)
        ahead.step(2)
        between("ahead")
        end(0)
        first.step(0)
        if late:
            behind.step(0)
            between(2)
            behind.step(1)
        behind.step(2)
        if not late:
            between(2)
        first.step(1)
        between(3)
        end(1)
        second.step(0)
        first.step(2)
        between(4)
        second.step(1)
        first.step(3)
        between(5)
        second.step(2)
        between(6)
        second.step(3)
        between(7)
    sems = (r.attn_x, r.attn_y, r.attn_far)
    half_q = q_rows // 32 * 16
    q_gather = AttnGather(place, aw, 0, half_q, q_rows - half_q, *sems, 0)
    out_gather = AttnGather(place, aw, qkv_rows, half_q, q_rows - half_q, *sems, 2)
    kv_gather = AttnGather(place, aw, q_rows, 2 * HEAD - 16, 16, *sems, 4)
    gather = WideGather(place, r.block, w, r.wide_x, r.wide_y, r.wide_far)
    count, base = gather.count, gather.base

    my_rows = rows_at(core * rows, rows)
    loads = [
        pltpu.make_async_copy(r.hidden, r.da.at[pl.ds(0, rows)], r.load_sem.at[0]),
        pltpu.make_async_copy(r.cotangent, r.da.at[pl.ds(rows, rows)], r.load_sem.at[1]),
    ]
    place.greet()
    for load in loads:
        load.start()
    to_lanes = chosen(part_rows, size, core * part_rows)

    def split(total):
        half = total.shape[0] // 2
        one, two = total[:half], total[half:]
        pair = jnp.where(core == 0, one, two), jnp.where(core == 0, two, one)
        return tuple(member.astype(low) for member in pair)

    def spread(tensor, dims):
        return split(lax.dot_general(tensor, to_lanes, dims, preferred_element_type=f32))

    plain = (((1,), (0,)), ((), ()))
    q_pair, k_pair, v_pair = (
        spread(r.query[...], TN),
        spread(r.key_t[...], plain),
        spread(r.value_t[...], plain),
    )
    qkv_give = r.part.at[pl.ds(0, qkv_rows), pl.ds(0, size)]
    qkv_take = r.mlp_part.at[pl.ds(0, qkv_rows), pl.ds(0, size)]
    out_give = r.part.at[pl.ds(0, q_rows), pl.ds(size, size)]
    out_take = r.mlp_part.at[pl.ds(0, q_rows), pl.ds(size, size)]
    qkv_give[...] = jnp.concatenate([q_pair[1], k_pair[1], v_pair[1]], axis=0)
    for load in loads:
        load.wait()
    hidden, cotangent = r.da.at[pl.ds(0, rows)], r.da.at[pl.ds(rows, rows)]
    slot = place.ctx * rows + lax.broadcasted_iota(jnp.int32, (rows, size), 0)
    for turn in range(4):
        block = cotangent[:, place.source(turn)].astype(f32)
        r.dm[my_rows, cut(turn)] = jnp.where(slot < length, block, 0.0).astype(low)
    row = lax.broadcasted_iota(jnp.int32, r.gains.shape, 0)
    gain_pair = [
        jnp.dot(jnp.broadcast_to(norm[...][None], (8, part_rows)), to_lanes, preferred_element_type=f32)
        for norm in (r.norm_one, r.norm_two)
    ]
    r.gains[...] = jnp.where(row == 0, gain_pair[0], jnp.where(row == 1, gain_pair[1], 0.0))
    r.gains_all[core] = r.gains[...]
    r.gain_part[...] = jnp.zeros_like(r.gain_part)

    def gain_copy(turn, flip):
        slot = 2 * turn + core
        return remote(
            r.gains, r.gains_all.at[slot], r.gain_sem, (2 * turn + flip,), place.plane[turn, flip]
        )

    place.enter()
    for turn, flip in place.plane:
        gain_copy(turn, flip).start()
    qkv_swap = remote(qkv_give, qkv_take, r.core_sem, (0,), place.sibling)
    qkv_swap.start()
    dm_cross = remote(
        r.dm.at[place.mine()], r.dm_x.at[place.mine()], r.dm_cross_sem, (0,), place.over_x
    )
    dm_cross.start()
    dm_copy = remote(r.dm.at[my_rows], r.dm.at[my_rows], r.dm_sem, (0,), place.sibling)
    dm_copy.start()

    qkv_keep = jnp.concatenate([q_pair[0], k_pair[0], v_pair[0]], axis=0)
    qkv_swap.wait_recv()
    aw[0, :qkv_rows] = qkv_keep + qkv_take[...]
    kv_gather.send(0)
    kv_gather.send(1)
    q_gather.send(0)
    q_gather.send(1)
    out_pair = spread(r.output_t[...], TN)
    out_give[...] = out_pair[1]
    out_swap = remote(out_give, out_take, r.core_sem, (1,), place.sibling)
    out_swap.start()

    def wide_copies(group, kind, source):
        from_here = lanes_at(core * ff + group * 128, 128)
        from_there = lanes_at((1 - core) * ff + group * 128, 128)
        to = lanes_at(group * GROUP + kind * 128, 128)
        owner_rows = rows_at(core * part_rows, part_rows)
        here = pltpu.make_async_copy(
            source.at[:, from_here], r.block.at[owner_rows, to], r.wide_here.at[kind, group]
        )
        there = remote(
            source.at[:, from_there],
            r.block.at[owner_rows, to],
            r.wide_there,
            (kind, group),
            place.sibling,
        )
        return here, there

    sources = (r.gate, r.up, r.down_t)

    def start_wide(group, carry):
        for kind, source in enumerate(sources):
            for copy in wide_copies(group, kind, source):
                copy.start()
        return carry

    def own_wide(group, carry):
        for kind, source in enumerate(sources):
            here, there = wide_copies(group, kind, source)
            here.wait()
            there.wait_recv()
        return carry

    for turn in range(4):
        r.inputs_own[:, cut(turn)] = r.da[place.block(place.z), place.source(turn)].astype(f32)
    out_swap.wait_recv()
    aw[0, qkv_rows:] = out_pair[0] + out_take[...]
    squares = jnp.zeros((rows, 1), f32)
    for turn in range(4):
        block = hidden[:, cut(turn)].astype(f32)
        squares += jnp.sum(block * block, axis=-1, keepdims=True)
    scale = lax.rsqrt(squares / width + EPS)
    for turn, flip in place.plane:
        gain_copy(turn, flip).wait_recv()
    for turn in range(4):
        gain = r.gains_all[2 * turn] + r.gains_all[2 * turn + 1]
        r.gain_rows[:, cut(turn)] = gain
        block = hidden[:, place.source(turn)].astype(f32)
        r.h1[my_rows, cut(turn)] = (block * scale * gain[:1]).astype(low)
    h1_copy = remote(r.h1.at[my_rows], r.h1.at[my_rows], r.h1_sem, (0,), place.sibling)
    h1_copy.start()

    qkv = r.dh2.at[pl.ds(0, qkv_rows), pl.ds(0, chip_rows)]
    q_part, kv_part = slice(0, q_rows), slice(q_rows, qkv_rows)

    def qkv_dot(turn, part):
        return lax.dot_general(
            aw[turn, part], r.h1[:, cut(turn)], NT, preferred_element_type=f32
        )

    def gathered_dot(group, part):
        group.cross(1, True).wait_recv()
        qkv[part] += qkv_dot(2, part)
        group.cross(0, False).wait_recv()
        qkv[part] += qkv_dot(1, part)
        group.relay(False).wait_recv()
        group.relay(True).wait_recv()
        qkv[part] += qkv_dot(3, part)

    h1_copy.wait_recv()
    qkv[...] = qkv_dot(0, slice(0, qkv_rows))
    kv_gather.pass_on()
    lax.fori_loop(0, groups, start_wide, 0)

    def sent_wide(group, carry):
        for kind, source in enumerate(sources):
            wide_copies(group, kind, source)[1].wait_send()
        return carry

    q_gather.pass_on()
    dm_cross.wait_recv()
    dm_share.step(0)
    gathered_dot(kv_gather, kv_part)

    def turned(first_row):
        ahead = qkv[first_row : first_row + HEAD // 2]
        behind = qkv[first_row + HEAD // 2 : first_row + HEAD]
        return jnp.concatenate(
            [ahead * cos_at - behind * sin_at, behind * cos_at + ahead * sin_at], axis=0
        )

    r.kv[place.y, :HEAD] = turned(q_rows).astype(low)
    r.kv[place.y, HEAD:] = qkv[q_rows + HEAD : qkv_rows].astype(low)
    kv_copy = remote(r.kv.at[place.y], r.kv.at[place.y], r.kv_sem, (0,), place.over_y)
    kv_copy.start()
    out_gather.send(0)
    out_gather.send(1)
    gathered_dot(q_gather, q_part)
    head_rows = [slice(head * HEAD, (head + 1) * HEAD) for head in range(heads)]
    for head in range(heads):
        r.q_t[head_rows[head]] = turned(head * HEAD).astype(low)
    dm_share.step(1)
    kv_copy.wait_recv()

    keys = [r.kv[block, :HEAD].T for block in range(2)]
    half_slots = chip_rows // 2
    query_halves = [
        (slice(half * half_slots, (half + 1) * half_slots), place.y * chip_rows + half * half_slots)
        for half in range(2)
    ]
    def head_forward(head, carry):
        at = rows_at(head * HEAD, HEAD)
        for lanes, first_query in query_halves:
            queries = r.q_t[at, lanes]
            scores = [
                masked(keys[block], queries, length, block, first_query) for block in range(2)
            ]
            top = jnp.maximum(*(jnp.max(score, axis=0, keepdims=True) for score in scores))
            exponents = [jnp.exp(score - top) for score in scores]
            total = sum(jnp.sum(exponent, axis=0, keepdims=True) for exponent in exponents)
            mixed = jnp.zeros((HEAD, half_slots), f32)
            for block in range(2):
                weights = (exponents[block] / total).astype(low)
                mixed += jnp.dot(r.kv[block, HEAD:], weights, preferred_element_type=f32)
            r.o_t[at, lanes] = mixed.astype(low)
            r.lse[pl.ds(head, 1), lanes] = top + jnp.log(total)
        return carry

    lax.fori_loop(0, heads, head_forward, 0)
    out_gather.pass_on()
    lax.fori_loop(0, groups, own_wide, 0)
    gather.start()
    dm_share.step(2)
    out_gather.cross(1, True).wait_recv()
    out_gather.cross(0, False).wait_recv()
    out_gather.relay(False).wait_recv()
    out_gather.relay(True).wait_recv()
    qkv_swap.wait_send()
    out_swap.wait_send()
    mixed_all = r.o_t[...].T
    for turn in range(4):
        r.part[:, cut(turn)] = jnp.dot(
            mixed_all, aw[turn, qkv_rows:], preferred_element_type=f32
        ).astype(low)

    each(branch_sum, "open")
    gain_two = r.gain_rows[1:2]

    def h2_cross(origin, half):
        block = place.block_of(core, origin, half)
        return remote(
            r.h2.at[block], r.h2_x.at[block], r.h2_cross_sem, (half, origin), place.over_x
        )

    def h2_across(origin, of_core, half):
        block = place.block_of(of_core, origin, half)
        return remote(
            r.h2_x.at[block], r.h2_x.at[block], r.h2_across_sem, (half, origin), place.sibling
        )

    def branch_end(half):
        inner = place.inner(half)
        branch_sum[half].close(r.middle)
        r.middle[inner] += r.inputs_own[inner]
        r.h2[place.mine(half)] = normed(r.middle[inner], gain_two).astype(low)
        h2_cross(place.z, half).start()

    def h2_on(half, step):
        for here, origin in h2_share[half].reached(step):

            @pl.when(here)
            def _(origin=origin):
                h2_cross(origin, half).start()

    def beside_branch(when):
        if when == 0:
            dm_share.step(3)
        if when == 2:
            gather.pump(0)
        if when == 3:
            h2_on(0, 1)
            gather.pump(1)
        if when == 4:
            h2_on(0, 2)
            gather.pump(2)
        if when == 5:
            h2_on(1, 1)
            h2_on(0, 3)
            gather.pump(3)
        if when == 6:
            h2_on(1, 2)
        if when == 7:
            h2_on(1, 3)

    chained(branch_sum, h2_share, branch_end, beside_branch, False)
    each(h2_share, "arrive")
    each(branch_sum, "drain")
    dm_copy.wait()
    dm_share.arrive()

    zd_rows = (slice(0, chip_rows), slice(chip_rows, 2 * chip_rows))
    tokens = ((r.h2, r.dm), (r.h2_x, r.dm_x))

    def cut_of(turn, which):
        return cut(turn ^ 2 if which else turn)

    def activate(group, which):
        left, d_left = tokens[which]
        gu = jnp.zeros((chip_rows, 256), f32)
        d_hidden = jnp.zeros((chip_rows, 128), f32)
        for turn in range(4):
            gu += jnp.dot(
                left[:, cut_of(turn, which)], gather.rows(turn, group, 0, 256), preferred_element_type=f32
            )
            d_hidden += jnp.dot(
                d_left[:, cut_of(turn, which)],
                gather.rows(turn, group, 256, 128),
                preferred_element_type=f32,
            )
        gate, up = gu[:, :128], gu[:, 128:]
        sigma = jax.nn.sigmoid(gate)
        silu = gate * sigma
        d_gate = d_hidden * up * sigma * (1.0 + gate * (1.0 - sigma))
        at = zd_rows[which]
        start = group * GROUP
        r.zd[at, lanes_at(start, 128)] = d_gate.astype(low)
        r.zd[at, lanes_at(start + 128, 128)] = (d_hidden * silu).astype(low)
        r.zd[at, lanes_at(start + 256, 128)] = (silu * up).astype(low)

    def gradients(group):
        cols = lanes_at(group * GROUP, GROUP)
        for turn in range(4):
            grad_gu = jnp.zeros((size, 256), f32)
            grad_down = jnp.zeros((size, 128), f32)
            for which, (left, d_left) in enumerate(tokens):
                at = zd_rows[which]
                grad_gu += lax.dot_general(
                    left[:, cut_of(turn, which)],
                    r.zd[at, lanes_at(group * GROUP, 256)],
                    TN,
                    preferred_element_type=f32,
                )
                grad_down += lax.dot_general(
                    d_left[:, cut_of(turn, which)],
                    r.zd[at, lanes_at(group * GROUP + 256, 128)],
                    TN,
                    preferred_element_type=f32,
                )
            if turn:
                r.tile[turn - 1, :, :256] = grad_gu.astype(low)
                r.tile[turn - 1, :, 256:] = grad_down.astype(low)
            else:
                r.tile_own[:, :256] = grad_gu
                r.tile_own[:, 256:] = grad_down
        keep = pltpu.make_async_copy(r.tile, r.stage.at[:, :, cols], r.keep_sem.at[0])
        keep_own = pltpu.make_async_copy(r.tile_own, r.own_grad.at[:, cols], r.keep_sem.at[1])
        keep.start()
        keep_own.start()
        keep.wait()
        keep_own.wait()

    def each_count(act):
        for number in sorted({groups // 2, (groups + 1) // 2}):

            @pl.when(count == number)
            def _(number=number):
                act(number)

    def summed(into, which, first, width_of, turns):
        def act(number):
            for turn in turns:
                out = jnp.zeros((chip_rows, size), f32)
                for group in range(number):
                    out += lax.dot_general(
                        r.zd[zd_rows[which], lanes_at(group * GROUP + first, width_of)],
                        gather.rows(turn, group, first, width_of),
                        NT,
                        preferred_element_type=f32,
                    )
                into[:, cut_of(turn, which)] = out.astype(low)

        each_count(act)

    home = WideHome(
        place,
        {"near": r.stage.at[0], "far": r.stage.at[2], "cross": w.at[0]},
        {"near": r.near, "far": r.far, "cross": r.crossed},
        r.home_sem,
    )

    def send_grads(group, kinds):
        for kind in kinds:
            home.copy(kind, group).start()

    def if_last(act):
        pl.when(count > least)(act)

    least = groups // 2
    gather.arrive(0)
    activate(0, 0)
    for half in both_halves:
        for origin in range(z_count):
            h2_cross(origin, half).wait_recv()
            h2_across(origin, core, half).start()
    gather.arrive(1)
    activate(1, 0)
    for half in both_halves:
        for origin in range(z_count):
            h2_across(origin, 1 - core, half).wait_recv()
    for group in range(least):
        if group > 1:
            gather.arrive(group)
            activate(group, 0)
        activate(group, 1)
    gradients(0)
    send_grads(0, ("far",))

    @if_last
    def _():
        gather.arrive(least)
        activate(least, 1)
        activate(least, 0)

    summed(r.mlp_part, 1, 0, 256, range(4))
    each(back_cross, "open")
    summed(r.part, 0, 0, 256, range(2))
    back_cross[0].send()
    summed(r.part, 0, 0, 256, range(2, 4))
    back_cross[1].send()
    each(back_sum, "open")

    def back_end(half):
        inner = place.inner(half)
        back_sum[half].close(r.d_middle)
        d_norm, d_gain = norm_back(r.middle[inner], gain_two, r.d_middle[inner])
        if half:
            d_gain = d_gain + r.gain_part[1]
        r.gain_part[1:2] = d_gain[None]
        r.d_middle[inner] = r.dm[place.mine(half)].astype(f32) + d_norm
        r.da[place.mine(half)] = r.d_middle[inner].astype(low)

    def beside_back(when):
        if when in (0, 1):
            gradients(when + 1)
            send_grads(when + 1, ("far",))
        if when == 2:

            @if_last
            def _():
                gradients(least)
                send_grads(least, ("far",))

            send_grads(0, ("near",))
            each(h2_share, "drain")
            dm_share.drain()
            lax.fori_loop(0, groups, sent_wide, 0)
            for half in both_halves:
                for origin in range(z_count):
                    h2_cross(origin, half).wait_send()
                    h2_across(origin, core, half).wait_send()
            for device in (place.sibling, place.over_x):
                quiet(r.quiet_sem, device)
            summed(r.h2_x, 1, 256, 128, range(4))
        if when == 3:
            pl.semaphore_wait(r.quiet_sem, 2)
            mlp_cross.open()
            summed(r.dm_x, 0, 256, 128, range(4))
            mlp_cross.send()
            send_grads(1, ("near",))
        if when == 4:
            quiet(r.chain_sem, place.sibling)

            @pl.when(place.z < place.last)
            def _():
                quiet(r.chain_sem, place.above)

            @pl.when(place.z > 0)
            def _():
                quiet(r.chain_sem, place.below)

        if when == 5:
            ends = jnp.where(place.z == 0, 1, 0) + jnp.where(place.z == place.last, 1, 0)
            pl.semaphore_wait(r.chain_sem, 3 - ends)
            mlp_sum.open()
            mlp_sum.step(0)
        if when == 7:
            mlp_sum.step(1)

    def quiet(sem, device):
        pl.semaphore_signal(sem, inc=1, device_id=device, device_id_type=MESH)

    chained(back_sum, da_share, back_end, beside_back, True)

    dm_cross.wait_send()
    for device in (place.over_x, place.over_y):
        pl.semaphore_signal(r.free_sem, inc=1, device_id=device, device_id_type=MESH)
    gather.drain()
    part_load = pltpu.make_async_copy(r.stage.at[1], w.at[0], r.load_sem.at[2])
    part_load.start()
    each(da_share, "arrive")
    each(back_sum, "drain")
    each(back_cross, "drain")
    do_t, d_t, kv_give = (
        r.mlp_part.at[pl.ds(0, number), pl.ds(at * chip_rows, chip_rows)]
        for at, number in enumerate((q_rows, qkv_rows, 2 * HEAD))
    )
    dk, dv = (
        [r.dh2.at[:, pl.ds(3 * 256 + 128 * at + 256 * which, HEAD)] for at in range(2)]
        for which in range(2)
    )

    d_out = jnp.zeros((q_rows, chip_rows), f32)
    for turn in range(4):
        d_out += lax.dot_general(
            aw[turn, qkv_rows:], r.da[:, cut(turn)], NT, preferred_element_type=f32
        )
    do_t[...] = d_out.astype(low)
    values = [r.kv[block, HEAD:].T for block in range(2)]
    keys = [r.kv[block, :HEAD].T for block in range(2)]
    scale = HEAD ** (-0.5)
    for ref in dk + dv:
        ref[...] = jnp.zeros(ref.shape, f32)

    def turned_back(tensor, cosine, sine):
        ahead, behind = tensor[: HEAD // 2], tensor[HEAD // 2 :]
        return jnp.concatenate(
            [ahead * cosine + behind * sine, behind * cosine - ahead * sine], axis=0
        )

    def far_load(group):
        cols = lanes_at(group * GROUP, GROUP)
        return pltpu.make_async_copy(r.far.at[:, cols], w.at[1, :, cols], r.add_sem.at[group])

    def fetch_far(group, carry):
        home.copy("far", group).wait_recv()
        far_load(group).start()
        return carry

    def send_cross(group, carry):
        cols = lanes_at(group * GROUP, GROUP)
        far_load(group).wait()
        mine = w[0, :, cols].astype(f32) + w[1, :, cols].astype(f32)
        w[0, :, cols] = mine.astype(low)
        home.copy("cross", group).start()
        return carry

    lax.fori_loop(0, count, fetch_far, 0)
    part_load.wait()
    def finish_layer():
        mlp_sum.close(r.mlp)
        slot = place.ctx * place.rows + place.z * place.owned
        slot += lax.broadcasted_iota(jnp.int32, r.middle.shape, 0)
        r.layer_all[place.block(place.z)] = jnp.where(
            slot < length, r.middle[...] + r.mlp[...], 0.0
        ).astype(low)
        layer_share.step(0)

    def head_back(head, carry):
        at = rows_at(head * HEAD, HEAD)
        for lanes, first_query in query_halves:
            queries, d_head = r.q_t[at, lanes], do_t[at, lanes]
            probs, d_probs = [], []
            inner = jnp.zeros((1, half_slots), f32)
            for block in range(2):
                scores = masked(keys[block], queries, length, block, first_query)
                prob = jnp.exp(scores - r.lse[pl.ds(head, 1), lanes])
                d_prob = jnp.dot(values[block], d_head, preferred_element_type=f32)
                inner += jnp.sum(prob * d_prob, axis=0, keepdims=True)
                probs.append(prob)
                d_probs.append(d_prob)
            d_query = jnp.zeros((HEAD, half_slots), f32)
            for block in range(2):
                d_scores = (probs[block] * (d_probs[block] - inner)).astype(low)
                dk[block][...] += (
                    lax.dot_general(d_scores, queries, NT, preferred_element_type=f32) * scale
                )
                dv[block][...] += lax.dot_general(
                    probs[block].astype(low), d_head, NT, preferred_element_type=f32
                )
                d_query += (
                    jnp.dot(r.kv[block, :HEAD], d_scores, preferred_element_type=f32) * scale
                )
            d_t[at, lanes] = turned_back(d_query, cos_at[:, lanes], sin_at[:, lanes]).astype(low)
        return carry

    send_cross(0, 0)
    lax.fori_loop(0, heads // 2, head_back, 0)
    mlp_sum.step(2)
    send_cross(1, 0)
    lax.fori_loop(heads // 2, heads, head_back, 0)

    def of_half(pair, which):
        return jnp.where(which == 0, pair[0][...], pair[1][...]).T

    kv_give[:HEAD] = of_half(dk, 1 - place.y).astype(low)
    kv_give[HEAD:] = of_half(dv, 1 - place.y).astype(low)
    kv_back = remote(kv_give, r.kv_take, r.kv_sem, (1,), place.over_y)
    kv_back.start()
    send_grads(2, ("near",))
    finish_layer()
    d_key, d_value = of_half(dk, place.y), of_half(dv, place.y)

    lax.fori_loop(2, count, send_cross, 0)
    kv_back.wait_recv()
    d_t[q_rows : q_rows + HEAD] = turned_back(
        d_key + r.kv_take[:HEAD].astype(f32), cos_at, sin_at
    ).astype(low)
    d_t[q_rows + HEAD :] = (d_value + r.kv_take[HEAD:].astype(f32)).astype(low)
    d_qkv = d_t[...].T
    for turn in range(4):
        r.part[:, cut(turn)] = jnp.dot(
            d_qkv, aw[turn, :qkv_rows], preferred_element_type=f32
        ).astype(low)

    each(input_sum, "open")

    def view(ref, at, half):
        return ref.at[pl.ds(0, attn_halves[half]), pl.ds(at * size, size)]

    def zd_view(at, half):
        return r.zd.at[pl.ds(at // 2 * chip_rows, attn_halves[half]), pl.ds(at % 2 * size, size)]

    far_kinds, straight_kinds, last_kinds = (
        ("upper", "lower"),
        ("x_one", "y_two"),
        ("y_one", "x_two"),
    )
    stage = {
        (turn, half): view(*((r.h2, 2 * (turn - 1) + half) if turn < 3 else (r.dm, half)), half)
        for turn in (1, 2, 3)
        for half in range(2)
    }
    attn_own = [view(r.dh2, 2 + half, half) for half in range(2)]
    attn_home = Home(
        place,
        {
            "upper": stage[3, 0],
            "lower": stage[3, 1],
            "x_one": stage[2, 0],
            "y_two": stage[1, 1],
            "y_one": stage[1, 0],
            "x_two": stage[2, 1],
        },
        {
            "upper": zd_view(0, 0),
            "lower": zd_view(1, 1),
            "x_one": zd_view(2, 0),
            "y_two": zd_view(3, 1),
            "y_one": view(r.dm, 2, 0),
            "x_two": view(r.dm, 3, 1),
        },
        r.attn_home_sem,
        lambda ref, group: ref,
    )
    def attn_gradients(turn):
        grad = jnp.dot(d_t[...], r.h1[:, cut(turn)], preferred_element_type=f32)
        grad_o = jnp.dot(r.o_t[...], r.da[:, cut(turn)], preferred_element_type=f32)
        top, bottom = (stage[turn, 0], stage[turn, 1]) if turn else attn_own
        first_rows = attn_halves[0]
        left_over = qkv_rows - first_rows
        top[...] = grad[:first_rows].astype(top.dtype)
        bottom[:left_over] = grad[first_rows:].astype(top.dtype)
        bottom[left_over:] = grad_o.astype(top.dtype)

    def input_end(half):
        inner = place.inner(half)
        input_sum[half].close(r.middle)
        d_norm, d_gain = norm_back(r.inputs_own[inner], r.gain_rows[0:1], r.middle[inner])
        if half:
            d_gain = d_gain + r.gain_part[0]
        r.gain_part[0:1] = d_gain[None]
        r.grad_all[place.block(place.z, half)] = (r.d_middle[inner] + d_norm).astype(low)

    def beside_input(when):
        if when == 0:
            pl.semaphore_wait(r.free_sem, 2)
            attn_gradients(3)
            attn_home.send(far_kinds, 0)
            attn_gradients(2)
            attn_gradients(1)
            layer_share.step(1)
        if when == 1:
            attn_gradients(0)
            attn_home.send(straight_kinds, 0)

            @if_last
            def _():
                send_grads(least, ("near",))

        if when == "ahead":
            layer_share.step(2)
        if when == 2:
            final_start(0)
            finish(0)
        if when == 3:
            layer_share.step(3)
            attn_second()
            finish(1)
        if when == 4:
            start_gains()
            finish(2)
            finish(3)
        if when == 5:
            finish(4)
        if when == 6:
            finish(5)
            for group in range(least):
                home.copy("far", group).wait_send()
                home.copy("near", group).wait_send()

            @if_last
            def _():
                home.copy("far", least).wait_send()
                home.copy("near", least).wait_send()

            q_gather.drain()
            kv_gather.drain()
            out_gather.drain()
        if when == 7:
            finish(6)
            finish(7)

    plane_gains = [
        remote(
            r.gain_part.at[:, pl.ds(turn * size, size)],
            r.gain_in.at[turn - 1],
            r.plane_gain_sem,
            (turn - 1,),
            place.plane[turn, 0],
        )
        for turn in (1, 2, 3)
    ]

    def start_gains():
        for copy in plane_gains:
            copy.start()

    top_half, low_half = pl.ds(0, middle), pl.ds(middle, middle)
    slots = (
        (r.tile_own.at[top_half], r.tile_own.at[low_half]),
        (r.dh2.at[top_half, pl.ds(0, GROUP)], r.dh2.at[top_half, pl.ds(GROUP, GROUP)]),
    )
    halves = (top_half, low_half)
    items = [("own", 0), ("own", 1), ("cross", 0), ("cross", 1)]
    items += [("cross", 2), ("own", 2), ("cross", 3), ("own", 3)]

    def guarded(index, act):
        kind, group = items[index]
        limit = count if kind == "own" else gather.other_count
        if group < groups // 2:
            act()
        else:
            pl.when(group < limit)(act)

    def final_loads(index):
        kind, group = items[index]
        cols = pl.ds(group * GROUP, GROUP)
        if kind == "own":
            for half in range(2):
                yield pltpu.make_async_copy(
                    r.own_grad.at[halves[half], cols],
                    slots[index % 2][half],
                    r.final_sem.at[half, index],
                )
            yield pltpu.make_async_copy(
                r.near.at[:, cols], w.at[2, :, cols], r.final_sem.at[2, index]
            )
        else:
            yield pltpu.make_async_copy(
                r.crossed.at[:, cols], w.at[1, :, cols], r.final_sem.at[2, index]
            )

    def final_out(index):
        kind, group = items[index]
        first = base if kind == "own" else gather.other_base
        to = lanes_at(core * ff + (first + group) * 128, 128)
        for which, into in enumerate((r.grad_gate, r.grad_up, r.grad_down)):
            cols = pl.ds(which * 128, 128)
            for half in range(2):
                source = slots[index % 2][half].at[:, cols]
                yield (
                    half,
                    pltpu.make_async_copy(
                        source, into.at[:, to], r.out_here.at[which, first + group]
                    ),
                    remote(
                        source, into.at[:, to], r.out_there, (which, first + group), place.sibling
                    ),
                )

    def final_start(index):
        def act():
            kind, group = items[index]
            home.copy("near" if kind == "own" else "cross", group).wait_recv()
            for load in final_loads(index):
                load.start()

        guarded(index, act)

    def final_sum(index):
        def act():
            kind, group = items[index]
            cols = pl.ds(group * GROUP, GROUP)
            for load in final_loads(index):
                load.wait()
            for half in range(2):
                if kind == "own":
                    slots[index % 2][half][...] += w[2, halves[half], cols].astype(f32)
                else:
                    slots[index % 2][half][...] = w[1, halves[half], cols].astype(f32)
            for half, here, there in final_out(index):

                @pl.when(core == half)
                def _(here=here):
                    here.start()

                @pl.when(core != half)
                def _(there=there):
                    there.start()

        guarded(index, act)

    def final_free(index):
        def act():
            for half, here, there in final_out(index):

                @pl.when(core == half)
                def _(here=here):
                    here.wait()

                @pl.when(core != half)
                def _(there=there):
                    there.wait_send()

        guarded(index, act)

    def finish(index):
        final_sum(index)
        if index:
            final_free(index - 1)
        if index + 1 < len(items):
            final_start(index + 1)

    def attn_second():
        attn_home.arrive(far_kinds, 0)
        for turn, half, kind in ((1, 0, "upper"), (2, 1, "lower")):
            mine = stage[turn, half]
            mine[...] = (
                mine[...].astype(f32) + attn_home.targets[kind][...].astype(f32)
            ).astype(low)
        attn_home.send(last_kinds, 0)

    chained(input_sum, grad_share, input_end, beside_input, False)
    for copy in plane_gains:
        copy.wait_recv()
    r.gain_sum[...] = r.gain_part[:, :size] + r.gain_in[0] + r.gain_in[1] + r.gain_in[2]
    column_gains = [
        remote(r.gain_sum, r.gain_all.at[index], r.column_gain_sem, (index,), device)
        for index, device in enumerate(place.column)
    ]
    for copy in column_gains:
        copy.start()
    attn_home.arrive(straight_kinds + last_kinds, 0)
    attn_own[0][...] += attn_home.targets["x_one"][...].astype(f32) + attn_home.targets["y_one"][
        ...
    ].astype(f32)
    attn_own[1][...] += attn_home.targets["x_two"][...].astype(f32) + attn_home.targets["y_two"][
        ...
    ].astype(f32)
    attn_out = []
    for half in range(2):
        to = pl.ds(half * attn_halves[0], attn_halves[half])
        attn_out.append(
            pltpu.make_async_copy(attn_own[half], r.grad_attn.at[core, to], r.out_attn.at[half])
        )
        attn_out.append(
            remote(
                attn_own[half], r.grad_attn.at[core, to], r.swap_attn, (half,), place.sibling
            )
        )
    for copy in attn_out:
        copy.start()
    gain_total = r.gain_sum[...]
    for index, copy in enumerate(column_gains):
        copy.wait_recv()
        gain_total += r.gain_all[index]
    r.gain_out[...] = gain_total

    final_free(len(items) - 1)

    def settle(group, carry):
        for kind in range(len(sources)):
            to = lanes_at(core * ff + group * 128, 128)
            into = (r.grad_gate, r.grad_up, r.grad_down)[kind]
            remote(
                r.tile_own.at[top_half, pl.ds(0, 128)],
                into.at[:, to],
                r.out_there,
                (kind, group),
                place.sibling,
            ).wait_recv()
        return carry

    def sent_home(group, carry):
        home.copy("cross", group).wait_send()
        return carry

    lax.fori_loop(0, groups, settle, 0)
    lax.fori_loop(0, count, sent_home, 0)
    for copy in attn_out:
        copy.wait()
    attn_home.drain(0)
    for copy in (kv_copy, kv_back, h1_copy, *plane_gains, *column_gains):
        copy.wait_send()
    for turn, flip in place.plane:
        gain_copy(turn, flip).wait_send()
    for chain in (*input_sum, mlp_sum, mlp_cross, *da_share, layer_share, *grad_share):
        chain.drain()


class Lists:
    def __init__(self):
        self.names, self.items = [], []

    def add(self, name, item):
        self.names.append(name)
        self.items.append(item)


def grouped_kernel(names, counts, *refs):
    given, at = [], 0
    for count in counts:
        given.append(refs[at] if count is None else refs[at : at + count])
        at += count or 1
    layer_kernel(names, *given)


def finish_kernel(
    layer_all,
    grad_all,
    gains,
    gate,
    up,
    down,
    attn,
    layer_out,
    input_grad,
    gain_one,
    gain_two,
    query,
    key_t,
    value_t,
    output_t,
    gate_out,
    up_out,
    down_out,
    attn_here,
    layer_here,
    grad_here,
    gate_here,
    up_here,
    down_here,
    in_sem,
    out_sem,
):
    part = key_t.shape[1]
    place = 2 * lax.axis_index("dp") + lax.axis_index("ctx") // 2
    first = lax.rem(lax.axis_index("ctx"), 2) == 0
    size = 2 * part
    here = (gate_here, up_here, down_here, layer_here, grad_here, attn_here)
    loads = [
        pltpu.make_async_copy(source, into, in_sem.at[index])
        for index, (source, into) in enumerate(
            zip((gate, up, down, layer_all, grad_all, attn), here, strict=True)
        )
    ]
    for load in loads:
        load.start()
    stores = []

    def store(source, into):
        stores.append(pltpu.make_async_copy(source, into, out_sem.at[len(stores)]))
        stores[-1].start()

    def own(tensor):
        return jnp.where(first, tensor[:, :part], tensor[:, part:])

    mine = own(gains[...])
    gain_one[...], gain_two[...] = mine[0], mine[1]
    for index, into in enumerate((gate_out, up_out, down_out)):
        loads[index].wait()
        store(here[index], into)
    for index, into in ((3, layer_out), (4, input_grad)):
        loads[index].wait()
        for turn in range(4):
            at = lanes_at((place ^ turn) * size, size)
            store(here[index].at[:, turn * size : (turn + 1) * size], into.at[:, at])
    loads[5].wait()
    q_rows = query.shape[1] // 2
    start = 0
    for into, size_of in ((query, q_rows), (key_t, HEAD), (value_t, HEAD), (output_t, q_rows)):
        rows = slice(start, start + size_of)
        start += size_of
        both = jnp.concatenate([own(attn_here[which, rows]) for which in range(2)], axis=0)
        into[...] = both if size_of == HEAD else both.T
    for copy in stores:
        copy.wait()


def on_plane(
    hidden_in,
    cotangent,
    lengths,
    norm_attn,
    w_query,
    w_key,
    w_value,
    w_output,
    norm_mlp,
    w_gate,
    w_up,
    w_down,
):
    low, f32 = jnp.bfloat16, jnp.float32
    _, rows, width = hidden_in.shape
    part = w_query.shape[0]
    chip_part, chip_rows = 2 * part, 2 * rows
    z_count = lax.axis_size("mp")
    owned, hops = rows // z_count, z_count - 1
    q_rows = w_query.shape[1] // 2
    qkv_rows = q_rows + 2 * HEAD
    attn_rows = qkv_rows + q_rows
    ff = w_gate.shape[1] // 2
    wide_cols = 3 * ff
    groups = wide_cols // GROUP
    most = (groups + 1) // 2
    held_cols = most * GROUP
    others = 2 * z_count - 1

    slots = np.arange(2 * chip_rows, dtype=np.float32)
    freq = np.float32(THETA) ** -(np.arange(HEAD // 2, dtype=np.float32) * 2.0 / HEAD)
    angle = (freq.astype(np.float32)[:, None] * slots[None]).reshape(HEAD // 2, 2, chip_rows)
    angle = angle.astype(np.float32).swapaxes(0, 1)
    cosine, sine = (jnp.asarray(table(angle), f32) for table in (np.cos, np.sin))

    hbm = pl.BlockSpec(memory_space=pl.ANY)
    smem = pl.BlockSpec(memory_space=pltpu.SMEM)
    vmem = pl.BlockSpec(memory_space=pltpu.VMEM)
    dma, vm = pltpu.SemaphoreType.DMA, pltpu.VMEM
    whole, own = (chip_rows, width), (owned, width)

    ins, outs, scratch = Lists(), Lists(), Lists()
    for name, value, spec in (
        ("hidden", hidden_in[0], hbm),
        ("cotangent", cotangent[0], hbm),
        ("length", lengths.reshape(1, 1), smem),
        ("norm_one", norm_attn, vmem),
        ("norm_two", norm_mlp, vmem),
        ("query", w_query, vmem),
        ("key_t", w_key.T, vmem),
        ("value_t", w_value.T, vmem),
        ("output_t", w_output.T, vmem),
        ("gate", w_gate, hbm),
        ("up", w_up, hbm),
        ("down_t", w_down.T, hbm),
        ("cos", cosine, vmem),
        ("sin", sine, vmem),
    ):
        ins.add(name, (value, spec))
    for name, shape, dtype, spec in (
        ("layer_all", (rows, width), low, vmem),
        ("grad_all", (rows, width), low, vmem),
        ("gain_out", (8, chip_part), f32, vmem),
        ("grad_gate", w_gate.shape, f32, hbm),
        ("grad_up", w_up.shape, f32, hbm),
        ("grad_down", w_gate.shape, f32, hbm),
        ("grad_attn", (2, attn_rows, chip_part), f32, hbm),
        ("own_grad", (chip_part, held_cols), f32, hbm),
        ("stage", (3, chip_part, held_cols), low, hbm),
        ("near", (chip_part, held_cols), low, hbm),
        ("far", (chip_part, held_cols), low, hbm),
        ("crossed", (chip_part, held_cols), low, hbm),
    ):
        outs.add(name, (jax.ShapeDtypeStruct(shape, dtype), spec))
    chain = [vm((rows, width), low), vm((2 * hops, *own), low)]
    ways = [dma((2, hops, SPLIT))] * 2
    cores = dma((2, z_count))
    for name, item in (
        ("block", vm((chip_part, wide_cols), low)),
        ("w", vm((3, chip_part, held_cols), low)),
        ("aw", vm((4, attn_rows, chip_part), low)),
        ("h1", vm(whole, low)),
        ("h2", vm(whole, low)),
        ("h2_x", vm(whole, low)),
        ("dm", vm(whole, low)),
        ("dm_x", vm(whole, low)),
        ("da", vm(whole, low)),
        ("part", vm(whole, low)),
        ("mlp_part", vm(whole, low)),
        ("dh2", vm(whole, f32)),
        ("zd", vm((2 * chip_rows, held_cols), low)),
        ("tile", vm((3, chip_part, GROUP), low)),
        ("tile_own", vm((chip_part, GROUP), f32)),
        ("chain_one", chain),
        ("chain_two", chain),
        ("inputs_own", vm(own, f32)),
        ("middle", vm(own, f32)),
        ("mlp", vm(own, f32)),
        ("d_middle", vm(own, f32)),
        ("gains", vm((8, chip_part), f32)),
        ("gains_all", vm((8, 8, chip_part), f32)),
        ("gain_rows", vm((8, width), f32)),
        ("kv", vm((2, 2 * HEAD, chip_rows), low)),
        ("q_t", vm((q_rows, chip_rows), low)),
        ("o_t", vm((q_rows, chip_rows), low)),
        ("lse", vm((8, chip_rows), f32)),
        ("kv_take", vm((2 * HEAD, chip_rows), low)),
        ("gain_part", vm((8, width), f32)),
        ("gain_in", vm((3, 8, chip_part), f32)),
        ("gain_sum", vm((8, chip_part), f32)),
        ("gain_all", vm((others, 8, chip_part), f32)),
        ("load_sem", dma((4,))),
        ("core_sem", dma((2, 2))),
        ("gain_sem", dma((2, 8))),
        ("attn_x", dma((2, 6))),
        ("attn_y", dma((2, 6))),
        ("attn_far", dma((2, 6))),
        ("wide_here", dma((3, groups))),
        ("wide_there", dma((2, 3, groups))),
        ("dm_sem", dma((2, 1))),
        ("h1_sem", dma((2, 1))),
        ("kv_sem", dma((2, 2))),
        ("wide_x", dma((2, most))),
        ("wide_y", dma((2, most))),
        ("wide_far", dma((2, most))),
        ("dm_cross_sem", dma((2, 1))),
        ("h2_cross_sem", dma((2, 2, z_count))),
        ("h2_across_sem", dma((2, 2, z_count))),
        ("keep_sem", dma((2,))),
        ("home_sem", dma((2, 3, most))),
        ("add_sem", dma((most,))),
        ("attn_home_sem", dma((2, 6, 1))),
        ("final_sem", dma((3, 2 * most))),
        ("out_here", dma((3, groups))),
        ("out_there", dma((2, 3, groups))),
        ("out_attn", dma((2,))),
        ("swap_attn", dma((2, 2))),
        ("plane_gain_sem", dma((2, 3))),
        ("column_gain_sem", dma((2, others))),
        ("free_sem", pltpu.SemaphoreType.REGULAR),
        ("quiet_sem", pltpu.SemaphoreType.REGULAR),
        ("chain_sem", pltpu.SemaphoreType.REGULAR),
        ("branch_sems", ([cores] + ways) * 2),
        ("back_sems", ([cores] + ways) * 2),
        ("mlp_sems", [cores] + ways),
        ("input_sems", ([cores] + ways) * 2),
        ("h2_sems", (ways + [cores]) * 2),
        ("dm_x_sems", ways + [cores]),
        ("back_cross_sems", [cores] * 4),
        ("mlp_cross_sems", [cores, cores]),
        ("da_sems", (ways + [cores]) * 2),
        ("layer_sems", ways),
        ("grad_sems", ways * 2),
    ):
        scratch.add(name, item)

    counts = [None] * (len(ins.items) + len(outs.items))
    flat = []
    for item in scratch.items:
        counts.append(len(item) if isinstance(item, list) else None)
        flat += item if isinstance(item, list) else [item]
    names = ins.names + outs.names + scratch.names
    results = pl.pallas_call(
        functools.partial(grouped_kernel, names, counts),
        out_shape=[shape for shape, _ in outs.items],
        in_specs=[spec for _, spec in ins.items],
        out_specs=[spec for _, spec in outs.items],
        scratch_shapes=flat,
        name="layer",
        compiler_params=pltpu.CompilerParams(
            collective_id=1, has_side_effects=True, vmem_limit_bytes=65_400 * 2**10
        ),
    )(*(value for value, _ in ins.items))
    layer_all, grad_all, gain_sums, grad_gate, grad_up, grad_down, grad_attn = results[:7]
    gate_like = jax.ShapeDtypeStruct(w_gate.shape, f32)
    tokens = jax.ShapeDtypeStruct((rows, width), low)
    gain_like = jax.ShapeDtypeStruct((part,), f32)
    square = jax.ShapeDtypeStruct((part, 2 * q_rows), f32)
    flat_heads = jax.ShapeDtypeStruct((2 * HEAD, part), f32)
    (
        layer_out,
        input_grad,
        gain_one,
        gain_two,
        grad_query,
        grad_key_t,
        grad_value_t,
        grad_output_t,
        grad_gate,
        grad_up,
        grad_down_t,
    ) = pl.pallas_call(
        finish_kernel,
        out_shape=[tokens] * 2
        + [gain_like] * 2
        + [square, flat_heads, flat_heads, square]
        + [gate_like] * 3,
        in_specs=[hbm, hbm, vmem, hbm, hbm, hbm, hbm],
        out_specs=[hbm] * 2 + [vmem] * 6 + [hbm] * 3,
        scratch_shapes=[vm((2, attn_rows, chip_part), f32)]
        + [vm((rows, width), low)] * 2
        + [vm(w_gate.shape, f32)] * 3
        + [dma((6,)), dma((11,))],
        name="finish",
        compiler_params=pltpu.CompilerParams(vmem_limit_bytes=65_400 * 2**10),
    )(layer_all, grad_all, gain_sums, grad_gate, grad_up, grad_down, grad_attn)
    return (
        layer_out[None],
        input_grad[None],
        gain_one,
        grad_query,
        grad_key_t.T,
        grad_value_t.T,
        grad_output_t.T,
        gain_two,
        grad_gate,
        grad_up,
        grad_down_t.T,
    )


def solution(mesh):
    plane = dict(mesh.shape) == {"dp": 2, "ctx": 4, "mp": 4}
    return jax.shard_map(
        on_plane if plane else any_mesh,
        mesh=mesh,
        in_specs=(
            P("dp", "ctx", None),
            P("dp", "ctx", None),
            P("dp"),
            P(("dp", "ctx")),
            P(("dp", "ctx"), "mp"),
            P(("dp", "ctx"), "mp"),
            P(("dp", "ctx"), "mp"),
            P("mp", ("dp", "ctx")),
            P(("dp", "ctx")),
            P(("dp", "ctx"), "mp"),
            P(("dp", "ctx"), "mp"),
            P("mp", ("dp", "ctx")),
        ),
        out_specs=(
            P("dp", "ctx", None),
            P("dp", "ctx", None),
            P(("dp", "ctx")),
            P(("dp", "ctx"), "mp"),
            P(("dp", "ctx"), "mp"),
            P(("dp", "ctx"), "mp"),
            P("mp", ("dp", "ctx")),
            P(("dp", "ctx")),
            P(("dp", "ctx"), "mp"),
            P(("dp", "ctx"), "mp"),
            P("mp", ("dp", "ctx")),
        ),
        check_vma=False,
    )
```
